32 devices in a mesh: dp: 8 (over z, x), blk: 4 (over y, core).
Axes of the slice: x: 2, y: 2, z: 4, core: 2. Of those that a mesh axis runs over, the one named last changes fastest.
Arguments:
- tokens: bfloat16 [8, 1024, 1024], P('dp', 'blk'), may hold values from -6 to 6
- cotangent: bfloat16 [8, 1024, 1024], P('dp', 'blk'), may hold values from -6 to 6
- stop_scale: int32 [8, 11], P('dp'), may hold values from 0 to 9, as said below
- labels: int32 [8, 12], P('dp'), may hold values from 0 to 1000
- class_table: bfloat16 [1001, 1024], replicated, may hold values from -6 to 6
- head_scale: float32 [2, 16], replicated, may hold values from 2.2 to 3
- w_qkv: bfloat16 [2, 1024, 3072], P(None, ('dp', 'blk')), may hold values from -0.1875 to 0.1875
- w_proj: bfloat16 [2, 1024, 1024], P(None, ('dp', 'blk')), may hold values from -0.75 to 0.75
- w_up: bfloat16 [2, 1024, 4096], P(None, ('dp', 'blk')), may hold values from -0.1875 to 0.1875
- w_down: bfloat16 [2, 4096, 1024], P(None, ('dp', 'blk')), may hold values from -0.09375 to 0.09375
- w_ada: bfloat16 [2, 1024, 6144], P(None, ('dp', 'blk')), may hold values from -0.1875 to 0.1875
Outputs:
- output: bfloat16 [8, 1024, 1024], P('dp', 'blk')
- tokens_grad: bfloat16 [8, 1024, 1024], P('dp', 'blk')
- class_table_grad: float32 [1001, 1024], replicated
- head_scale_grad: float32 [2, 16], replicated
- w_qkv_grad: float32 [2, 1024, 3072], P(None, ('dp', 'blk'))
- w_proj_grad: float32 [2, 1024, 1024], P(None, ('dp', 'blk'))
- w_up_grad: float32 [2, 1024, 4096], P(None, ('dp', 'blk'))
- w_down_grad: float32 [2, 4096, 1024], P(None, ('dp', 'blk'))
- w_ada_grad: float32 [2, 1024, 6144], P(None, ('dp', 'blk'))
The draws below stay inside these ranges and needn't reach their ends.
Inputs may be any that keep to these rules, and one draw needn't show every extreme that they name: `stop_scale`: entries are 0 or 6 to 9; in every stream the nonzero entries come first, and their items hold at most 1024 tokens together.
All inputs are finite; a program needn't handle non-finite values.
Results may differ from the reference program's by a relative error of at most 0.035.
Values may be sent and summed in bfloat16 or wider, within the bound.
A program may use at most 512 MiB of HBM per device.

```python
import jax
import jax.numpy as jnp
from jax import lax

D = 1024
HEADS = 16
FF = 4096
CLASSES = 1001
LAYERS = 2
STREAM_LEN = 1024
STREAMS = 8
ITEMS = 11


def draw_stop_scale(key, part):
    picks = jax.random.randint(key, (STREAMS, ITEMS), 6, 10, dtype=jnp.int32)
    areas = jnp.array((1, 4, 9, 16, 25, 36, 64, 100, 169), dtype=jnp.int32)
    levels = jnp.arange(9, dtype=jnp.int32)
    counts = jnp.sum(jnp.where(levels[None, None, :] < picks[:, :, None], areas[None, None, :], 0), axis=2).astype(jnp.int32)
    ends = jnp.cumsum(counts, axis=1).astype(jnp.int32)
    return jnp.where(ends <= STREAM_LEN, picks, 0).astype(jnp.int32)


def plant(entries, stream_key, smallest, largest):
    index_at = [jax.random.randint(jax.random.fold_in(stream_key, axis), (), 0, length) for axis, length in enumerate(entries.shape)]
    longest = entries.shape.index(max(entries.shape))
    neighbour = index_at[:longest] + [(index_at[longest] + 1) % entries.shape[longest]] + index_at[longest + 1:]
    return entries.at[tuple(index_at)].set(smallest).at[tuple(neighbour)].set(largest)


def shard_levels(stream_key, shape, shards, least, largest):
    level, own = 1.0, jax.random.fold_in(stream_key, 6)
    for axis_at, parts in shards:
        draws = jnp.exp(jax.random.uniform(jax.random.fold_in(own, axis_at), (parts,), jnp.float32, least / len(shards), largest / len(shards)))
        level = level * jnp.repeat(draws, shape[axis_at] // parts).reshape([-1 if axis == axis_at else 1 for axis in range(len(shape))])
    return level


def normal_values(key, extent, scale, reach, pieces=(), held_as=jnp.bfloat16):
    loudness = shard_levels(key, extent, pieces, -0.22, 0.18) if pieces else 1.0
    values = jax.random.normal(key, extent, jnp.float32) * scale * loudness
    return jnp.minimum(jnp.maximum(values, -reach), reach).astype(held_as)


def setup_inputs(seed: int = 0) -> dict:
    arg_keys = jax.random.split(jax.random.key(seed), 12)
    tokens = normal_values(arg_keys[0], (STREAMS, STREAM_LEN, D), 1.0, 6.0, ((0, 8), (1, 4)))
    cotangent = normal_values(arg_keys[1], (STREAMS, STREAM_LEN, D), 1.0, 6.0, ((0, 8), (1, 4)))
    stop_scale = draw_stop_scale(jax.random.fold_in(arg_keys[11], 71), 0)
    labels = plant(jax.random.randint(arg_keys[3], (STREAMS, ITEMS + 1), 0, CLASSES), jax.random.fold_in(arg_keys[3], 1), 0, CLASSES - 1).astype(jnp.int32)
    class_table = normal_values(arg_keys[4], (CLASSES, D), 1.0, 6.0)
    head_scale = jnp.clip(jax.random.uniform(arg_keys[5], (LAYERS, HEADS), jnp.float32, 2.2, 3.0), 2.2, 3.0)
    w_qkv = normal_values(arg_keys[6], (LAYERS, D, 3 * D), D ** -0.5, 0.1875, ((1, 32),))
    w_proj = normal_values(arg_keys[7], (LAYERS, D, D), (D // 16) ** -0.5, 0.75, ((1, 32),))
    w_up = normal_values(arg_keys[8], (LAYERS, D, FF), D ** -0.5, 0.1875, ((1, 32),))
    w_down = normal_values(arg_keys[9], (LAYERS, FF, D), FF ** -0.5, 0.09375, ((1, 32),))
    w_ada = normal_values(arg_keys[10], (LAYERS, D, 6 * D), D ** -0.5, 0.1875, ((1, 32),))
    return {"tokens": tokens, "cotangent": cotangent, "stop_scale": stop_scale, "labels": labels, "class_table": class_table, "head_scale": head_scale, "w_qkv": w_qkv, "w_proj": w_proj, "w_up": w_up, "w_down": w_down, "w_ada": w_ada}


@jax.custom_vjp
def low(v):
    return lax.optimization_barrier(v.astype(jnp.bfloat16)).astype(jnp.float32)

@jax.custom_vjp
def low_back(v):
    return v

def low_keep(v):
    return (low(v), None)

def low_pass(kept, grad):
    return (grad,)

def back_keep(v):
    return (v, None)

def back_low(kept, grad):
    return (low(grad),)
low.defvjp(low_keep, low_pass)
low_back.defvjp(back_keep, back_low)
patch_areas = (1, 4, 9, 16, 25, 36, 64, 100, 169)
scale_starts = (1, 5, 14, 30, 55, 91, 155, 255)

def token_meta(stops, length):
    areas = jnp.array(patch_areas, dtype=jnp.int32)
    levels = jnp.arange(9, dtype=jnp.int32)
    counts = lax.optimization_barrier(jnp.sum(jnp.where(levels[None, :] < stops[:, None], areas[None, :], 0), axis=1)).astype(jnp.int32)
    ends = jnp.cumsum(counts).astype(jnp.int32)
    places = jnp.arange(length, dtype=jnp.int32)
    passed = places[:, None] >= ends[None, :]
    item = lax.optimization_barrier(jnp.sum(passed.astype(jnp.int32), axis=1)).astype(jnp.int32)
    begin = lax.optimization_barrier(jnp.sum(jnp.where(passed, counts[None, :], 0), axis=1)).astype(jnp.int32)
    inner = places - begin
    bounds = jnp.array(scale_starts, dtype=jnp.int32)
    level = lax.optimization_barrier(jnp.sum((inner[:, None] >= bounds[None, :]).astype(jnp.int32), axis=1)).astype(jnp.int32)
    level = jnp.where(item == stops.shape[0], 0, level).astype(jnp.int32)
    return (item, level)

def modulate(values, scale, shift):
    centre = lax.optimization_barrier(jnp.mean(values, axis=-1, keepdims=True))
    centred = values - centre
    spread = lax.optimization_barrier(jnp.mean(centred * centred, axis=-1, keepdims=True))
    return centred * lax.rsqrt(spread + 1e-06) * (1.0 + scale) + shift

def qk_norm(query, keys, scale):
    query = query * lax.rsqrt(lax.optimization_barrier(jnp.sum(query * query, axis=-1, keepdims=True)) + 1e-06) * jnp.exp(scale)[None, :, None]
    keys = keys * lax.rsqrt(lax.optimization_barrier(jnp.sum(keys * keys, axis=-1, keepdims=True)) + 1e-06)
    return (query, keys)

def dense(left, right):
    return jnp.dot(left, right, precision=lax.Precision.HIGHEST)

def block(state, modulation, item, visible, weights, scale, limit_row):
    w_query, w_out, w_first, w_second = weights
    gamma1, gamma2, scale1, scale2, shift1, shift2 = jnp.split(modulation[item], 6, axis=1)
    length, width = state.shape
    heads = scale.shape[0]
    size = width // heads
    normed = modulate(state, scale1, shift1)
    packed = low_back(dense(low(normed), w_query))
    query, keys, values = jnp.split(packed, 3, axis=1)
    query, keys = qk_norm(query.reshape(length, heads, size), keys.reshape(length, heads, size), scale)
    query = low(query)
    keys = low(keys)
    values = low(values.reshape(length, heads, size))
    scores = low_back(jnp.einsum('qhe,khe->hqk', query, keys, precision=lax.Precision.HIGHEST))
    limit = limit_row[:, None, None]
    weights_exp = jnp.where(visible[None], jnp.exp(scores - limit), 0.0)
    total = lax.optimization_barrier(jnp.sum(weights_exp, axis=-1))
    mixed = jnp.einsum('hqk,khe->qhe', low(weights_exp), values, precision=lax.Precision.HIGHEST)
    mixed = (mixed / total.transpose(1, 0)[:, :, None]).reshape(length, width)
    branch = low_back(dense(low(low_back(mixed)), w_out))
    state = state + gamma1 * branch
    normed = modulate(state, scale2, shift2)
    hidden = low_back(dense(low(normed), w_first))
    hidden = jax.nn.gelu(hidden, approximate=True)
    result = low_back(dense(low(hidden), w_second))
    return state + gamma2 * result

def stream(state, stops, names, table, scales, limits, w_qkv, w_proj, w_up, w_down, w_ada):
    item, level = token_meta(stops, state.shape[0])
    visible = (item[:, None] == item[None, :]) & (level[None, :] <= level[:, None])
    cond = low(jax.nn.silu(table[names]))
    for layer in range(w_qkv.shape[0]):
        modulation = low_back(dense(cond, w_ada[layer]))
        state = block(state, modulation, item, visible, (w_qkv[layer], w_proj[layer], w_up[layer], w_down[layer]), scales[layer], limits[layer])
    return state

def reference(tokens, cotangent, stop_scale, labels, class_table, head_scale, w_qkv, w_proj, w_up, w_down, w_ada):
    widen = lambda value: value.astype(jnp.float32)
    limits = jnp.exp(widen(head_scale))

    def forward(states, table, scales, w_one, w_two, w_three, w_four, w_five):

        def single(state, stops, names):
            return stream(state, stops, names, table, scales, limits, w_one, w_two, w_three, w_four, w_five)
        single = jax.checkpoint(single)

        def step(carry, inputs):
            return (carry, single(inputs[0], inputs[1], inputs[2]))
        carry, results = lax.scan(step, None, (states, stop_scale, labels))
        return results
    results, pull = jax.vjp(forward, widen(tokens), widen(class_table), widen(head_scale), widen(w_qkv), widen(w_proj), widen(w_up), widen(w_down), widen(w_ada))
    grads = pull(widen(cotangent))
    return (results.astype(jnp.bfloat16), grads[0].astype(jnp.bfloat16), grads[1], grads[2], grads[3], grads[4], grads[5], grads[6], grads[7])
```

```python
from functools import partial

import jax
import jax.numpy as jnp
from jax import lax
from jax.sharding import PartitionSpec as P

patch_areas = (1, 4, 9, 16, 25, 36, 64, 100, 169)
scale_starts = (1, 5, 14, 30, 55, 91, 155, 255)
f32 = jnp.float32
bf16 = jnp.bfloat16


def token_meta(stops, length):
    areas = jnp.array(patch_areas, dtype=jnp.int32)
    levels = jnp.arange(9, dtype=jnp.int32)
    counts = jnp.sum(jnp.where(levels[None, :] < stops[:, None], areas[None, :], 0), axis=1)
    ends = jnp.cumsum(counts)
    places = jnp.arange(length, dtype=jnp.int32)
    passed = places[:, None] >= ends[None, :]
    item = jnp.sum(passed.astype(jnp.int32), axis=1)
    begin = jnp.sum(jnp.where(passed, counts[None, :], 0), axis=1)
    inner = places - begin
    bounds = jnp.array(scale_starts, dtype=jnp.int32)
    level = jnp.sum((inner[:, None] >= bounds[None, :]).astype(jnp.int32), axis=1)
    level = jnp.where(item == stops.shape[0], 0, level)
    return (item, level)


def modulate(values, scale, shift):
    centre = jnp.mean(values, axis=-1, keepdims=True)
    centred = values - centre
    spread = jnp.mean(centred * centred, axis=-1, keepdims=True)
    return centred * lax.rsqrt(spread + 1e-06) * (1.0 + scale) + shift


def qk_norm(query, keys, scale):
    query = (
        query
        * lax.rsqrt(jnp.sum(query * query, axis=-1, keepdims=True) + 1e-06)
        * jnp.exp(scale)[None, :, None]
    )
    keys = keys * lax.rsqrt(jnp.sum(keys * keys, axis=-1, keepdims=True) + 1e-06)
    return (query, keys)


def mm(left, right):
    return jnp.dot(left, right, preferred_element_type=f32)


def mm_t(left, right):
    return lax.dot_general(left, right, (((1,), (1,)), ((), ())), preferred_element_type=f32)


def rows_mm(left, right, precision=None):
    return lax.dot_general(
        left, right, (((0,), (0,)), ((), ())), precision=precision, preferred_element_type=f32
    )


def gather(values, axes):
    return lax.all_gather(values, axes, axis=0, tiled=True)


def scatter(values, axes):
    return lax.psum_scatter(values, axes, scatter_dimension=0, tiled=True)


def per_device(
    tokens,
    cotangent,
    stop_scale,
    labels,
    class_table,
    head_scale,
    w_qkv,
    w_proj,
    w_up,
    w_down,
    w_ada,
):
    rows, width = tokens.shape[1:]
    layers, heads = head_scale.shape
    size = width // heads
    dps, blks = lax.axis_size("dp"), lax.axis_size("blk")
    count = dps * blks
    length = rows * blks
    d, b = lax.axis_index("dp"), lax.axis_index("blk")
    own_heads = heads // blks
    piece = own_heads * size
    wrows = w_qkv.shape[1]
    ffrows = w_down.shape[1]
    ff = ffrows * dps
    slots = labels.shape[1]

    item_all, level_all = token_meta(stop_scale[0], length)
    item_own = lax.dynamic_slice_in_dim(item_all, b * rows, rows)
    visible = (item_all[:, None] == item_all[None, :]) & (level_all[None, :] <= level_all[:, None])
    item_onehot = (item_own[:, None] == jnp.arange(slots, dtype=jnp.int32)[None, :]).astype(f32)

    labels_all = gather(labels, "dp").reshape(-1)
    chosen = labels_all[:, None] == jnp.arange(class_table.shape[0], dtype=jnp.int32)[None, :]
    cond = mm(chosen.astype(bf16), class_table)
    cond_act, silu_pull = jax.vjp(jax.nn.silu, cond)
    cond_low = cond_act.astype(bf16)

    wide = w_ada.shape[2]
    columns = layers * wide // count
    ada_cols = w_ada.transpose(1, 0, 2).reshape(wrows, count, columns).transpose(1, 0, 2)
    ada_cols = lax.all_to_all(ada_cols, ("dp", "blk"), 0, 0, tiled=True)
    ada_part = mm(cond_low, ada_cols.reshape(count * wrows, columns))
    ada_part = lax.all_to_all(ada_part.reshape(dps, slots, columns), "dp", 0, 0, tiled=True)
    ada_all = lax.all_gather(ada_part, "blk", axis=1, tiled=False)
    ada_all = ada_all.transpose(2, 0, 1, 3).reshape(slots, layers, wide)

    qkv_cols = w_qkv.reshape(layers, wrows, 3, blks, piece).transpose(3, 0, 1, 2, 4)
    up_cols = w_up.reshape(layers, wrows, dps, blks, ffrows).transpose(3, 0, 1, 2, 4)
    moved = jnp.concatenate(
        [
            qkv_cols.reshape(blks, layers, wrows, 3 * piece),
            up_cols.reshape(blks, layers, wrows, ff),
        ],
        axis=3,
    )
    moved = lax.all_to_all(moved, "blk", 0, 0, tiled=True)
    moved = moved.transpose(1, 0, 2, 3).reshape(layers, blks * wrows, 3 * piece + ff)
    to_heads = [(i, (i % dps) * blks + i // dps) for i in range(count)]
    to_rows = [(j, i) for i, j in to_heads]
    proj_own = lax.ppermute(w_proj, ("dp", "blk"), to_heads)
    weights = []
    for layer in range(layers):
        weights.append(
            (
                gather(moved[layer, :, : 3 * piece], "dp"),
                gather(proj_own[layer], "dp"),
                gather(moved[layer, :, 3 * piece :], "dp"),
                gather(w_down[layer], "dp"),
            )
        )

    def modulations(layer):
        per_token = jnp.dot(item_onehot, ada_all[:, layer], precision=lax.Precision.HIGHEST)
        return jnp.split(per_token, 6, axis=1)

    def split_heads(values):
        return values.reshape(length, own_heads, size)

    state = tokens[0].astype(f32)
    saved = []
    for layer in range(layers):
        w_query, w_out, w_first, w_second = weights[layer]
        own_scale = lax.dynamic_slice_in_dim(head_scale[layer], b * own_heads, own_heads)
        bound = jnp.exp(own_scale)
        gamma1, gamma2, scale1, scale2, shift1, shift2 = modulations(layer)
        normed_one = gather(modulate(state, scale1, shift1).astype(bf16), "blk")
        packed = mm(normed_one, w_query)
        query, keys, values = jnp.split(packed, 3, axis=1)
        (query, keys), pull_norm = jax.vjp(
            qk_norm, split_heads(query), split_heads(keys), own_scale
        )
        q_low, k_low = query.astype(bf16), keys.astype(bf16)
        v_low = split_heads(values.astype(bf16))
        scores = jnp.einsum("qhe,khe->hqk", q_low, k_low, preferred_element_type=f32)
        exps = jnp.where(visible[None], jnp.exp(scores - bound[:, None, None]), 0.0)
        total = jnp.sum(exps, axis=-1)
        mixed = jnp.einsum("hqk,khe->qhe", exps.astype(bf16), v_low, preferred_element_type=f32)
        mixed = (mixed / total.transpose(1, 0)[..., None]).reshape(length, piece)
        mixed_low = mixed.astype(bf16)
        branch = scatter(mm(mixed_low, w_out).astype(bf16), "blk").astype(f32)
        state_mid = state + gamma1 * branch
        normed_two = gather(modulate(state_mid, scale2, shift2).astype(bf16), "blk")
        upward = mm(normed_two, w_first)
        hidden_low = jax.nn.gelu(upward, approximate=True).astype(bf16)
        result = scatter(mm(hidden_low, w_second).astype(bf16), "blk").astype(f32)
        saved.append(
            (
                state,
                state_mid,
                normed_one,
                normed_two,
                q_low,
                k_low,
                v_low,
                pull_norm,
                mixed,
                total,
                branch,
                upward,
                hidden_low,
                result,
            )
        )
        state = state_mid + gamma2 * result
    output = state.astype(bf16)[None]

    grad = cotangent[0].astype(f32)
    cond_grad = 0.0
    scale_grads, pieces = [None] * layers, [None] * layers
    for layer in reversed(range(layers)):
        w_query, w_out, w_first, w_second = weights[layer]
        (
            state,
            state_mid,
            normed_one,
            normed_two,
            q_low,
            k_low,
            v_low,
            pull_norm,
            mixed,
            total,
            branch,
            upward,
            hidden_low,
            result,
        ) = saved[layer]
        own_scale = lax.dynamic_slice_in_dim(head_scale[layer], b * own_heads, own_heads)
        bound = jnp.exp(own_scale)
        gamma1, gamma2, scale1, scale2, shift1, shift2 = modulations(layer)
        gamma2_grad = grad * result
        result_grad = gather((gamma2 * grad).astype(bf16), "blk")
        hidden_grad = mm_t(result_grad, w_second)
        _, pull_gelu = jax.vjp(partial(jax.nn.gelu, approximate=True), upward)
        upward_grad = pull_gelu(hidden_grad)[0].astype(bf16)
        normed_grad = scatter(mm_t(upward_grad, w_first).astype(bf16), "blk").astype(f32)
        down_grad = scatter(rows_mm(hidden_low, result_grad).astype(bf16), "dp").astype(f32)
        up_grad = scatter(rows_mm(normed_two, upward_grad).astype(bf16), "dp")
        _, pull_second = jax.vjp(modulate, state_mid, scale2, shift2)
        mid_part, scale2_grad, shift2_grad = pull_second(normed_grad)
        mid_grad = grad + mid_part
        gamma1_grad = mid_grad * branch
        branch_grad = gather((gamma1 * mid_grad).astype(bf16), "blk")
        mixed_grad = mm_t(branch_grad, w_out).astype(bf16)
        proj_grad = scatter(rows_mm(mixed.astype(bf16), branch_grad).astype(bf16), "dp")
        row_term = jnp.sum(split_heads(mixed_grad.astype(f32) * mixed), axis=-1).transpose(1, 0)
        out_grad = split_heads(mixed_grad)
        scores = jnp.einsum("qhe,khe->hqk", q_low, k_low, preferred_element_type=f32)
        exps = jnp.where(visible[None], jnp.exp(scores - bound[:, None, None]), 0.0)
        probs = exps / total[..., None]
        prob_grad = jnp.einsum("qhe,khe->hqk", out_grad, v_low, preferred_element_type=f32)
        score_grad = (probs * (prob_grad - row_term[..., None])).astype(bf16)
        query_grad = jnp.einsum("hqk,khe->qhe", score_grad, k_low, preferred_element_type=f32)
        key_grad = jnp.einsum("hqk,qhe->khe", score_grad, q_low, preferred_element_type=f32)
        scaled = (out_grad.astype(f32) / total.transpose(1, 0)[..., None]).astype(bf16)
        value_grad = jnp.einsum("hqk,qhe->khe", exps.astype(bf16), scaled, preferred_element_type=f32)
        raw_query, raw_keys, scale_grad = pull_norm((query_grad, key_grad))
        packed_grad = jnp.concatenate(
            [x.reshape(length, piece) for x in (raw_query, raw_keys, value_grad)], axis=1
        ).astype(bf16)
        normed_grad = scatter(mm_t(packed_grad, w_query).astype(bf16), "blk").astype(f32)
        qkv_grad = scatter(rows_mm(normed_one, packed_grad).astype(bf16), "dp")
        _, pull_first = jax.vjp(modulate, state, scale1, shift1)
        input_part, scale1_grad, shift1_grad = pull_first(normed_grad)
        grad = mid_grad + input_part
        scale_grads[layer] = lax.dynamic_update_slice_in_dim(
            jnp.zeros((heads,), f32), scale_grad, b * own_heads, 0
        )
        token_mod_grad = jnp.concatenate(
            [gamma1_grad, gamma2_grad, scale1_grad, scale2_grad, shift1_grad, shift2_grad], axis=1
        )
        item_grad = rows_mm(item_onehot, token_mod_grad, lax.Precision.HIGHEST)
        item_grad = item_grad.reshape(slots, blks, wide // blks).transpose(1, 0, 2)
        item_grad = scatter(item_grad, "blk").astype(bf16)
        item_grad = gather(item_grad, ("dp", "blk")).reshape(dps, blks, slots, wide // blks)
        item_grad = item_grad.transpose(0, 2, 1, 3).reshape(dps * slots, wide)
        cond_grad = cond_grad + mm_t(item_grad, w_ada[layer])
        own_cond = lax.dynamic_slice_in_dim(cond_low, (d * blks + b) * wrows, wrows, axis=1)
        ada_grad = rows_mm(own_cond, item_grad)
        back = jnp.concatenate([qkv_grad, up_grad], axis=1)
        back = lax.all_to_all(back.reshape(blks, wrows, 3 * piece + ff), "blk", 0, 0, tiled=True)
        qkv_grad = back[:, :, : 3 * piece].reshape(blks, wrows, 3, piece)
        qkv_grad = qkv_grad.transpose(1, 2, 0, 3).reshape(wrows, 3 * width).astype(f32)
        up_grad = back[:, :, 3 * piece :].reshape(blks, wrows, dps, ffrows)
        up_grad = up_grad.transpose(1, 2, 0, 3).reshape(wrows, ff * blks).astype(f32)
        proj_grad = lax.ppermute(proj_grad, ("dp", "blk"), to_rows).astype(f32)
        pieces[layer] = (qkv_grad, proj_grad, up_grad, down_grad, ada_grad)
    cond_grad = gather(cond_grad.T, ("dp", "blk")).T
    cond_pre = silu_pull(cond_grad)[0]
    table_grad = rows_mm(chosen.astype(f32), cond_pre, lax.Precision.HIGHEST)
    head_grad = lax.psum(jnp.stack(scale_grads), ("dp", "blk"))
    stacked = [jnp.stack([one[i] for one in pieces]) for i in range(5)]
    return (output, grad.astype(bf16)[None], table_grad, head_grad, *stacked)


def solution(mesh):
    in_specs = (
        P("dp", "blk", None),
        P("dp", "blk", None),
        P("dp", None),
        P("dp", None),
        P(),
        P(),
        P(None, ("dp", "blk"), None),
        P(None, ("dp", "blk"), None),
        P(None, ("dp", "blk"), None),
        P(None, ("dp", "blk"), None),
        P(None, ("dp", "blk"), None),
    )
    out_specs = (
        P("dp", "blk", None),
        P("dp", "blk", None),
        P(),
        P(),
        P(None, ("dp", "blk"), None),
        P(None, ("dp", "blk"), None),
        P(None, ("dp", "blk"), None),
        P(None, ("dp", "blk"), None),
        P(None, ("dp", "blk"), None),
    )
    return jax.shard_map(
        per_device, mesh=mesh, in_specs=in_specs, out_specs=out_specs, check_vma=False
    )
```

```python
from functools import partial

import jax
import jax.numpy as jnp
from jax import lax
from jax.experimental import pallas as pl
from jax.experimental.pallas import tpu as pltpu
from jax.sharding import PartitionSpec as P

patch_areas = (1, 4, 9, 16, 25, 36, 64, 100, 169)
scale_starts = (1, 5, 14, 30, 55, 91, 155, 255)
f32 = jnp.float32
bf16 = jnp.bfloat16
MESH = pl.DeviceIdType.MESH
TILE = 256
HALF = 128
STEP = 32


def token_meta(stops, length):
    areas = jnp.array(patch_areas, dtype=jnp.int32)
    levels = jnp.arange(9, dtype=jnp.int32)
    counts = jnp.sum(jnp.where(levels[None, :] < stops[:, None], areas[None, :], 0), axis=1)
    ends = jnp.cumsum(counts)
    places = jnp.arange(length, dtype=jnp.int32)
    passed = places[:, None] >= ends[None, :]
    item = jnp.sum(passed.astype(jnp.int32), axis=1)
    begin = jnp.sum(jnp.where(passed, counts[None, :], 0), axis=1)
    inner = places - begin
    bounds = jnp.array(scale_starts, dtype=jnp.int32)
    level = jnp.sum((inner[:, None] >= bounds[None, :]).astype(jnp.int32), axis=1)
    level = jnp.where(item == stops.shape[0], 0, level)
    return (item, level)


def mm(left, right):
    return jnp.dot(left, right, preferred_element_type=f32)


def mm_t(left, right):
    return lax.dot_general(left, right, (((1,), (1,)), ((), ())), preferred_element_type=f32)


def rows_mm(left, right, precision=None):
    return lax.dot_general(
        left, right, (((0,), (0,)), ((), ())), precision=precision, preferred_element_type=f32
    )


def gather(values, axes):
    return lax.all_gather(values, axes, axis=0, tiled=True)


def scatter(values, axes):
    return lax.psum_scatter(values, axes, scatter_dimension=0, tiled=True)


def partners():
    d, b = lax.axis_index("dp"), lax.axis_index("blk")
    return (d, b + 1 - 2 * (b % 2)), (d, (b + 2) % 4)


def greet(sibling, peer):
    barrier = pltpu.get_barrier_semaphore()
    for other in (sibling, peer):
        pl.semaphore_signal(barrier, inc=1, device_id=other, device_id_type=MESH)
    pl.semaphore_wait(barrier, 2)


def remote(src, dst, send, recv, target):
    return pltpu.make_async_remote_copy(
        src_ref=src, dst_ref=dst, send_sem=send, recv_sem=recv, device_id=target, device_id_type=MESH
    )


class Spread:
    def __init__(self, buf, send, recv, sibling, peer):
        def copy(src, dst, k, target):
            return remote(
                buf.at[pl.ds(src, HALF)], buf.at[pl.ds(dst, HALF)], send.at[k], recv.at[k], target
            )

        self.to_peer = [copy(HALF * c, 2 * TILE + TILE * c, c, peer) for c in range(2)]
        self.to_sibling = [copy(HALF * c, TILE + HALF * c, 2 + c, sibling) for c in range(2)]
        self.forward = [
            copy(2 * TILE + TILE * c, 2 * TILE + TILE * c + HALF, 4 + c, sibling) for c in range(2)
        ]

    def start(self, c):
        self.to_peer[c].start()
        self.to_sibling[c].start()

    def wait_block(self, i):
        @pl.when(i == 1)
        def _():
            for c in range(2):
                self.to_sibling[c].wait_recv()

        for c in range(2):

            @pl.when(i == 2 + c)
            def _():
                self.to_peer[c].wait_recv()
                self.forward[c].start()
                self.forward[c].wait_recv()

    def finish(self):
        for c in range(2):
            self.to_peer[c].wait_send()
            self.to_sibling[c].wait_send()
            self.forward[c].wait_send()


class Collect:
    def __init__(self, parts, out, mid, own, far, send, recv, sibling, peer):
        self.parts, self.out, self.mid, self.own, self.far = parts, out, mid, own, far
        self.cross = [
            remote(
                parts.at[pl.ds(2 * TILE + TILE * c + HALF, HALF)],
                mid.at[pl.ds(HALF * c, HALF)],
                send.at[c],
                recv.at[c],
                sibling,
            )
            for c in range(2)
        ]
        self.over = [
            remote(
                out.at[pl.ds(HALF * c, HALF)],
                far.at[pl.ds(HALF * c, HALF)],
                send.at[2 + c],
                recv.at[2 + c],
                peer,
            )
            for c in range(2)
        ]
        self.home = remote(parts.at[pl.ds(TILE, TILE)], own, send.at[4], recv.at[4], sibling)

    def block_done(self, j):
        for c in range(2):

            @pl.when(j == 2 + c)
            def _():
                self.cross[c].start()
                self.cross[c].wait_recv()

                @pl.loop(0, HALF // STEP)
                def _(s):
                    at = pl.multiple_of(s * STEP, STEP)
                    mine = self.parts[pl.ds(2 * TILE + TILE * c + at, STEP), :].astype(f32)
                    theirs = self.mid[pl.ds(HALF * c + at, STEP), :].astype(f32)
                    self.out[pl.ds(HALF * c + at, STEP), :] = (mine + theirs).astype(bf16)

                self.over[c].start()

        @pl.when(j == 1)
        def _():
            self.home.start()

    def wait(self):
        self.home.wait_recv()
        for c in range(2):
            self.over[c].wait_recv()

    def rows(self, at):
        span = pl.ds(at, STEP)
        total = self.parts[span, :].astype(f32) + self.own[span, :].astype(f32)
        return total + self.far[span, :].astype(f32)

    def finish(self):
        self.home.wait_send()
        for c in range(2):
            self.cross[c].wait_send()
            self.over[c].wait_send()


def spread_scratch(width):
    return [
        pltpu.VMEM((4 * TILE, width), bf16),
        pltpu.SemaphoreType.DMA((6,)),
        pltpu.SemaphoreType.DMA((6,)),
    ]


def collect_scratch(width):
    return [pltpu.VMEM((4 * TILE, width), bf16)] + [pltpu.VMEM((TILE, width), bf16)] * 4 + [
        pltpu.SemaphoreType.DMA((5,)),
        pltpu.SemaphoreType.DMA((5,)),
    ]


class Moves:
    def __init__(self, sems):
        self.sems, self.used = sems, 0

    def copy(self, src, dst):
        made = pltpu.make_async_copy(src, dst, self.sems.at[self.used])
        self.used += 1
        made.start()
        return made


def expand(onehot, ada, which, outs):
    width = outs[0].shape[1]
    for k, out in zip(which, outs):
        for n in range(0, width, TILE):
            out[:, n : n + TILE] = mm(onehot[...], ada[:, k * width + n : k * width + n + TILE])


def normed(values):
    centre = jnp.mean(values, axis=-1, keepdims=True)
    centred = values - centre
    spread = jnp.mean(centred * centred, axis=-1, keepdims=True)
    rate = lax.rsqrt(spread + 1e-06)
    return centred * rate, rate


def norm_back(grad, values_hat, rate):
    first = jnp.mean(grad, axis=-1, keepdims=True)
    second = jnp.mean(grad * values_hat, axis=-1, keepdims=True)
    return rate * (grad - first - values_hat * second)


def row_steps(start, rows, body):
    @pl.loop(0, rows // STEP)
    def _(s):
        body(pl.multiple_of(start + s * STEP, STEP))


def block_ones(size):
    shape = (TILE, TILE)
    one = lax.broadcasted_iota(jnp.int32, shape, 0) // size
    two = lax.broadcasted_iota(jnp.int32, shape, 1) // size
    return (one == two).astype(bf16)


def split_mm(dot, values, ones):
    high = values.astype(bf16)
    low = (values - high.astype(f32)).astype(bf16)
    return dot(high, ones) + dot(low, ones)


def head_lanes(values, h, size):
    lane = lax.broadcasted_iota(jnp.int32, values.shape, 1) // size
    return jnp.where(lane == h, values, jnp.zeros_like(values))


def hidden_bias(keyc, keyr, rows, cols):
    keys = keyc[pl.ds(rows, TILE), :]
    top = keyr[cols]
    low = top - top % 16
    return jnp.where((keys >= low) & (keys <= top), 0.0, -1e30)


def attend_kernel(
    size,
    x,
    onehot,
    ada,
    qscale,
    keyc,
    keyr,
    wqkv_in,
    wproj_in,
    h_out,
    qkv_out,
    rate_out,
    o_out,
    inv_out,
    branch_out,
    mid_out,
    wqkv,
    wproj,
    qkv,
    vt,
    rates,
    gamma,
    scale,
    shift,
    moves,
    hbuf,
    ag_send,
    ag_recv,
    parts,
    out,
    mid,
    own,
    far,
    rs_send,
    rs_recv,
):
    sibling, peer = partners()
    mover = Moves(moves)
    load_qkv = mover.copy(wqkv_in, wqkv)
    load_proj = mover.copy(wproj_in, wproj)
    expand(onehot, ada, (0, 2, 4), (gamma, scale, shift))
    greet(sibling, peer)
    spread = Spread(hbuf, ag_send, ag_recv, sibling, peer)
    collect = Collect(parts, out, mid, own, far, rs_send, rs_recv, sibling, peer)

    def modulated(at):
        span = pl.ds(at, STEP)
        hat, _ = normed(x[span, :])
        hbuf[span, :] = (hat * (1.0 + scale[span, :]) + shift[span, :]).astype(bf16)

    for c in range(2):
        row_steps(HALF * c, HALF, modulated)
        spread.start(c)
    load_qkv.wait()
    ones = block_ones(size)

    @pl.loop(0, 4)
    def _(i):
        spread.wait_block(i)
        span = pl.ds(pl.multiple_of(i * TILE, TILE), TILE)
        h = hbuf[span, :]
        for part in range(3):
            columns = slice(part * TILE, (part + 1) * TILE)
            value = mm(h, wqkv[:, columns])
            if part < 2:
                rate = lax.rsqrt(split_mm(mm, value * value, ones) + 1e-06)
                if part == 0:
                    rate = rate * qscale[...]
                rates[span, columns] = rate
                value = value * rate
            else:
                vt[:, span] = value.T.astype(bf16)
            qkv[span, columns] = value.astype(bf16)

    save_h = mover.copy(hbuf, h_out)
    save_qkv = mover.copy(qkv, qkv_out)
    save_rates = mover.copy(rates, rate_out)
    load_proj.wait()
    heads = TILE // size

    @pl.loop(0, 4)
    def _(i):
        j = (i + 2) % 4
        span = pl.ds(pl.multiple_of(j * TILE, TILE), TILE)
        queries = [head_lanes(qkv[span, 0:TILE], h, size) for h in range(heads)]
        sums = [jnp.zeros((1, TILE), f32)] * heads
        mixed = [jnp.zeros((size, TILE), f32)] * heads
        for k in range(4):
            keys = qkv[k * TILE : (k + 1) * TILE, TILE : 2 * TILE]
            bias = hidden_bias(keyc, keyr, k * TILE, j)
            for h in range(heads):
                grown = jnp.exp(mm_t(keys, queries[h]) + bias)
                sums[h] = sums[h] + jnp.sum(grown, axis=0, keepdims=True)
                mixed[h] = mixed[h] + mm(
                    vt[h * size : (h + 1) * size, k * TILE : (k + 1) * TILE], grown.astype(bf16)
                )
        inverse = [1.0 / one for one in sums]
        for h in range(heads):
            inv_out[j, h : h + 1, :] = inverse[h]
        whole = jnp.concatenate([mixed[h] * inverse[h] for h in range(heads)], axis=0)
        low = whole.T.astype(bf16)
        o_out[span, :] = low
        for n in range(0, parts.shape[1], TILE):
            parts[span, n : n + TILE] = mm(low, wproj[:, n : n + TILE]).astype(bf16)
        collect.block_done(j)

    collect.wait()

    def added(at):
        span = pl.ds(at, STEP)
        branch = collect.rows(at)
        branch_out[span, :] = branch
        mid_out[span, :] = x[span, :] + gamma[span, :] * branch

    row_steps(0, TILE, added)
    spread.finish()
    collect.finish()
    for one in (save_h, save_qkv, save_rates):
        one.wait()


def mlp_kernel(
    x,
    onehot,
    ada,
    wup_in,
    wdown_in,
    h_out,
    g_out,
    slope_out,
    result_out,
    x_out,
    wup,
    wdown,
    hidden,
    slope,
    gamma,
    scale,
    shift,
    moves,
    hbuf,
    ag_send,
    ag_recv,
    parts,
    out,
    mid,
    own,
    far,
    rs_send,
    rs_recv,
):
    sibling, peer = partners()
    mover = Moves(moves)
    load_up = mover.copy(wup_in, wup)
    load_down = mover.copy(wdown_in, wdown)
    expand(onehot, ada, (1, 3, 5), (gamma, scale, shift))
    greet(sibling, peer)
    spread = Spread(hbuf, ag_send, ag_recv, sibling, peer)
    collect = Collect(parts, out, mid, own, far, rs_send, rs_recv, sibling, peer)

    def modulated(at):
        span = pl.ds(at, STEP)
        hat, _ = normed(x[span, :])
        hbuf[span, :] = (hat * (1.0 + scale[span, :]) + shift[span, :]).astype(bf16)

    for c in range(2):
        row_steps(HALF * c, HALF, modulated)
        spread.start(c)
    load_up.wait()
    load_down.wait()

    @pl.loop(0, 4)
    def _(i):
        spread.wait_block(i)
        span = pl.ds(pl.multiple_of(i * TILE, TILE), TILE)
        h = hbuf[span, :]
        for n in range(0, wup.shape[1], TILE):
            columns = slice(n, n + TILE)
            up = mm(h, wup[:, columns])
            square = up * up
            bent = jnp.tanh(0.7978845608 * (up * (1.0 + 0.044715 * square)))
            half = 0.5 * (1.0 + bent)
            hidden[span, columns] = (up * half).astype(bf16)
            inner = 0.7978845608 + (3.0 * 0.044715 * 0.7978845608) * square
            slope[span, columns] = (half + 0.5 * up * (1.0 - bent * bent) * inner).astype(bf16)
        g = hidden[span, :]
        for n in range(0, parts.shape[1], TILE):
            parts[span, n : n + TILE] = mm(g, wdown[:, n : n + TILE]).astype(bf16)
        collect.block_done(i)

    saves = [mover.copy(a, b) for a, b in ((hbuf, h_out), (hidden, g_out), (slope, slope_out))]
    collect.wait()

    def added(at):
        span = pl.ds(at, STEP)
        result = collect.rows(at)
        result_out[span, :] = result
        x_out[span, :] = x[span, :] + gamma[span, :] * result

    row_steps(0, TILE, added)
    spread.finish()
    collect.finish()
    for one in saves:
        one.wait()


def item_sums(onehot_t, terms, out):
    for k, term in enumerate(terms):
        width = term.shape[1]
        out[:, k * width : (k + 1) * width] = mm(onehot_t[...], term[...])


def mlp_back_kernel(
    dx,
    result,
    mid_state,
    onehot,
    onehot_t,
    ada,
    wup_in,
    wdown_in,
    h_in,
    g_in,
    slope_in,
    dmid_out,
    dwup_out,
    dwdown_out,
    items_out,
    wup,
    wdown,
    hall,
    gall,
    slope,
    dwup,
    dwdown,
    dgamma,
    dscale,
    dshift,
    gamma,
    scale,
    moves,
    hbuf,
    ag_send,
    ag_recv,
    parts,
    out,
    mid,
    own,
    far,
    rs_send,
    rs_recv,
):
    sibling, peer = partners()
    mover = Moves(moves)
    load_down = mover.copy(wdown_in, wdown)
    load_slope = mover.copy(slope_in, slope)
    load_up = mover.copy(wup_in, wup)
    load_g = mover.copy(g_in, gall)
    load_h = mover.copy(h_in, hall)
    expand(onehot, ada, (1, 3), (gamma, scale))
    greet(sibling, peer)
    spread = Spread(hbuf, ag_send, ag_recv, sibling, peer)
    collect = Collect(parts, out, mid, own, far, rs_send, rs_recv, sibling, peer)

    def scaled(at):
        span = pl.ds(at, STEP)
        hbuf[span, :] = (gamma[span, :] * dx[span, :]).astype(bf16)

    for c in range(2):
        row_steps(HALF * c, HALF, scaled)
        spread.start(c)
    for one in (load_down, load_slope, load_up):
        one.wait()

    @pl.loop(0, 4)
    def _(i):
        spread.wait_block(i)
        span = pl.ds(pl.multiple_of(i * TILE, TILE), TILE)
        dm = hbuf[span, :]
        for n in range(0, slope.shape[1], TILE):
            columns = slice(n, n + TILE)
            dg = mm_t(dm, wdown[columns, :])
            slope[span, columns] = (dg * slope[span, columns].astype(f32)).astype(bf16)
        du = slope[span, :]
        for n in range(0, parts.shape[1], TILE):
            parts[span, n : n + TILE] = mm_t(du, wup[n : n + TILE, :]).astype(bf16)
        collect.block_done(i)

    load_g.wait()
    load_h.wait()

    @pl.loop(0, gall.shape[1] // TILE)
    def _(k):
        columns = pl.ds(pl.multiple_of(k * TILE, TILE), TILE)
        for n in range(0, hbuf.shape[1], 2 * TILE):
            dwdown[columns, n : n + 2 * TILE] = rows_mm(
                gall[:, columns], hbuf[:, n : n + 2 * TILE]
            ).astype(bf16)

    save_down = mover.copy(dwdown, dwdown_out)

    @pl.loop(0, hall.shape[1] // TILE)
    def _(k):
        columns = pl.ds(pl.multiple_of(k * TILE, TILE), TILE)
        for n in range(0, slope.shape[1], 2 * TILE):
            dwup[columns, n : n + 2 * TILE] = rows_mm(
                hall[:, columns], slope[:, n : n + 2 * TILE]
            ).astype(bf16)

    save_up = mover.copy(dwup, dwup_out)
    collect.wait()

    def added(at):
        span = pl.ds(at, STEP)
        dh = collect.rows(at)
        hat, rate = normed(mid_state[span, :])
        grad = dx[span, :]
        dgamma[span, :] = (grad * result[span, :]).astype(bf16)
        dscale[span, :] = (dh * hat).astype(bf16)
        dshift[span, :] = dh.astype(bf16)
        dmid_out[span, :] = grad + norm_back(dh * (1.0 + scale[span, :]), hat, rate)

    row_steps(0, TILE, added)
    item_sums(onehot_t, (dgamma, dscale, dshift), items_out)
    spread.finish()
    collect.finish()
    save_down.wait()
    save_up.wait()


def attend_back_kernel(
    size,
    dmid,
    branch,
    x,
    onehot,
    onehot_t,
    ada,
    qscale,
    keyc,
    keyr,
    inverse,
    wqkv_in,
    wproj_in,
    h_in,
    qkv_in,
    rate_in,
    o_in,
    dx_out,
    dwqkv_out,
    dwproj_out,
    items_out,
    head_out,
    wqkv,
    wproj,
    hall,
    qkv,
    rates,
    oall,
    kt,
    dkeys,
    dvalues,
    dqkv,
    dwqkv,
    dwproj,
    dgamma,
    dscale,
    dshift,
    gamma,
    scale,
    moves,
    hbuf,
    ag_send,
    ag_recv,
    parts,
    out,
    mid,
    own,
    far,
    rs_send,
    rs_recv,
):
    sibling, peer = partners()
    mover = Moves(moves)
    load_proj = mover.copy(wproj_in, wproj)
    load_qkv = mover.copy(qkv_in, qkv)
    load_o = mover.copy(o_in, oall)
    load_rates = mover.copy(rate_in, rates)
    load_w = mover.copy(wqkv_in, wqkv)
    load_h = mover.copy(h_in, hall)
    expand(onehot, ada, (0, 2), (gamma, scale))
    greet(sibling, peer)
    spread = Spread(hbuf, ag_send, ag_recv, sibling, peer)
    collect = Collect(parts, out, mid, own, far, rs_send, rs_recv, sibling, peer)

    def scaled(at):
        span = pl.ds(at, STEP)
        hbuf[span, :] = (gamma[span, :] * dmid[span, :]).astype(bf16)

    for c in range(2):
        row_steps(HALF * c, HALF, scaled)
        spread.start(c)
    for one in (load_proj, load_qkv, load_o, load_rates):
        one.wait()
    heads = TILE // size
    ones = block_ones(size)
    inv_square = 1.0 / (qscale[...] * qscale[...])
    select = (
        lax.broadcasted_iota(jnp.int32, (8, TILE), 1) // size
        == lax.broadcasted_iota(jnp.int32, (8, TILE), 0)
    ).astype(bf16)
    dkeys[...] = jnp.zeros_like(dkeys)
    dvalues[...] = jnp.zeros_like(dvalues)
    head_out[...] = jnp.zeros_like(head_out)
    for k in range(4):
        rows = slice(k * TILE, (k + 1) * TILE)
        kt[:, rows] = qkv[rows, TILE : 2 * TILE].astype(f32).T.astype(bf16)

    @pl.loop(0, 4)
    def _(i):
        spread.wait_block(i)
        span = pl.ds(pl.multiple_of(i * TILE, TILE), TILE)
        dout = mm_t(hbuf[span, :], wproj[...]).astype(bf16)
        product = dout.astype(f32) * oall[span, :].astype(f32)
        row_term = split_mm(lambda a, b: mm_t(b, a), product, select)
        q_low = qkv[span, 0:TILE]
        queries = [head_lanes(q_low, h, size) for h in range(heads)]
        douts = [head_lanes(dout, h, size) for h in range(heads)]
        dquery = [jnp.zeros((size, TILE), f32)] * heads
        for k in range(4):
            rows = slice(k * TILE, (k + 1) * TILE)
            keys = qkv[rows, TILE : 2 * TILE]
            values = qkv[rows, 2 * TILE : 3 * TILE]
            bias = hidden_bias(keyc, keyr, k * TILE, i)
            dkey = jnp.zeros((TILE, TILE), f32)
            dvalue = jnp.zeros((TILE, TILE), f32)
            for h in range(heads):
                share = jnp.exp(mm_t(keys, queries[h]) + bias) * inverse[i, h : h + 1, :]
                dshare = mm_t(values, douts[h])
                dscore = (share * (dshare - row_term[h : h + 1, :])).astype(bf16)
                dvalue = dvalue + mm(share.astype(bf16), douts[h])
                dkey = dkey + mm(dscore, queries[h])
                dquery[h] = dquery[h] + mm(kt[h * size : (h + 1) * size, rows], dscore)
            dkeys[rows, :] += dkey
            dvalues[rows, :] += dvalue
        dq = jnp.concatenate(dquery, axis=0).T
        qhat = q_low.astype(f32)
        along = split_mm(mm, dq * qhat, ones)
        head_out[...] += jnp.sum(along, axis=0, keepdims=True)
        dqkv[span, 0:TILE] = (rates[span, 0:TILE] * (dq - qhat * (along * inv_square))).astype(bf16)

    load_w.wait()

    @pl.loop(0, 4)
    def _(i):
        j = (i + 2) % 4
        span = pl.ds(pl.multiple_of(j * TILE, TILE), TILE)
        dk = dkeys[span, :]
        khat = qkv[span, TILE : 2 * TILE].astype(f32)
        along = split_mm(mm, dk * khat, ones)
        dqkv[span, TILE : 2 * TILE] = (
            rates[span, TILE : 2 * TILE] * (dk - khat * along)
        ).astype(bf16)
        dqkv[span, 2 * TILE : 3 * TILE] = dvalues[span, :].astype(bf16)
        low = dqkv[span, :]
        for n in range(0, parts.shape[1], TILE):
            parts[span, n : n + TILE] = mm_t(low, wqkv[n : n + TILE, :]).astype(bf16)
        collect.block_done(j)

    for n in range(0, hbuf.shape[1], 2 * TILE):
        dwproj[:, n : n + 2 * TILE] = rows_mm(oall[...], hbuf[:, n : n + 2 * TILE]).astype(bf16)
    save_proj = mover.copy(dwproj, dwproj_out)
    load_h.wait()

    @pl.loop(0, hall.shape[1] // TILE)
    def _(k):
        columns = pl.ds(pl.multiple_of(k * TILE, TILE), TILE)
        dwqkv[columns, :] = rows_mm(hall[:, columns], dqkv[...]).astype(bf16)

    save_w = mover.copy(dwqkv, dwqkv_out)
    collect.wait()

    def added(at):
        span = pl.ds(at, STEP)
        dh = collect.rows(at)
        hat, rate = normed(x[span, :])
        grad = dmid[span, :]
        dgamma[span, :] = (grad * branch[span, :]).astype(bf16)
        dscale[span, :] = (dh * hat).astype(bf16)
        dshift[span, :] = dh.astype(bf16)
        dx_out[span, :] = grad + norm_back(dh * (1.0 + scale[span, :]), hat, rate)

    row_steps(0, TILE, added)
    item_sums(onehot_t, (dgamma, dscale, dshift), items_out)
    spread.finish()
    collect.finish()
    save_proj.wait()
    save_w.wait()


ANY = pl.BlockSpec(memory_space=pl.ANY)
VMEM = pl.BlockSpec(memory_space=pltpu.VMEM)


def shaped(*shape, dtype=f32):
    return jax.ShapeDtypeStruct(shape, dtype)


def run(kernel, ident, inputs, outs, scratch, flops):
    return pl.pallas_call(
        kernel,
        out_shape=[one for one, _ in outs],
        in_specs=[where for _, where in inputs],
        out_specs=[where for _, where in outs],
        scratch_shapes=scratch,
        compiler_params=pltpu.CompilerParams(
            collective_id=ident, has_side_effects=True, vmem_limit_bytes=56 * 2**20
        ),
        cost_estimate=pl.CostEstimate(flops=flops, bytes_accessed=2**24, transcendentals=0),
    )(*[one for one, _ in inputs])


def attend(layer, size, x, onehot, ada, qscale, keyc, keyr, wqkv, wproj):
    rows, width = x.shape
    length, wide = wqkv.shape
    big = pltpu.VMEM((rows, width), f32)
    return run(
        partial(attend_kernel, size),
        layer,
        [(a, VMEM) for a in (x, onehot, ada, qscale, keyc, keyr)] + [(wqkv, ANY), (wproj, ANY)],
        [
            (shaped(length, width, dtype=bf16), ANY),
            (shaped(length, wide, dtype=bf16), ANY),
            (shaped(length, 2 * TILE), ANY),
            (shaped(length, TILE, dtype=bf16), VMEM),
            (shaped(4, 8, TILE), VMEM),
            (shaped(rows, width), VMEM),
            (shaped(rows, width), VMEM),
        ],
        [
            pltpu.VMEM(wqkv.shape, bf16),
            pltpu.VMEM(wproj.shape, bf16),
            pltpu.VMEM((length, wide), bf16),
            pltpu.VMEM((TILE, length), bf16),
            pltpu.VMEM((length, 2 * TILE), f32),
            big,
            big,
            big,
            pltpu.SemaphoreType.DMA((5,)),
        ]
        + spread_scratch(width)
        + collect_scratch(width),
        2**35,
    )


def mlp(layer, x, onehot, ada, wup, wdown):
    rows, width = x.shape
    length, ff = 4 * rows, wup.shape[1]
    big = pltpu.VMEM((rows, width), f32)
    return run(
        mlp_kernel,
        2 + layer,
        [(a, VMEM) for a in (x, onehot, ada)] + [(wup, ANY), (wdown, ANY)],
        [
            (shaped(length, width, dtype=bf16), ANY),
            (shaped(length, ff, dtype=bf16), ANY),
            (shaped(length, ff, dtype=bf16), ANY),
            (shaped(rows, width), VMEM),
            (shaped(rows, width), VMEM),
        ],
        [
            pltpu.VMEM(wup.shape, bf16),
            pltpu.VMEM(wdown.shape, bf16),
            pltpu.VMEM((length, ff), bf16),
            pltpu.VMEM((length, ff), bf16),
            big,
            big,
            big,
            pltpu.SemaphoreType.DMA((5,)),
        ]
        + spread_scratch(width)
        + collect_scratch(width),
        2**35,
    )


def mlp_back(layer, dx, result, mid, onehot, onehot_t, ada, wup, wdown, h, g, slope):
    rows, width = dx.shape
    length, ff = 4 * rows, wup.shape[1]
    big = pltpu.VMEM((rows, width), f32)
    small = pltpu.VMEM((rows, width), bf16)
    return run(
        mlp_back_kernel,
        4 + layer,
        [(a, VMEM) for a in (dx, result, mid, onehot, onehot_t, ada)]
        + [(a, ANY) for a in (wup, wdown, h, g, slope)],
        [
            (shaped(rows, width), VMEM),
            (shaped(*wup.shape, dtype=bf16), ANY),
            (shaped(*wdown.shape, dtype=bf16), ANY),
            (shaped(onehot_t.shape[0], 3 * width), VMEM),
        ],
        [
            pltpu.VMEM(wup.shape, bf16),
            pltpu.VMEM(wdown.shape, bf16),
            pltpu.VMEM((length, width), bf16),
            pltpu.VMEM((length, ff), bf16),
            pltpu.VMEM((length, ff), bf16),
            pltpu.VMEM(wup.shape, bf16),
            pltpu.VMEM(wdown.shape, bf16),
            small,
            small,
            small,
            big,
            big,
            pltpu.SemaphoreType.DMA((7,)),
        ]
        + spread_scratch(width)
        + collect_scratch(width),
        2**35,
    )


def attend_back(
    layer, size, dmid, branch, x, onehot, onehot_t, ada, qscale, keyc, keyr, inverse, wqkv, wproj, h, qkv, rates, o
):
    rows, width = dmid.shape
    length, wide = qkv.shape
    big = pltpu.VMEM((rows, width), f32)
    small = pltpu.VMEM((rows, width), bf16)
    return run(
        partial(attend_back_kernel, size),
        6 + layer,
        [(a, VMEM) for a in (dmid, branch, x, onehot, onehot_t, ada, qscale, keyc, keyr, inverse)]
        + [(a, ANY) for a in (wqkv, wproj, h, qkv, rates, o)],
        [
            (shaped(rows, width), VMEM),
            (shaped(*wqkv.shape, dtype=bf16), ANY),
            (shaped(*wproj.shape, dtype=bf16), ANY),
            (shaped(onehot_t.shape[0], 3 * width), VMEM),
            (shaped(1, TILE), VMEM),
        ],
        [
            pltpu.VMEM(wqkv.shape, bf16),
            pltpu.VMEM(wproj.shape, bf16),
            pltpu.VMEM((length, width), bf16),
            pltpu.VMEM((length, wide), bf16),
            pltpu.VMEM((length, 2 * TILE), f32),
            pltpu.VMEM((length, TILE), bf16),
            pltpu.VMEM((TILE, length), bf16),
            pltpu.VMEM((length, TILE), f32),
            pltpu.VMEM((length, TILE), f32),
            pltpu.VMEM((length, wide), bf16),
            pltpu.VMEM(wqkv.shape, bf16),
            pltpu.VMEM(wproj.shape, bf16),
            small,
            small,
            small,
            big,
            big,
            pltpu.SemaphoreType.DMA((8,)),
        ]
        + spread_scratch(width)
        + collect_scratch(width),
        2**35,
    )


def per_device(
    tokens,
    cotangent,
    stop_scale,
    labels,
    class_table,
    head_scale,
    w_qkv,
    w_proj,
    w_up,
    w_down,
    w_ada,
):
    rows, width = tokens.shape[1:]
    layers, heads = head_scale.shape
    size = width // heads
    dps, blks = lax.axis_size("dp"), lax.axis_size("blk")
    count = dps * blks
    length = rows * blks
    d, b = lax.axis_index("dp"), lax.axis_index("blk")
    own_heads = heads // blks
    piece = own_heads * size
    wrows = w_qkv.shape[1]
    ffrows = w_down.shape[1]
    ff = ffrows * dps
    slots = labels.shape[1]
    padded = 16

    item_all, level_all = token_meta(stop_scale[0], length)
    item_own = lax.dynamic_slice_in_dim(item_all, b * rows, rows)
    key = (item_all * 16 + level_all).reshape(blks, rows)
    sib = b + 1 - 2 * (b % 2)
    far, far_sib = (b + 2) % 4, (sib + 2) % 4
    key = jnp.concatenate(
        [key[b], key[sib], key[far, :HALF], key[far_sib, :HALF], key[far, HALF:], key[far_sib, HALF:]]
    )
    keyc, keyr = key[:, None], key.reshape(4, 1, TILE)
    slot_id = jnp.arange(padded, dtype=jnp.int32)
    onehot_t = (slot_id[:, None] == item_own[None, :]).astype(bf16)
    onehot = (item_own[:, None] == jnp.concatenate([slot_id, slot_id])[None, :]).astype(bf16)

    labels_all = gather(labels, "dp").reshape(-1)
    chosen = labels_all[:, None] == jnp.arange(class_table.shape[0], dtype=jnp.int32)[None, :]
    cond = mm(chosen.astype(bf16), class_table)
    cond_act, silu_pull = jax.vjp(jax.nn.silu, cond)
    cond_low = cond_act.astype(bf16)

    wide = w_ada.shape[2]
    columns = layers * wide // count
    ada_cols = w_ada.transpose(1, 0, 2).reshape(wrows, count, columns).transpose(1, 0, 2)
    ada_cols = lax.all_to_all(ada_cols, ("dp", "blk"), 0, 0, tiled=True)
    ada_part = mm(cond_low, ada_cols.reshape(count * wrows, columns))
    ada_part = lax.all_to_all(ada_part.reshape(dps, slots, columns), "dp", 0, 0, tiled=True)
    ada_all = lax.all_gather(ada_part, "blk", axis=1, tiled=False)
    ada_all = ada_all.transpose(2, 0, 1, 3).reshape(slots, layers, wide)
    ada_all = jnp.pad(ada_all.transpose(1, 0, 2), ((0, 0), (0, padded - slots), (0, 0)))
    ada_high = ada_all.astype(bf16)
    ada_low = (ada_all - ada_high.astype(f32)).astype(bf16)
    ada = jnp.concatenate([ada_high, ada_low], axis=1)

    qkv_cols = w_qkv.reshape(layers, wrows, 3, blks, piece).transpose(3, 0, 1, 2, 4)
    up_cols = w_up.reshape(layers, wrows, dps, blks, ffrows).transpose(3, 0, 1, 2, 4)
    moved = jnp.concatenate(
        [
            qkv_cols.reshape(blks, layers, wrows, 3 * piece),
            up_cols.reshape(blks, layers, wrows, ff),
        ],
        axis=3,
    )
    moved = lax.all_to_all(moved, "blk", 0, 0, tiled=True)
    moved = moved.transpose(1, 0, 2, 3).reshape(layers, blks * wrows, 3 * piece + ff)
    to_heads = [(i, (i % dps) * blks + i // dps) for i in range(count)]
    to_rows = [(j, i) for i, j in to_heads]
    proj_own = lax.ppermute(w_proj, ("dp", "blk"), to_heads)
    weights = []
    for layer in range(layers):
        weights.append(
            (
                gather(moved[layer, :, : 3 * piece], "dp"),
                gather(proj_own[layer], "dp"),
                gather(moved[layer, :, 3 * piece :], "dp"),
                gather(w_down[layer], "dp"),
            )
        )

    own_scale = lax.dynamic_slice_in_dim(head_scale, b * own_heads, own_heads, axis=1)
    qscales = jnp.repeat(jnp.exp(own_scale), size, axis=1)

    state = tokens[0].astype(f32)
    saved = []
    for layer in range(layers):
        w_query, w_out, w_first, w_second = weights[layer]
        qscale = qscales[layer][None, :]
        h, qkv, rates, o, inverse, branch, mid = attend(
            layer, size, state, onehot, ada[layer], qscale, keyc, keyr, w_query, w_out
        )
        h2, g, slope, result, following = mlp(layer, mid, onehot, ada[layer], w_first, w_second)
        saved.append((state, h, qkv, rates, o, inverse, branch, mid, h2, g, slope, result))
        state = following
    output = state.astype(bf16)[None]

    grad = cotangent[0].astype(f32)
    cond_grad = 0.0
    scale_grads, pieces = [None] * layers, [None] * layers
    for layer in reversed(range(layers)):
        w_query, w_out, w_first, w_second = weights[layer]
        qscale = qscales[layer][None, :]
        state, h, qkv, rates, o, inverse, branch, mid, h2, g, slope, result = saved[layer]
        mid_grad, up_grad, down_grad, items_two = mlp_back(
            layer, grad, result, mid, onehot, onehot_t, ada[layer], w_first, w_second, h2, g, slope
        )
        wide_grad = scatter(
            jnp.concatenate(
                [down_grad.reshape(dps, ffrows, width), up_grad.reshape(dps, blks * wrows, ff)], axis=1
            ).reshape(-1, width),
            "dp",
        )
        down_grad, up_grad = wide_grad[:ffrows].astype(f32), wide_grad[ffrows:]
        grad, qkv_grad, proj_grad, items_one, scale_grad = attend_back(
            layer,
            size,
            mid_grad,
            branch,
            state,
            onehot,
            onehot_t,
            ada[layer],
            qscale,
            keyc,
            keyr,
            inverse,
            w_query,
            w_out,
            h,
            qkv,
            rates,
            o,
        )
        qkv_grad = scatter(qkv_grad, "dp")
        proj_grad = scatter(proj_grad, "dp")
        scale_grads[layer] = lax.dynamic_update_slice_in_dim(
            jnp.zeros((heads,), f32), scale_grad[0, ::size], b * own_heads, 0
        )
        parts_one, parts_two = jnp.split(items_one, 3, axis=1), jnp.split(items_two, 3, axis=1)
        item_grad = jnp.concatenate(
            [part for pair in zip(parts_one, parts_two) for part in pair], axis=1
        )[:slots]
        item_grad = item_grad.reshape(slots, blks, wide // blks).transpose(1, 0, 2)
        item_grad = scatter(item_grad, "blk").astype(bf16)
        item_grad = gather(item_grad, ("dp", "blk")).reshape(dps, blks, slots, wide // blks)
        item_grad = item_grad.transpose(0, 2, 1, 3).reshape(dps * slots, wide)
        cond_grad = cond_grad + mm_t(item_grad, w_ada[layer])
        own_cond = lax.dynamic_slice_in_dim(cond_low, (d * blks + b) * wrows, wrows, axis=1)
        ada_grad = rows_mm(own_cond, item_grad)
        back = jnp.concatenate([qkv_grad, up_grad], axis=1)
        back = lax.all_to_all(back.reshape(blks, wrows, 3 * piece + ff), "blk", 0, 0, tiled=True)
        qkv_grad = back[:, :, : 3 * piece].reshape(blks, wrows, 3, piece)
        qkv_grad = qkv_grad.transpose(1, 2, 0, 3).reshape(wrows, 3 * width).astype(f32)
        up_grad = back[:, :, 3 * piece :].reshape(blks, wrows, dps, ffrows)
        up_grad = up_grad.transpose(1, 2, 0, 3).reshape(wrows, ff * blks).astype(f32)
        proj_grad = lax.ppermute(proj_grad, ("dp", "blk"), to_rows).astype(f32)
        pieces[layer] = (qkv_grad, proj_grad, up_grad, down_grad, ada_grad)
    cond_grad = gather(cond_grad.T, ("dp", "blk")).T
    cond_pre = silu_pull(cond_grad)[0]
    table_grad = rows_mm(chosen.astype(f32), cond_pre, lax.Precision.HIGHEST)
    head_grad = lax.psum(jnp.stack(scale_grads), ("dp", "blk"))
    stacked = [jnp.stack([one[i] for one in pieces]) for i in range(5)]
    return (output, grad.astype(bf16)[None], table_grad, head_grad, *stacked)


def solution(mesh):
    in_specs = (
        P("dp", "blk", None),
        P("dp", "blk", None),
        P("dp", None),
        P("dp", None),
        P(),
        P(),
        P(None, ("dp", "blk"), None),
        P(None, ("dp", "blk"), None),
        P(None, ("dp", "blk"), None),
        P(None, ("dp", "blk"), None),
        P(None, ("dp", "blk"), None),
    )
    out_specs = (
        P("dp", "blk", None),
        P("dp", "blk", None),
        P(),
        P(),
        P(None, ("dp", "blk"), None),
        P(None, ("dp", "blk"), None),
        P(None, ("dp", "blk"), None),
        P(None, ("dp", "blk"), None),
        P(None, ("dp", "blk"), None),
    )
    return jax.shard_map(
        per_device, mesh=mesh, in_specs=in_specs, out_specs=out_specs, check_vma=False
    )
```

```python
from functools import partial

import jax
import jax.numpy as jnp
from jax import lax
from jax.experimental import pallas as pl
from jax.experimental.pallas import tpu as pltpu
from jax.sharding import PartitionSpec as P

patch_areas = (1, 4, 9, 16, 25, 36, 64, 100, 169)
scale_starts = (1, 5, 14, 30, 55, 91, 155, 255)
f32 = jnp.float32
bf16 = jnp.bfloat16
MESH = pl.DeviceIdType.MESH
TILE = 256
HALF = 128
STEP = 32


def token_meta(stops, length):
    areas = jnp.array(patch_areas, dtype=jnp.int32)
    levels = jnp.arange(9, dtype=jnp.int32)
    counts = jnp.sum(jnp.where(levels[None, :] < stops[:, None], areas[None, :], 0), axis=1)
    ends = jnp.cumsum(counts)
    places = jnp.arange(length, dtype=jnp.int32)
    passed = places[:, None] >= ends[None, :]
    item = jnp.sum(passed.astype(jnp.int32), axis=1)
    begin = jnp.sum(jnp.where(passed, counts[None, :], 0), axis=1)
    inner = places - begin
    bounds = jnp.array(scale_starts, dtype=jnp.int32)
    level = jnp.sum((inner[:, None] >= bounds[None, :]).astype(jnp.int32), axis=1)
    level = jnp.where(item == stops.shape[0], 0, level)
    return (item, level)


def mm(left, right):
    return jnp.dot(left, right, preferred_element_type=f32)


def mm_t(left, right):
    return lax.dot_general(left, right, (((1,), (1,)), ((), ())), preferred_element_type=f32)


def rows_mm(left, right, precision=None):
    return lax.dot_general(
        left, right, (((0,), (0,)), ((), ())), precision=precision, preferred_element_type=f32
    )


def gather(values, axes):
    return lax.all_gather(values, axes, axis=0, tiled=True)


def scatter(values, axes):
    return lax.psum_scatter(values, axes, scatter_dimension=0, tiled=True)


def partners():
    d, b = lax.axis_index("dp"), lax.axis_index("blk")
    return (d, b + 1 - 2 * (b % 2)), (d, (b + 2) % 4)


def greet(others):
    barrier = pltpu.get_barrier_semaphore()
    for other in others:
        pl.semaphore_signal(barrier, inc=1, device_id=other, device_id_type=MESH)
    pl.semaphore_wait(barrier, len(others))


def remote(src, dst, send, recv, target):
    return pltpu.make_async_remote_copy(
        src_ref=src, dst_ref=dst, send_sem=send, recv_sem=recv, device_id=target, device_id_type=MESH
    )


class Spread:
    def __init__(self, buf, send, recv, sibling, peer):
        def copy(src, dst, k, target):
            return remote(
                buf.at[pl.ds(src, HALF)], buf.at[pl.ds(dst, HALF)], send.at[k], recv.at[k], target
            )

        self.to_peer = [copy(HALF * c, 2 * TILE + TILE * c, c, peer) for c in range(2)]
        self.to_sibling = [copy(HALF * c, TILE + HALF * c, 2 + c, sibling) for c in range(2)]
        self.forward = [
            copy(2 * TILE + TILE * c, 2 * TILE + TILE * c + HALF, 4 + c, sibling) for c in range(2)
        ]

    def start(self, c):
        self.to_peer[c].start()
        self.to_sibling[c].start()

    def wait_block(self, i):
        @pl.when(i == 1)
        def _():
            for c in range(2):
                self.to_sibling[c].wait_recv()

        for c in range(2):

            @pl.when(i == 2 + c)
            def _():
                self.to_peer[c].wait_recv()
                self.forward[c].start()
                self.forward[c].wait_recv()

    def finish(self):
        for c in range(2):
            self.to_peer[c].wait_send()
            self.to_sibling[c].wait_send()
            self.forward[c].wait_send()


class Collect:
    def __init__(self, parts, out, mid, own, far, send, recv, sibling, peer):
        self.parts, self.out, self.mid, self.own, self.far = parts, out, mid, own, far
        self.cross = [
            remote(
                parts.at[pl.ds(2 * TILE + TILE * c + HALF, HALF)],
                mid.at[pl.ds(HALF * c, HALF)],
                send.at[c],
                recv.at[c],
                sibling,
            )
            for c in range(2)
        ]
        self.over = [
            remote(
                out.at[pl.ds(HALF * c, HALF)],
                far.at[pl.ds(HALF * c, HALF)],
                send.at[2 + c],
                recv.at[2 + c],
                peer,
            )
            for c in range(2)
        ]
        self.home = remote(parts.at[pl.ds(TILE, TILE)], own, send.at[4], recv.at[4], sibling)

    def block_done(self, j):
        for c in range(2):

            @pl.when(j == 2 + c)
            def _():
                self.cross[c].start()
                self.cross[c].wait_recv()

                @pl.loop(0, HALF // STEP)
                def _(s):
                    at = pl.multiple_of(s * STEP, STEP)
                    mine = self.parts[pl.ds(2 * TILE + TILE * c + at, STEP), :].astype(f32)
                    theirs = self.mid[pl.ds(HALF * c + at, STEP), :].astype(f32)
                    self.out[pl.ds(HALF * c + at, STEP), :] = (mine + theirs).astype(bf16)

                self.over[c].start()

        @pl.when(j == 1)
        def _():
            self.home.start()

    def wait(self):
        self.home.wait_recv()
        for c in range(2):
            self.over[c].wait_recv()

    def rows(self, at):
        span = pl.ds(at, STEP)
        total = self.parts[span, :].astype(f32) + self.own[span, :].astype(f32)
        return total + self.far[span, :].astype(f32)

    def finish(self):
        self.home.wait_send()
        for c in range(2):
            self.cross[c].wait_send()
            self.over[c].wait_send()


def spread_scratch(width):
    return [
        pltpu.VMEM((4 * TILE, width), bf16),
        pltpu.SemaphoreType.DMA((6,)),
        pltpu.SemaphoreType.DMA((6,)),
    ]


def collect_scratch(width):
    return [pltpu.VMEM((4 * TILE, width), bf16)] + [pltpu.VMEM((TILE, width), bf16)] * 4 + [
        pltpu.SemaphoreType.DMA((5,)),
        pltpu.SemaphoreType.DMA((5,)),
    ]


class Moves:
    def __init__(self, sems):
        self.sems, self.used = sems, 0

    def copy(self, src, dst):
        made = pltpu.make_async_copy(src, dst, self.sems.at[self.used])
        self.used += 1
        made.start()
        return made


def expand(onehot, ada, which, outs):
    width = outs[0].shape[1]
    for k, out in zip(which, outs):
        for n in range(0, width, TILE):
            out[:, n : n + TILE] = mm(onehot[...], ada[:, k * width + n : k * width + n + TILE])


def normed(values):
    centre = jnp.mean(values, axis=-1, keepdims=True)
    centred = values - centre
    spread = jnp.mean(centred * centred, axis=-1, keepdims=True)
    rate = lax.rsqrt(spread + 1e-06)
    return centred * rate, rate


def norm_back(grad, values_hat, rate):
    first = jnp.mean(grad, axis=-1, keepdims=True)
    second = jnp.mean(grad * values_hat, axis=-1, keepdims=True)
    return rate * (grad - first - values_hat * second)


def row_steps(start, rows, body):
    @pl.loop(0, rows // STEP)
    def _(s):
        body(pl.multiple_of(start + s * STEP, STEP))


def block_ones(size):
    shape = (TILE, TILE)
    one = lax.broadcasted_iota(jnp.int32, shape, 0) // size
    two = lax.broadcasted_iota(jnp.int32, shape, 1) // size
    return (one == two).astype(bf16)


def split_mm(dot, values, ones):
    high = values.astype(bf16)
    low = (values - high.astype(f32)).astype(bf16)
    return dot(high, ones) + dot(low, ones)


def head_lanes(values, h, size):
    lane = lax.broadcasted_iota(jnp.int32, values.shape, 1) // size
    return jnp.where(lane == h, values, jnp.zeros_like(values))


def hidden_bias(keyc, keyr, rows, cols):
    keys = keyc[pl.ds(rows, TILE), :]
    top = keyr[cols]
    low = top - top % 16
    return jnp.where((keys >= low) & (keys <= top), 0.0, -1e30)


def attend_kernel(
    size,
    jobs,
    x,
    onehot,
    ada,
    qscale,
    keyc,
    keyr,
    wqkv_in,
    wproj_in,
    h_out,
    qkv_out,
    rate_out,
    o_out,
    inv_out,
    branch_out,
    mid_out,
    wqkv,
    wproj,
    qkv,
    vt,
    rates,
    gamma,
    scale,
    shift,
    moves,
    hbuf,
    ag_send,
    ag_recv,
    parts,
    out,
    mid,
    own,
    far,
    rs_send,
    rs_recv,
):
    sibling, peer = partners()
    mover = Moves(moves)
    load_qkv = mover.copy(wqkv_in, wqkv)
    load_proj = mover.copy(wproj_in, wproj)
    expand(onehot, ada, (0, 2, 4), (gamma, scale, shift))
    jobs.greet(sibling, peer)
    jobs.start()
    spread = Spread(hbuf, ag_send, ag_recv, sibling, peer)
    collect = Collect(parts, out, mid, own, far, rs_send, rs_recv, sibling, peer)

    def modulated(at):
        span = pl.ds(at, STEP)
        hat, _ = normed(x[span, :])
        hbuf[span, :] = (hat * (1.0 + scale[span, :]) + shift[span, :]).astype(bf16)

    for c in range(2):
        row_steps(HALF * c, HALF, modulated)
        spread.start(c)
    load_qkv.wait()
    ones = block_ones(size)

    @pl.loop(0, 4)
    def _(i):
        spread.wait_block(i)
        span = pl.ds(pl.multiple_of(i * TILE, TILE), TILE)
        h = hbuf[span, :]
        for part in range(3):
            columns = slice(part * TILE, (part + 1) * TILE)
            value = mm(h, wqkv[:, columns])
            if part < 2:
                rate = lax.rsqrt(split_mm(mm, value * value, ones) + 1e-06)
                if part == 0:
                    rate = rate * qscale[...]
                rates[span, columns] = rate
                value = value * rate
            else:
                vt[:, span] = value.T.astype(bf16)
            qkv[span, columns] = value.astype(bf16)

    jobs.step(0)
    save_h = mover.copy(hbuf, h_out)
    save_qkv = mover.copy(qkv, qkv_out)
    save_rates = mover.copy(rates, rate_out)
    load_proj.wait()
    heads = TILE // size

    @pl.loop(0, 4)
    def _(i):
        j = (i + 2) % 4
        span = pl.ds(pl.multiple_of(j * TILE, TILE), TILE)
        queries = [head_lanes(qkv[span, 0:TILE], h, size) for h in range(heads)]
        sums = [jnp.zeros((1, TILE), f32)] * heads
        mixed = [jnp.zeros((size, TILE), f32)] * heads
        for k in range(4):
            keys = qkv[k * TILE : (k + 1) * TILE, TILE : 2 * TILE]
            bias = hidden_bias(keyc, keyr, k * TILE, j)
            for h in range(heads):
                grown = jnp.exp(mm_t(keys, queries[h]) + bias)
                sums[h] = sums[h] + jnp.sum(grown, axis=0, keepdims=True)
                mixed[h] = mixed[h] + mm(
                    vt[h * size : (h + 1) * size, k * TILE : (k + 1) * TILE], grown.astype(bf16)
                )
        inverse = [1.0 / one for one in sums]
        for h in range(heads):
            inv_out[j, h : h + 1, :] = inverse[h]
        whole = jnp.concatenate([mixed[h] * inverse[h] for h in range(heads)], axis=0)
        low = whole.T.astype(bf16)
        o_out[span, :] = low
        for n in range(0, parts.shape[1], TILE):
            parts[span, n : n + TILE] = mm(low, wproj[:, n : n + TILE]).astype(bf16)
        collect.block_done(j)

    jobs.step(1)
    jobs.step(2)
    collect.wait()

    def added(at):
        span = pl.ds(at, STEP)
        branch = collect.rows(at)
        branch_out[span, :] = branch
        mid_out[span, :] = x[span, :] + gamma[span, :] * branch

    row_steps(0, TILE, added)
    spread.finish()
    collect.finish()
    for one in (save_h, save_qkv, save_rates):
        one.wait()
    jobs.finish()


def early_hooks(jobs, i):
    for hook in range(2):

        @pl.when(i == 2 + hook)
        def _():
            jobs.step(hook)


def mlp_kernel(
    jobs,
    x,
    onehot,
    ada,
    wup_in,
    wdown_in,
    h_out,
    g_out,
    slope_out,
    result_out,
    x_out,
    wup,
    wdown,
    hidden,
    slope,
    gamma,
    scale,
    shift,
    moves,
    hbuf,
    ag_send,
    ag_recv,
    parts,
    out,
    mid,
    own,
    far,
    rs_send,
    rs_recv,
):
    sibling, peer = partners()
    mover = Moves(moves)
    load_up = mover.copy(wup_in, wup)
    load_down = mover.copy(wdown_in, wdown)
    expand(onehot, ada, (1, 3, 5), (gamma, scale, shift))
    jobs.greet(sibling, peer)
    jobs.start()
    spread = Spread(hbuf, ag_send, ag_recv, sibling, peer)
    collect = Collect(parts, out, mid, own, far, rs_send, rs_recv, sibling, peer)

    def modulated(at):
        span = pl.ds(at, STEP)
        hat, _ = normed(x[span, :])
        hbuf[span, :] = (hat * (1.0 + scale[span, :]) + shift[span, :]).astype(bf16)

    for c in range(2):
        row_steps(HALF * c, HALF, modulated)
        spread.start(c)
    load_up.wait()
    load_down.wait()

    @pl.loop(0, 4)
    def _(i):
        spread.wait_block(i)
        early_hooks(jobs, i)
        span = pl.ds(pl.multiple_of(i * TILE, TILE), TILE)
        h = hbuf[span, :]
        for n in range(0, wup.shape[1], TILE):
            columns = slice(n, n + TILE)
            up = mm(h, wup[:, columns])
            square = up * up
            bent = jnp.tanh(0.7978845608 * (up * (1.0 + 0.044715 * square)))
            half = 0.5 * (1.0 + bent)
            hidden[span, columns] = (up * half).astype(bf16)
            inner = 0.7978845608 + (3.0 * 0.044715 * 0.7978845608) * square
            slope[span, columns] = (half + 0.5 * up * (1.0 - bent * bent) * inner).astype(bf16)
        g = hidden[span, :]
        for n in range(0, parts.shape[1], TILE):
            parts[span, n : n + TILE] = mm(g, wdown[:, n : n + TILE]).astype(bf16)
        collect.block_done(i)

    jobs.step(2)
    saves = [mover.copy(a, b) for a, b in ((hbuf, h_out), (hidden, g_out), (slope, slope_out))]
    collect.wait()

    def added(at):
        span = pl.ds(at, STEP)
        result = collect.rows(at)
        result_out[span, :] = result
        x_out[span, :] = x[span, :] + gamma[span, :] * result

    row_steps(0, TILE, added)
    spread.finish()
    collect.finish()
    for one in saves:
        one.wait()
    jobs.finish()


def item_sums(onehot_t, terms, out):
    for k, term in enumerate(terms):
        width = term.shape[1]
        out[:, k * width : (k + 1) * width] = mm(onehot_t[...], term[...])


def mlp_back_kernel(
    jobs,
    dx,
    result,
    mid_state,
    onehot,
    onehot_t,
    ada,
    wup_in,
    wdown_in,
    h_in,
    g_in,
    slope_in,
    dmid_out,
    dwup_out,
    dwdown_out,
    items_out,
    wup,
    wdown,
    hall,
    gall,
    slope,
    dwup,
    dwdown,
    dgamma,
    dscale,
    dshift,
    gamma,
    scale,
    moves,
    hbuf,
    ag_send,
    ag_recv,
    parts,
    out,
    mid,
    own,
    far,
    rs_send,
    rs_recv,
):
    sibling, peer = partners()
    mover = Moves(moves)
    load_down = mover.copy(wdown_in, wdown)
    load_slope = mover.copy(slope_in, slope)
    load_up = mover.copy(wup_in, wup)
    load_g = mover.copy(g_in, gall)
    load_h = mover.copy(h_in, hall)
    expand(onehot, ada, (1, 3), (gamma, scale))
    jobs.greet(sibling, peer)
    jobs.start()
    spread = Spread(hbuf, ag_send, ag_recv, sibling, peer)
    collect = Collect(parts, out, mid, own, far, rs_send, rs_recv, sibling, peer)

    def scaled(at):
        span = pl.ds(at, STEP)
        hbuf[span, :] = (gamma[span, :] * dx[span, :]).astype(bf16)

    for c in range(2):
        row_steps(HALF * c, HALF, scaled)
        spread.start(c)
    for one in (load_down, load_slope, load_up):
        one.wait()

    @pl.loop(0, 4)
    def _(i):
        spread.wait_block(i)
        early_hooks(jobs, i)
        span = pl.ds(pl.multiple_of(i * TILE, TILE), TILE)
        dm = hbuf[span, :]
        for n in range(0, slope.shape[1], TILE):
            columns = slice(n, n + TILE)
            dg = mm_t(dm, wdown[columns, :])
            slope[span, columns] = (dg * slope[span, columns].astype(f32)).astype(bf16)
        du = slope[span, :]
        for n in range(0, parts.shape[1], TILE):
            parts[span, n : n + TILE] = mm_t(du, wup[n : n + TILE, :]).astype(bf16)
        collect.block_done(i)

    jobs.step(2)
    load_g.wait()
    load_h.wait()

    @pl.loop(0, gall.shape[1] // TILE)
    def _(k):
        columns = pl.ds(pl.multiple_of(k * TILE, TILE), TILE)
        for n in range(0, hbuf.shape[1], 2 * TILE):
            dwdown[columns, n : n + 2 * TILE] = rows_mm(
                gall[:, columns], hbuf[:, n : n + 2 * TILE]
            ).astype(bf16)

    save_down = mover.copy(dwdown, dwdown_out)

    @pl.loop(0, hall.shape[1] // TILE)
    def _(k):
        columns = pl.ds(pl.multiple_of(k * TILE, TILE), TILE)
        for n in range(0, slope.shape[1], 2 * TILE):
            dwup[columns, n : n + 2 * TILE] = rows_mm(
                hall[:, columns], slope[:, n : n + 2 * TILE]
            ).astype(bf16)

    save_up = mover.copy(dwup, dwup_out)
    collect.wait()

    def added(at):
        span = pl.ds(at, STEP)
        dh = collect.rows(at)
        hat, rate = normed(mid_state[span, :])
        grad = dx[span, :]
        dgamma[span, :] = (grad * result[span, :]).astype(bf16)
        dscale[span, :] = (dh * hat).astype(bf16)
        dshift[span, :] = dh.astype(bf16)
        dmid_out[span, :] = grad + norm_back(dh * (1.0 + scale[span, :]), hat, rate)

    row_steps(0, TILE, added)
    item_sums(onehot_t, (dgamma, dscale, dshift), items_out)
    spread.finish()
    collect.finish()
    save_down.wait()
    save_up.wait()
    jobs.finish()


def attend_back_kernel(
    size,
    jobs,
    dmid,
    branch,
    x,
    onehot,
    onehot_t,
    ada,
    qscale,
    keyc,
    keyr,
    inverse,
    wqkv_in,
    wproj_in,
    h_in,
    qkv_in,
    rate_in,
    o_in,
    dx_out,
    dwqkv_out,
    dwproj_out,
    items_out,
    head_out,
    wqkv,
    wproj,
    hall,
    qkv,
    rates,
    oall,
    kt,
    dkeys,
    dvalues,
    dqkv,
    dwqkv,
    dwproj,
    dgamma,
    dscale,
    dshift,
    gamma,
    scale,
    moves,
    hbuf,
    ag_send,
    ag_recv,
    parts,
    out,
    mid,
    own,
    far,
    rs_send,
    rs_recv,
):
    sibling, peer = partners()
    mover = Moves(moves)
    load_proj = mover.copy(wproj_in, wproj)
    load_qkv = mover.copy(qkv_in, qkv)
    load_o = mover.copy(o_in, oall)
    load_rates = mover.copy(rate_in, rates)
    load_w = mover.copy(wqkv_in, wqkv)
    load_h = mover.copy(h_in, hall)
    expand(onehot, ada, (0, 2), (gamma, scale))
    jobs.greet(sibling, peer)
    jobs.start()
    spread = Spread(hbuf, ag_send, ag_recv, sibling, peer)
    collect = Collect(parts, out, mid, own, far, rs_send, rs_recv, sibling, peer)

    def scaled(at):
        span = pl.ds(at, STEP)
        hbuf[span, :] = (gamma[span, :] * dmid[span, :]).astype(bf16)

    for c in range(2):
        row_steps(HALF * c, HALF, scaled)
        spread.start(c)
    for one in (load_proj, load_qkv, load_o, load_rates):
        one.wait()
    heads = TILE // size
    ones = block_ones(size)
    inv_square = 1.0 / (qscale[...] * qscale[...])
    select = (
        lax.broadcasted_iota(jnp.int32, (8, TILE), 1) // size
        == lax.broadcasted_iota(jnp.int32, (8, TILE), 0)
    ).astype(bf16)
    dkeys[...] = jnp.zeros_like(dkeys)
    dvalues[...] = jnp.zeros_like(dvalues)
    head_out[...] = jnp.zeros_like(head_out)
    for k in range(4):
        rows = slice(k * TILE, (k + 1) * TILE)
        kt[:, rows] = qkv[rows, TILE : 2 * TILE].astype(f32).T.astype(bf16)

    @pl.loop(0, 4)
    def _(i):
        spread.wait_block(i)

        @pl.when(i == 3)
        def _():
            jobs.step(0)

        span = pl.ds(pl.multiple_of(i * TILE, TILE), TILE)
        dout = mm_t(hbuf[span, :], wproj[...]).astype(bf16)
        product = dout.astype(f32) * oall[span, :].astype(f32)
        row_term = split_mm(lambda a, b: mm_t(b, a), product, select)
        q_low = qkv[span, 0:TILE]
        queries = [head_lanes(q_low, h, size) for h in range(heads)]
        douts = [head_lanes(dout, h, size) for h in range(heads)]
        dquery = [jnp.zeros((size, TILE), f32)] * heads
        for k in range(4):
            rows = slice(k * TILE, (k + 1) * TILE)
            keys = qkv[rows, TILE : 2 * TILE]
            values = qkv[rows, 2 * TILE : 3 * TILE]
            bias = hidden_bias(keyc, keyr, k * TILE, i)
            dkey = jnp.zeros((TILE, TILE), f32)
            dvalue = jnp.zeros((TILE, TILE), f32)
            for h in range(heads):
                share = jnp.exp(mm_t(keys, queries[h]) + bias) * inverse[i, h : h + 1, :]
                dshare = mm_t(values, douts[h])
                dscore = (share * (dshare - row_term[h : h + 1, :])).astype(bf16)
                dvalue = dvalue + mm(share.astype(bf16), douts[h])
                dkey = dkey + mm(dscore, queries[h])
                dquery[h] = dquery[h] + mm(kt[h * size : (h + 1) * size, rows], dscore)
            dkeys[rows, :] += dkey
            dvalues[rows, :] += dvalue
        dq = jnp.concatenate(dquery, axis=0).T
        qhat = q_low.astype(f32)
        along = split_mm(mm, dq * qhat, ones)
        head_out[...] += jnp.sum(along, axis=0, keepdims=True)
        dqkv[span, 0:TILE] = (rates[span, 0:TILE] * (dq - qhat * (along * inv_square))).astype(bf16)

    load_w.wait()
    jobs.step(1)

    @pl.loop(0, 4)
    def _(i):
        j = (i + 2) % 4
        span = pl.ds(pl.multiple_of(j * TILE, TILE), TILE)
        dk = dkeys[span, :]
        khat = qkv[span, TILE : 2 * TILE].astype(f32)
        along = split_mm(mm, dk * khat, ones)
        dqkv[span, TILE : 2 * TILE] = (
            rates[span, TILE : 2 * TILE] * (dk - khat * along)
        ).astype(bf16)
        dqkv[span, 2 * TILE : 3 * TILE] = dvalues[span, :].astype(bf16)
        low = dqkv[span, :]
        for n in range(0, parts.shape[1], TILE):
            parts[span, n : n + TILE] = mm_t(low, wqkv[n : n + TILE, :]).astype(bf16)
        collect.block_done(j)

    jobs.step(2)
    for n in range(0, hbuf.shape[1], 2 * TILE):
        dwproj[:, n : n + 2 * TILE] = rows_mm(oall[...], hbuf[:, n : n + 2 * TILE]).astype(bf16)
    save_proj = mover.copy(dwproj, dwproj_out)
    load_h.wait()

    @pl.loop(0, hall.shape[1] // TILE)
    def _(k):
        columns = pl.ds(pl.multiple_of(k * TILE, TILE), TILE)
        dwqkv[columns, :] = rows_mm(hall[:, columns], dqkv[...]).astype(bf16)

    save_w = mover.copy(dwqkv, dwqkv_out)
    collect.wait()

    def added(at):
        span = pl.ds(at, STEP)
        dh = collect.rows(at)
        hat, rate = normed(x[span, :])
        grad = dmid[span, :]
        dgamma[span, :] = (grad * branch[span, :]).astype(bf16)
        dscale[span, :] = (dh * hat).astype(bf16)
        dshift[span, :] = dh.astype(bf16)
        dx_out[span, :] = grad + norm_back(dh * (1.0 + scale[span, :]), hat, rate)

    row_steps(0, TILE, added)
    item_sums(onehot_t, (dgamma, dscale, dshift), items_out)
    spread.finish()
    collect.finish()
    save_proj.wait()
    save_w.wait()
    jobs.finish()


def groups(dps):
    d, b = lax.axis_index("dp"), lax.axis_index("blk")
    side, pairs = d % 2, dps // 2
    pair = d // 2
    ahead = [((pair + k) % pairs) * 2 + side for k in range(pairs)]
    behind = [((pair - k + pairs) % pairs) * 2 + side for k in range(pairs)]
    return d, b, d + 1 - 2 * side, ahead, behind


class DpGather:
    def __init__(self, shards):
        self.shards = list(shards)
        self.dps = lax.axis_size("dp")
        self.inputs = [(one, ANY) for one in self.shards]
        self.outs = [
            (shaped(self.dps, *one.shape, dtype=one.dtype), ANY) for one in self.shards
        ]
        count = len(self.shards)
        sems = pltpu.SemaphoreType.DMA((count, self.dps))
        self.scratch = [sems, sems, pltpu.SemaphoreType.DMA((count,))]

    def bind(self, ins, outs, scratch):
        send, recv, local = scratch
        d, b, other, ahead, behind = groups(self.dps)
        pairs = self.dps // 2
        self.partners = [(other, b)] + [(t, b) for t in ahead[1:]]
        self.first, self.direct, self.forward, self.local = [], [], [], []
        for a, (src, dst) in enumerate(zip(ins, outs)):
            self.local.append(pltpu.make_async_copy(src, dst.at[d], local.at[a]))
            self.first.append(remote(src, dst.at[d], send.at[a, 0], recv.at[a, 0], (other, b)))
            self.direct.append([None])
            self.forward.append([None])
            for k in range(1, pairs):
                self.direct[a].append(
                    remote(src, dst.at[d], send.at[a, k], recv.at[a, k], (ahead[k], b))
                )
                at = pairs + k
                self.forward[a].append(
                    remote(
                        dst.at[behind[k]], dst.at[behind[k]], send.at[a, at], recv.at[a, at], (other, b)
                    )
                )
        self.order = [(k, a) for k in range(1, pairs) for a in range(len(ins))]

    def start(self):
        for k, a in self.order:
            self.direct[a][k].start()
        for one in self.first + self.local:
            one.start()

    def step(self, hook, hooks):
        low, high = (len(self.order) * hook) // hooks, (len(self.order) * (hook + 1)) // hooks
        for k, a in self.order[low:high]:
            self.direct[a][k].wait_recv()
            self.forward[a][k].start()

    def finish(self):
        for one in self.local:
            one.wait()
        for one in self.first:
            one.wait()
        for k, a in self.order:
            self.direct[a][k].wait_send()
            self.forward[a][k].wait()


class DpScatter:
    def __init__(self, values, dtypes):
        self.values = list(values)
        self.dps = lax.axis_size("dp")
        self.inputs = [(one, ANY) for one in self.values]
        self.outs = [
            (shaped(*one.shape[1:], dtype=dtype), VMEM) for one, dtype in zip(self.values, dtypes)
        ]
        pairs = self.dps // 2
        self.scratch = []
        for one in self.values:
            self.scratch += [pltpu.VMEM((pairs, *one.shape[1:]), bf16)] * 3
            self.scratch += [pltpu.SemaphoreType.DMA((2 * pairs,))] * 2
            self.scratch += [pltpu.SemaphoreType.DMA((pairs,))]

    def bind(self, ins, outs, scratch):
        d, b, other, ahead, behind = groups(self.dps)
        pairs = self.dps // 2
        self.partners = [(other, b)] + [(t, b) for t in ahead[1:]]
        self.results = outs
        self.bufs, self.local, self.cross, self.direct = [], [], [], []
        for a, src in enumerate(ins):
            mine, near, far, send, recv, local = scratch[6 * a : 6 * a + 6]
            self.bufs.append((mine, near, far))
            self.local.append([])
            self.cross.append([])
            self.direct.append([None])
            for k in range(pairs):
                target = ahead[k]
                theirs = target + 1 - 2 * (target % 2)
                self.local[a].append(
                    pltpu.make_async_copy(src.at[target], mine.at[k], local.at[k])
                )
                self.cross[a].append(
                    remote(src.at[theirs], near.at[k], send.at[k], recv.at[k], (other, b))
                )
                if k:
                    at = pairs + k
                    self.direct[a].append(
                        remote(mine.at[k], far.at[k], send.at[at], recv.at[at], (target, b))
                    )
        self.order = [(k, a) for k in range(1, pairs) for a in range(len(ins))]
        self.last = [(0, a) for a in range(len(ins))]

    def start(self):
        for k, a in self.order + self.last:
            self.cross[a][k].start()
            self.local[a][k].start()

    def add(self, a, k):
        self.local[a][k].wait()
        self.cross[a][k].wait_recv()
        mine, near, _ = self.bufs[a]
        rows = mine.shape[1]
        step = min(rows, STEP)

        @pl.loop(0, rows // step)
        def _(s):
            span = pl.ds(pl.multiple_of(s * step, step), step)
            total = mine[k, span, :].astype(f32) + near[k, span, :].astype(f32)
            mine[k, span, :] = total.astype(bf16)

    def step(self, hook, hooks):
        low, high = (len(self.order) * hook) // hooks, (len(self.order) * (hook + 1)) // hooks
        for k, a in self.order[low:high]:
            self.add(a, k)
            self.direct[a][k].start()

    def finish(self):
        for k, a in self.last:
            self.add(a, k)
        for k, a in self.order:
            self.direct[a][k].wait()
        for k, a in self.order + self.last:
            self.cross[a][k].wait_send()
        for a, result in enumerate(self.results):
            mine, _, far = self.bufs[a]
            rows = mine.shape[1]
            step = min(rows, STEP)

            @pl.loop(0, rows // step)
            def _(s):
                span = pl.ds(pl.multiple_of(s * step, step), step)
                total = mine[0, span, :].astype(f32)
                for k in range(1, self.dps // 2):
                    total = total + far[k, span, :].astype(f32)
                result[span, :] = total.astype(result.dtype)


class Swap:
    def __init__(self, values):
        self.values = list(values)
        self.inputs = [(one, ANY) for one in self.values]
        self.outs = [(shaped(*one.shape, dtype=one.dtype), ANY) for one in self.values]
        sems = pltpu.SemaphoreType.DMA((len(self.values), 4))
        self.scratch = [sems, sems]

    def bind(self, ins, outs, scratch):
        send, recv = scratch
        d, b = lax.axis_index("dp"), lax.axis_index("blk")
        self.partners = [(d, (b + k) % 4) for k in range(1, 4)]
        self.local, self.sent = [], []
        for a, (src, dst) in enumerate(zip(ins, outs)):
            self.local.append(pltpu.make_async_copy(src.at[b], dst.at[b], send.at[a, 0]))
            for k in range(1, 4):
                to = (b + k) % 4
                self.sent.append(
                    remote(src.at[to], dst.at[b], send.at[a, k], recv.at[a, k], (d, to))
                )

    def start(self):
        for one in self.sent + self.local:
            one.start()

    def step(self, hook, hooks):
        pass

    def finish(self):
        for one in self.sent + self.local:
            one.wait()


class Jobs:
    def __init__(self, jobs):
        self.jobs = jobs

    def greet(self, sibling, peer):
        d, b = lax.axis_index("dp"), lax.axis_index("blk")
        others = [sibling, peer]
        if any(isinstance(job, Swap) for job in self.jobs):
            others.append((d, 3 - b))
        dps = [job for job in self.jobs if not isinstance(job, Swap)]
        if dps:
            others += dps[0].partners
        greet(others)

    def start(self):
        for job in self.jobs:
            job.start()

    def step(self, hook):
        for job in self.jobs:
            job.step(hook, 3)

    def finish(self):
        for job in self.jobs:
            job.finish()


def prepare_kernel(
    gather_job,
    cond,
    ada_in,
    qkv_in,
    up_in,
    ada_out,
    cond_out,
    qkv_out,
    up_out,
    conds,
    columns,
    answers,
    ada,
    cond_send,
    cond_recv,
    ada_send,
    ada_recv,
    answer_send,
    answer_recv,
    blk_send,
    blk_recv,
    local,
):
    dps, blks = lax.axis_size("dp"), lax.axis_size("blk")
    count = dps * blks
    d, b = lax.axis_index("dp"), lax.axis_index("blk")
    me = d * blks + b
    layers = qkv_in.shape[1]
    rows, wide = ada_in.shape[1:]
    slots = cond.shape[0]
    others = [(me + k) % count for k in range(count)]
    barrier = pltpu.get_barrier_semaphore()
    for t in others[1:]:
        pl.semaphore_signal(barrier, inc=1, device_id=(t // blks, t % blks), device_id_type=MESH)
    pl.semaphore_wait(barrier, count - 1)

    locals_ = [pltpu.make_async_copy(cond, conds.at[d], local.at[0])]
    sends = []
    for k in range(1, dps):
        to = (d + k) % dps
        sends.append(remote(cond, conds.at[d], cond_send.at[k], cond_recv.at[k], (to, b)))
    swaps = []
    for layer in range(layers):
        pieces = []
        for a, (src, dst) in enumerate(((qkv_in, qkv_out), (up_in, up_out))):
            at = layer * 2 + a
            locals_.append(
                pltpu.make_async_copy(src.at[b, layer], dst.at[layer, b], local.at[1 + at])
            )
            for k in range(1, blks):
                to = (b + k) % blks
                pieces.append(
                    remote(
                        src.at[to, layer],
                        dst.at[layer, b],
                        blk_send.at[at, k],
                        blk_recv.at[at, k],
                        (d, to),
                    )
                )
        swaps.append(pieces)
    moves = []
    for k in range(1, count):
        t = others[k]
        moves.append(
            remote(
                ada_in.at[t],
                columns.at[pl.ds(pl.multiple_of(me * rows, rows), rows)],
                ada_send.at[k],
                ada_recv.at[k],
                (t // blks, t % blks),
            )
        )
    locals_.append(
        pltpu.make_async_copy(
            ada_in.at[me],
            columns.at[pl.ds(pl.multiple_of(me * rows, rows), rows)],
            local.at[1 + 2 * layers],
        )
    )
    for one in locals_ + sends + swaps[0] + moves:
        one.start()
    for one in swaps[1:]:
        for piece in one:
            piece.start()
    for one in swaps[0]:
        one.wait_recv()
    for one in locals_:
        one.wait()
    gather_job.start()
    for one in sends:
        one.wait_recv()
    for one in moves:
        one.wait_recv()
    whole = mm(conds[...].reshape(dps * slots, conds.shape[2]), columns[...])
    answers[...] = whole.reshape(dps, slots, wide)
    place = pl.ds(pl.multiple_of(me * wide, 128), wide)
    replies = []
    for k in range(1, count):
        t = others[k]
        replies.append(
            remote(
                answers.at[t // blks],
                ada.at[:, place],
                answer_send.at[k],
                answer_recv.at[k],
                (t // blks, t % blks),
            )
        )
    for one in replies:
        one.start()
    ada[:, place] = answers[d]
    gather_job.step(0)
    gather_job.step(1)
    for one in replies:
        one.wait_recv()
    each = ada_out.shape[2]
    for layer in range(layers):
        value = ada[:, layer * each : (layer + 1) * each]
        high = value.astype(bf16)
        ada_out[layer, 0:slots, :] = high
        ada_out[layer, slots : 2 * slots, :] = (value - high.astype(f32)).astype(bf16)
    cond_out[...] = conds[...]
    gather_job.step(2)
    for one in sends + moves + replies:
        one.wait_send()
    for layer, pieces in enumerate(swaps):
        for one in pieces:
            one.wait_send()
            if layer:
                one.wait_recv()
    gather_job.finish()


def prepare(cond, ada_in, qkv_in, up_in, proj):
    dps, blks = lax.axis_size("dp"), lax.axis_size("blk")
    count = dps * blks
    slots, width = cond.shape
    layers = qkv_in.shape[1]
    rows, wide = ada_in.shape[1:]
    sems = pltpu.SemaphoreType.DMA
    qkv_shard = (layers, blks, *qkv_in.shape[2:])
    up_shard = (layers, blks, *up_in.shape[2:])
    gather_outs = [
        shaped(dps, *qkv_shard[1:], dtype=bf16),
        shaped(dps, *proj.shape, dtype=bf16),
    ]

    def body(cond, ada_in, qkv_in, up_in, proj, ada_out, cond_out, qkv_out, up_out, whole_qkv, whole_proj, *scratch):
        job = DpGather([jax.ShapeDtypeStruct(qkv_shard[1:], bf16), proj])
        job.bind([qkv_out.at[0], proj], [whole_qkv, whole_proj], scratch[-3:])
        prepare_kernel(
            Jobs([job]), cond, ada_in, qkv_in, up_in, ada_out, cond_out, qkv_out, up_out, *scratch[:-3]
        )

    outs = [
        (shaped(layers, 2 * slots, count * wide // layers, dtype=bf16), VMEM),
        (shaped(dps, slots, width, dtype=bf16), VMEM),
        (shaped(*qkv_shard, dtype=bf16), ANY),
        (shaped(*up_shard, dtype=bf16), ANY),
    ] + [(one, ANY) for one in gather_outs]
    results = pl.pallas_call(
        body,
        out_shape=[one for one, _ in outs],
        in_specs=[VMEM, ANY, ANY, ANY, ANY],
        out_specs=[where for _, where in outs],
        scratch_shapes=[
            pltpu.VMEM((dps, slots, width), bf16),
            pltpu.VMEM((count * rows, wide), bf16),
            pltpu.VMEM((dps, slots, wide), f32),
            pltpu.VMEM((slots, count * wide), f32),
            sems((dps,)),
            sems((dps,)),
            sems((count,)),
            sems((count,)),
            sems((count,)),
            sems((count,)),
            sems((2 * layers, blks)),
            sems((2 * layers, blks)),
            sems((2 + 2 * layers,)),
            sems((2, dps)),
            sems((2, dps)),
            sems((2,)),
        ],
        compiler_params=pltpu.CompilerParams(
            collective_id=8, has_side_effects=True, vmem_limit_bytes=40 * 2**20
        ),
        cost_estimate=pl.CostEstimate(flops=2**35, bytes_accessed=2**24, transcendentals=0),
    )(cond, ada_in, qkv_in, up_in, proj)
    return results[:4], results[4:]


def finish_kernel(jobs, out, staged, local, send, recv):
    sibling, peer = partners()
    jobs.greet(sibling, peer)
    jobs.start()
    for hook in range(3):
        jobs.step(hook)
    jobs.finish()
    d, b = lax.axis_index("dp"), lax.axis_index("blk")
    result = jobs.jobs[0].results[0]
    rows = staged.shape[1]
    for i in range(4):
        staged[i] = result[i * rows : (i + 1) * rows, :]
    sent = [pltpu.make_async_copy(staged.at[b], out.at[b], local)]
    for k in range(1, 4):
        to = (b + k) % 4
        sent.append(remote(staged.at[to], out.at[b], send.at[k], recv.at[k], (d, to)))
    for one in sent:
        one.start()
    for one in sent:
        one.wait()


def finish(scatter_job, swap_job):
    rows, columns = scatter_job.values[0].shape[1:]
    shape = (4, rows // 4, columns)
    sems = pltpu.SemaphoreType.DMA
    return run(
        finish_kernel,
        9,
        [],
        [(shaped(*shape, dtype=bf16), VMEM)],
        [pltpu.VMEM(shape, bf16), sems, sems((4,)), sems((4,))],
        2**30,
        [scatter_job, swap_job],
    )


ANY = pl.BlockSpec(memory_space=pl.ANY)
VMEM = pl.BlockSpec(memory_space=pltpu.VMEM)


def shaped(*shape, dtype=f32):
    return jax.ShapeDtypeStruct(shape, dtype)


def run(kernel, ident, inputs, outs, scratch, flops, jobs=()):
    sizes = [(len(inputs), len(outs), len(scratch))]
    sizes += [(len(job.inputs), len(job.outs), len(job.scratch)) for job in jobs]
    own_outs = len(outs)
    for job in jobs:
        inputs, outs, scratch = inputs + job.inputs, outs + job.outs, scratch + job.scratch

    def body(*refs):
        at = 0
        shares = [[] for _ in sizes]
        for kind in range(3):
            for i, size in enumerate(sizes):
                shares[i].append(refs[at : at + size[kind]])
                at += size[kind]
        for job, share in zip(jobs, shares[1:]):
            job.bind(*share)
        kernel(Jobs(jobs), *shares[0][0], *shares[0][1], *shares[0][2])

    results = pl.pallas_call(
        body,
        out_shape=[one for one, _ in outs],
        in_specs=[where for _, where in inputs],
        out_specs=[where for _, where in outs],
        scratch_shapes=scratch,
        compiler_params=pltpu.CompilerParams(
            collective_id=ident, has_side_effects=True, vmem_limit_bytes=56 * 2**20
        ),
        cost_estimate=pl.CostEstimate(flops=flops, bytes_accessed=2**24, transcendentals=0),
    )(*[one for one, _ in inputs])
    return results[:own_outs], results[own_outs:]


def attend(layer, size, x, onehot, ada, qscale, keyc, keyr, wqkv, wproj, jobs=()):
    rows, width = x.shape
    length, wide = wqkv.shape
    big = pltpu.VMEM((rows, width), f32)
    return run(
        partial(attend_kernel, size),
        layer,
        [(a, VMEM) for a in (x, onehot, ada, qscale, keyc, keyr)] + [(wqkv, ANY), (wproj, ANY)],
        [
            (shaped(length, width, dtype=bf16), ANY),
            (shaped(length, wide, dtype=bf16), ANY),
            (shaped(length, 2 * TILE), ANY),
            (shaped(length, TILE, dtype=bf16), VMEM),
            (shaped(4, 8, TILE), VMEM),
            (shaped(rows, width), VMEM),
            (shaped(rows, width), VMEM),
        ],
        [
            pltpu.VMEM(wqkv.shape, bf16),
            pltpu.VMEM(wproj.shape, bf16),
            pltpu.VMEM((length, wide), bf16),
            pltpu.VMEM((TILE, length), bf16),
            pltpu.VMEM((length, 2 * TILE), f32),
            big,
            big,
            big,
            pltpu.SemaphoreType.DMA((5,)),
        ]
        + spread_scratch(width)
        + collect_scratch(width),
        2**35,
        jobs,
    )


def mlp(layer, x, onehot, ada, wup, wdown, jobs=()):
    rows, width = x.shape
    length, ff = 4 * rows, wup.shape[1]
    big = pltpu.VMEM((rows, width), f32)
    return run(
        mlp_kernel,
        2 + layer,
        [(a, VMEM) for a in (x, onehot, ada)] + [(wup, ANY), (wdown, ANY)],
        [
            (shaped(length, width, dtype=bf16), ANY),
            (shaped(length, ff, dtype=bf16), ANY),
            (shaped(length, ff, dtype=bf16), ANY),
            (shaped(rows, width), VMEM),
            (shaped(rows, width), VMEM),
        ],
        [
            pltpu.VMEM(wup.shape, bf16),
            pltpu.VMEM(wdown.shape, bf16),
            pltpu.VMEM((length, ff), bf16),
            pltpu.VMEM((length, ff), bf16),
            big,
            big,
            big,
            pltpu.SemaphoreType.DMA((5,)),
        ]
        + spread_scratch(width)
        + collect_scratch(width),
        2**35,
        jobs,
    )


def mlp_back(layer, dx, result, mid, onehot, onehot_t, ada, wup, wdown, h, g, slope, jobs=()):
    rows, width = dx.shape
    length, ff = 4 * rows, wup.shape[1]
    big = pltpu.VMEM((rows, width), f32)
    small = pltpu.VMEM((rows, width), bf16)
    return run(
        mlp_back_kernel,
        4 + layer,
        [(a, VMEM) for a in (dx, result, mid, onehot, onehot_t, ada)]
        + [(a, ANY) for a in (wup, wdown, h, g, slope)],
        [
            (shaped(rows, width), VMEM),
            (shaped(*wup.shape, dtype=bf16), ANY),
            (shaped(*wdown.shape, dtype=bf16), ANY),
            (shaped(onehot_t.shape[0], 3 * width), VMEM),
        ],
        [
            pltpu.VMEM(wup.shape, bf16),
            pltpu.VMEM(wdown.shape, bf16),
            pltpu.VMEM((length, width), bf16),
            pltpu.VMEM((length, ff), bf16),
            pltpu.VMEM((length, ff), bf16),
            pltpu.VMEM(wup.shape, bf16),
            pltpu.VMEM(wdown.shape, bf16),
            small,
            small,
            small,
            big,
            big,
            pltpu.SemaphoreType.DMA((7,)),
        ]
        + spread_scratch(width)
        + collect_scratch(width),
        2**35,
        jobs,
    )


def attend_back(
    layer,
    size,
    dmid,
    branch,
    x,
    onehot,
    onehot_t,
    ada,
    qscale,
    keyc,
    keyr,
    inverse,
    wqkv,
    wproj,
    h,
    qkv,
    rates,
    o,
    jobs=(),
):
    rows, width = dmid.shape
    length, wide = qkv.shape
    big = pltpu.VMEM((rows, width), f32)
    small = pltpu.VMEM((rows, width), bf16)
    return run(
        partial(attend_back_kernel, size),
        6 + layer,
        [(a, VMEM) for a in (dmid, branch, x, onehot, onehot_t, ada, qscale, keyc, keyr, inverse)]
        + [(a, ANY) for a in (wqkv, wproj, h, qkv, rates, o)],
        [
            (shaped(rows, width), VMEM),
            (shaped(*wqkv.shape, dtype=bf16), ANY),
            (shaped(*wproj.shape, dtype=bf16), ANY),
            (shaped(onehot_t.shape[0], 3 * width), VMEM),
            (shaped(1, TILE), VMEM),
        ],
        [
            pltpu.VMEM(wqkv.shape, bf16),
            pltpu.VMEM(wproj.shape, bf16),
            pltpu.VMEM((length, width), bf16),
            pltpu.VMEM((length, wide), bf16),
            pltpu.VMEM((length, 2 * TILE), f32),
            pltpu.VMEM((length, TILE), bf16),
            pltpu.VMEM((TILE, length), bf16),
            pltpu.VMEM((length, TILE), f32),
            pltpu.VMEM((length, TILE), f32),
            pltpu.VMEM((length, wide), bf16),
            pltpu.VMEM(wqkv.shape, bf16),
            pltpu.VMEM(wproj.shape, bf16),
            small,
            small,
            small,
            big,
            big,
            pltpu.SemaphoreType.DMA((8,)),
        ]
        + spread_scratch(width)
        + collect_scratch(width),
        2**35,
        jobs,
    )


def per_device(
    tokens,
    cotangent,
    stop_scale,
    labels,
    class_table,
    head_scale,
    w_qkv,
    w_proj,
    w_up,
    w_down,
    w_ada,
):
    rows, width = tokens.shape[1:]
    layers, heads = head_scale.shape
    size = width // heads
    dps, blks = lax.axis_size("dp"), lax.axis_size("blk")
    count = dps * blks
    length = rows * blks
    d, b = lax.axis_index("dp"), lax.axis_index("blk")
    own_heads = heads // blks
    piece = own_heads * size
    wrows = w_qkv.shape[1]
    ffrows = w_down.shape[1]
    ff = ffrows * dps
    slots = labels.shape[1]
    padded = 16

    item_all, level_all = token_meta(stop_scale[0], length)
    item_own = lax.dynamic_slice_in_dim(item_all, b * rows, rows)
    key = (item_all * 16 + level_all).reshape(blks, rows)
    sib = b + 1 - 2 * (b % 2)
    far, far_sib = (b + 2) % 4, (sib + 2) % 4
    key = jnp.concatenate(
        [key[b], key[sib], key[far, :HALF], key[far_sib, :HALF], key[far, HALF:], key[far_sib, HALF:]]
    )
    keyc, keyr = key[:, None], key.reshape(4, 1, TILE)
    slot_id = jnp.arange(padded, dtype=jnp.int32)
    onehot_t = (slot_id[:, None] == item_own[None, :]).astype(bf16)
    onehot = (item_own[:, None] == jnp.concatenate([slot_id, slot_id])[None, :]).astype(bf16)

    def one_hot(names):
        return (names[:, None] == jnp.arange(class_table.shape[0], dtype=jnp.int32)[None, :]).astype(bf16)

    wide = w_ada.shape[2]
    columns = layers * wide // count
    ada_cols = w_ada.transpose(1, 0, 2).reshape(wrows, count, columns).transpose(1, 0, 2)
    qkv_cols = w_qkv.reshape(layers, wrows, 3, blks, piece).transpose(3, 0, 1, 2, 4)
    qkv_cols = qkv_cols.reshape(blks, layers, wrows, 3 * piece)
    up_cols = w_up.reshape(layers, wrows, dps, blks, ffrows).transpose(3, 0, 1, 2, 4)
    up_cols = up_cols.reshape(blks, layers, wrows, ff)
    to_heads = [(i, (i % dps) * blks + i // dps) for i in range(count)]
    to_rows = [(j, i) for i, j in to_heads]
    proj_own = lax.ppermute(w_proj, ("dp", "blk"), to_heads)
    own_cond = jax.nn.silu(mm(one_hot(labels[0]), class_table)).astype(bf16)
    own_cond = jnp.pad(own_cond, ((0, padded - slots), (0, 0)))
    if columns % 128 == 0 and wrows % 16 == 0:
        (ada, cond_all, qkv_shards, up_shards), (first_qkv, first_proj) = prepare(
            own_cond, ada_cols, qkv_cols, up_cols, proj_own[0]
        )
        cond_all = cond_all.reshape(dps * padded, width)
    else:
        cond_all = gather(own_cond, "dp")
        ada_cols = lax.all_to_all(ada_cols, ("dp", "blk"), 0, 0, tiled=True)
        ada_part = mm(cond_all, ada_cols.reshape(count * wrows, columns))
        ada_part = lax.all_to_all(ada_part.reshape(dps, padded, columns), "dp", 0, 0, tiled=True)
        ada_all = lax.all_gather(ada_part, "blk", axis=1, tiled=False)
        ada_all = ada_all.transpose(2, 0, 1, 3).reshape(padded, layers, wide).transpose(1, 0, 2)
        ada_high = ada_all.astype(bf16)
        ada_low = (ada_all - ada_high.astype(f32)).astype(bf16)
        ada = jnp.concatenate([ada_high, ada_low], axis=1)
        qkv_shards = lax.all_to_all(qkv_cols, "blk", 0, 0, tiled=True).transpose(1, 0, 2, 3)
        up_shards = lax.all_to_all(up_cols, "blk", 0, 0, tiled=True).transpose(1, 0, 2, 3)
        first_qkv, first_proj = gather(qkv_shards[:1], "dp"), gather(proj_own[:1], "dp")

    own_scale = lax.dynamic_slice_in_dim(head_scale, b * own_heads, own_heads, axis=1)
    qscales = jnp.repeat(jnp.exp(own_scale), size, axis=1)

    state = tokens[0].astype(f32)
    saved, weights = [], []
    w_query, w_out = first_qkv, first_proj
    for layer in range(layers):
        w_query = w_query.reshape(length, 3 * piece)
        w_out = w_out.reshape(piece, width)
        qscale = qscales[layer][None, :]
        (h, qkv, rates, o, inverse, branch, mid), (w_first, w_second) = attend(
            layer,
            size,
            state,
            onehot,
            ada[layer],
            qscale,
            keyc,
            keyr,
            w_query,
            w_out,
            [DpGather([up_shards[layer], w_down[layer]])],
        )
        w_first, w_second = w_first.reshape(width, ff), w_second.reshape(ff, width)
        weights.append((w_query, w_out, w_first, w_second))
        more = layer + 1 < layers
        (h2, g, slope, result, following), gathered = mlp(
            layer,
            mid,
            onehot,
            ada[layer],
            w_first,
            w_second,
            [DpGather([qkv_shards[layer + 1], proj_own[layer + 1]])] if more else [],
        )
        if more:
            w_query, w_out = gathered
        saved.append((state, h, qkv, rates, o, inverse, branch, mid, h2, g, slope, result))
        state = following
    output = state.astype(bf16)[None]

    grad = cotangent[0].astype(f32)
    own_rows = lax.dynamic_slice_in_dim(cond_all, (d * blks + b) * wrows, wrows, axis=1)
    cond_grad = 0.0
    scale_grads = [None] * layers
    ada_grads, up_grads, down_grads, qkv_grads, proj_grads = ([None] * layers for _ in range(5))

    def item_term(items):
        columns = items.shape[1] // blks
        items = items.reshape(padded, blks, columns).transpose(1, 0, 2)
        items = scatter(items, "blk").astype(bf16)
        items = gather(items, ("dp", "blk")).reshape(dps, blks, padded, columns)
        return items.transpose(0, 2, 1, 3).reshape(dps * padded, blks * columns)

    waiting_scatter, waiting_swap = None, None
    for layer in reversed(range(layers)):
        w_query, w_out, w_first, w_second = weights[layer]
        qscale = qscales[layer][None, :]
        state, h, qkv, rates, o, inverse, branch, mid, h2, g, slope, result = saved[layer]
        jobs = []
        if waiting_scatter is not None:
            jobs = [DpScatter(waiting_scatter, (bf16, f32)), Swap([waiting_swap])]
        (mid_grad, up_grad, down_grad, items_two), done = mlp_back(
            layer, grad, result, mid, onehot, onehot_t, ada[layer], w_first, w_second, h2, g, slope, jobs
        )
        swaps = []
        if waiting_scatter is not None:
            qkv_sum, proj_grads[layer + 1], up_grads[layer + 1] = done
            swaps = [Swap([qkv_sum.reshape(blks, wrows, 3 * piece)])]
        (grad, qkv_grad, proj_grad, items_one, scale_grad), done = attend_back(
            layer,
            size,
            mid_grad,
            branch,
            state,
            onehot,
            onehot_t,
            ada[layer],
            qscale,
            keyc,
            keyr,
            inverse,
            w_query,
            w_out,
            h,
            qkv,
            rates,
            o,
            [
                DpScatter(
                    [up_grad.reshape(dps, blks * wrows, ff), down_grad.reshape(dps, ffrows, width)],
                    (bf16, f32),
                )
            ]
            + swaps,
        )
        up_sum, down_grads[layer] = done[:2]
        if swaps:
            qkv_grads[layer + 1] = done[2]
        waiting_scatter = [
            qkv_grad.reshape(dps, blks * wrows, 3 * piece),
            proj_grad.reshape(dps, piece // dps, width),
        ]
        waiting_swap = up_sum.reshape(blks, wrows, ff)
        scale_grads[layer] = lax.dynamic_update_slice_in_dim(
            jnp.zeros((heads,), f32), scale_grad[0, ::size], b * own_heads, 0
        )
        terms = [jnp.split(item_term(one), 3, axis=1) for one in (items_one, items_two)]
        item_grad = jnp.concatenate([part for pair in zip(*terms) for part in pair], axis=1)
        cond_grad = cond_grad + mm_t(item_grad, w_ada[layer])
        ada_grads[layer] = rows_mm(own_rows, item_grad)
    (qkv_grads[0],), (_, proj_grads[0], up_grads[0]) = finish(
        DpScatter(waiting_scatter, (bf16, f32)), Swap([waiting_swap])
    )
    for layer in range(layers):
        one = qkv_grads[layer].reshape(blks, wrows, 3, piece)
        qkv_grads[layer] = one.transpose(1, 2, 0, 3).reshape(wrows, 3 * width).astype(f32)
        one = up_grads[layer].reshape(blks, wrows, dps, ffrows)
        up_grads[layer] = one.transpose(1, 2, 0, 3).reshape(wrows, ff * blks).astype(f32)
    proj_whole = lax.ppermute(jnp.stack(proj_grads), ("dp", "blk"), to_rows)
    cond_grad = gather(cond_grad.T, ("dp", "blk")).T.reshape(dps, padded, width)[:, :slots]
    chosen = one_hot(gather(labels, "dp").reshape(-1))
    _, silu_pull = jax.vjp(jax.nn.silu, mm(chosen, class_table))
    cond_pre = silu_pull(cond_grad.reshape(dps * slots, width))[0]
    table_grad = rows_mm(chosen.astype(f32), cond_pre, lax.Precision.HIGHEST)
    head_grad = lax.psum(jnp.stack(scale_grads), ("dp", "blk"))
    return (
        output,
        grad.astype(bf16)[None],
        table_grad,
        head_grad,
        jnp.stack(qkv_grads),
        proj_whole,
        jnp.stack(up_grads),
        jnp.stack(down_grads),
        jnp.stack(ada_grads),
    )


def solution(mesh):
    in_specs = (
        P("dp", "blk", None),
        P("dp", "blk", None),
        P("dp", None),
        P("dp", None),
        P(),
        P(),
        P(None, ("dp", "blk"), None),
        P(None, ("dp", "blk"), None),
        P(None, ("dp", "blk"), None),
        P(None, ("dp", "blk"), None),
        P(None, ("dp", "blk"), None),
    )
    out_specs = (
        P("dp", "blk", None),
        P("dp", "blk", None),
        P(),
        P(),
        P(None, ("dp", "blk"), None),
        P(None, ("dp", "blk"), None),
        P(None, ("dp", "blk"), None),
        P(None, ("dp", "blk"), None),
        P(None, ("dp", "blk"), None),
    )
    return jax.shard_map(
        per_device, mesh=mesh, in_specs=in_specs, out_specs=out_specs, check_vma=False
    )
```

```python
from functools import partial

import jax
import jax.numpy as jnp
from jax import lax
from jax.experimental import pallas as pl
from jax.experimental.pallas import tpu as pltpu
from jax.sharding import PartitionSpec as P

patch_areas = (1, 4, 9, 16, 25, 36, 64, 100, 169)
scale_starts = (1, 5, 14, 30, 55, 91, 155, 255)
f32 = jnp.float32
bf16 = jnp.bfloat16
MESH = pl.DeviceIdType.MESH
TILE = 256
HALF = 128
STEP = 32


def token_meta(stops, length):
    areas = jnp.array(patch_areas, dtype=jnp.int32)
    levels = jnp.arange(9, dtype=jnp.int32)
    counts = jnp.sum(jnp.where(levels[None, :] < stops[:, None], areas[None, :], 0), axis=1)
    ends = jnp.cumsum(counts)
    places = jnp.arange(length, dtype=jnp.int32)
    passed = places[:, None] >= ends[None, :]
    item = jnp.sum(passed.astype(jnp.int32), axis=1)
    begin = jnp.sum(jnp.where(passed, counts[None, :], 0), axis=1)
    inner = places - begin
    bounds = jnp.array(scale_starts, dtype=jnp.int32)
    level = jnp.sum((inner[:, None] >= bounds[None, :]).astype(jnp.int32), axis=1)
    level = jnp.where(item == stops.shape[0], 0, level)
    return (item, level)


def mm(left, right):
    return jnp.dot(left, right, preferred_element_type=f32)


def mm_t(left, right):
    return lax.dot_general(left, right, (((1,), (1,)), ((), ())), preferred_element_type=f32)


def rows_mm(left, right, precision=None):
    return lax.dot_general(
        left, right, (((0,), (0,)), ((), ())), precision=precision, preferred_element_type=f32
    )


def gather(values, axes):
    return lax.all_gather(values, axes, axis=0, tiled=True)


def scatter(values, axes):
    return lax.psum_scatter(values, axes, scatter_dimension=0, tiled=True)


def partners():
    d, b = lax.axis_index("dp"), lax.axis_index("blk")
    return (d, b + 1 - 2 * (b % 2)), (d, (b + 2) % 4)


def greet(others):
    barrier = pltpu.get_barrier_semaphore()
    for other in others:
        pl.semaphore_signal(barrier, inc=1, device_id=other, device_id_type=MESH)
    pl.semaphore_wait(barrier, len(others))


def remote(src, dst, send, recv, target):
    return pltpu.make_async_remote_copy(
        src_ref=src, dst_ref=dst, send_sem=send, recv_sem=recv, device_id=target, device_id_type=MESH
    )


class Spread:
    def __init__(self, buf, send, recv, sibling, peer):
        def copy(src, dst, k, target):
            return remote(
                buf.at[pl.ds(src, HALF)], buf.at[pl.ds(dst, HALF)], send.at[k], recv.at[k], target
            )

        self.to_peer = [copy(HALF * c, 2 * TILE + TILE * c, c, peer) for c in range(2)]
        self.to_sibling = [copy(HALF * c, TILE + HALF * c, 2 + c, sibling) for c in range(2)]
        self.forward = [
            copy(2 * TILE + TILE * c, 2 * TILE + TILE * c + HALF, 4 + c, sibling) for c in range(2)
        ]

    def start(self, c):
        self.to_peer[c].start()
        self.to_sibling[c].start()

    def wait_block(self, i):
        @pl.when(i == 1)
        def _():
            for c in range(2):
                self.to_sibling[c].wait_recv()

        for c in range(2):

            @pl.when(i == 2 + c)
            def _():
                self.to_peer[c].wait_recv()
                self.forward[c].start()
                self.forward[c].wait_recv()

    def finish(self):
        for c in range(2):
            self.to_peer[c].wait_send()
            self.to_sibling[c].wait_send()
            self.forward[c].wait_send()


class Collect:
    def __init__(self, parts, out, mid, own, far, send, recv, sibling, peer):
        self.parts, self.out, self.mid, self.own, self.far = parts, out, mid, own, far
        self.cross = [
            remote(
                parts.at[pl.ds(2 * TILE + TILE * c + HALF, HALF)],
                mid.at[pl.ds(HALF * c, HALF)],
                send.at[c],
                recv.at[c],
                sibling,
            )
            for c in range(2)
        ]
        self.over = [
            remote(
                out.at[pl.ds(HALF * c, HALF)],
                far.at[pl.ds(HALF * c, HALF)],
                send.at[2 + c],
                recv.at[2 + c],
                peer,
            )
            for c in range(2)
        ]
        self.home = remote(parts.at[pl.ds(TILE, TILE)], own, send.at[4], recv.at[4], sibling)

    def block_done(self, j):
        for c in range(2):

            @pl.when(j == 2 + c)
            def _():
                self.cross[c].start()
                self.cross[c].wait_recv()

                @pl.loop(0, HALF // STEP)
                def _(s):
                    at = pl.multiple_of(s * STEP, STEP)
                    mine = self.parts[pl.ds(2 * TILE + TILE * c + at, STEP), :].astype(f32)
                    theirs = self.mid[pl.ds(HALF * c + at, STEP), :].astype(f32)
                    self.out[pl.ds(HALF * c + at, STEP), :] = (mine + theirs).astype(bf16)

                self.over[c].start()

        @pl.when(j == 1)
        def _():
            self.home.start()

    def wait(self):
        self.home.wait_recv()
        for c in range(2):
            self.over[c].wait_recv()

    def rows(self, at):
        span = pl.ds(at, STEP)
        total = self.parts[span, :].astype(f32) + self.own[span, :].astype(f32)
        return total + self.far[span, :].astype(f32)

    def finish(self):
        self.home.wait_send()
        for c in range(2):
            self.cross[c].wait_send()
            self.over[c].wait_send()


def spread_scratch(width):
    return [
        pltpu.VMEM((4 * TILE, width), bf16),
        pltpu.SemaphoreType.DMA((6,)),
        pltpu.SemaphoreType.DMA((6,)),
    ]


def collect_scratch(width):
    return [pltpu.VMEM((4 * TILE, width), bf16)] + [pltpu.VMEM((TILE, width), bf16)] * 4 + [
        pltpu.SemaphoreType.DMA((5,)),
        pltpu.SemaphoreType.DMA((5,)),
    ]


class Moves:
    def __init__(self, sems):
        self.sems, self.used = sems, 0

    def copy(self, src, dst):
        made = pltpu.make_async_copy(src, dst, self.sems.at[self.used])
        self.used += 1
        made.start()
        return made


def expand(onehot, ada, which, outs):
    width = outs[0].shape[1]
    for k, out in zip(which, outs):
        for n in range(0, width, TILE):
            out[:, n : n + TILE] = mm(onehot[...], ada[:, k * width + n : k * width + n + TILE])


def normed(values):
    centre = jnp.mean(values, axis=-1, keepdims=True)
    centred = values - centre
    spread = jnp.mean(centred * centred, axis=-1, keepdims=True)
    rate = lax.rsqrt(spread + 1e-06)
    return centred * rate, rate


def norm_back(grad, values_hat, rate):
    first = jnp.mean(grad, axis=-1, keepdims=True)
    second = jnp.mean(grad * values_hat, axis=-1, keepdims=True)
    return rate * (grad - first - values_hat * second)


def row_steps(start, rows, body):
    @pl.loop(0, rows // STEP)
    def _(s):
        body(pl.multiple_of(start + s * STEP, STEP))


def block_ones(size):
    shape = (TILE, TILE)
    one = lax.broadcasted_iota(jnp.int32, shape, 0) // size
    two = lax.broadcasted_iota(jnp.int32, shape, 1) // size
    return (one == two).astype(bf16)


def split_mm(dot, values, ones):
    high = values.astype(bf16)
    low = (values - high.astype(f32)).astype(bf16)
    return dot(high, ones) + dot(low, ones)


def head_lanes(values, h, size):
    lane = lax.broadcasted_iota(jnp.int32, values.shape, 1) // size
    return jnp.where(lane == h, values, jnp.zeros_like(values))


def hidden_bias(keyc, keyr, rows, cols):
    keys = keyc[pl.ds(rows, TILE), :]
    top = keyr[cols]
    low = top - top % 16
    return jnp.where((keys >= low) & (keys <= top), 0.0, -1e30)


def attend_kernel(
    size,
    jobs,
    x,
    onehot,
    ada,
    qscale,
    keyc,
    keyr,
    wqkv_in,
    wproj_in,
    h_out,
    qkv_out,
    rate_out,
    o_out,
    inv_out,
    branch_out,
    mid_out,
    wqkv,
    wproj,
    qkv,
    vt,
    rates,
    gamma,
    scale,
    shift,
    moves,
    hbuf,
    ag_send,
    ag_recv,
    parts,
    out,
    mid,
    own,
    far,
    rs_send,
    rs_recv,
):
    sibling, peer = partners()
    mover = Moves(moves)
    load_qkv = mover.copy(wqkv_in, wqkv)
    load_proj = mover.copy(wproj_in, wproj)
    expand(onehot, ada, (0, 2, 4), (gamma, scale, shift))
    jobs.greet(sibling, peer)
    jobs.start()
    spread = Spread(hbuf, ag_send, ag_recv, sibling, peer)
    collect = Collect(parts, out, mid, own, far, rs_send, rs_recv, sibling, peer)

    def modulated(at):
        span = pl.ds(at, STEP)
        hat, _ = normed(x[span, :])
        hbuf[span, :] = (hat * (1.0 + scale[span, :]) + shift[span, :]).astype(bf16)

    for c in range(2):
        row_steps(HALF * c, HALF, modulated)
        spread.start(c)
    load_qkv.wait()
    ones = block_ones(size)

    @pl.loop(0, 4)
    def _(i):
        spread.wait_block(i)
        span = pl.ds(pl.multiple_of(i * TILE, TILE), TILE)
        h = hbuf[span, :]
        for part in range(3):
            columns = slice(part * TILE, (part + 1) * TILE)
            value = mm(h, wqkv[:, columns])
            if part < 2:
                rate = lax.rsqrt(split_mm(mm, value * value, ones) + 1e-06)
                if part == 0:
                    rate = rate * qscale[...]
                rates[span, columns] = rate
                value = value * rate
            else:
                vt[:, span] = value.T.astype(bf16)
            qkv[span, columns] = value.astype(bf16)

    jobs.step(0)
    save_h = mover.copy(hbuf, h_out)
    save_qkv = mover.copy(qkv, qkv_out)
    save_rates = mover.copy(rates, rate_out)
    load_proj.wait()
    heads = TILE // size

    @pl.loop(0, 4)
    def _(i):
        j = (i + 2) % 4
        span = pl.ds(pl.multiple_of(j * TILE, TILE), TILE)
        queries = [head_lanes(qkv[span, 0:TILE], h, size) for h in range(heads)]
        sums = [jnp.zeros((1, TILE), f32)] * heads
        mixed = [jnp.zeros((size, TILE), f32)] * heads
        for k in range(4):
            keys = qkv[k * TILE : (k + 1) * TILE, TILE : 2 * TILE]
            bias = hidden_bias(keyc, keyr, k * TILE, j)
            for h in range(heads):
                grown = jnp.exp(mm_t(keys, queries[h]) + bias)
                sums[h] = sums[h] + jnp.sum(grown, axis=0, keepdims=True)
                mixed[h] = mixed[h] + mm(
                    vt[h * size : (h + 1) * size, k * TILE : (k + 1) * TILE], grown.astype(bf16)
                )
        inverse = [1.0 / one for one in sums]
        for h in range(heads):
            inv_out[j, h : h + 1, :] = inverse[h]
        whole = jnp.concatenate([mixed[h] * inverse[h] for h in range(heads)], axis=0)
        low = whole.T.astype(bf16)
        o_out[span, :] = low
        for n in range(0, parts.shape[1], TILE):
            parts[span, n : n + TILE] = mm(low, wproj[:, n : n + TILE]).astype(bf16)
        collect.block_done(j)

    jobs.step(1)
    jobs.step(2)
    collect.wait()

    def added(at):
        span = pl.ds(at, STEP)
        branch = collect.rows(at)
        branch_out[span, :] = branch
        mid_out[span, :] = x[span, :] + gamma[span, :] * branch

    row_steps(0, TILE, added)
    spread.finish()
    collect.finish()
    for one in (save_h, save_qkv, save_rates):
        one.wait()
    jobs.finish()


def early_hooks(jobs, i):
    for hook in range(2):

        @pl.when(i == 2 + hook)
        def _():
            jobs.step(hook)


def mlp_kernel(
    jobs,
    x,
    onehot,
    ada,
    wup_in,
    wdown_in,
    h_out,
    g_out,
    slope_out,
    result_out,
    x_out,
    wup,
    wdown,
    hidden,
    slope,
    gamma,
    scale,
    shift,
    moves,
    hbuf,
    ag_send,
    ag_recv,
    parts,
    out,
    mid,
    own,
    far,
    rs_send,
    rs_recv,
):
    sibling, peer = partners()
    mover = Moves(moves)
    load_up = mover.copy(wup_in, wup)
    load_down = mover.copy(wdown_in, wdown)
    expand(onehot, ada, (1, 3, 5), (gamma, scale, shift))
    jobs.greet(sibling, peer)
    jobs.start()
    spread = Spread(hbuf, ag_send, ag_recv, sibling, peer)
    collect = Collect(parts, out, mid, own, far, rs_send, rs_recv, sibling, peer)

    def modulated(at):
        span = pl.ds(at, STEP)
        hat, _ = normed(x[span, :])
        hbuf[span, :] = (hat * (1.0 + scale[span, :]) + shift[span, :]).astype(bf16)

    for c in range(2):
        row_steps(HALF * c, HALF, modulated)
        spread.start(c)
    load_up.wait()
    load_down.wait()

    @pl.loop(0, 4)
    def _(i):
        spread.wait_block(i)
        early_hooks(jobs, i)
        span = pl.ds(pl.multiple_of(i * TILE, TILE), TILE)
        h = hbuf[span, :]
        for n in range(0, wup.shape[1], TILE):
            columns = slice(n, n + TILE)
            up = mm(h, wup[:, columns])
            square = up * up
            bent = jnp.tanh(0.7978845608 * (up * (1.0 + 0.044715 * square)))
            half = 0.5 * (1.0 + bent)
            hidden[span, columns] = (up * half).astype(bf16)
            inner = 0.7978845608 + (3.0 * 0.044715 * 0.7978845608) * square
            slope[span, columns] = (half + 0.5 * up * (1.0 - bent * bent) * inner).astype(bf16)
        g = hidden[span, :]
        for n in range(0, parts.shape[1], TILE):
            parts[span, n : n + TILE] = mm(g, wdown[:, n : n + TILE]).astype(bf16)
        collect.block_done(i)

    jobs.step(2)
    saves = [mover.copy(a, b) for a, b in ((hbuf, h_out), (hidden, g_out), (slope, slope_out))]
    collect.wait()

    def added(at):
        span = pl.ds(at, STEP)
        result = collect.rows(at)
        result_out[span, :] = result
        x_out[span, :] = x[span, :] + gamma[span, :] * result

    row_steps(0, TILE, added)
    spread.finish()
    collect.finish()
    for one in saves:
        one.wait()
    jobs.finish()


def item_sums(onehot_t, terms, out):
    for k, term in enumerate(terms):
        width = term.shape[1]
        out[:, k * width : (k + 1) * width] = mm(onehot_t[...], term[...])


def mlp_back_kernel(
    jobs,
    dx,
    result,
    mid_state,
    onehot,
    onehot_t,
    ada,
    wup_in,
    wdown_in,
    h_in,
    g_in,
    slope_in,
    dmid_out,
    dwup_out,
    dwdown_out,
    items_out,
    wup,
    wdown,
    hall,
    gall,
    slope,
    dwup,
    dwdown,
    dgamma,
    dscale,
    dshift,
    gamma,
    scale,
    moves,
    hbuf,
    ag_send,
    ag_recv,
    parts,
    out,
    mid,
    own,
    far,
    rs_send,
    rs_recv,
):
    sibling, peer = partners()
    mover = Moves(moves)
    load_down = mover.copy(wdown_in, wdown)
    load_slope = mover.copy(slope_in, slope)
    load_up = mover.copy(wup_in, wup)
    load_g = mover.copy(g_in, gall)
    load_h = mover.copy(h_in, hall)
    expand(onehot, ada, (1, 3), (gamma, scale))
    jobs.greet(sibling, peer)
    jobs.start()
    spread = Spread(hbuf, ag_send, ag_recv, sibling, peer)
    collect = Collect(parts, out, mid, own, far, rs_send, rs_recv, sibling, peer)

    def scaled(at):
        span = pl.ds(at, STEP)
        hbuf[span, :] = (gamma[span, :] * dx[span, :]).astype(bf16)

    for c in range(2):
        row_steps(HALF * c, HALF, scaled)
        spread.start(c)
    for one in (load_down, load_slope, load_up):
        one.wait()

    @pl.loop(0, 4)
    def _(i):
        spread.wait_block(i)
        early_hooks(jobs, i)
        span = pl.ds(pl.multiple_of(i * TILE, TILE), TILE)
        dm = hbuf[span, :]
        for n in range(0, slope.shape[1], TILE):
            columns = slice(n, n + TILE)
            dg = mm_t(dm, wdown[columns, :])
            slope[span, columns] = (dg * slope[span, columns].astype(f32)).astype(bf16)
        du = slope[span, :]
        for n in range(0, parts.shape[1], TILE):
            parts[span, n : n + TILE] = mm_t(du, wup[n : n + TILE, :]).astype(bf16)
        collect.block_done(i)

    jobs.step(2)
    load_g.wait()
    load_h.wait()

    @pl.loop(0, gall.shape[1] // TILE)
    def _(k):
        columns = pl.ds(pl.multiple_of(k * TILE, TILE), TILE)
        for n in range(0, hbuf.shape[1], 2 * TILE):
            dwdown[columns, n : n + 2 * TILE] = rows_mm(
                gall[:, columns], hbuf[:, n : n + 2 * TILE]
            ).astype(bf16)

    save_down = mover.copy(dwdown, dwdown_out)

    @pl.loop(0, hall.shape[1] // TILE)
    def _(k):
        columns = pl.ds(pl.multiple_of(k * TILE, TILE), TILE)
        for n in range(0, slope.shape[1], 2 * TILE):
            dwup[columns, n : n + 2 * TILE] = rows_mm(
                hall[:, columns], slope[:, n : n + 2 * TILE]
            ).astype(bf16)

    save_up = mover.copy(dwup, dwup_out)
    collect.wait()

    def added(at):
        span = pl.ds(at, STEP)
        dh = collect.rows(at)
        hat, rate = normed(mid_state[span, :])
        grad = dx[span, :]
        dgamma[span, :] = (grad * result[span, :]).astype(bf16)
        dscale[span, :] = (dh * hat).astype(bf16)
        dshift[span, :] = dh.astype(bf16)
        dmid_out[span, :] = grad + norm_back(dh * (1.0 + scale[span, :]), hat, rate)

    row_steps(0, TILE, added)
    item_sums(onehot_t, (dgamma, dscale, dshift), items_out)
    spread.finish()
    collect.finish()
    save_down.wait()
    save_up.wait()
    jobs.finish()


def attend_back_kernel(
    size,
    jobs,
    dmid,
    branch,
    x,
    onehot,
    onehot_t,
    ada,
    qscale,
    keyc,
    keyr,
    inverse,
    wqkv_in,
    wproj_in,
    h_in,
    qkv_in,
    rate_in,
    o_in,
    dx_out,
    dwqkv_out,
    dwproj_out,
    items_out,
    head_out,
    wqkv,
    wproj,
    hall,
    qkv,
    rates,
    oall,
    kt,
    dkeys,
    dvalues,
    dqkv,
    dwqkv,
    dwproj,
    dgamma,
    dscale,
    dshift,
    gamma,
    scale,
    moves,
    hbuf,
    ag_send,
    ag_recv,
    parts,
    out,
    mid,
    own,
    far,
    rs_send,
    rs_recv,
):
    sibling, peer = partners()
    mover = Moves(moves)
    load_proj = mover.copy(wproj_in, wproj)
    load_qkv = mover.copy(qkv_in, qkv)
    load_o = mover.copy(o_in, oall)
    load_rates = mover.copy(rate_in, rates)
    load_w = mover.copy(wqkv_in, wqkv)
    load_h = mover.copy(h_in, hall)
    expand(onehot, ada, (0, 2), (gamma, scale))
    jobs.greet(sibling, peer)
    jobs.start()
    spread = Spread(hbuf, ag_send, ag_recv, sibling, peer)
    collect = Collect(parts, out, mid, own, far, rs_send, rs_recv, sibling, peer)

    def scaled(at):
        span = pl.ds(at, STEP)
        hbuf[span, :] = (gamma[span, :] * dmid[span, :]).astype(bf16)

    for c in range(2):
        row_steps(HALF * c, HALF, scaled)
        spread.start(c)
    for one in (load_proj, load_qkv, load_o, load_rates):
        one.wait()
    heads = TILE // size
    ones = block_ones(size)
    inv_square = 1.0 / (qscale[...] * qscale[...])
    select = (
        lax.broadcasted_iota(jnp.int32, (8, TILE), 1) // size
        == lax.broadcasted_iota(jnp.int32, (8, TILE), 0)
    ).astype(bf16)
    dkeys[...] = jnp.zeros_like(dkeys)
    dvalues[...] = jnp.zeros_like(dvalues)
    head_out[...] = jnp.zeros_like(head_out)
    for k in range(4):
        rows = slice(k * TILE, (k + 1) * TILE)
        kt[:, rows] = qkv[rows, TILE : 2 * TILE].astype(f32).T.astype(bf16)

    @pl.loop(0, 4)
    def _(i):
        spread.wait_block(i)

        @pl.when(i == 3)
        def _():
            jobs.step(0)

        span = pl.ds(pl.multiple_of(i * TILE, TILE), TILE)
        dout = mm_t(hbuf[span, :], wproj[...]).astype(bf16)
        product = dout.astype(f32) * oall[span, :].astype(f32)
        row_term = split_mm(lambda a, b: mm_t(b, a), product, select)
        q_low = qkv[span, 0:TILE]
        queries = [head_lanes(q_low, h, size) for h in range(heads)]
        douts = [head_lanes(dout, h, size) for h in range(heads)]
        dquery = [jnp.zeros((size, TILE), f32)] * heads
        for k in range(4):
            rows = slice(k * TILE, (k + 1) * TILE)
            keys = qkv[rows, TILE : 2 * TILE]
            values = qkv[rows, 2 * TILE : 3 * TILE]
            bias = hidden_bias(keyc, keyr, k * TILE, i)
            dkey = jnp.zeros((TILE, TILE), f32)
            dvalue = jnp.zeros((TILE, TILE), f32)
            for h in range(heads):
                share = jnp.exp(mm_t(keys, queries[h]) + bias) * inverse[i, h : h + 1, :]
                dshare = mm_t(values, douts[h])
                dscore = (share * (dshare - row_term[h : h + 1, :])).astype(bf16)
                dvalue = dvalue + mm(share.astype(bf16), douts[h])
                dkey = dkey + mm(dscore, queries[h])
                dquery[h] = dquery[h] + mm(kt[h * size : (h + 1) * size, rows], dscore)
            dkeys[rows, :] += dkey
            dvalues[rows, :] += dvalue
        dq = jnp.concatenate(dquery, axis=0).T
        qhat = q_low.astype(f32)
        along = split_mm(mm, dq * qhat, ones)
        head_out[...] += jnp.sum(along, axis=0, keepdims=True)
        dqkv[span, 0:TILE] = (rates[span, 0:TILE] * (dq - qhat * (along * inv_square))).astype(bf16)

    load_w.wait()
    jobs.step(1)

    @pl.loop(0, 4)
    def _(i):
        j = (i + 2) % 4
        span = pl.ds(pl.multiple_of(j * TILE, TILE), TILE)
        dk = dkeys[span, :]
        khat = qkv[span, TILE : 2 * TILE].astype(f32)
        along = split_mm(mm, dk * khat, ones)
        dqkv[span, TILE : 2 * TILE] = (
            rates[span, TILE : 2 * TILE] * (dk - khat * along)
        ).astype(bf16)
        dqkv[span, 2 * TILE : 3 * TILE] = dvalues[span, :].astype(bf16)
        low = dqkv[span, :]
        for n in range(0, parts.shape[1], TILE):
            parts[span, n : n + TILE] = mm_t(low, wqkv[n : n + TILE, :]).astype(bf16)
        collect.block_done(j)

    jobs.step(2)
    for n in range(0, hbuf.shape[1], 2 * TILE):
        dwproj[:, n : n + 2 * TILE] = rows_mm(oall[...], hbuf[:, n : n + 2 * TILE]).astype(bf16)
    save_proj = mover.copy(dwproj, dwproj_out)
    load_h.wait()

    @pl.loop(0, hall.shape[1] // TILE)
    def _(k):
        columns = pl.ds(pl.multiple_of(k * TILE, TILE), TILE)
        dwqkv[columns, :] = rows_mm(hall[:, columns], dqkv[...]).astype(bf16)

    save_w = mover.copy(dwqkv, dwqkv_out)
    collect.wait()

    def added(at):
        span = pl.ds(at, STEP)
        dh = collect.rows(at)
        hat, rate = normed(x[span, :])
        grad = dmid[span, :]
        dgamma[span, :] = (grad * branch[span, :]).astype(bf16)
        dscale[span, :] = (dh * hat).astype(bf16)
        dshift[span, :] = dh.astype(bf16)
        dx_out[span, :] = grad + norm_back(dh * (1.0 + scale[span, :]), hat, rate)

    row_steps(0, TILE, added)
    item_sums(onehot_t, (dgamma, dscale, dshift), items_out)
    spread.finish()
    collect.finish()
    save_proj.wait()
    save_w.wait()
    jobs.finish()


def groups(dps):
    d, b = lax.axis_index("dp"), lax.axis_index("blk")
    side, pairs = d % 2, dps // 2
    pair = d // 2
    ahead = [((pair + k) % pairs) * 2 + side for k in range(pairs)]
    behind = [((pair - k + pairs) % pairs) * 2 + side for k in range(pairs)]
    return d, b, d + 1 - 2 * side, ahead, behind


class DpGather:
    def __init__(self, shards):
        self.shards = list(shards)
        self.dps = lax.axis_size("dp")
        self.inputs = [(one, ANY) for one in self.shards]
        self.outs = [
            (shaped(self.dps, *one.shape, dtype=one.dtype), ANY) for one in self.shards
        ]
        count = len(self.shards)
        sems = pltpu.SemaphoreType.DMA((count, self.dps))
        self.scratch = [sems, sems, pltpu.SemaphoreType.DMA((count,))]

    def bind(self, ins, outs, scratch):
        send, recv, local = scratch
        d, b, other, ahead, behind = groups(self.dps)
        pairs = self.dps // 2
        self.partners = [(other, b)] + [(t, b) for t in ahead[1:]]
        self.first, self.direct, self.forward, self.local = [], [], [], []
        for a, (src, dst) in enumerate(zip(ins, outs)):
            self.local.append(pltpu.make_async_copy(src, dst.at[d], local.at[a]))
            self.first.append(remote(src, dst.at[d], send.at[a, 0], recv.at[a, 0], (other, b)))
            self.direct.append([None])
            self.forward.append([None])
            for k in range(1, pairs):
                self.direct[a].append(
                    remote(src, dst.at[d], send.at[a, k], recv.at[a, k], (ahead[k], b))
                )
                at = pairs + k
                self.forward[a].append(
                    remote(
                        dst.at[behind[k]], dst.at[behind[k]], send.at[a, at], recv.at[a, at], (other, b)
                    )
                )
        self.order = [(k, a) for k in range(1, pairs) for a in range(len(ins))]

    def start(self):
        for k, a in self.order:
            self.direct[a][k].start()
        for one in self.first + self.local:
            one.start()

    def step(self, hook, hooks):
        low, high = (len(self.order) * hook) // hooks, (len(self.order) * (hook + 1)) // hooks
        for k, a in self.order[low:high]:
            self.direct[a][k].wait_recv()
            self.forward[a][k].start()

    def finish(self):
        for one in self.local:
            one.wait()
        for one in self.first:
            one.wait()
        for k, a in self.order:
            self.direct[a][k].wait_send()
            self.forward[a][k].wait()


class DpScatter:
    def __init__(self, values, dtypes):
        self.values = list(values)
        self.dps = lax.axis_size("dp")
        self.inputs = [(one, ANY) for one in self.values]
        self.outs = [
            (shaped(*one.shape[1:], dtype=dtype), VMEM) for one, dtype in zip(self.values, dtypes)
        ]
        pairs = self.dps // 2
        self.scratch = []
        for one in self.values:
            self.scratch += [pltpu.VMEM((pairs, *one.shape[1:]), bf16)] * 3
            self.scratch += [pltpu.SemaphoreType.DMA((2 * pairs,))] * 2
            self.scratch += [pltpu.SemaphoreType.DMA((pairs,))]

    def bind(self, ins, outs, scratch):
        d, b, other, ahead, behind = groups(self.dps)
        pairs = self.dps // 2
        self.partners = [(other, b)] + [(t, b) for t in ahead[1:]]
        self.results = outs
        self.bufs, self.local, self.cross, self.direct = [], [], [], []
        for a, src in enumerate(ins):
            mine, near, far, send, recv, local = scratch[6 * a : 6 * a + 6]
            self.bufs.append((mine, near, far))
            self.local.append([])
            self.cross.append([])
            self.direct.append([None])
            for k in range(pairs):
                target = ahead[k]
                theirs = target + 1 - 2 * (target % 2)
                self.local[a].append(
                    pltpu.make_async_copy(src.at[target], mine.at[k], local.at[k])
                )
                self.cross[a].append(
                    remote(src.at[theirs], near.at[k], send.at[k], recv.at[k], (other, b))
                )
                if k:
                    at = pairs + k
                    self.direct[a].append(
                        remote(mine.at[k], far.at[k], send.at[at], recv.at[at], (target, b))
                    )
        self.order = [(k, a) for k in range(1, pairs) for a in range(len(ins))]
        self.last = [(0, a) for a in range(len(ins))]

    def start(self):
        for k, a in self.order + self.last:
            self.cross[a][k].start()
            self.local[a][k].start()

    def add(self, a, k):
        self.local[a][k].wait()
        self.cross[a][k].wait_recv()
        mine, near, _ = self.bufs[a]
        rows = mine.shape[1]
        step = min(rows, STEP)

        @pl.loop(0, rows // step)
        def _(s):
            span = pl.ds(pl.multiple_of(s * step, step), step)
            total = mine[k, span, :].astype(f32) + near[k, span, :].astype(f32)
            mine[k, span, :] = total.astype(bf16)

    def step(self, hook, hooks):
        low, high = (len(self.order) * hook) // hooks, (len(self.order) * (hook + 1)) // hooks
        for k, a in self.order[low:high]:
            self.add(a, k)
            self.direct[a][k].start()

    def finish(self):
        for k, a in self.last:
            self.add(a, k)
        for k, a in self.order:
            self.direct[a][k].wait()
        for k, a in self.order + self.last:
            self.cross[a][k].wait_send()
        for a, result in enumerate(self.results):
            mine, _, far = self.bufs[a]
            rows = mine.shape[1]
            step = min(rows, STEP)

            @pl.loop(0, rows // step)
            def _(s):
                span = pl.ds(pl.multiple_of(s * step, step), step)
                total = mine[0, span, :].astype(f32)
                for k in range(1, self.dps // 2):
                    total = total + far[k, span, :].astype(f32)
                result[span, :] = total.astype(result.dtype)


class Swap:
    def __init__(self, values):
        self.values = list(values)
        self.inputs = [(one, ANY) for one in self.values]
        self.outs = [(shaped(*one.shape, dtype=one.dtype), ANY) for one in self.values]
        sems = pltpu.SemaphoreType.DMA((len(self.values), 4))
        self.scratch = [sems, sems]

    def bind(self, ins, outs, scratch):
        send, recv = scratch
        d, b = lax.axis_index("dp"), lax.axis_index("blk")
        self.partners = [(d, (b + k) % 4) for k in range(1, 4)]
        self.local, self.sent = [], []
        for a, (src, dst) in enumerate(zip(ins, outs)):
            self.local.append(pltpu.make_async_copy(src.at[b], dst.at[b], send.at[a, 0]))
            for k in range(1, 4):
                to = (b + k) % 4
                self.sent.append(
                    remote(src.at[to], dst.at[b], send.at[a, k], recv.at[a, k], (d, to))
                )

    def start(self):
        for one in self.sent + self.local:
            one.start()

    def step(self, hook, hooks):
        pass

    def finish(self):
        for one in self.sent + self.local:
            one.wait()


class Items:
    def __init__(self, items):
        self.dps = lax.axis_size("dp")
        slots, columns = items.shape
        self.quarter = columns // 4
        self.inputs = [(items, ANY)]
        self.outs = [(shaped(4, self.dps, slots, self.quarter, dtype=bf16), VMEM)]
        sems = pltpu.SemaphoreType.DMA
        self.scratch = [
            pltpu.VMEM((4, slots, self.quarter), f32),
            pltpu.VMEM((self.dps, slots, self.quarter), bf16),
            sems((8,)),
            sems((8,)),
            sems((self.dps,)),
            sems((self.dps,)),
        ]

    def bind(self, ins, outs, scratch):
        (src,), (out,) = ins, outs
        self.terms, self.held, send, recv, dp_send, dp_recv = scratch
        d, b = lax.axis_index("dp"), lax.axis_index("blk")
        self.here, self.out = (d, b), out
        self.partners = [((d + k) % self.dps, b) for k in range(1, self.dps)]

        def quarter(i):
            return src.at[:, pl.ds(pl.multiple_of(i * self.quarter, 128), self.quarter)]

        self.first = [pltpu.make_async_copy(quarter(b), self.terms.at[0], send.at[0])]
        self.last = []
        for k in range(1, 4):
            to = (b + k) % 4
            self.first.append(
                remote(quarter(to), self.terms.at[k], send.at[k], recv.at[k], (d, to))
            )
            self.last.append(
                remote(self.held, out.at[b], send.at[4 + k], recv.at[4 + k], (d, to))
            )
        self.over = [
            remote(self.held.at[d], self.held.at[d], dp_send.at[k], dp_recv.at[k], to)
            for k, to in enumerate(self.partners)
        ]

    def start(self):
        for one in self.first:
            one.start()

    def step(self, hook, hooks):
        d, b = self.here
        if hook == 0:
            for one in self.first:
                one.wait()
            total = (self.terms[0] + self.terms[1]) + (self.terms[2] + self.terms[3])
            self.held[d] = total.astype(bf16)
            for one in self.over:
                one.start()
        if hook == 1:
            for one in self.over:
                one.wait()
            for one in self.last:
                one.start()
            self.out[b] = self.held[...]

    def finish(self):
        for one in self.last:
            one.wait()


def greet_all():
    dps, blks = lax.axis_size("dp"), lax.axis_size("blk")
    me = lax.axis_index("dp") * blks + lax.axis_index("blk")
    others = [(me + k) % (dps * blks) for k in range(1, dps * blks)]
    greet([(t // blks, t % blks) for t in others])


class Permute:
    def __init__(self, src, dst, send, recv, back):
        dps, blks = lax.axis_size("dp"), lax.axis_size("blk")
        d, b = lax.axis_index("dp"), lax.axis_index("blk")
        owner, user = d * blks + b, b * dps + d
        self.moves = owner != user
        to = (user // blks, user % blks) if back else (owner % dps, owner // dps)
        self.away = remote(src, dst, send, recv, to)
        self.stay = pltpu.make_async_copy(src, dst, send)

    def start(self):
        @pl.when(self.moves)
        def _():
            self.away.start()

        @pl.when(jnp.logical_not(self.moves))
        def _():
            self.stay.start()

    def wait(self):
        @pl.when(self.moves)
        def _():
            self.away.wait()

        @pl.when(jnp.logical_not(self.moves))
        def _():
            self.stay.wait()


class Jobs:
    def __init__(self, jobs):
        self.jobs = jobs

    def greet(self, sibling, peer):
        d, b = lax.axis_index("dp"), lax.axis_index("blk")
        others = [sibling, peer]
        if any(isinstance(job, (Swap, Items)) for job in self.jobs):
            others.append((d, 3 - b))
        dps = [job for job in self.jobs if not isinstance(job, Swap)]
        if dps:
            others += max((job.partners for job in dps), key=len)
        greet(others)

    def start(self):
        for job in self.jobs:
            job.start()

    def step(self, hook):
        for job in self.jobs:
            job.step(hook, 3)

    def finish(self):
        for job in self.jobs:
            job.finish()


def prepare_kernel(
    rows_in,
    ada_in,
    qkv_in,
    up_in,
    proj_in,
    ada_out,
    rows_out,
    qkv_shard,
    up_shard,
    proj_shard,
    qkv_out,
    proj_out,
    columns,
    answers,
    ada,
    dp_send,
    dp_recv,
    ada_send,
    ada_recv,
    answer_send,
    answer_recv,
    blk_send,
    blk_recv,
    proj_send,
    proj_recv,
    local,
    *gather_scratch,
):
    dps, blks = lax.axis_size("dp"), lax.axis_size("blk")
    count = dps * blks
    d, b = lax.axis_index("dp"), lax.axis_index("blk")
    me = d * blks + b
    layers, double, each = ada_out.shape
    slots = double // 2
    rows, wide = ada_in.shape[1:]
    greet_all()
    job = DpGather([shaped(*qkv_shard.shape, dtype=bf16), shaped(*proj_shard.shape[1:], dtype=bf16)])
    job.bind([qkv_shard, proj_shard.at[0]], [qkv_out, proj_out], gather_scratch)

    permutes = [
        Permute(proj_in.at[i], proj_shard.at[i], proj_send.at[i], proj_recv.at[i], False)
        for i in range(layers)
    ]
    copies = [pltpu.make_async_copy(rows_in, rows_out.at[d], local.at[0])]
    sends = []
    for k in range(1, dps):
        sends.append(
            remote(rows_in, rows_out.at[d], dp_send.at[k], dp_recv.at[k], ((d + k) % dps, b))
        )
    swaps = []
    for a, (src, dst) in enumerate(((qkv_in, qkv_shard), (up_in, up_shard))):
        copies.append(pltpu.make_async_copy(src.at[b], dst.at[b], local.at[1 + a]))
        for k in range(1, blks):
            to = (b + k) % blks
            swaps.append(
                remote(src.at[to], dst.at[b], blk_send.at[a, k], blk_recv.at[a, k], (d, to))
            )
    moves = []
    span = pl.ds(pl.multiple_of(me * rows, rows), rows)
    copies.append(pltpu.make_async_copy(ada_in.at[me], columns.at[span], local.at[3]))
    for k in range(1, count):
        t = (me + k) % count
        to = (t // blks, t % blks)
        moves.append(remote(ada_in.at[t], columns.at[span], ada_send.at[k], ada_recv.at[k], to))
    for one in permutes[:1] + swaps[: blks - 1] + copies + sends + moves:
        one.start()
    for one in swaps[: blks - 1]:
        one.wait_recv()
    for one in copies:
        one.wait()
    permutes[0].wait()
    job.start()
    for one in swaps[blks - 1 :] + permutes[1:]:
        one.start()
    for one in sends + moves:
        one.wait_recv()
    value = rows_out[...].astype(f32)
    value = (value / (1.0 + jnp.exp(-value))).astype(bf16)
    whole = mm(value.reshape(dps * slots, rows_out.shape[2]), columns[...])
    answers[...] = whole.reshape(dps, slots, wide)
    place = pl.ds(pl.multiple_of(me * wide, 128), wide)
    replies = []
    for k in range(1, count):
        t = (me + k) % count
        to = (t // blks, t % blks)
        replies.append(
            remote(
                answers.at[t // blks], ada.at[:, place], answer_send.at[k], answer_recv.at[k], to
            )
        )
    for one in replies:
        one.start()
    ada[:, place] = answers[d]
    for one in replies:
        one.wait_recv()
    for layer in range(layers):
        value = ada[:, layer * each : (layer + 1) * each]
        high = value.astype(bf16)
        ada_out[layer, 0:slots, :] = high
        ada_out[layer, slots:double, :] = (value - high.astype(f32)).astype(bf16)
    for hook in range(3):
        job.step(hook, 3)
    for one in sends + moves + replies + swaps:
        one.wait_send()
    for one in swaps[blks - 1 :]:
        one.wait_recv()
    for one in permutes[1:]:
        one.wait()
    job.finish()


def prepare(rows_in, ada_in, qkv_in, up_in, proj):
    dps, blks = lax.axis_size("dp"), lax.axis_size("blk")
    count = dps * blks
    slots, width = rows_in.shape
    layers = proj.shape[0]
    rows, wide = ada_in.shape[1:]
    sems = pltpu.SemaphoreType.DMA
    outs = [
        (shaped(layers, 2 * slots, count * wide // layers, dtype=bf16), VMEM),
        (shaped(dps, slots, width, dtype=bf16), VMEM),
        (shaped(*qkv_in.shape, dtype=bf16), ANY),
        (shaped(*up_in.shape, dtype=bf16), ANY),
        (shaped(*proj.shape, dtype=bf16), ANY),
        (shaped(dps, *qkv_in.shape, dtype=bf16), ANY),
        (shaped(dps, *proj.shape[1:], dtype=bf16), ANY),
    ]
    scratch = [
        pltpu.VMEM((count * rows, wide), bf16),
        pltpu.VMEM((dps, slots, wide), f32),
        pltpu.VMEM((slots, count * wide), f32),
    ]
    scratch += [sems((dps,))] * 2 + [sems((count,))] * 4
    scratch += [sems((2, blks))] * 2 + [sems((layers,))] * 2 + [sems((4,))]
    scratch += [sems((2, dps))] * 2 + [sems((2,))]
    return run(
        lambda jobs, *refs: prepare_kernel(*refs),
        8,
        [(rows_in, ANY), (ada_in, ANY), (qkv_in, ANY), (up_in, ANY), (proj, ANY)],
        outs,
        scratch,
        2**35,
    )[0]


def finish_kernel(
    jobs,
    cond,
    w_ada,
    notes,
    proj_next,
    two_next,
    one_next,
    two,
    qkv_out,
    proj_out,
    ada_grad,
    message_out,
    staged,
    message,
    blk_send,
    blk_recv,
    proj_send,
    proj_recv,
    all_send,
    all_recv,
    local,
):
    items, scatter_job, swap = jobs.jobs
    dps, blks = lax.axis_size("dp"), lax.axis_size("blk")
    count = dps * blks
    d, b = lax.axis_index("dp"), lax.axis_index("blk")
    me = d * blks + b
    greet_all()
    for job in jobs.jobs:
        job.start()
    permute_next = Permute(proj_next, proj_out.at[1], proj_send.at[1], proj_recv.at[1], True)
    permute_next.start()
    rows = w_ada.shape[1]
    width = w_ada.shape[2] // 6
    people = cond.shape[1]

    def fold(layer, second, dada, total):
        quarter = dada.shape[3]
        for c in range(0, 3 * width, TILE):
            at = (c // width) * 2 * width + second * width + c % width
            inner = c % quarter
            value = dada[c // quarter, :, :, inner : inner + TILE].reshape(people, TILE)
            ada_grad[layer, :, at : at + TILE] = mm(cond[...], value)
            total = total + mm_t(w_ada[layer, :, at : at + TILE], value)
        return total

    items.step(0, 3)
    total = fold(1, 1, two_next, jnp.zeros((rows, people), f32))
    items.step(1, 3)
    total = fold(1, 0, one_next, total)
    scatter_job.step(0, 3)
    total = fold(0, 1, two, total)
    items.finish()
    total = fold(0, 0, items.out, total)
    message[0:rows, :] = total
    message[rows:, :] = notes[...]
    told = [pltpu.make_async_copy(message, message_out.at[me], local.at[0])]
    for k in range(1, count):
        t = (me + k) % count
        to = (t // blks, t % blks)
        told.append(remote(message, message_out.at[me], all_send.at[k], all_recv.at[k], to))
    for one in told:
        one.start()
    scatter_job.step(1, 3)
    scatter_job.step(2, 3)
    scatter_job.finish()
    qkv_sum, proj_sum = scatter_job.results
    permute = Permute(proj_sum, proj_out.at[0], proj_send.at[0], proj_recv.at[0], True)
    permute.start()
    height = staged.shape[1]
    for i in range(4):
        staged[i] = qkv_sum[i * height : (i + 1) * height, :]
    sent = [pltpu.make_async_copy(staged.at[b], qkv_out.at[b], local.at[1])]
    for k in range(1, 4):
        to = (b + k) % 4
        sent.append(remote(staged.at[to], qkv_out.at[b], blk_send.at[k], blk_recv.at[k], (d, to)))
    for one in sent:
        one.start()
    swap.finish()
    for one in sent + told + [permute, permute_next]:
        one.wait()


def finish(scatter_job, swap_job, items_job, cond, w_ada, notes, proj_next, dadas):
    dps, blks = lax.axis_size("dp"), lax.axis_size("blk")
    count = dps * blks
    rows, columns = scatter_job.values[0].shape[1:]
    shape = (4, rows // 4, columns)
    sems = pltpu.SemaphoreType.DMA
    message = shaped(w_ada.shape[1] + notes.shape[0], cond.shape[1])
    inputs = [cond, w_ada, notes, proj_next, *dadas]
    return run(
        finish_kernel,
        9,
        [(one, VMEM) for one in inputs],
        [
            (shaped(*shape, dtype=bf16), VMEM),
            (shaped(2, *proj_next.shape), VMEM),
            (shaped(*w_ada.shape), VMEM),
            (shaped(count, *message.shape), VMEM),
        ],
        [pltpu.VMEM(shape, bf16), pltpu.VMEM(message.shape, f32)]
        + [sems((4,))] * 2
        + [sems((2,))] * 2
        + [sems((count,))] * 2
        + [sems((2,))],
        2**30,
        [items_job, scatter_job, swap_job],
    )


ANY = pl.BlockSpec(memory_space=pl.ANY)
VMEM = pl.BlockSpec(memory_space=pltpu.VMEM)


def shaped(*shape, dtype=f32):
    return jax.ShapeDtypeStruct(shape, dtype)


def run(kernel, ident, inputs, outs, scratch, flops, jobs=()):
    sizes = [(len(inputs), len(outs), len(scratch))]
    sizes += [(len(job.inputs), len(job.outs), len(job.scratch)) for job in jobs]
    own_outs = len(outs)
    for job in jobs:
        inputs, outs, scratch = inputs + job.inputs, outs + job.outs, scratch + job.scratch

    def body(*refs):
        at = 0
        shares = [[] for _ in sizes]
        for kind in range(3):
            for i, size in enumerate(sizes):
                shares[i].append(refs[at : at + size[kind]])
                at += size[kind]
        for job, share in zip(jobs, shares[1:]):
            job.bind(*share)
        kernel(Jobs(jobs), *shares[0][0], *shares[0][1], *shares[0][2])

    results = pl.pallas_call(
        body,
        out_shape=[one for one, _ in outs],
        in_specs=[where for _, where in inputs],
        out_specs=[where for _, where in outs],
        scratch_shapes=scratch,
        compiler_params=pltpu.CompilerParams(
            collective_id=ident, has_side_effects=True, vmem_limit_bytes=56 * 2**20
        ),
        cost_estimate=pl.CostEstimate(flops=flops, bytes_accessed=2**24, transcendentals=0),
    )(*[one for one, _ in inputs])
    return results[:own_outs], results[own_outs:]


def attend(layer, size, x, onehot, ada, qscale, keyc, keyr, wqkv, wproj, jobs=()):
    rows, width = x.shape
    length, wide = wqkv.shape
    big = pltpu.VMEM((rows, width), f32)
    return run(
        partial(attend_kernel, size),
        layer,
        [(a, VMEM) for a in (x, onehot, ada, qscale, keyc, keyr)] + [(wqkv, ANY), (wproj, ANY)],
        [
            (shaped(length, width, dtype=bf16), ANY),
            (shaped(length, wide, dtype=bf16), ANY),
            (shaped(length, 2 * TILE), ANY),
            (shaped(length, TILE, dtype=bf16), VMEM),
            (shaped(4, 8, TILE), VMEM),
            (shaped(rows, width), VMEM),
            (shaped(rows, width), VMEM),
        ],
        [
            pltpu.VMEM(wqkv.shape, bf16),
            pltpu.VMEM(wproj.shape, bf16),
            pltpu.VMEM((length, wide), bf16),
            pltpu.VMEM((TILE, length), bf16),
            pltpu.VMEM((length, 2 * TILE), f32),
            big,
            big,
            big,
            pltpu.SemaphoreType.DMA((5,)),
        ]
        + spread_scratch(width)
        + collect_scratch(width),
        2**35,
        jobs,
    )


def mlp(layer, x, onehot, ada, wup, wdown, jobs=()):
    rows, width = x.shape
    length, ff = 4 * rows, wup.shape[1]
    big = pltpu.VMEM((rows, width), f32)
    return run(
        mlp_kernel,
        2 + layer,
        [(a, VMEM) for a in (x, onehot, ada)] + [(wup, ANY), (wdown, ANY)],
        [
            (shaped(length, width, dtype=bf16), ANY),
            (shaped(length, ff, dtype=bf16), ANY),
            (shaped(length, ff, dtype=bf16), ANY),
            (shaped(rows, width), VMEM),
            (shaped(rows, width), VMEM),
        ],
        [
            pltpu.VMEM(wup.shape, bf16),
            pltpu.VMEM(wdown.shape, bf16),
            pltpu.VMEM((length, ff), bf16),
            pltpu.VMEM((length, ff), bf16),
            big,
            big,
            big,
            pltpu.SemaphoreType.DMA((5,)),
        ]
        + spread_scratch(width)
        + collect_scratch(width),
        2**35,
        jobs,
    )


def mlp_back(layer, dx, result, mid, onehot, onehot_t, ada, wup, wdown, h, g, slope, jobs=()):
    rows, width = dx.shape
    length, ff = 4 * rows, wup.shape[1]
    big = pltpu.VMEM((rows, width), f32)
    small = pltpu.VMEM((rows, width), bf16)
    return run(
        mlp_back_kernel,
        4 + layer,
        [(a, VMEM) for a in (dx, result, mid, onehot, onehot_t, ada)]
        + [(a, ANY) for a in (wup, wdown, h, g, slope)],
        [
            (shaped(rows, width), VMEM),
            (shaped(*wup.shape, dtype=bf16), ANY),
            (shaped(*wdown.shape, dtype=bf16), ANY),
            (shaped(onehot_t.shape[0], 3 * width), VMEM),
        ],
        [
            pltpu.VMEM(wup.shape, bf16),
            pltpu.VMEM(wdown.shape, bf16),
            pltpu.VMEM((length, width), bf16),
            pltpu.VMEM((length, ff), bf16),
            pltpu.VMEM((length, ff), bf16),
            pltpu.VMEM(wup.shape, bf16),
            pltpu.VMEM(wdown.shape, bf16),
            small,
            small,
            small,
            big,
            big,
            pltpu.SemaphoreType.DMA((7,)),
        ]
        + spread_scratch(width)
        + collect_scratch(width),
        2**35,
        jobs,
    )


def attend_back(
    layer,
    size,
    dmid,
    branch,
    x,
    onehot,
    onehot_t,
    ada,
    qscale,
    keyc,
    keyr,
    inverse,
    wqkv,
    wproj,
    h,
    qkv,
    rates,
    o,
    jobs=(),
):
    rows, width = dmid.shape
    length, wide = qkv.shape
    big = pltpu.VMEM((rows, width), f32)
    small = pltpu.VMEM((rows, width), bf16)
    return run(
        partial(attend_back_kernel, size),
        6 + layer,
        [(a, VMEM) for a in (dmid, branch, x, onehot, onehot_t, ada, qscale, keyc, keyr, inverse)]
        + [(a, ANY) for a in (wqkv, wproj, h, qkv, rates, o)],
        [
            (shaped(rows, width), VMEM),
            (shaped(*wqkv.shape, dtype=bf16), ANY),
            (shaped(*wproj.shape, dtype=bf16), ANY),
            (shaped(onehot_t.shape[0], 3 * width), VMEM),
            (shaped(1, TILE), VMEM),
        ],
        [
            pltpu.VMEM(wqkv.shape, bf16),
            pltpu.VMEM(wproj.shape, bf16),
            pltpu.VMEM((length, width), bf16),
            pltpu.VMEM((length, wide), bf16),
            pltpu.VMEM((length, 2 * TILE), f32),
            pltpu.VMEM((length, TILE), bf16),
            pltpu.VMEM((TILE, length), bf16),
            pltpu.VMEM((length, TILE), f32),
            pltpu.VMEM((length, TILE), f32),
            pltpu.VMEM((length, wide), bf16),
            pltpu.VMEM(wqkv.shape, bf16),
            pltpu.VMEM(wproj.shape, bf16),
            small,
            small,
            small,
            big,
            big,
            pltpu.SemaphoreType.DMA((8,)),
        ]
        + spread_scratch(width)
        + collect_scratch(width),
        2**35,
        jobs,
    )


def per_device(
    tokens,
    cotangent,
    stop_scale,
    labels,
    class_table,
    head_scale,
    w_qkv,
    w_proj,
    w_up,
    w_down,
    w_ada,
):
    rows, width = tokens.shape[1:]
    layers, heads = head_scale.shape
    size = width // heads
    dps, blks = lax.axis_size("dp"), lax.axis_size("blk")
    count = dps * blks
    length = rows * blks
    d, b = lax.axis_index("dp"), lax.axis_index("blk")
    own_heads = heads // blks
    piece = own_heads * size
    wrows = w_qkv.shape[1]
    ffrows = w_down.shape[1]
    ff = ffrows * dps
    slots = labels.shape[1]
    padded = 16

    item_all, level_all = token_meta(stop_scale[0], length)
    item_own = lax.dynamic_slice_in_dim(item_all, b * rows, rows)
    key = (item_all * 16 + level_all).reshape(blks, rows)
    sib = b + 1 - 2 * (b % 2)
    far, far_sib = (b + 2) % 4, (sib + 2) % 4
    key = jnp.concatenate(
        [key[b], key[sib], key[far, :HALF], key[far_sib, :HALF], key[far, HALF:], key[far_sib, HALF:]]
    )
    keyc, keyr = key[:, None], key.reshape(4, 1, TILE)
    slot_id = jnp.arange(padded, dtype=jnp.int32)
    onehot_t = (slot_id[:, None] == item_own[None, :]).astype(bf16)
    onehot = (item_own[:, None] == jnp.concatenate([slot_id, slot_id])[None, :]).astype(bf16)

    names = jnp.pad(labels[0], (0, padded - slots), constant_values=-1)

    def one_hot(names):
        return (names[:, None] == jnp.arange(class_table.shape[0], dtype=jnp.int32)[None, :]).astype(bf16)

    wide = w_ada.shape[2]
    columns = layers * wide // count
    ada_cols = w_ada.transpose(1, 0, 2).reshape(wrows, count, columns).transpose(1, 0, 2)
    qkv_cols = w_qkv.reshape(layers, wrows, 3, blks, piece).transpose(0, 3, 1, 2, 4)
    qkv_cols = qkv_cols.reshape(layers, blks, wrows, 3 * piece)
    up_cols = w_up.reshape(layers, wrows, dps, blks, ffrows).transpose(0, 3, 1, 2, 4)
    up_cols = up_cols.reshape(layers, blks, wrows, ff)
    class_rows = mm(one_hot(names), class_table).astype(bf16)
    if columns % 128 == 0 and wrows % 16 == 0:
        ada, class_rows, qkv_shard, up_shard, proj_own, first_qkv, first_proj = prepare(
            class_rows, ada_cols, qkv_cols[0], up_cols[0], w_proj
        )
        class_rows = class_rows.reshape(dps * padded, width)
        cond_all = jax.nn.silu(class_rows.astype(f32)).astype(bf16)
    else:
        to_heads = [(i, (i % dps) * blks + i // dps) for i in range(count)]
        proj_own = lax.ppermute(w_proj, ("dp", "blk"), to_heads)
        class_rows = gather(class_rows, "dp")
        cond_all = jax.nn.silu(class_rows.astype(f32)).astype(bf16)
        ada_cols = lax.all_to_all(ada_cols, ("dp", "blk"), 0, 0, tiled=True)
        ada_part = mm(cond_all, ada_cols.reshape(count * wrows, columns))
        ada_part = lax.all_to_all(ada_part.reshape(dps, padded, columns), "dp", 0, 0, tiled=True)
        ada_all = lax.all_gather(ada_part, "blk", axis=1, tiled=False)
        ada_all = ada_all.transpose(2, 0, 1, 3).reshape(padded, layers, wide).transpose(1, 0, 2)
        ada_high = ada_all.astype(bf16)
        ada_low = (ada_all - ada_high.astype(f32)).astype(bf16)
        ada = jnp.concatenate([ada_high, ada_low], axis=1)
        qkv_shard = lax.all_to_all(qkv_cols[0], "blk", 0, 0, tiled=True)
        up_shard = lax.all_to_all(up_cols[0], "blk", 0, 0, tiled=True)
        first_qkv, first_proj = gather(qkv_shard[None], "dp"), gather(proj_own[:1], "dp")

    own_scale = lax.dynamic_slice_in_dim(head_scale, b * own_heads, own_heads, axis=1)
    qscales = jnp.repeat(jnp.exp(own_scale), size, axis=1)

    state = tokens[0].astype(f32)
    saved, weights = [], []
    w_query, w_out = first_qkv, first_proj
    for layer in range(layers):
        w_query = w_query.reshape(length, 3 * piece)
        w_out = w_out.reshape(piece, width)
        qscale = qscales[layer][None, :]
        more = layer + 1 < layers
        jobs = [DpGather([up_shard, w_down[layer]])]
        if more:
            jobs.append(Swap([qkv_cols[layer + 1], up_cols[layer + 1]]))
        (h, qkv, rates, o, inverse, branch, mid), (w_first, w_second, *shards) = attend(
            layer,
            size,
            state,
            onehot,
            ada[layer],
            qscale,
            keyc,
            keyr,
            w_query,
            w_out,
            jobs,
        )
        w_first, w_second = w_first.reshape(width, ff), w_second.reshape(ff, width)
        weights.append((w_query, w_out, w_first, w_second))
        if more:
            qkv_shard, up_shard = shards
        (h2, g, slope, result, following), gathered = mlp(
            layer,
            mid,
            onehot,
            ada[layer],
            w_first,
            w_second,
            [DpGather([qkv_shard, proj_own[layer + 1]])] if more else [],
        )
        if more:
            w_query, w_out = gathered
        saved.append((state, h, qkv, rates, o, inverse, branch, mid, h2, g, slope, result))
        state = following
    output = state.astype(bf16)[None]

    grad = cotangent[0].astype(f32)
    up_grads, down_grads, qkv_grads, proj_grads = ([None] * layers for _ in range(4))
    notes, dadas = [], []
    waiting_scatter, waiting_swap, waiting_items = None, None, None
    for layer in reversed(range(layers)):
        w_query, w_out, w_first, w_second = weights[layer]
        qscale = qscales[layer][None, :]
        state, h, qkv, rates, o, inverse, branch, mid, h2, g, slope, result = saved[layer]
        jobs = []
        if waiting_scatter is not None:
            jobs = [
                DpScatter(waiting_scatter, (bf16, f32)),
                Swap([waiting_swap]),
                Items(waiting_items),
            ]
        (mid_grad, up_grad, down_grad, items_two), done = mlp_back(
            layer, grad, result, mid, onehot, onehot_t, ada[layer], w_first, w_second, h2, g, slope, jobs
        )
        swaps = []
        if waiting_scatter is not None:
            qkv_sum, proj_grads[layer + 1], up_grads[layer + 1], dada = done
            dadas.append(dada)
            swaps = [Swap([qkv_sum.reshape(blks, wrows, 3 * piece)])]
        (grad, qkv_grad, proj_grad, waiting_items, scale_grad), done = attend_back(
            layer,
            size,
            mid_grad,
            branch,
            state,
            onehot,
            onehot_t,
            ada[layer],
            qscale,
            keyc,
            keyr,
            inverse,
            w_query,
            w_out,
            h,
            qkv,
            rates,
            o,
            [
                DpScatter(
                    [up_grad.reshape(dps, blks * wrows, ff), down_grad.reshape(dps, ffrows, width)],
                    (bf16, f32),
                ),
                Items(items_two),
            ]
            + swaps,
        )
        up_sum, down_grads[layer], dada = done[:3]
        dadas.append(dada)
        if swaps:
            qkv_grads[layer + 1] = done[3]
        waiting_scatter = [
            qkv_grad.reshape(dps, blks * wrows, 3 * piece),
            proj_grad.reshape(dps, piece // dps, width),
        ]
        waiting_swap = up_sum.reshape(blks, wrows, ff)
        notes.append(scale_grad[:, ::size])
    lanes = dps * padded
    notes = [jnp.pad(one, ((0, 0), (0, lanes - own_heads))) for one in notes[::-1]]
    notes.append(jnp.pad(names.astype(f32)[None, :], ((0, 0), (0, lanes - padded))))
    notes = jnp.pad(jnp.concatenate(notes), ((0, 8 - len(notes)), (0, 0)))
    cond_own = lax.dynamic_slice_in_dim(cond_all, (d * blks + b) * wrows, wrows, axis=1).T
    (qkv_grads[0], proj_whole, ada_grads, told), done = finish(
        DpScatter(waiting_scatter, (bf16, f32)),
        Swap([waiting_swap]),
        Items(waiting_items),
        cond_own,
        w_ada,
        notes,
        proj_grads[1],
        dadas,
    )
    up_grads[0] = done[3]
    for layer in range(layers):
        one = qkv_grads[layer].reshape(blks, wrows, 3, piece)
        qkv_grads[layer] = one.transpose(1, 2, 0, 3).reshape(wrows, 3 * width).astype(f32)
        one = up_grads[layer].reshape(blks, wrows, dps, ffrows)
        up_grads[layer] = one.transpose(1, 2, 0, 3).reshape(wrows, ff * blks).astype(f32)
    head_grad = told[:, wrows : wrows + layers, :own_heads].reshape(dps, blks, layers, own_heads)
    head_grad = jnp.sum(head_grad, axis=0).transpose(1, 0, 2).reshape(layers, heads)
    every_name = told[::blks, wrows + layers, :padded].reshape(-1).astype(jnp.int32)
    cond_grad = told[:, :wrows, :].reshape(width, lanes).T
    _, silu_pull = jax.vjp(jax.nn.silu, class_rows.astype(f32))
    cond_pre = silu_pull(cond_grad)[0]
    pre_high = cond_pre.astype(bf16)
    pre_low = (cond_pre - pre_high.astype(f32)).astype(bf16)
    chosen = one_hot(jnp.concatenate([every_name, every_name]))
    table_grad = rows_mm(chosen, jnp.concatenate([pre_high, pre_low]))
    return (
        output,
        grad.astype(bf16)[None],
        table_grad,
        head_grad,
        jnp.stack(qkv_grads),
        proj_whole,
        jnp.stack(up_grads),
        jnp.stack(down_grads),
        ada_grads,
    )


def solution(mesh):
    in_specs = (
        P("dp", "blk", None),
        P("dp", "blk", None),
        P("dp", None),
        P("dp", None),
        P(),
        P(),
        P(None, ("dp", "blk"), None),
        P(None, ("dp", "blk"), None),
        P(None, ("dp", "blk"), None),
        P(None, ("dp", "blk"), None),
        P(None, ("dp", "blk"), None),
    )
    out_specs = (
        P("dp", "blk", None),
        P("dp", "blk", None),
        P(),
        P(),
        P(None, ("dp", "blk"), None),
        P(None, ("dp", "blk"), None),
        P(None, ("dp", "blk"), None),
        P(None, ("dp", "blk"), None),
        P(None, ("dp", "blk"), None),
    )
    return jax.shard_map(
        per_device, mesh=mesh, in_specs=in_specs, out_specs=out_specs, check_vma=False
    )
```

```python
from functools import partial
from types import SimpleNamespace

import jax
import jax.numpy as jnp
from jax import lax
from jax.experimental import pallas as pl
from jax.experimental.pallas import tpu as pltpu
from jax.sharding import PartitionSpec as P

patch_areas = (1, 4, 9, 16, 25, 36, 64, 100, 169)
scale_starts = (1, 5, 14, 30, 55, 91, 155, 255)
f32 = jnp.float32
bf16 = jnp.bfloat16
MESH = pl.DeviceIdType.MESH
TILE = 256
HALF = 128
STEP = 32


def sizes():
    return lax.axis_size("dp"), lax.axis_size("blk")


def place():
    return lax.axis_index("dp"), lax.axis_index("blk")


def flat_place():
    return place()[0] * sizes()[1] + place()[1]


def token_meta(stops, length):
    areas = jnp.array(patch_areas, dtype=jnp.int32)
    levels = jnp.arange(9, dtype=jnp.int32)
    counts = jnp.sum(jnp.where(levels[None, :] < stops[:, None], areas[None, :], 0), axis=1)
    ends = jnp.cumsum(counts)
    places = jnp.arange(length, dtype=jnp.int32)
    passed = places[:, None] >= ends[None, :]
    item = jnp.sum(passed.astype(jnp.int32), axis=1)
    begin = jnp.sum(jnp.where(passed, counts[None, :], 0), axis=1)
    inner = places - begin
    bounds = jnp.array(scale_starts, dtype=jnp.int32)
    level = jnp.sum((inner[:, None] >= bounds[None, :]).astype(jnp.int32), axis=1)
    level = jnp.where(item == stops.shape[0], 0, level)
    return (item, level)


def mm(left, right):
    return jnp.dot(left, right, preferred_element_type=f32)


def mm_t(left, right):
    return lax.dot_general(left, right, (((1,), (1,)), ((), ())), preferred_element_type=f32)


def rows_mm(left, right, precision=None):
    return lax.dot_general(
        left, right, (((0,), (0,)), ((), ())), precision=precision, preferred_element_type=f32
    )


def gather(values, axes):
    return lax.all_gather(values, axes, axis=0, tiled=True)


def scatter(values, axes):
    return lax.psum_scatter(values, axes, scatter_dimension=0, tiled=True)


def partners():
    d, b = place()
    return (d, b + 1 - 2 * (b % 2)), (d, (b + 2) % 4)


def greet(others):
    barrier = pltpu.get_barrier_semaphore()
    for other in others:
        pl.semaphore_signal(barrier, inc=1, device_id=other, device_id_type=MESH)
    return lambda: pl.semaphore_wait(barrier, len(others))


def greet_all():
    dps, blks = sizes()
    me = flat_place()
    others = [(me + k) % (dps * blks) for k in range(1, dps * blks)]
    return greet([(t // blks, t % blks) for t in others])


def remote(src, dst, send, recv, target):
    return pltpu.make_async_remote_copy(
        src_ref=src, dst_ref=dst, send_sem=send, recv_sem=recv, device_id=target, device_id_type=MESH
    )


class Spread:
    def __init__(self, buf, send, recv, sibling, peer):
        def copy(src, dst, k, target):
            return remote(
                buf.at[pl.ds(src, HALF)], buf.at[pl.ds(dst, HALF)], send.at[k], recv.at[k], target
            )

        self.to_peer = [copy(HALF * c, 2 * TILE + TILE * c, c, peer) for c in range(2)]
        self.to_sibling = [copy(HALF * c, TILE + HALF * c, 2 + c, sibling) for c in range(2)]
        self.forward = [
            copy(2 * TILE + TILE * c, 2 * TILE + TILE * c + HALF, 4 + c, sibling) for c in range(2)
        ]

    def start(self, c):
        self.to_peer[c].start()
        self.to_sibling[c].start()

    def wait_block(self, i):
        @pl.when(i == 1)
        def _():
            for c in range(2):
                self.to_sibling[c].wait_recv()

        for c in range(2):

            @pl.when(i == 2 + c)
            def _():
                self.to_peer[c].wait_recv()
                self.forward[c].start()
                self.forward[c].wait_recv()

    def finish(self):
        for c in range(2):
            self.to_peer[c].wait_send()
            self.to_sibling[c].wait_send()
            self.forward[c].wait_send()


class Collect:
    def __init__(self, parts, out, mid, own, far, send, recv, sibling, peer):
        self.parts, self.out, self.mid, self.own, self.far = parts, out, mid, own, far
        self.cross = [
            remote(
                parts.at[pl.ds(2 * TILE + TILE * c + HALF, HALF)],
                mid.at[pl.ds(HALF * c, HALF)],
                send.at[c],
                recv.at[c],
                sibling,
            )
            for c in range(2)
        ]
        self.over = [
            remote(
                out.at[pl.ds(HALF * c, HALF)],
                far.at[pl.ds(HALF * c, HALF)],
                send.at[2 + c],
                recv.at[2 + c],
                peer,
            )
            for c in range(2)
        ]
        self.home = remote(parts.at[pl.ds(TILE, TILE)], own, send.at[4], recv.at[4], sibling)

    def block_done(self, j):
        for c in range(2):

            @pl.when(j == 2 + c)
            def _():
                self.cross[c].start()
                self.cross[c].wait_recv()

                @pl.loop(0, HALF // STEP)
                def _(s):
                    at = pl.multiple_of(s * STEP, STEP)
                    mine = self.parts[pl.ds(2 * TILE + TILE * c + at, STEP), :].astype(f32)
                    theirs = self.mid[pl.ds(HALF * c + at, STEP), :].astype(f32)
                    self.out[pl.ds(HALF * c + at, STEP), :] = (mine + theirs).astype(bf16)

                self.over[c].start()

        @pl.when(j == 1)
        def _():
            self.home.start()

    def wait(self):
        self.home.wait_recv()
        for c in range(2):
            self.over[c].wait_recv()

    def rows(self, at):
        span = pl.ds(at, STEP)
        total = self.parts[span, :].astype(f32) + self.own[span, :].astype(f32)
        return total + self.far[span, :].astype(f32)

    def finish(self):
        self.home.wait_send()
        for c in range(2):
            self.cross[c].wait_send()
            self.over[c].wait_send()


def spread_scratch(width):
    return [
        pltpu.VMEM((4 * TILE, width), bf16),
        pltpu.SemaphoreType.DMA((6,)),
        pltpu.SemaphoreType.DMA((6,)),
    ]


def collect_scratch(width):
    return [pltpu.VMEM((4 * TILE, width), bf16)] + [pltpu.VMEM((TILE, width), bf16)] * 4 + [
        pltpu.SemaphoreType.DMA((5,)),
        pltpu.SemaphoreType.DMA((5,)),
    ]


class Moves:
    def __init__(self, sems):
        self.sems, self.used = sems, 0

    def copy(self, src, dst):
        made = pltpu.make_async_copy(src, dst, self.sems.at[self.used])
        self.used += 1
        made.start()
        return made


def expand(onehot, ada, which, outs):
    width = outs[0].shape[1]
    for k, out in zip(which, outs):
        for n in range(0, width, TILE):
            out[:, n : n + TILE] = mm(onehot[...], ada[:, k * width + n : k * width + n + TILE])


def normed(values):
    centre = jnp.mean(values, axis=-1, keepdims=True)
    centred = values - centre
    spread = jnp.mean(centred * centred, axis=-1, keepdims=True)
    rate = lax.rsqrt(spread + 1e-06)
    return centred * rate, rate


def norm_back(grad, values_hat, rate):
    first = jnp.mean(grad, axis=-1, keepdims=True)
    second = jnp.mean(grad * values_hat, axis=-1, keepdims=True)
    return rate * (grad - first - values_hat * second)


def row_steps(start, rows, body):
    @pl.loop(0, rows // STEP)
    def _(s):
        body(pl.multiple_of(start + s * STEP, STEP))


def block_ones(size):
    shape = (TILE, TILE)
    one = lax.broadcasted_iota(jnp.int32, shape, 0) // size
    two = lax.broadcasted_iota(jnp.int32, shape, 1) // size
    return (one == two).astype(bf16)


def split_mm(dot, values, ones):
    high = values.astype(bf16)
    low = (values - high.astype(f32)).astype(bf16)
    return dot(high, ones) + dot(low, ones)


def head_lanes(values, h, size):
    lane = lax.broadcasted_iota(jnp.int32, values.shape, 1) // size
    return jnp.where(lane == h, values, jnp.zeros_like(values))


def hidden_bias(keyc, keyr, rows, cols):
    keys = keyc[pl.ds(rows, TILE), :]
    top = keyr[cols]
    low = top - top % 16
    return jnp.where((keys >= low) & (keys <= top), 0.0, -1e30)


def nothing():
    pass


class Hooks:
    def __init__(self, **table):
        self.start = self.sent = self.need = self.a = self.b = self.c = self.d = self.dw = nothing
        vars(self).update(table)


def modulate_rows(x, scale, shift, hbuf, spread):
    def modulated(at):
        span = pl.ds(at, STEP)
        hat, _ = normed(x[span, :])
        hbuf[span, :] = (hat * (1.0 + scale[span, :]) + shift[span, :]).astype(bf16)

    for c in range(2):
        row_steps(HALF * c, HALF, modulated)
        spread.start(c)


def exchange(refs):
    hbuf, ag_send, ag_recv, parts, out, mid, own, far, rs_send, rs_recv = refs
    sibling, peer = partners()
    spread = Spread(hbuf, ag_send, ag_recv, sibling, peer)
    collect = Collect(parts, out, mid, own, far, rs_send, rs_recv, sibling, peer)
    return hbuf, parts, spread, collect


def attend_segment(
    hooks,
    size,
    x,
    onehot,
    ada,
    qscale,
    keyc,
    keyr,
    weights_in,
    weights,
    saves_out,
    inv_out,
    branch_out,
    mid_out,
    held,
    mods,
    moves,
    refs,
):
    qkv, vt, rates, o_out = held
    gamma, scale, shift = mods
    wqkv, wproj = weights
    hbuf, parts, spread, collect = exchange(refs)
    mover = Moves(moves)
    expand(onehot, ada, (0, 2, 4), (gamma, scale, shift))
    modulate_rows(x, scale, shift, hbuf, spread)
    hooks.need()
    load_qkv = mover.copy(weights_in[0], wqkv)
    load_proj = mover.copy(weights_in[1], wproj)
    load_qkv.wait()
    ones = block_ones(size)

    @pl.loop(0, 4)
    def _(i):
        spread.wait_block(i)
        span = pl.ds(pl.multiple_of(i * TILE, TILE), TILE)
        h = hbuf[span, :]
        for part in range(3):
            columns = slice(part * TILE, (part + 1) * TILE)
            value = mm(h, wqkv[:, columns])
            if part < 2:
                rate = lax.rsqrt(split_mm(mm, value * value, ones) + 1e-06)
                if part == 0:
                    rate = rate * qscale[...]
                rates[span, columns] = rate
                value = value * rate
            else:
                vt[:, span] = value.T.astype(bf16)
            qkv[span, columns] = value.astype(bf16)

    hooks.a()
    saves = [mover.copy(a, b) for a, b in zip((hbuf, qkv, rates), saves_out)]
    load_proj.wait()
    heads = TILE // size

    @pl.loop(0, 4)
    def _(i):
        j = (i + 2) % 4
        span = pl.ds(pl.multiple_of(j * TILE, TILE), TILE)
        queries = [head_lanes(qkv[span, 0:TILE], h, size) for h in range(heads)]
        sums = [jnp.zeros((1, TILE), f32)] * heads
        mixed = [jnp.zeros((size, TILE), f32)] * heads
        for k in range(4):
            keys = qkv[k * TILE : (k + 1) * TILE, TILE : 2 * TILE]
            bias = hidden_bias(keyc, keyr, k * TILE, j)
            for h in range(heads):
                grown = jnp.exp(mm_t(keys, queries[h]) + bias)
                sums[h] = sums[h] + jnp.sum(grown, axis=0, keepdims=True)
                mixed[h] = mixed[h] + mm(
                    vt[h * size : (h + 1) * size, k * TILE : (k + 1) * TILE], grown.astype(bf16)
                )
        inverse = [1.0 / one for one in sums]
        for h in range(heads):
            inv_out[j, h : h + 1, :] = inverse[h]
        whole = jnp.concatenate([mixed[h] * inverse[h] for h in range(heads)], axis=0)
        low = whole.T.astype(bf16)
        o_out[span, :] = low
        for n in range(0, parts.shape[1], TILE):
            parts[span, n : n + TILE] = mm(low, wproj[:, n : n + TILE]).astype(bf16)
        collect.block_done(j)

    hooks.b()
    collect.wait()
    hooks.c()

    def added(at):
        span = pl.ds(at, STEP)
        branch = collect.rows(at)
        branch_out[span, :] = branch
        mid_out[span, :] = x[span, :] + gamma[span, :] * branch

    row_steps(0, TILE, added)
    spread.finish()
    collect.finish()
    for one in saves:
        one.wait()


def mlp_segment(
    hooks, x, onehot, ada, weights_in, weights, saves_out, result_out, x_out, held, mods, moves, refs
):
    hidden, slope = held
    gamma, scale, shift = mods
    wup, wdown = weights
    hbuf, parts, spread, collect = exchange(refs)
    mover = Moves(moves)
    expand(onehot, ada, (1, 3, 5), (gamma, scale, shift))
    modulate_rows(x, scale, shift, hbuf, spread)
    hooks.need()
    loads = [mover.copy(a, b) for a, b in zip(weights_in, weights)]
    for one in loads:
        one.wait()

    @pl.loop(0, 4)
    def _(i):
        spread.wait_block(i)
        for at, hook in ((2, hooks.a), (3, hooks.b)):

            @pl.when(i == at)
            def _():
                hook()

        span = pl.ds(pl.multiple_of(i * TILE, TILE), TILE)
        h = hbuf[span, :]
        for n in range(0, wup.shape[1], TILE):
            columns = slice(n, n + TILE)
            up = mm(h, wup[:, columns])
            square = up * up
            bent = jnp.tanh(0.7978845608 * (up * (1.0 + 0.044715 * square)))
            half = 0.5 * (1.0 + bent)
            hidden[span, columns] = (up * half).astype(bf16)
            inner = 0.7978845608 + (3.0 * 0.044715 * 0.7978845608) * square
            slope[span, columns] = (half + 0.5 * up * (1.0 - bent * bent) * inner).astype(bf16)
        g = hidden[span, :]
        for n in range(0, parts.shape[1], TILE):
            parts[span, n : n + TILE] = mm(g, wdown[:, n : n + TILE]).astype(bf16)
        collect.block_done(i)

    hooks.c()
    saves = [mover.copy(a, b) for a, b in zip((hbuf, hidden, slope), saves_out)]
    collect.wait()

    def added(at):
        span = pl.ds(at, STEP)
        result = collect.rows(at)
        result_out[span, :] = result
        x_out[span, :] = x[span, :] + gamma[span, :] * result

    row_steps(0, TILE, added)
    spread.finish()
    collect.finish()
    for one in saves:
        one.wait()


def item_sums(onehot_t, terms, out):
    for k, term in enumerate(terms):
        width = term.shape[1]
        out[:, k * width : (k + 1) * width] = mm(onehot_t[...], term[...])


def scaled_rows(x, gamma, hbuf, spread):
    def scaled(at):
        span = pl.ds(at, STEP)
        hbuf[span, :] = (gamma[span, :] * x[span, :]).astype(bf16)

    for c in range(2):
        row_steps(HALF * c, HALF, scaled)
        spread.start(c)


def back_rows(collect, x, grad, branch, scale, terms, out):
    dgamma, dscale, dshift = terms

    def added(at):
        span = pl.ds(at, STEP)
        dh = collect.rows(at)
        hat, rate = normed(x[span, :])
        above = grad[span, :]
        dgamma[span, :] = (above * branch[span, :]).astype(bf16)
        dscale[span, :] = (dh * hat).astype(bf16)
        dshift[span, :] = dh.astype(bf16)
        out[span, :] = above + norm_back(dh * (1.0 + scale[span, :]), hat, rate)

    row_steps(0, TILE, added)


def mlp_back_segment(
    hooks, dx, onehot, onehot_t, ada, ins, outs, dmid, items, held, mods, terms, moves, refs
):
    wup_in, wdown_in, h_in, g_in, slope_in, result_in, mid_in = ins
    wup, wdown, hall, gall, slope, dwup, dwdown, result, mid_state = held
    gamma, scale = mods
    hbuf, parts, spread, collect = exchange(refs)
    mover = Moves(moves)
    load_down = mover.copy(wdown_in, wdown)
    load_slope = mover.copy(slope_in, slope)
    load_up = mover.copy(wup_in, wup)
    later = [mover.copy(g_in, gall), mover.copy(h_in, hall)]
    later += [mover.copy(result_in, result), mover.copy(mid_in, mid_state)]
    expand(onehot, ada, (1, 3), (gamma, scale))
    hooks.start()
    scaled_rows(dx, gamma, hbuf, spread)
    hooks.sent()
    for one in (load_down, load_slope, load_up):
        one.wait()

    @pl.loop(0, 4)
    def _(i):
        spread.wait_block(i)
        for at, hook in ((2, hooks.a), (3, hooks.b)):

            @pl.when(i == at)
            def _():
                hook()

        span = pl.ds(pl.multiple_of(i * TILE, TILE), TILE)
        dm = hbuf[span, :]
        for n in range(0, slope.shape[1], TILE):
            columns = slice(n, n + TILE)
            dg = mm_t(dm, wdown[columns, :])
            slope[span, columns] = (dg * slope[span, columns].astype(f32)).astype(bf16)
        du = slope[span, :]
        for n in range(0, parts.shape[1], TILE):
            parts[span, n : n + TILE] = mm_t(du, wup[n : n + TILE, :]).astype(bf16)
        collect.block_done(i)

    hooks.c()
    for one in later:
        one.wait()

    @pl.loop(0, gall.shape[1] // TILE)
    def _(k):
        columns = pl.ds(pl.multiple_of(k * TILE, TILE), TILE)
        for n in range(0, hbuf.shape[1], 2 * TILE):
            dwdown[columns, n : n + 2 * TILE] = rows_mm(
                gall[:, columns], hbuf[:, n : n + 2 * TILE]
            ).astype(bf16)

    save_down = mover.copy(dwdown, outs[1])

    @pl.loop(0, hall.shape[1] // TILE)
    def _(k):
        columns = pl.ds(pl.multiple_of(k * TILE, TILE), TILE)
        for n in range(0, slope.shape[1], 2 * TILE):
            dwup[columns, n : n + 2 * TILE] = rows_mm(
                hall[:, columns], slope[:, n : n + 2 * TILE]
            ).astype(bf16)

    save_up = mover.copy(dwup, outs[0])
    save_down.wait()
    save_up.wait()
    hooks.dw()
    collect.wait()
    back_rows(collect, mid_state, dx, result, scale, terms, dmid)
    item_sums(onehot_t, terms, items)
    spread.finish()
    collect.finish()


def attend_back_segment(
    hooks,
    size,
    dmid,
    onehot,
    onehot_t,
    ada,
    qscale,
    keyc,
    keyr,
    inverse,
    ins,
    outs,
    dx,
    items,
    head_out,
    held,
    mods,
    terms,
    moves,
    refs,
):
    wqkv_in, wproj_in, h_in, qkv_in, rate_in, o_in, branch_in, x_in = ins
    wqkv, wproj, hall, qkv, rates, oall, kt, dkeys, dvalues, dqkv, dwqkv, dwproj, branch, x = held
    gamma, scale = mods
    hbuf, parts, spread, collect = exchange(refs)
    mover = Moves(moves)
    loads = [mover.copy(wproj_in, wproj), mover.copy(qkv_in, qkv)]
    loads += [mover.copy(o_in, oall), mover.copy(rate_in, rates)]
    load_w = mover.copy(wqkv_in, wqkv)
    later = [mover.copy(h_in, hall), mover.copy(branch_in, branch)]
    if x_in is not None:
        later.append(mover.copy(x_in, x))
    expand(onehot, ada, (0, 2), (gamma, scale))
    hooks.start()
    scaled_rows(dmid, gamma, hbuf, spread)
    hooks.sent()
    for one in loads:
        one.wait()
    heads = TILE // size
    ones = block_ones(size)
    inv_square = 1.0 / (qscale[...] * qscale[...])
    select = (
        lax.broadcasted_iota(jnp.int32, (8, TILE), 1) // size
        == lax.broadcasted_iota(jnp.int32, (8, TILE), 0)
    ).astype(bf16)
    dkeys[...] = jnp.zeros_like(dkeys)
    dvalues[...] = jnp.zeros_like(dvalues)
    head_out[...] = jnp.zeros_like(head_out)
    for k in range(4):
        rows = slice(k * TILE, (k + 1) * TILE)
        kt[:, rows] = qkv[rows, TILE : 2 * TILE].astype(f32).T.astype(bf16)

    @pl.loop(0, 4)
    def _(i):
        spread.wait_block(i)
        for at, hook in ((2, hooks.a), (3, hooks.b)):

            @pl.when(i == at)
            def _():
                hook()

        span = pl.ds(pl.multiple_of(i * TILE, TILE), TILE)
        dout = mm_t(hbuf[span, :], wproj[...]).astype(bf16)
        product = dout.astype(f32) * oall[span, :].astype(f32)
        row_term = split_mm(lambda a, b: mm_t(b, a), product, select)
        q_low = qkv[span, 0:TILE]
        queries = [head_lanes(q_low, h, size) for h in range(heads)]
        douts = [head_lanes(dout, h, size) for h in range(heads)]
        dquery = [jnp.zeros((size, TILE), f32)] * heads
        for k in range(4):
            rows = slice(k * TILE, (k + 1) * TILE)
            keys = qkv[rows, TILE : 2 * TILE]
            values = qkv[rows, 2 * TILE : 3 * TILE]
            bias = hidden_bias(keyc, keyr, k * TILE, i)
            dkey = jnp.zeros((TILE, TILE), f32)
            dvalue = jnp.zeros((TILE, TILE), f32)
            for h in range(heads):
                share = jnp.exp(mm_t(keys, queries[h]) + bias) * inverse[i, h : h + 1, :]
                dshare = mm_t(values, douts[h])
                dscore = (share * (dshare - row_term[h : h + 1, :])).astype(bf16)
                dvalue = dvalue + mm(share.astype(bf16), douts[h])
                dkey = dkey + mm(dscore, queries[h])
                dquery[h] = dquery[h] + mm(kt[h * size : (h + 1) * size, rows], dscore)
            dkeys[rows, :] += dkey
            dvalues[rows, :] += dvalue
        dq = jnp.concatenate(dquery, axis=0).T
        qhat = q_low.astype(f32)
        along = split_mm(mm, dq * qhat, ones)
        head_out[...] += jnp.sum(along, axis=0, keepdims=True)
        dqkv[span, 0:TILE] = (rates[span, 0:TILE] * (dq - qhat * (along * inv_square))).astype(bf16)

    load_w.wait()
    hooks.c()

    @pl.loop(0, 4)
    def _(i):
        j = (i + 2) % 4
        span = pl.ds(pl.multiple_of(j * TILE, TILE), TILE)
        dk = dkeys[span, :]
        khat = qkv[span, TILE : 2 * TILE].astype(f32)
        along = split_mm(mm, dk * khat, ones)
        dqkv[span, TILE : 2 * TILE] = (
            rates[span, TILE : 2 * TILE] * (dk - khat * along)
        ).astype(bf16)
        dqkv[span, 2 * TILE : 3 * TILE] = dvalues[span, :].astype(bf16)
        low = dqkv[span, :]
        for n in range(0, parts.shape[1], TILE):
            parts[span, n : n + TILE] = mm_t(low, wqkv[n : n + TILE, :]).astype(bf16)
        collect.block_done(j)

    hooks.d()
    for n in range(0, hbuf.shape[1], 2 * TILE):
        dwproj[:, n : n + 2 * TILE] = rows_mm(oall[...], hbuf[:, n : n + 2 * TILE]).astype(bf16)
    save_proj = mover.copy(dwproj, outs[1])
    for one in later:
        one.wait()

    @pl.loop(0, hall.shape[1] // TILE)
    def _(k):
        columns = pl.ds(pl.multiple_of(k * TILE, TILE), TILE)
        dwqkv[columns, :] = rows_mm(hall[:, columns], dqkv[...]).astype(bf16)

    save_w = mover.copy(dwqkv, outs[0])
    save_proj.wait()
    save_w.wait()
    hooks.dw()
    collect.wait()
    back_rows(collect, x, dmid, branch, scale, terms, dx)
    item_sums(onehot_t, terms, items)
    spread.finish()
    collect.finish()


def groups(dps):
    d, b = place()
    side, pairs = d % 2, dps // 2
    pair = d // 2
    ahead = [((pair + k) % pairs) * 2 + side for k in range(pairs)]
    behind = [((pair - k + pairs) % pairs) * 2 + side for k in range(pairs)]
    return d, b, d + 1 - 2 * side, ahead, behind


class DpGather:
    def __init__(self):
        self.dps = sizes()[0]

    def bind(self, ins, outs, scratch):
        send, recv, local = scratch
        d, b, other, ahead, behind = groups(self.dps)
        pairs = self.dps // 2
        self.partners = [(other, b)] + [(t, b) for t in ahead[1:]]
        self.first, self.direct, self.forward, self.local = [], [], [], []
        for a, (src, dst) in enumerate(zip(ins, outs)):
            self.local.append(pltpu.make_async_copy(src, dst.at[d], local.at[a]))
            self.first.append(remote(src, dst.at[d], send.at[a, 0], recv.at[a, 0], (other, b)))
            self.direct.append([None])
            self.forward.append([None])
            for k in range(1, pairs):
                self.direct[a].append(
                    remote(src, dst.at[d], send.at[a, k], recv.at[a, k], (ahead[k], b))
                )
                at = pairs + k
                self.forward[a].append(
                    remote(
                        dst.at[behind[k]], dst.at[behind[k]], send.at[a, at], recv.at[a, at], (other, b)
                    )
                )
        self.order = [(k, a) for k in range(1, pairs) for a in range(len(ins))]

    def start_far(self):
        for k, a in self.order:
            self.direct[a][k].start()
        for one in self.local:
            one.start()

    def start_near(self):
        for one in self.first:
            one.start()

    def step(self, hook, hooks=3):
        low, high = (len(self.order) * hook) // hooks, (len(self.order) * (hook + 1)) // hooks
        for k, a in self.order[low:high]:
            self.direct[a][k].wait_recv()
            self.forward[a][k].start()

    def finish(self):
        for one in self.local:
            one.wait()
        for one in self.first:
            one.wait()
        for k, a in self.order:
            self.direct[a][k].wait_send()
            self.forward[a][k].wait()


class DpScatter:
    def __init__(self):
        self.dps = sizes()[0]

    def bind(self, ins, outs, scratch):
        d, b, other, ahead, behind = groups(self.dps)
        pairs = self.dps // 2
        self.partners = [(other, b)] + [(t, b) for t in ahead[1:]]
        self.results = outs
        self.bufs, self.local, self.cross, self.direct = [], [], [], []
        for a, src in enumerate(ins):
            mine, near, far, send, recv, local = scratch[6 * a : 6 * a + 6]
            self.bufs.append((mine, near, far))
            self.local.append([])
            self.cross.append([])
            self.direct.append([None])
            for k in range(pairs):
                target = ahead[k]
                theirs = target + 1 - 2 * (target % 2)
                self.local[a].append(
                    pltpu.make_async_copy(src.at[target], mine.at[k], local.at[k])
                )
                self.cross[a].append(
                    remote(src.at[theirs], near.at[k], send.at[k], recv.at[k], (other, b))
                )
                if k:
                    at = pairs + k
                    self.direct[a].append(
                        remote(mine.at[k], far.at[k], send.at[at], recv.at[at], (target, b))
                    )
        self.order = [(k, a) for k in range(1, pairs) for a in range(len(ins))]
        self.last = [(0, a) for a in range(len(ins))]

    def start(self):
        for k, a in self.order + self.last:
            self.cross[a][k].start()
            self.local[a][k].start()

    def add(self, a, k):
        self.local[a][k].wait()
        self.cross[a][k].wait_recv()
        mine, near, _ = self.bufs[a]
        rows = mine.shape[1]
        step = min(rows, STEP)

        @pl.loop(0, rows // step)
        def _(s):
            span = pl.ds(pl.multiple_of(s * step, step), step)
            total = mine[k, span, :].astype(f32) + near[k, span, :].astype(f32)
            mine[k, span, :] = total.astype(bf16)

    def step(self, hook, hooks=3):
        low, high = (len(self.order) * hook) // hooks, (len(self.order) * (hook + 1)) // hooks
        for k, a in self.order[low:high]:
            self.add(a, k)
            self.direct[a][k].start()

    def own(self):
        for k, a in self.last:
            self.add(a, k)
        for k, a in self.order + self.last:
            self.cross[a][k].wait_send()

    def finish(self):
        for k, a in self.order:
            self.direct[a][k].wait()
        for a, result in enumerate(self.results):
            mine, _, far = self.bufs[a]
            step = result.shape[1] if len(result.shape) == 3 else min(mine.shape[1], STEP)

            @pl.loop(0, mine.shape[1] // step)
            def _(s):
                span = pl.ds(pl.multiple_of(s * step, step), step)
                total = mine[0, span, :].astype(f32)
                for k in range(1, self.dps // 2):
                    total = total + far[k, span, :].astype(f32)
                if len(result.shape) == 3:
                    result[s] = total.astype(result.dtype)
                else:
                    result[span, :] = total.astype(result.dtype)

    def release(self, credit):
        for other in self.partners:
            pl.semaphore_signal(credit, inc=1, device_id=other, device_id_type=MESH)

    def acquire(self, credit):
        pl.semaphore_wait(credit, len(self.partners))


class Items:
    def __init__(self, src, out, scratch):
        self.terms, self.held, send, recv, dp_send, dp_recv = scratch
        dps = sizes()[0]
        d, b = place()
        self.here, self.out = (d, b), out
        wide = self.held.shape[2]

        def quarter(i):
            return src.at[:, pl.ds(pl.multiple_of(i * wide, 128), wide)]

        self.first = [pltpu.make_async_copy(quarter(b), self.terms.at[0], send.at[0])]
        for k in range(1, 4):
            to = (b + k) % 4
            self.first.append(
                remote(quarter(to), self.terms.at[k], send.at[k], recv.at[k], (d, to))
            )
        self.over = [
            remote(self.held.at[0], out.at[b, d], dp_send.at[k], dp_recv.at[k], ((d + k) % dps, b))
            for k in range(1, dps)
        ]
        self.keep = pltpu.make_async_copy(self.held.at[0], out.at[b, d], send.at[7])
        self.share = Share(out, send.at[pl.ds(4, 3)], recv.at[pl.ds(4, 3)])

    def start(self):
        for one in self.first:
            one.start()

    def sum(self):
        d, b = self.here
        for one in self.first:
            one.wait()
        total = (self.terms[0] + self.terms[1]) + (self.terms[2] + self.terms[3])
        low = total.astype(bf16)
        self.held[0] = low
        for one in self.over + [self.keep]:
            one.start()

    def spread(self):
        for one in self.over + [self.keep]:
            one.wait()
        self.share.start()

    def forward(self):
        self.share.forward()

    def finish(self):
        self.share.finish()


class Permute:
    def __init__(self, src, dst, send, recv, back):
        dps, blks = sizes()
        d, b = place()
        owner, user = d * blks + b, b * dps + d
        self.moves = owner != user
        to = (user // blks, user % blks) if back else (owner % dps, owner // dps)
        self.away = remote(src, dst, send, recv, to)
        self.stay = pltpu.make_async_copy(src, dst, send)

    def start(self):
        @pl.when(self.moves)
        def _():
            self.away.start()

        @pl.when(jnp.logical_not(self.moves))
        def _():
            self.stay.start()

    def finish(self):
        @pl.when(self.moves)
        def _():
            self.away.wait()

        @pl.when(jnp.logical_not(self.moves))
        def _():
            self.stay.wait()


def modulations_start(rows_in, ada_in, rows_out, columns, sems):
    dp_send, dp_recv, ada_send, ada_recv, local = sems
    dps, blks = sizes()
    count = dps * blks
    d, b = place()
    me = d * blks + b
    rows = ada_in.shape[1]
    span = pl.ds(pl.multiple_of(me * rows, rows), rows)
    sends = [
        pltpu.make_async_copy(rows_in, rows_out.at[d], local.at[0]),
        pltpu.make_async_copy(ada_in.at[me], columns.at[span], local.at[1]),
    ]
    for k in range(1, dps):
        to = ((d + k) % dps, b)
        sends.append(remote(rows_in, rows_out.at[d], dp_send.at[k], dp_recv.at[k], to))
    for k in range(1, count):
        t = (me + k) % count
        to = (t // blks, t % blks)
        sends.append(remote(ada_in.at[t], columns.at[span], ada_send.at[k], ada_recv.at[k], to))
    for one in sends:
        one.start()
    return sends


def modulations_answer(rows_out, columns, answers, quarters, sems):
    send, recv = sems
    dps = sizes()[0]
    d, b = place()
    slots, wide = answers.shape[1:]
    value = rows_out[...].astype(f32)
    value = (value / (1.0 + jnp.exp(-value))).astype(bf16)
    whole = mm(value.reshape(dps * slots, rows_out.shape[2]), columns[...])
    answers[...] = whole.reshape(dps, slots, wide)
    replies = []
    for k in range(1, dps):
        to = (d + k) % dps
        replies.append(
            remote(answers.at[to], quarters.at[b, d], send.at[k], recv.at[k], (to, b))
        )
    for one in replies:
        one.start()
    quarters[b, d] = answers[d]
    return replies


class Share:
    def __init__(self, buf, send, recv):
        d, b = place()
        sibling, peer = partners()
        far = peer[1]
        self.moves = [
            remote(buf.at[b], buf.at[b], send.at[0], recv.at[0], peer),
            remote(buf.at[b], buf.at[b], send.at[1], recv.at[1], sibling),
            remote(buf.at[far], buf.at[far], send.at[2], recv.at[2], sibling),
        ]

    def start(self):
        self.moves[0].start()
        self.moves[1].start()

    def forward(self):
        self.moves[0].wait_recv()
        self.moves[2].start()

    def finish(self):
        self.moves[1].wait_recv()
        self.moves[2].wait_recv()
        for one in self.moves:
            one.wait_send()


class PieceSwap:
    def __init__(self, pairs, send, recv):
        d, b = place()
        self.sent = []
        for a, (src, dst) in enumerate(pairs):
            self.sent.append(pltpu.make_async_copy(src.at[b], dst.at[b], send.at[a, 0]))
            for k in range(1, 4):
                to = (b + k) % 4
                self.sent.append(
                    remote(src.at[to], dst.at[b], send.at[a, k], recv.at[a, k], (d, to))
                )

    def start(self):
        for one in self.sent:
            one.start()

    def finish(self):
        for one in self.sent:
            one.wait()


def flat(value):
    return [leaf for one in value for leaf in flat(one)] if isinstance(value, list) else [value]


def refill(value, leaves):
    return [refill(one, leaves) for one in value] if isinstance(value, list) else next(leaves)


class Names:
    def __init__(self):
        self.ins, self.outs, self.scratch = SimpleNamespace(), SimpleNamespace(), SimpleNamespace()

    def call(self, kernel, ident, vmem):
        ins, outs, scratch = (flat(list(vars(one).values())) for one in (self.ins, self.outs, self.scratch))

        def fill(bags, refs):
            leaves, found = iter(refs), SimpleNamespace()
            for bag in bags:
                for name, value in vars(bag).items():
                    vars(found)[name] = refill(value, leaves)
            return found

        results = pl.pallas_call(
            lambda *refs: kernel(fill((self.ins, self.outs, self.scratch), refs)),
            out_shape=[one for one, _ in outs],
            in_specs=[where for _, where in ins],
            out_specs=[where for _, where in outs],
            scratch_shapes=scratch,
            compiler_params=pltpu.CompilerParams(
                collective_id=ident, has_side_effects=True, vmem_limit_bytes=vmem * 2**20
            ),
            cost_estimate=pl.CostEstimate(flops=2**36, bytes_accessed=2**26, transcendentals=0),
        )(*[one for one, _ in ins])
        return fill((self.outs,), results)


def add_exchanges(names, width):
    names.scratch.spreads = [spread_scratch(width) for _ in range(2)]
    names.scratch.parts, names.scratch.out = collect_scratch(width)[:2]
    names.scratch.collects = [collect_scratch(width)[2:] for _ in range(2)]


def exchange_set(r, turn):
    return r.spreads[turn] + [r.parts, r.out] + r.collects[turn]


def forward_kernel(lead, layers, size, r):
    dps, blks = sizes()
    d, b = place()
    sibling, peer = partners()
    ada = r.ada
    qkv_shard = r.qkv_shard if lead else [r.qkv_first] + r.qkv_shard
    up_shard = r.up_shard if lead else [r.up_first] + r.up_shard
    gathers = []
    for layer in range(layers):
        first = [qkv_shard[layer], r.proj_shard.at[layer]]
        second = [up_shard[layer], r.w_down.at[layer]]
        for part, (srcs, dsts) in enumerate(((first, (r.wq, r.wp)), (second, (r.wu, r.wd)))):
            job = DpGather()
            job.bind(srcs, [one[layer] for one in dsts], r.gather_sems[2 * layer + part])
            gathers.append(job)
    if lead:
        arrived = greet_all()
    else:
        arrived = greet([sibling, peer, (d, 3 - b)] + gathers[0].partners)
    r.state[...] = r.tokens[...].astype(f32)
    arrived()
    swaps = [
        PieceSwap(
            [(r.qkv_cols[n], r.qkv_shard[n]), (r.up_cols[n], r.up_shard[n])],
            r.swap_send[n],
            r.swap_recv[n],
        )
        for n in range(len(r.qkv_cols))
    ]
    if lead:
        permutes = [
            Permute(
                r.w_proj.at[n], r.proj_shard.at[n], r.permute_send.at[n], r.permute_recv.at[n], False
            )
            for n in range(layers)
        ]
        permutes[0].start()
        swaps[0].start()
        moves = modulations_start(
            r.rows_in,
            r.ada_in,
            r.rows,
            r.columns,
            (r.dp_send, r.dp_recv, r.ada_send, r.ada_recv, r.ada_local),
        )
        for one in moves:
            one.wait()
        replies = modulations_answer(
            r.rows, r.columns, r.answers, r.quarters, (r.answer_send, r.answer_recv)
        )
        swaps[0].finish()
        permutes[0].finish()
        gathers[0].start_far()
        gathers[0].start_near()
        for one in permutes[1:]:
            one.start()
        share = Share(r.quarters, r.share_send, r.share_recv)
        for one in replies:
            one.wait()
        share.start()
        share.forward()
        gathers[0].step(0)
        share.finish()
        slots = r.answers.shape[1]
        wide = r.answers.shape[2]
        each = ada.shape[2]
        for i in range(dps * blks):
            value = r.quarters[i % blks, i // blks]
            layer, at = (i * wide) // each, (i * wide) % each
            high = value.astype(bf16)
            ada[layer, 0:slots, at : at + wide] = high
            ada[layer, slots : 2 * slots, at : at + wide] = (value - high.astype(f32)).astype(bf16)
    else:
        gathers[0].start_far()
        gathers[0].start_near()
        gathers[0].step(0)
    gathers[1].start_far()
    for one in swaps[-(layers - 1) :]:
        one.start()

    def need_first(layer):
        job, following = gathers[2 * layer], gathers[2 * layer + 1]
        if layer == 0:
            job.step(1)
            job.step(2)
        following.start_near()
        job.finish()

    def early(layer):
        if layer == 0:
            for one in swaps[-(layers - 1) :]:
                one.finish()
            if lead:
                for one in permutes[1:]:
                    one.finish()
            for one in gathers[2:]:
                one.start_far()
        else:
            gathers[2 * layer + 1].step(0)

    def middle(layer):
        gathers[2 * layer + 1].step(0 if layer == 0 else 1)

    def late(layer):
        gathers[2 * layer + 1].step(1 if layer == 0 else 2)

    def need_second(layer):
        if layer == 0:
            gathers[1].step(2)
        if layer + 1 < layers:
            gathers[2 * layer + 2].start_near()
        gathers[2 * layer + 1].finish()

    def weights(ref, rows):
        return ref.reshape(rows, ref.shape[-1])

    pending = []
    saver = Moves(r.save_sems)
    width = r.state.shape[1]
    for layer in range(layers):
        last = layer + 1 == layers
        attend_segment(
            Hooks(
                need=partial(need_first, layer),
                a=partial(early, layer),
                b=partial(middle, layer),
                c=partial(late, layer),
            ),
            size,
            r.state,
            r.onehot,
            ada.at[layer],
            r.qscale.at[layer],
            r.keyc,
            r.keyr,
            (weights(r.wq[layer], width), weights(r.wp[layer], width // 4)),
            (r.wqkv, r.wproj),
            (r.h.at[layer], r.qkv.at[layer], r.rates.at[layer]),
            r.inverse.at[layer],
            r.branch_buf,
            r.middle,
            (r.qkv_buf, r.vt, r.rate_buf, r.o_buf),
            (r.gamma, r.scale, r.shift),
            r.moves.at[2 * layer],
            exchange_set(r, 0),
        )
        for one in pending:
            one.wait()
        pending = [
            saver.copy(r.o_buf, r.o.at[layer]),
            saver.copy(r.branch_buf, r.branch.at[layer]),
            saver.copy(r.middle, r.mids.at[layer]),
        ]
        hooks = Hooks(need=partial(need_second, layer))
        if not last:
            hooks.a, hooks.b, hooks.c = [partial(gathers[2 * layer + 2].step, i) for i in range(3)]
        mlp_segment(
            hooks,
            r.middle,
            r.onehot,
            ada.at[layer],
            (weights(r.wu[layer], width), weights(r.wd[layer], width)),
            (r.wup, r.wdown),
            (r.h2.at[layer], r.g.at[layer], r.slope.at[layer]),
            r.result_buf,
            r.state,
            (r.hidden, r.slope_buf),
            (r.gamma, r.scale, r.shift),
            r.moves.at[2 * layer + 1],
            exchange_set(r, 1),
        )
        for one in pending:
            one.wait()
        pending = [saver.copy(r.result_buf, r.result.at[layer])]
        if not last:
            pending.append(saver.copy(r.state, r.states.at[layer]))
    r.output[...] = r.state[...].astype(bf16)
    for one in pending:
        one.wait()


def forward(size, tokens, onehot, keyc, keyr, qscale, w_down, proj, qkv_cols, up_cols, rows_in, ada_in, ada, qkv_shard, up_shard):
    lead = ada_in is not None
    dps, blks = sizes()
    count = dps * blks
    rows, width = tokens.shape
    layers = proj.shape[0]
    length = rows * blks
    wide, ff = qkv_cols[0].shape[2], up_cols[0].shape[2]
    sems = pltpu.SemaphoreType.DMA
    n = Names()
    vars(n.ins).update(
        tokens=(tokens, VMEM), onehot=(onehot, VMEM), keyc=(keyc, VMEM), keyr=(keyr, VMEM), qscale=(qscale, VMEM)
    )
    n.ins.w_down = (w_down, ANY)
    low = partial(shaped, dtype=bf16)
    if lead:
        vars(n.ins).update(rows_in=(rows_in, ANY), ada_in=(ada_in, ANY), w_proj=(proj, ANY))
        slots = rows_in.shape[0]
        columns = ada_in.shape[2]
        vars(n.outs).update(
            ada=(low(layers, 2 * slots, count * columns // layers), VMEM),
            rows=(low(dps, slots, width), VMEM),
            proj_shard=(low(*proj.shape), ANY),
        )
        vars(n.scratch).update(
            columns=pltpu.VMEM((width, columns), bf16),
            answers=pltpu.VMEM((dps, slots, columns), f32),
            quarters=pltpu.VMEM((blks, dps, slots, columns), f32),
            dp_send=sems((dps,)),
            dp_recv=sems((dps,)),
            answer_send=sems((dps,)),
            answer_recv=sems((dps,)),
            ada_send=sems((count,)),
            ada_recv=sems((count,)),
            ada_local=sems((2,)),
            share_send=sems((3,)),
            share_recv=sems((3,)),
            permute_send=sems((layers,)),
            permute_recv=sems((layers,)),
        )
    else:
        vars(n.ins).update(
            ada=(ada, VMEM), proj_shard=(proj, ANY), qkv_first=(qkv_shard, ANY), up_first=(up_shard, ANY)
        )
    moved_qkv, moved_up = (one if lead else one[1:] for one in (qkv_cols, up_cols))
    n.ins.qkv_cols = [(one, ANY) for one in moved_qkv]
    n.ins.up_cols = [(one, ANY) for one in moved_up]
    n.outs.qkv_shard = [(low(*one.shape), ANY) for one in moved_qkv]
    n.outs.up_shard = [(low(*one.shape), ANY) for one in moved_up]
    n.scratch.swap_send = [sems((2, 4)) for _ in moved_qkv]
    n.scratch.swap_recv = [sems((2, 4)) for _ in moved_qkv]
    n.outs.wq = [(low(dps, *one.shape), ANY) for one in qkv_cols]
    n.outs.wp = [(low(dps, *proj.shape[1:]), ANY)] * layers
    n.outs.wu = [(low(dps, *one.shape), ANY) for one in up_cols]
    n.outs.wd = [(low(dps, *w_down.shape[1:]), ANY)] * layers
    n.scratch.gather_sems = [[sems((2, dps)), sems((2, dps)), sems((2,))] for _ in range(2 * layers)]
    vars(n.outs).update(
        output=(low(rows, width), VMEM),
        inverse=(shaped(layers, 4, 8, TILE), VMEM),
        h=(low(layers, length, width), ANY),
        qkv=(low(layers, length, wide), ANY),
        rates=(shaped(layers, length, 2 * TILE), ANY),
        o=(low(layers, length, TILE), ANY),
        branch=(shaped(layers, rows, width), ANY),
        mids=(shaped(layers, rows, width), ANY),
        h2=(low(layers, length, width), ANY),
        g=(low(layers, length, ff), ANY),
        slope=(low(layers, length, ff), ANY),
        result=(shaped(layers, rows, width), ANY),
        states=(shaped(layers, rows, width), ANY),
    )
    big = pltpu.VMEM((rows, width), f32)
    vars(n.scratch).update(
        state=big, middle=big, branch_buf=big, result_buf=big, gamma=big, scale=big, shift=big
    )
    vars(n.scratch).update(
        wqkv=pltpu.VMEM((width, wide), bf16),
        wproj=pltpu.VMEM((TILE, width), bf16),
        wup=pltpu.VMEM((width, ff), bf16),
        wdown=pltpu.VMEM((ff, width), bf16),
        qkv_buf=pltpu.VMEM((length, wide), bf16),
        vt=pltpu.VMEM((TILE, length), bf16),
        rate_buf=pltpu.VMEM((length, 2 * TILE), f32),
        o_buf=pltpu.VMEM((length, TILE), bf16),
        hidden=pltpu.VMEM((length, ff), bf16),
        slope_buf=pltpu.VMEM((length, ff), bf16),
        moves=sems((2 * layers, 5)),
        save_sems=sems((5 * layers,)),
    )
    add_exchanges(n, width)
    return n.call(partial(forward_kernel, lead, layers, size), 8, 56)


def backward_kernel(layers, size, r):
    dps, blks = sizes()
    d, b = place()
    arrived = greet_all()
    width = r.grad.shape[1]
    rows = r.w_ada.shape[1]
    people = r.cond.shape[1]
    r.grad[...] = r.cotangent[...].astype(f32)
    arrived()

    wides, narrows, swaps, permutes, items = {}, {}, {}, {}, {}
    r.dadas = [r.near_dada] + r.far_dadas
    for n in range(layers):
        wides[n], narrows[n] = DpScatter(), DpScatter()
        shared = r.wide
        wides[n].bind([r.dwu[n], r.dwd[n]], [r.up_sum[n], r.down_grad.at[n]], shared)
        shared = r.narrow
        narrows[n].bind([r.dwq[n], r.dwp[n]], [r.qkv_sum[n], r.proj_sum[n]], shared)
        for k, (src, dst) in enumerate(((r.up_sum, r.up_grad), (r.qkv_sum, r.qkv_grad))):
            swaps[k, n] = PieceSwap(
                [(src[n], dst.at[n])], r.swap_send.at[2 * n + k], r.swap_recv.at[2 * n + k]
            )
        permutes[n] = Permute(
            r.proj_sum[n], r.proj_grad.at[n], r.permute_send.at[n], r.permute_recv.at[n], True
        )
        for part in range(2):
            at = 2 * n + part
            items[n, part] = Items(r.items[at], r.dadas[at], r.items_scratch[at])

    def wide_done(n):
        wides[n].finish()
        swaps[0, n].start()
        if n:
            wides[n].release(r.credit.at[0])

    def narrow_done(n):
        narrows[n].finish()
        swaps[1, n].start()
        permutes[n].start()
        if n:
            narrows[n].release(r.credit.at[1])

    def weights(ref, count):
        return ref.reshape(count, ref.shape[-1])

    wide = 3 * TILE
    length = 4 * TILE
    for layer in reversed(range(layers)):
        top = layer + 1 == layers
        above = layer + 1

        def begin_mlp():
            if not top:
                items[above, 0].start()

        def late_mlp():
            if not top:
                narrows[above].step(2)
                items[above, 1].spread()
                items[above, 0].sum()

        def done_mlp():
            if not top:
                wide_done(above)
                wides[layer].acquire(r.credit.at[0])
            wides[layer].start()

        hooks = Hooks(start=begin_mlp, c=late_mlp, dw=done_mlp)
        if not top:
            hooks.sent = wides[above].own
            hooks.a, hooks.b = [partial(narrows[above].step, i) for i in range(2)]
        ff = r.slope.shape[2]
        mlp_back_segment(
            hooks,
            r.grad,
            r.onehot,
            r.onehot_t,
            r.ada.at[layer],
            (
                weights(r.wu[layer], width),
                weights(r.wd[layer], ff),
                r.h2.at[layer],
                r.g.at[layer],
                r.slope.at[layer],
                r.result.at[layer],
                r.mids.at[layer],
            ),
            (weights(r.dwu[layer], width), weights(r.dwd[layer], ff)),
            r.dmid,
            r.items[2 * layer + 1],
            (r.wup, r.wdown, r.hall, r.gall, r.du, r.dwup, r.dwdown, r.load_a, r.load_b),
            (r.gamma, r.scale),
            (r.dgamma, r.dscale, r.dshift),
            r.moves.at[2 * layer],
            exchange_set(r, 0),
        )

        def begin_attend():
            items[layer, 1].start()

        def sent_attend():
            if not top:
                narrows[above].own()

        def second_attend():
            wides[layer].step(1)
            if not top:
                narrow_done(above)

        def late_attend():
            wides[layer].step(2)
            items[layer, 1].sum()
            if not top:
                items[above, 1].forward()
                items[above, 0].spread()

        def done_attend():
            if not top:
                narrows[layer].acquire(r.credit.at[1])
            narrows[layer].start()

        attend_back_segment(
            Hooks(
                start=begin_attend,
                sent=sent_attend,
                a=partial(wides[layer].step, 0),
                b=second_attend,
                d=late_attend,
                dw=done_attend,
            ),
            size,
            r.dmid,
            r.onehot,
            r.onehot_t,
            r.ada.at[layer],
            r.qscale.at[layer],
            r.keyc,
            r.keyr,
            r.inverse.at[layer],
            (
                weights(r.wq[layer], width),
                weights(r.wp[layer], TILE),
                r.h.at[layer],
                r.qkv.at[layer],
                r.rates.at[layer],
                r.o.at[layer],
                r.branch.at[layer],
                r.states.at[layer - 1] if layer else None,
            ),
            (weights(r.dwq[layer], width), weights(r.dwp[layer], TILE)),
            r.grad,
            r.items[2 * layer],
            r.heads.at[layer],
            (
                r.wup.at[:, 0:wide],
                r.wdown.at[0:TILE],
                r.hall,
                r.gall.at[:, 0:wide],
                r.rates_buf,
                r.gall.at[:, wide : wide + TILE],
                r.dwdown.at[TILE : 2 * TILE],
                r.dkeys,
                r.dvalues,
                r.du.at[:, 0:wide],
                r.dwup.at[:, 0:wide],
                r.dwdown.at[0:TILE],
                r.load_a,
                r.load_b if layer else r.tokens,
            ),
            (r.gamma, r.scale),
            (r.dgamma, r.dscale, r.dshift),
            r.moves.at[2 * layer + 1],
            exchange_set(r, 1),
        )
    items[0, 0].start()
    r.tokens_grad[...] = r.grad[...].astype(bf16)
    wides[0].own()
    items[0, 0].sum()

    def fold(layer, part, total):
        dada = r.dadas[2 * layer + part]
        if layer or part:
            load = pltpu.make_async_copy(dada, r.dada, r.dada_sem)
            load.start()
            load.wait()
            dada = r.dada
        quarter = dada.shape[3]
        for c in range(0, 3 * width, TILE):
            at = (c // width) * 2 * width + part * width + c % width
            inner = c % quarter
            value = dada[c // quarter, :, :, inner : inner + TILE].reshape(people, TILE)
            r.ada_grad[layer, :, at : at + TILE] = mm(r.cond[...], value)
            total = total + mm_t(r.w_ada[layer, :, at : at + TILE], value)
        return total

    items[1, 1].finish()
    total = fold(1, 1, jnp.zeros((rows, people), f32))
    items[1, 0].forward()
    items[0, 1].spread()
    narrows[0].step(0)
    items[1, 0].finish()
    total = fold(1, 0, total)
    items[0, 1].forward()
    items[0, 0].spread()
    narrows[0].step(1)
    items[0, 1].finish()
    total = fold(0, 1, total)
    items[0, 0].forward()
    narrows[0].step(2)
    items[0, 0].finish()
    total = fold(0, 0, total)
    message = r.message
    message[0:rows, :] = total
    message[rows:, :] = r.notes[...]
    lane = lax.broadcasted_iota(jnp.int32, (TILE, people), 0)
    pick = (lane == lax.broadcasted_iota(jnp.int32, (TILE, people), 1) * size).astype(bf16)
    for layer in range(layers):
        message[rows + layer : rows + layer + 1, :] = split_three(r.heads[layer], pick)
    told = [
        remote(message, r.heard.at[b, d], r.told_send.at[k], r.told_recv.at[k], ((d + k) % dps, b))
        for k in range(1, dps)
    ]
    told.append(pltpu.make_async_copy(message, r.heard.at[b, d], r.told_send.at[0]))
    for one in told:
        one.start()
    narrows[0].own()
    wide_done(0)
    for one in told:
        one.wait()
    share = Share(r.heard, r.share_send, r.share_recv)
    share.start()
    share.forward()
    narrow_done(0)
    share.finish()
    for one in list(swaps.values()) + list(permutes.values()):
        one.finish()


def split_three(values, ones):
    high = values.astype(bf16)
    rest = values - high.astype(f32)
    low = rest.astype(bf16)
    least = (rest - low.astype(f32)).astype(bf16)
    return mm(high, ones) + (mm(low, ones) + mm(least, ones))


def backward(size, keep, extra):
    dps, blks = sizes()
    layers = keep.h.shape[0]
    rows, width = extra.cotangent.shape
    length = rows * blks
    wide, ff = keep.qkv.shape[2], keep.slope.shape[2]
    wrows = extra.w_ada.shape[1]
    slots, people = extra.onehot_t.shape[0], extra.cond.shape[1]
    sems = pltpu.SemaphoreType.DMA
    low = partial(shaped, dtype=bf16)
    n = Names()
    for name, one in vars(extra).items():
        vars(n.ins)[name] = (one, VMEM)
    for name in vars(keep):
        vars(n.ins)[name] = [(one, ANY) for one in flat(vars(keep)[name])]
        if not isinstance(vars(keep)[name], list):
            vars(n.ins)[name] = vars(n.ins)[name][0]
    pairs = dps // 2

    def scatter_scratch(shapes):
        found = []
        for shape in shapes:
            found += [pltpu.VMEM((pairs, *shape), bf16)] * 3
            found += [sems((2 * pairs,)), sems((2 * pairs,)), sems((pairs,))]
        return found

    quarter = 3 * width // 4
    whole = (4, dps, slots, quarter)
    sets = 2 * layers
    n.outs.dwu = [(low(dps, blks * wrows, ff), ANY)] * layers
    n.outs.dwd = [(low(dps, ff // dps, width), ANY)] * layers
    n.outs.dwq = [(low(dps, blks * wrows, wide), ANY)] * layers
    n.outs.dwp = [(low(dps, TILE // dps, width), ANY)] * layers
    n.outs.far_dadas = [(low(*whole), ANY)] * (sets - 1)
    n.scratch.near_dada = pltpu.VMEM(whole, bf16)
    n.scratch.dada = pltpu.VMEM(whole, bf16)
    n.scratch.dada_sem = sems
    n.scratch.up_sum = [pltpu.VMEM((blks, wrows, ff), bf16)] * layers
    n.scratch.qkv_sum = [pltpu.VMEM((blks, wrows, wide), bf16)] * layers
    n.scratch.proj_sum = [pltpu.VMEM((TILE // dps, width), f32)] * layers
    n.scratch.items = [pltpu.VMEM((slots, 3 * width), f32)] * sets
    n.scratch.items_scratch = [
        [
            pltpu.VMEM((4, slots, quarter), f32),
            pltpu.VMEM((1, slots, quarter), bf16),
            sems((8,)),
            sems((7,)),
            sems((dps,)),
            sems((dps,)),
        ]
    ] * sets
    n.scratch.wide = scatter_scratch([(blks * wrows, ff), (ff // dps, width)])
    n.scratch.narrow = scatter_scratch([(blks * wrows, wide), (TILE // dps, width)])
    vars(n.outs).update(
        tokens_grad=(low(rows, width), VMEM),
        ada_grad=(shaped(layers, wrows, 6 * width), VMEM),
        up_grad=(low(layers, blks, wrows, ff), ANY),
        qkv_grad=(low(layers, blks, wrows, wide), ANY),
        proj_grad=(shaped(layers, TILE // dps, width), ANY),
        down_grad=(shaped(layers, ff // dps, width), VMEM),
        heard=(shaped(blks, dps, wrows + 8, people), ANY),
    )
    big, small = pltpu.VMEM((rows, width), f32), pltpu.VMEM((rows, width), bf16)
    vars(n.scratch).update(
        grad=big,
        dmid=big,
        load_a=big,
        load_b=big,
        gamma=big,
        scale=big,
        dgamma=small,
        dscale=small,
        dshift=small,
        wup=pltpu.VMEM((width, ff), bf16),
        wdown=pltpu.VMEM((ff, width), bf16),
        hall=pltpu.VMEM((length, width), bf16),
        gall=pltpu.VMEM((length, ff), bf16),
        du=pltpu.VMEM((length, ff), bf16),
        dwup=pltpu.VMEM((width, ff), bf16),
        dwdown=pltpu.VMEM((ff, width), bf16),
        rates_buf=pltpu.VMEM((length, 2 * TILE), f32),
        dkeys=pltpu.VMEM((length, TILE), f32),
        dvalues=pltpu.VMEM((length, TILE), f32),
        heads=pltpu.VMEM((layers, 1, TILE), f32),
        message=pltpu.VMEM((wrows + 8, people), f32),
        moves=sems((2 * layers, 10)),
        credit=pltpu.SemaphoreType.REGULAR((2,)),
        permute_send=sems((layers,)),
        permute_recv=sems((layers,)),
        told_send=sems((dps,)),
        told_recv=sems((dps,)),
        share_send=sems((3,)),
        share_recv=sems((3,)),
    )
    n.scratch.swap_send = sems((2 * layers, 1, 4))
    n.scratch.swap_recv = sems((2 * layers, 1, 4))
    add_exchanges(n, width)
    return n.call(partial(backward_kernel, layers, size), 9, 60)


ANY = pl.BlockSpec(memory_space=pl.ANY)
VMEM = pl.BlockSpec(memory_space=pltpu.VMEM)


def shaped(*shape, dtype=f32):
    return jax.ShapeDtypeStruct(shape, dtype)


def per_device(
    tokens,
    cotangent,
    stop_scale,
    labels,
    class_table,
    head_scale,
    w_qkv,
    w_proj,
    w_up,
    w_down,
    w_ada,
):
    rows, width = tokens.shape[1:]
    layers, heads = head_scale.shape
    size = width // heads
    dps, blks = sizes()
    count = dps * blks
    length = rows * blks
    d, b = place()
    own_heads = heads // blks
    piece = own_heads * size
    wrows = w_qkv.shape[1]
    ffrows = w_down.shape[1]
    ff = ffrows * dps
    slots = labels.shape[1]
    padded = 16

    item_all, level_all = token_meta(stop_scale[0], length)
    item_own = lax.dynamic_slice_in_dim(item_all, b * rows, rows)
    key = (item_all * 16 + level_all).reshape(blks, rows)
    sib = b + 1 - 2 * (b % 2)
    far, far_sib = (b + 2) % 4, (sib + 2) % 4
    key = jnp.concatenate(
        [key[b], key[sib], key[far, :HALF], key[far_sib, :HALF], key[far, HALF:], key[far_sib, HALF:]]
    )
    keyc, keyr = key[:, None], key.reshape(4, 1, TILE)
    slot_id = jnp.arange(padded, dtype=jnp.int32)
    onehot_t = (slot_id[:, None] == item_own[None, :]).astype(bf16)
    onehot = (item_own[:, None] == jnp.concatenate([slot_id, slot_id])[None, :]).astype(bf16)

    names = jnp.pad(labels[0], (0, padded - slots), constant_values=-1)

    def one_hot(names):
        return (names[:, None] == jnp.arange(class_table.shape[0], dtype=jnp.int32)[None, :]).astype(bf16)

    wide = w_ada.shape[2]
    columns = layers * wide // count
    ada_cols = w_ada.transpose(1, 0, 2).reshape(wrows, count, columns).transpose(1, 0, 2)
    qkv_cols = w_qkv.reshape(layers, wrows, 3, blks, piece).transpose(0, 3, 1, 2, 4)
    qkv_cols = qkv_cols.reshape(layers, blks, wrows, 3 * piece)
    up_cols = w_up.reshape(layers, wrows, dps, blks, ffrows).transpose(0, 3, 1, 2, 4)
    up_cols = up_cols.reshape(layers, blks, wrows, ff)
    class_rows = mm(one_hot(names), class_table).astype(bf16)
    own_scale = lax.dynamic_slice_in_dim(head_scale, b * own_heads, own_heads, axis=1)
    qscales = jnp.repeat(jnp.exp(own_scale), size, axis=1)
    common = (size, tokens[0], onehot, keyc, keyr, qscales[:, None, :], w_down)
    qkv_list, up_list = [qkv_cols[i] for i in range(layers)], [up_cols[i] for i in range(layers)]
    if columns % 128 == 0 and wrows % 16 == 0:
        kept = forward(*common, w_proj, qkv_list, up_list, class_rows, ada_cols, None, None, None)
        ada = kept.ada
        class_rows = kept.rows.reshape(dps * padded, width)
        cond_all = jax.nn.silu(class_rows.astype(f32)).astype(bf16)
    else:
        to_heads = [(i, (i % dps) * blks + i // dps) for i in range(count)]
        proj_own = lax.ppermute(w_proj, ("dp", "blk"), to_heads)
        class_rows = gather(class_rows, "dp")
        cond_all = jax.nn.silu(class_rows.astype(f32)).astype(bf16)
        ada_cols = lax.all_to_all(ada_cols, ("dp", "blk"), 0, 0, tiled=True)
        ada_part = mm(cond_all, ada_cols.reshape(count * wrows, columns))
        ada_part = lax.all_to_all(ada_part.reshape(dps, padded, columns), "dp", 0, 0, tiled=True)
        ada_all = lax.all_gather(ada_part, "blk", axis=1, tiled=False)
        ada_all = ada_all.transpose(2, 0, 1, 3).reshape(padded, layers, wide).transpose(1, 0, 2)
        ada_high = ada_all.astype(bf16)
        ada_low = (ada_all - ada_high.astype(f32)).astype(bf16)
        ada = jnp.concatenate([ada_high, ada_low], axis=1)
        qkv_shard = lax.all_to_all(qkv_cols[0], "blk", 0, 0, tiled=True)
        up_shard = lax.all_to_all(up_cols[0], "blk", 0, 0, tiled=True)
        kept = forward(*common, proj_own, qkv_list, up_list, None, None, ada, qkv_shard, up_shard)
    output = kept.output[None]
    lanes = dps * padded
    notes = jnp.pad(names.astype(f32)[None, :], ((layers, 7 - layers), (0, lanes - padded)))
    cond_own = lax.dynamic_slice_in_dim(cond_all, (d * blks + b) * wrows, wrows, axis=1).T
    keep = SimpleNamespace(
        h=kept.h,
        qkv=kept.qkv,
        rates=kept.rates,
        o=kept.o,
        branch=kept.branch,
        mids=kept.mids,
        h2=kept.h2,
        g=kept.g,
        slope=kept.slope,
        result=kept.result,
        states=kept.states,
        wq=kept.wq,
        wp=kept.wp,
        wu=kept.wu,
        wd=kept.wd,
    )
    extra = SimpleNamespace(
        tokens=tokens[0],
        cotangent=cotangent[0],
        onehot=onehot,
        onehot_t=onehot_t,
        keyc=keyc,
        keyr=keyr,
        qscale=qscales[:, None, :],
        ada=ada,
        inverse=kept.inverse,
        cond=cond_own,
        w_ada=w_ada,
        notes=notes,
    )
    grads = backward(size, keep, extra)
    one = grads.qkv_grad.reshape(layers, blks, wrows, 3, piece)
    qkv_grad = one.transpose(0, 2, 3, 1, 4).reshape(layers, wrows, 3 * width).astype(f32)
    one = grads.up_grad.reshape(layers, blks, wrows, dps, ffrows)
    up_grad = one.transpose(0, 2, 3, 1, 4).reshape(layers, wrows, ff * blks).astype(f32)
    told = grads.heard
    head_grad = jnp.sum(told[:, :, wrows : wrows + layers, :own_heads], axis=1)
    head_grad = head_grad.transpose(1, 0, 2).reshape(layers, heads)
    every_name = told[0, :, wrows + layers, :padded].reshape(-1).astype(jnp.int32)
    cond_grad = told[:, :, :wrows, :].transpose(1, 0, 2, 3).reshape(width, lanes).T
    _, silu_pull = jax.vjp(jax.nn.silu, class_rows.astype(f32))
    cond_pre = silu_pull(cond_grad)[0]
    pre_high = cond_pre.astype(bf16)
    pre_low = (cond_pre - pre_high.astype(f32)).astype(bf16)
    chosen = one_hot(jnp.concatenate([every_name, every_name]))
    table_grad = rows_mm(chosen, jnp.concatenate([pre_high, pre_low]))
    return (
        output,
        grads.tokens_grad[None],
        table_grad,
        head_grad,
        qkv_grad,
        grads.proj_grad,
        up_grad,
        grads.down_grad,
        grads.ada_grad,
    )


def solution(mesh):
    in_specs = (
        P("dp", "blk", None),
        P("dp", "blk", None),
        P("dp", None),
        P("dp", None),
        P(),
        P(),
        P(None, ("dp", "blk"), None),
        P(None, ("dp", "blk"), None),
        P(None, ("dp", "blk"), None),
        P(None, ("dp", "blk"), None),
        P(None, ("dp", "blk"), None),
    )
    out_specs = (
        P("dp", "blk", None),
        P("dp", "blk", None),
        P(),
        P(),
        P(None, ("dp", "blk"), None),
        P(None, ("dp", "blk"), None),
        P(None, ("dp", "blk"), None),
        P(None, ("dp", "blk"), None),
        P(None, ("dp", "blk"), None),
    )
    return jax.shard_map(
        per_device, mesh=mesh, in_specs=in_specs, out_specs=out_specs, check_vma=False
    )
```

```python
from functools import partial
from types import SimpleNamespace

import jax
import jax.numpy as jnp
from jax import lax
from jax.experimental import pallas as pl
from jax.experimental.pallas import tpu as pltpu
from jax.sharding import PartitionSpec as P

patch_areas = (1, 4, 9, 16, 25, 36, 64, 100, 169)
scale_starts = (1, 5, 14, 30, 55, 91, 155, 255)
f32 = jnp.float32
bf16 = jnp.bfloat16
MESH = pl.DeviceIdType.MESH
TILE = 256
HALF = 128
STEP = 32


def sizes():
    return lax.axis_size("dp"), lax.axis_size("blk")


def place():
    return lax.axis_index("dp"), lax.axis_index("blk")


def flat_place():
    return place()[0] * sizes()[1] + place()[1]


def token_meta(stops, length):
    areas = jnp.array(patch_areas, dtype=jnp.int32)
    levels = jnp.arange(9, dtype=jnp.int32)
    counts = jnp.sum(jnp.where(levels[None, :] < stops[:, None], areas[None, :], 0), axis=1)
    ends = jnp.cumsum(counts)
    places = jnp.arange(length, dtype=jnp.int32)
    passed = places[:, None] >= ends[None, :]
    item = jnp.sum(passed.astype(jnp.int32), axis=1)
    begin = jnp.sum(jnp.where(passed, counts[None, :], 0), axis=1)
    inner = places - begin
    bounds = jnp.array(scale_starts, dtype=jnp.int32)
    level = jnp.sum((inner[:, None] >= bounds[None, :]).astype(jnp.int32), axis=1)
    level = jnp.where(item == stops.shape[0], 0, level)
    return (item, level)


def mm(left, right):
    return jnp.dot(left, right, preferred_element_type=f32)


def mm_t(left, right):
    return lax.dot_general(left, right, (((1,), (1,)), ((), ())), preferred_element_type=f32)


def rows_mm(left, right, precision=None):
    return lax.dot_general(
        left, right, (((0,), (0,)), ((), ())), precision=precision, preferred_element_type=f32
    )


def gather(values, axes):
    return lax.all_gather(values, axes, axis=0, tiled=True)


def scatter(values, axes):
    return lax.psum_scatter(values, axes, scatter_dimension=0, tiled=True)


def partners():
    d, b = place()
    return (d, b + 1 - 2 * (b % 2)), (d, (b + 2) % 4)


def greet(others):
    barrier = pltpu.get_barrier_semaphore()
    for other in others:
        pl.semaphore_signal(barrier, inc=1, device_id=other, device_id_type=MESH)
    return lambda: pl.semaphore_wait(barrier, len(others))


def greet_all():
    dps, blks = sizes()
    me = flat_place()
    others = [(me + k) % (dps * blks) for k in range(1, dps * blks)]
    return greet([(t // blks, t % blks) for t in others])


def remote(src, dst, send, recv, target):
    return pltpu.make_async_remote_copy(
        src_ref=src, dst_ref=dst, send_sem=send, recv_sem=recv, device_id=target, device_id_type=MESH
    )


class Spread:
    def __init__(self, buf, send, recv, sibling, peer):
        def copy(src, dst, k, target):
            return remote(
                buf.at[pl.ds(src, HALF)], buf.at[pl.ds(dst, HALF)], send.at[k], recv.at[k], target
            )

        self.to_peer = [copy(HALF * c, 2 * TILE + TILE * c, c, peer) for c in range(2)]
        self.to_sibling = [copy(HALF * c, TILE + HALF * c, 2 + c, sibling) for c in range(2)]
        self.forward = [
            copy(2 * TILE + TILE * c, 2 * TILE + TILE * c + HALF, 4 + c, sibling) for c in range(2)
        ]

    def start(self, c):
        self.to_peer[c].start()
        self.to_sibling[c].start()

    def wait_block(self, i):
        @pl.when(i == 1)
        def _():
            for c in range(2):
                self.to_sibling[c].wait_recv()

        for c in range(2):

            @pl.when(i == 2 + c)
            def _():
                self.to_peer[c].wait_recv()
                self.forward[c].start()
                self.forward[c].wait_recv()

    def finish(self):
        for c in range(2):
            self.to_peer[c].wait_send()
            self.to_sibling[c].wait_send()
            self.forward[c].wait_send()


class Collect:
    def __init__(self, parts, out, mid, own, far, send, recv, sibling, peer):
        self.parts, self.out, self.mid, self.own, self.far = parts, out, mid, own, far
        self.cross = [
            remote(
                parts.at[pl.ds(2 * TILE + TILE * c + HALF, HALF)],
                mid.at[pl.ds(HALF * c, HALF)],
                send.at[c],
                recv.at[c],
                sibling,
            )
            for c in range(2)
        ]
        self.over = [
            remote(
                out.at[pl.ds(HALF * c, HALF)],
                far.at[pl.ds(HALF * c, HALF)],
                send.at[2 + c],
                recv.at[2 + c],
                peer,
            )
            for c in range(2)
        ]
        self.home = remote(parts.at[pl.ds(TILE, TILE)], own, send.at[4], recv.at[4], sibling)

    def block_done(self, j):
        for c in range(2):

            @pl.when(j == 2 + c)
            def _():
                self.cross[c].start()
                self.cross[c].wait_recv()

                @pl.loop(0, HALF // STEP)
                def _(s):
                    at = pl.multiple_of(s * STEP, STEP)
                    mine = self.parts[pl.ds(2 * TILE + TILE * c + at, STEP), :].astype(f32)
                    theirs = self.mid[pl.ds(HALF * c + at, STEP), :].astype(f32)
                    self.out[pl.ds(HALF * c + at, STEP), :] = (mine + theirs).astype(bf16)

                self.over[c].start()

        @pl.when(j == 1)
        def _():
            self.home.start()

    def wait(self):
        self.home.wait_recv()
        for c in range(2):
            self.over[c].wait_recv()

    def rows(self, at):
        span = pl.ds(at, STEP)
        total = self.parts[span, :].astype(f32) + self.own[span, :].astype(f32)
        return total + self.far[span, :].astype(f32)

    def finish(self):
        self.home.wait_send()
        for c in range(2):
            self.cross[c].wait_send()
            self.over[c].wait_send()


def spread_scratch(width):
    return [
        pltpu.VMEM((4 * TILE, width), bf16),
        pltpu.SemaphoreType.DMA((6,)),
        pltpu.SemaphoreType.DMA((6,)),
    ]


def collect_scratch(width):
    return [pltpu.VMEM((4 * TILE, width), bf16)] + [pltpu.VMEM((TILE, width), bf16)] * 4 + [
        pltpu.SemaphoreType.DMA((5,)),
        pltpu.SemaphoreType.DMA((5,)),
    ]


class Moves:
    def __init__(self, sems):
        self.sems, self.used = sems, 0

    def copy(self, src, dst):
        made = pltpu.make_async_copy(src, dst, self.sems.at[self.used])
        self.used += 1
        made.start()
        return made


def expand(onehot, ada, which, outs):
    width = outs[0].shape[1]
    for k, out in zip(which, outs):
        for n in range(0, width, TILE):
            out[:, n : n + TILE] = mm(onehot[...], ada[:, k * width + n : k * width + n + TILE])


def normed(values):
    centre = jnp.mean(values, axis=-1, keepdims=True)
    centred = values - centre
    spread = jnp.mean(centred * centred, axis=-1, keepdims=True)
    rate = lax.rsqrt(spread + 1e-06)
    return centred * rate, rate


def norm_back(grad, values_hat, rate):
    first = jnp.mean(grad, axis=-1, keepdims=True)
    second = jnp.mean(grad * values_hat, axis=-1, keepdims=True)
    return rate * (grad - first - values_hat * second)


def row_steps(start, rows, body):
    @pl.loop(0, rows // STEP)
    def _(s):
        body(pl.multiple_of(start + s * STEP, STEP))


def block_ones(size):
    shape = (TILE, TILE)
    one = lax.broadcasted_iota(jnp.int32, shape, 0) // size
    two = lax.broadcasted_iota(jnp.int32, shape, 1) // size
    return (one == two).astype(bf16)


def split_mm(dot, values, ones):
    high = values.astype(bf16)
    low = (values - high.astype(f32)).astype(bf16)
    return dot(high, ones) + dot(low, ones)


def head_lanes(values, h, size):
    lane = lax.broadcasted_iota(jnp.int32, values.shape, 1) // size
    return jnp.where(lane == h, values, jnp.zeros_like(values))


def hidden_bias(keyc, keyr, rows, cols):
    keys = keyc[pl.ds(rows, TILE), :]
    top = keyr[cols]
    low = top - top % 16
    return jnp.where((keys >= low) & (keys <= top), 0.0, -1e30)


def nothing():
    pass


class Hooks:
    def __init__(self, **table):
        self.start = self.sent = self.need = self.a = self.b = self.c = self.d = self.dw = nothing
        vars(self).update(table)


def modulate_rows(x, scale, shift, hbuf, spread):
    def modulated(at):
        span = pl.ds(at, STEP)
        hat, _ = normed(x[span, :])
        hbuf[span, :] = (hat * (1.0 + scale[span, :]) + shift[span, :]).astype(bf16)

    for c in range(2):
        row_steps(HALF * c, HALF, modulated)
        spread.start(c)


def exchange(refs):
    hbuf, ag_send, ag_recv, parts, out, mid, own, far, rs_send, rs_recv = refs
    sibling, peer = partners()
    spread = Spread(hbuf, ag_send, ag_recv, sibling, peer)
    collect = Collect(parts, out, mid, own, far, rs_send, rs_recv, sibling, peer)
    return hbuf, parts, spread, collect


def attend_segment(
    hooks,
    size,
    x,
    onehot,
    ada,
    qscale,
    keyc,
    keyr,
    weights_in,
    weights,
    saves_out,
    inv_out,
    branch_out,
    mid_out,
    held,
    mods,
    moves,
    refs,
):
    qkv, vt, rates, o_out = held
    gamma, scale, shift = mods
    wqkv, wproj = weights
    hbuf, parts, spread, collect = exchange(refs)
    mover = Moves(moves)
    expand(onehot, ada, (0, 2, 4), (gamma, scale, shift))
    modulate_rows(x, scale, shift, hbuf, spread)
    hooks.need()
    load_qkv = mover.copy(weights_in[0], wqkv)
    load_proj = mover.copy(weights_in[1], wproj)
    load_qkv.wait()
    ones = block_ones(size)

    @pl.loop(0, 4)
    def _(i):
        spread.wait_block(i)
        span = pl.ds(pl.multiple_of(i * TILE, TILE), TILE)
        h = hbuf[span, :]
        for part in range(3):
            columns = slice(part * TILE, (part + 1) * TILE)
            value = mm(h, wqkv[:, columns])
            if part < 2:
                rate = lax.rsqrt(split_mm(mm, value * value, ones) + 1e-06)
                if part == 0:
                    rate = rate * qscale[...]
                rates[span, columns] = rate
                value = value * rate
            else:
                vt[:, span] = value.T.astype(bf16)
            qkv[span, columns] = value.astype(bf16)

    hooks.a()
    saves = [mover.copy(a, b) for a, b in zip((hbuf, qkv, rates), saves_out)]
    load_proj.wait()
    heads = TILE // size

    @pl.loop(0, 4)
    def _(i):
        j = (i + 2) % 4
        span = pl.ds(pl.multiple_of(j * TILE, TILE), TILE)
        queries = [head_lanes(qkv[span, 0:TILE], h, size) for h in range(heads)]
        sums = [jnp.zeros((1, TILE), f32)] * heads
        mixed = [jnp.zeros((size, TILE), f32)] * heads
        for k in range(4):
            keys = qkv[k * TILE : (k + 1) * TILE, TILE : 2 * TILE]
            bias = hidden_bias(keyc, keyr, k * TILE, j)
            for h in range(heads):
                grown = jnp.exp(mm_t(keys, queries[h]) + bias)
                sums[h] = sums[h] + jnp.sum(grown, axis=0, keepdims=True)
                mixed[h] = mixed[h] + mm(
                    vt[h * size : (h + 1) * size, k * TILE : (k + 1) * TILE], grown.astype(bf16)
                )
        inverse = [1.0 / one for one in sums]
        for h in range(heads):
            inv_out[j, h : h + 1, :] = inverse[h]
        whole = jnp.concatenate([mixed[h] * inverse[h] for h in range(heads)], axis=0)
        low = whole.T.astype(bf16)
        o_out[span, :] = low
        for n in range(0, parts.shape[1], TILE):
            parts[span, n : n + TILE] = mm(low, wproj[:, n : n + TILE]).astype(bf16)
        collect.block_done(j)

    hooks.b()
    collect.wait()
    hooks.c()

    def added(at):
        span = pl.ds(at, STEP)
        branch = collect.rows(at)
        branch_out[span, :] = branch
        mid_out[span, :] = x[span, :] + gamma[span, :] * branch

    row_steps(0, TILE, added)
    spread.finish()
    collect.finish()
    for one in saves:
        one.wait()


def mlp_segment(
    hooks, x, onehot, ada, weights_in, weights, saves_out, result_out, x_out, held, mods, moves, refs
):
    hidden, slope = held
    gamma, scale, shift = mods
    wup, wdown = weights
    hbuf, parts, spread, collect = exchange(refs)
    mover = Moves(moves)
    expand(onehot, ada, (1, 3, 5), (gamma, scale, shift))
    modulate_rows(x, scale, shift, hbuf, spread)
    hooks.need()
    loads = [mover.copy(a, b) for a, b in zip(weights_in, weights)]
    for one in loads:
        one.wait()

    @pl.loop(0, 4)
    def _(i):
        spread.wait_block(i)
        for at, hook in ((2, hooks.a), (3, hooks.b)):

            @pl.when(i == at)
            def _():
                hook()

        span = pl.ds(pl.multiple_of(i * TILE, TILE), TILE)
        h = hbuf[span, :]
        for n in range(0, wup.shape[1], TILE):
            columns = slice(n, n + TILE)
            up = mm(h, wup[:, columns])
            square = up * up
            bent = jnp.tanh(0.7978845608 * (up * (1.0 + 0.044715 * square)))
            half = 0.5 * (1.0 + bent)
            hidden[span, columns] = (up * half).astype(bf16)
            inner = 0.7978845608 + (3.0 * 0.044715 * 0.7978845608) * square
            slope[span, columns] = (half + 0.5 * up * (1.0 - bent * bent) * inner).astype(bf16)
        g = hidden[span, :]
        for n in range(0, parts.shape[1], TILE):
            parts[span, n : n + TILE] = mm(g, wdown[:, n : n + TILE]).astype(bf16)
        collect.block_done(i)

    hooks.c()
    saves = [mover.copy(a, b) for a, b in zip((hbuf, hidden, slope), saves_out)]
    collect.wait()

    def added(at):
        span = pl.ds(at, STEP)
        result = collect.rows(at)
        result_out[span, :] = result
        x_out[span, :] = x[span, :] + gamma[span, :] * result

    row_steps(0, TILE, added)
    spread.finish()
    collect.finish()
    for one in saves:
        one.wait()


def item_sums(onehot_t, terms, out):
    for k, term in enumerate(terms):
        width = term.shape[1]
        out[:, k * width : (k + 1) * width] = mm(onehot_t[...], term[...])


def scaled_rows(x, gamma, hbuf, spread):
    def scaled(at):
        span = pl.ds(at, STEP)
        hbuf[span, :] = (gamma[span, :] * x[span, :]).astype(bf16)

    for c in range(2):
        row_steps(HALF * c, HALF, scaled)
        spread.start(c)


def back_rows(collect, x, grad, branch, scale, terms, out):
    dgamma, dscale, dshift = terms

    def added(at):
        span = pl.ds(at, STEP)
        dh = collect.rows(at)
        hat, rate = normed(x[span, :])
        above = grad[span, :]
        dgamma[span, :] = (above * branch[span, :]).astype(bf16)
        dscale[span, :] = (dh * hat).astype(bf16)
        dshift[span, :] = dh.astype(bf16)
        out[span, :] = above + norm_back(dh * (1.0 + scale[span, :]), hat, rate)

    row_steps(0, TILE, added)


def mlp_back_segment(
    hooks, begun, dx, onehot, onehot_t, ada, ins, outs, dmid, items, held, mods, terms, moves, refs
):
    wup_in, wdown_in, h_in, g_in, slope_in, result_in, mid_in = ins
    wup, wdown, hall, gall, slope, dwup, dwdown, result, mid_state = held
    gamma, scale = mods
    hbuf, parts, spread, collect = exchange(refs)
    mover = Moves(moves)
    load_down = mover.copy(wdown_in, wdown)
    load_slope = mover.copy(slope_in, slope)
    load_up = mover.copy(wup_in, wup)
    later = [mover.copy(g_in, gall), mover.copy(h_in, hall)]
    later += [mover.copy(result_in, result), mover.copy(mid_in, mid_state)]
    if not begun:
        expand(onehot, ada, (1, 3), (gamma, scale))
    hooks.start()
    if not begun:
        scaled_rows(dx, gamma, hbuf, spread)
    hooks.sent()
    for one in (load_down, load_slope, load_up):
        one.wait()

    @pl.loop(0, 4)
    def _(i):
        spread.wait_block(i)
        for at, hook in ((2, hooks.a), (3, hooks.b)):

            @pl.when(i == at)
            def _():
                hook()

        span = pl.ds(pl.multiple_of(i * TILE, TILE), TILE)
        dm = hbuf[span, :]
        for n in range(0, slope.shape[1], TILE):
            columns = slice(n, n + TILE)
            dg = mm_t(dm, wdown[columns, :])
            slope[span, columns] = (dg * slope[span, columns].astype(f32)).astype(bf16)
        du = slope[span, :]
        for n in range(0, parts.shape[1], TILE):
            parts[span, n : n + TILE] = mm_t(du, wup[n : n + TILE, :]).astype(bf16)
        collect.block_done(i)

    hooks.c()
    for one in later:
        one.wait()

    @pl.loop(0, gall.shape[1] // TILE)
    def _(k):
        columns = pl.ds(pl.multiple_of(k * TILE, TILE), TILE)
        for n in range(0, hbuf.shape[1], 2 * TILE):
            dwdown[columns, n : n + 2 * TILE] = rows_mm(
                gall[:, columns], hbuf[:, n : n + 2 * TILE]
            ).astype(bf16)

    save_down = mover.copy(dwdown, outs[1])

    @pl.loop(0, hall.shape[1] // TILE)
    def _(k):
        columns = pl.ds(pl.multiple_of(k * TILE, TILE), TILE)
        for n in range(0, slope.shape[1], 2 * TILE):
            dwup[columns, n : n + 2 * TILE] = rows_mm(
                hall[:, columns], slope[:, n : n + 2 * TILE]
            ).astype(bf16)

    save_up = mover.copy(dwup, outs[0])
    save_down.wait()
    save_up.wait()
    hooks.dw()
    collect.wait()
    back_rows(collect, mid_state, dx, result, scale, terms, dmid)
    item_sums(onehot_t, terms, items)
    spread.finish()
    collect.finish()


def attend_back_segment(
    hooks,
    size,
    dmid,
    onehot,
    onehot_t,
    ada,
    qscale,
    keyc,
    keyr,
    inverse,
    ins,
    outs,
    dx,
    items,
    head_out,
    held,
    mods,
    terms,
    moves,
    refs,
):
    wqkv_in, wproj_in, h_in, qkv_in, rate_in, o_in, branch_in, x_in = ins
    wqkv, wproj, hall, qkv, rates, oall, kt, dkeys, dvalues, dqkv, dwqkv, dwproj, branch, x = held
    gamma, scale = mods
    hbuf, parts, spread, collect = exchange(refs)
    mover = Moves(moves)
    loads = [mover.copy(wproj_in, wproj), mover.copy(qkv_in, qkv)]
    loads += [mover.copy(o_in, oall), mover.copy(rate_in, rates)]
    load_w = mover.copy(wqkv_in, wqkv)
    later = [mover.copy(h_in, hall), mover.copy(branch_in, branch)]
    if x_in is not None:
        later.append(mover.copy(x_in, x))
    expand(onehot, ada, (0, 2), (gamma, scale))
    hooks.start()
    scaled_rows(dmid, gamma, hbuf, spread)
    hooks.sent()
    for one in loads:
        one.wait()
    heads = TILE // size
    ones = block_ones(size)
    inv_square = 1.0 / (qscale[...] * qscale[...])
    select = (
        lax.broadcasted_iota(jnp.int32, (8, TILE), 1) // size
        == lax.broadcasted_iota(jnp.int32, (8, TILE), 0)
    ).astype(bf16)
    dkeys[...] = jnp.zeros_like(dkeys)
    dvalues[...] = jnp.zeros_like(dvalues)
    head_out[...] = jnp.zeros_like(head_out)
    for k in range(4):
        rows = slice(k * TILE, (k + 1) * TILE)
        kt[:, rows] = qkv[rows, TILE : 2 * TILE].astype(f32).T.astype(bf16)

    @pl.loop(0, 4)
    def _(i):
        spread.wait_block(i)
        for at, hook in ((2, hooks.a), (3, hooks.b)):

            @pl.when(i == at)
            def _():
                hook()

        span = pl.ds(pl.multiple_of(i * TILE, TILE), TILE)
        dout = mm_t(hbuf[span, :], wproj[...]).astype(bf16)
        product = dout.astype(f32) * oall[span, :].astype(f32)
        row_term = split_mm(lambda a, b: mm_t(b, a), product, select)
        q_low = qkv[span, 0:TILE]
        queries = [head_lanes(q_low, h, size) for h in range(heads)]
        douts = [head_lanes(dout, h, size) for h in range(heads)]
        dquery = [jnp.zeros((size, TILE), f32)] * heads
        for k in range(4):
            rows = slice(k * TILE, (k + 1) * TILE)
            keys = qkv[rows, TILE : 2 * TILE]
            values = qkv[rows, 2 * TILE : 3 * TILE]
            bias = hidden_bias(keyc, keyr, k * TILE, i)
            dkey = jnp.zeros((TILE, TILE), f32)
            dvalue = jnp.zeros((TILE, TILE), f32)
            for h in range(heads):
                share = jnp.exp(mm_t(keys, queries[h]) + bias) * inverse[i, h : h + 1, :]
                dshare = mm_t(values, douts[h])
                dscore = (share * (dshare - row_term[h : h + 1, :])).astype(bf16)
                dvalue = dvalue + mm(share.astype(bf16), douts[h])
                dkey = dkey + mm(dscore, queries[h])
                dquery[h] = dquery[h] + mm(kt[h * size : (h + 1) * size, rows], dscore)
            dkeys[rows, :] += dkey
            dvalues[rows, :] += dvalue
        dq = jnp.concatenate(dquery, axis=0).T
        qhat = q_low.astype(f32)
        along = split_mm(mm, dq * qhat, ones)
        head_out[...] += jnp.sum(along, axis=0, keepdims=True)
        dqkv[span, 0:TILE] = (rates[span, 0:TILE] * (dq - qhat * (along * inv_square))).astype(bf16)

    load_w.wait()
    hooks.c()

    @pl.loop(0, 4)
    def _(i):
        j = (i + 2) % 4
        span = pl.ds(pl.multiple_of(j * TILE, TILE), TILE)
        dk = dkeys[span, :]
        khat = qkv[span, TILE : 2 * TILE].astype(f32)
        along = split_mm(mm, dk * khat, ones)
        dqkv[span, TILE : 2 * TILE] = (
            rates[span, TILE : 2 * TILE] * (dk - khat * along)
        ).astype(bf16)
        dqkv[span, 2 * TILE : 3 * TILE] = dvalues[span, :].astype(bf16)
        low = dqkv[span, :]
        for n in range(0, parts.shape[1], TILE):
            parts[span, n : n + TILE] = mm_t(low, wqkv[n : n + TILE, :]).astype(bf16)
        collect.block_done(j)

    hooks.d()
    for n in range(0, hbuf.shape[1], 2 * TILE):
        dwproj[:, n : n + 2 * TILE] = rows_mm(oall[...], hbuf[:, n : n + 2 * TILE]).astype(bf16)
    save_proj = mover.copy(dwproj, outs[1])
    for one in later:
        one.wait()

    @pl.loop(0, hall.shape[1] // TILE)
    def _(k):
        columns = pl.ds(pl.multiple_of(k * TILE, TILE), TILE)
        dwqkv[columns, :] = rows_mm(hall[:, columns], dqkv[...]).astype(bf16)

    save_w = mover.copy(dwqkv, outs[0])
    save_proj.wait()
    save_w.wait()
    hooks.dw()
    collect.wait()
    back_rows(collect, x, dmid, branch, scale, terms, dx)
    item_sums(onehot_t, terms, items)
    spread.finish()
    collect.finish()


def groups(dps):
    d, b = place()
    side, pairs = d % 2, dps // 2
    pair = d // 2
    ahead = [((pair + k) % pairs) * 2 + side for k in range(pairs)]
    behind = [((pair - k + pairs) % pairs) * 2 + side for k in range(pairs)]
    return d, b, d + 1 - 2 * side, ahead, behind


class DpGather:
    def __init__(self):
        self.dps = sizes()[0]

    def bind(self, ins, outs, scratch):
        send, recv, local = scratch
        d, b, other, ahead, behind = groups(self.dps)
        pairs = self.dps // 2
        self.partners = [(other, b)] + [(t, b) for t in ahead[1:]]
        self.first, self.direct, self.forward, self.local = [], [], [], []
        for a, (src, dst) in enumerate(zip(ins, outs)):
            self.local.append(pltpu.make_async_copy(src, dst.at[d], local.at[a]))
            self.first.append(remote(src, dst.at[d], send.at[a, 0], recv.at[a, 0], (other, b)))
            self.direct.append([None])
            self.forward.append([None])
            for k in range(1, pairs):
                self.direct[a].append(
                    remote(src, dst.at[d], send.at[a, k], recv.at[a, k], (ahead[k], b))
                )
                at = pairs + k
                self.forward[a].append(
                    remote(
                        dst.at[behind[k]], dst.at[behind[k]], send.at[a, at], recv.at[a, at], (other, b)
                    )
                )
        self.order = [(k, a) for k in range(1, pairs) for a in range(len(ins))]

    def start_far(self):
        for k, a in self.order:
            self.direct[a][k].start()
        for one in self.local:
            one.start()

    def start_near(self):
        for one in self.first:
            one.start()

    def step(self, hook, hooks=3):
        low, high = (len(self.order) * hook) // hooks, (len(self.order) * (hook + 1)) // hooks
        for k, a in self.order[low:high]:
            self.direct[a][k].wait_recv()
            self.forward[a][k].start()

    def finish(self):
        for one in self.local:
            one.wait()
        for one in self.first:
            one.wait()
        for k, a in self.order:
            self.direct[a][k].wait_send()
            self.forward[a][k].wait()


class DpScatter:
    def __init__(self):
        self.dps = sizes()[0]

    def bind(self, ins, outs, scratch):
        d, b, other, ahead, behind = groups(self.dps)
        pairs = self.dps // 2
        self.partners = [(other, b)] + [(t, b) for t in ahead[1:]]
        self.results = outs
        self.bufs, self.local, self.cross, self.direct = [], [], [], []
        for a, src in enumerate(ins):
            mine, near, far, send, recv, local = scratch[6 * a : 6 * a + 6]
            self.bufs.append((mine, near, far))
            self.local.append([])
            self.cross.append([])
            self.direct.append([None])
            for k in range(pairs):
                target = ahead[k]
                theirs = target + 1 - 2 * (target % 2)
                self.local[a].append(
                    pltpu.make_async_copy(src.at[target], mine.at[k], local.at[k])
                )
                self.cross[a].append(
                    remote(src.at[theirs], near.at[k], send.at[k], recv.at[k], (other, b))
                )
                if k:
                    at = pairs + k
                    self.direct[a].append(
                        remote(mine.at[k], far.at[k], send.at[at], recv.at[at], (target, b))
                    )
        self.order = [(k, a) for k in range(1, pairs) for a in range(len(ins))]
        self.last = [(0, a) for a in range(len(ins))]

    def start(self):
        for k, a in self.order + self.last:
            self.cross[a][k].start()
            self.local[a][k].start()

    def add(self, a, k):
        self.local[a][k].wait()
        self.cross[a][k].wait_recv()
        mine, near, _ = self.bufs[a]
        rows = mine.shape[1]
        step = min(rows, STEP)

        @pl.loop(0, rows // step)
        def _(s):
            span = pl.ds(pl.multiple_of(s * step, step), step)
            total = mine[k, span, :].astype(f32) + near[k, span, :].astype(f32)
            mine[k, span, :] = total.astype(bf16)

    def step(self, hook, hooks=3):
        low, high = (len(self.order) * hook) // hooks, (len(self.order) * (hook + 1)) // hooks
        for k, a in self.order[low:high]:
            self.add(a, k)
            self.direct[a][k].start()

    def own(self):
        for k, a in self.last:
            self.add(a, k)
        for k, a in self.order + self.last:
            self.cross[a][k].wait_send()

    def finish(self):
        for k, a in self.order:
            self.direct[a][k].wait()
        for a, result in enumerate(self.results):
            mine, _, far = self.bufs[a]
            step = result.shape[1] if len(result.shape) == 3 else min(mine.shape[1], STEP)

            @pl.loop(0, mine.shape[1] // step)
            def _(s):
                span = pl.ds(pl.multiple_of(s * step, step), step)
                total = mine[0, span, :].astype(f32)
                for k in range(1, self.dps // 2):
                    total = total + far[k, span, :].astype(f32)
                if len(result.shape) == 3:
                    result[s] = total.astype(result.dtype)
                else:
                    result[span, :] = total.astype(result.dtype)

    def release(self, credit):
        for other in self.partners:
            pl.semaphore_signal(credit, inc=1, device_id=other, device_id_type=MESH)

    def acquire(self, credit):
        pl.semaphore_wait(credit, len(self.partners))


class Items:
    def __init__(self, src, out, scratch):
        self.terms, self.held, send, recv, dp_send, dp_recv = scratch
        dps = sizes()[0]
        d, b = place()
        self.here, self.out = (d, b), out
        wide = self.held.shape[2]

        def quarter(i):
            return src.at[:, pl.ds(pl.multiple_of(i * wide, 128), wide)]

        self.first = [pltpu.make_async_copy(quarter(b), self.terms.at[0], send.at[0])]
        for k in range(1, 4):
            to = (b + k) % 4
            self.first.append(
                remote(quarter(to), self.terms.at[k], send.at[k], recv.at[k], (d, to))
            )
        self.over = [
            remote(self.held.at[0], out.at[b, d], dp_send.at[k], dp_recv.at[k], ((d + k) % dps, b))
            for k in range(1, dps)
        ]
        self.keep = pltpu.make_async_copy(self.held.at[0], out.at[b, d], send.at[7])
        self.share = Share(out, send.at[pl.ds(4, 3)], recv.at[pl.ds(4, 3)])

    def start(self):
        for one in self.first:
            one.start()

    def sum(self):
        d, b = self.here
        for one in self.first:
            one.wait()
        total = (self.terms[0] + self.terms[1]) + (self.terms[2] + self.terms[3])
        low = total.astype(bf16)
        self.held[0] = low
        for one in self.over + [self.keep]:
            one.start()

    def spread(self):
        for one in self.over + [self.keep]:
            one.wait()
        self.share.start()

    def forward(self):
        self.share.forward()

    def finish(self):
        self.share.finish()


class Permute:
    def __init__(self, src, dst, send, recv, back):
        dps, blks = sizes()
        d, b = place()
        owner, user = d * blks + b, b * dps + d
        self.moves = owner != user
        to = (user // blks, user % blks) if back else (owner % dps, owner // dps)
        self.away = remote(src, dst, send, recv, to)
        self.stay = pltpu.make_async_copy(src, dst, send)

    def start(self):
        @pl.when(self.moves)
        def _():
            self.away.start()

        @pl.when(jnp.logical_not(self.moves))
        def _():
            self.stay.start()

    def finish(self):
        @pl.when(self.moves)
        def _():
            self.away.wait()

        @pl.when(jnp.logical_not(self.moves))
        def _():
            self.stay.wait()


def modulations_start(rows_in, ada_in, rows_out, columns, sems):
    dp_send, dp_recv, ada_send, ada_recv, local = sems
    dps, blks = sizes()
    count = dps * blks
    d, b = place()
    me = d * blks + b
    rows = ada_in.shape[1]
    span = pl.ds(pl.multiple_of(me * rows, rows), rows)
    sends = [
        pltpu.make_async_copy(rows_in, rows_out.at[d], local.at[0]),
        pltpu.make_async_copy(ada_in.at[me], columns.at[span], local.at[1]),
    ]
    for k in range(1, dps):
        to = ((d + k) % dps, b)
        sends.append(remote(rows_in, rows_out.at[d], dp_send.at[k], dp_recv.at[k], to))
    for k in range(1, count):
        t = (me + k) % count
        to = (t // blks, t % blks)
        sends.append(remote(ada_in.at[t], columns.at[span], ada_send.at[k], ada_recv.at[k], to))
    for one in sends:
        one.start()
    return sends


def modulations_answer(rows_out, columns, answers, quarters, sems):
    send, recv = sems
    dps = sizes()[0]
    d, b = place()
    slots, wide = answers.shape[1:]
    value = rows_out[...].astype(f32)
    value = (value / (1.0 + jnp.exp(-value))).astype(bf16)
    whole = mm(value.reshape(dps * slots, rows_out.shape[2]), columns[...])
    answers[...] = whole.reshape(dps, slots, wide)
    replies = []
    for k in range(1, dps):
        to = (d + k) % dps
        replies.append(
            remote(answers.at[to], quarters.at[b, d], send.at[k], recv.at[k], (to, b))
        )
    for one in replies:
        one.start()
    quarters[b, d] = answers[d]
    return replies


class Share:
    def __init__(self, buf, send, recv):
        d, b = place()
        sibling, peer = partners()
        far = peer[1]
        self.moves = [
            remote(buf.at[b], buf.at[b], send.at[0], recv.at[0], peer),
            remote(buf.at[b], buf.at[b], send.at[1], recv.at[1], sibling),
            remote(buf.at[far], buf.at[far], send.at[2], recv.at[2], sibling),
        ]

    def start(self):
        self.moves[0].start()
        self.moves[1].start()

    def forward(self):
        self.moves[0].wait_recv()
        self.moves[2].start()

    def finish(self):
        self.moves[1].wait_recv()
        self.moves[2].wait_recv()
        for one in self.moves:
            one.wait_send()


class PieceSwap:
    def __init__(self, pairs, send, recv):
        d, b = place()
        self.sent = []
        for a, (src, dst) in enumerate(pairs):
            self.sent.append(pltpu.make_async_copy(src.at[b], dst.at[b], send.at[a, 0]))
            for k in range(1, 4):
                to = (b + k) % 4
                self.sent.append(
                    remote(src.at[to], dst.at[b], send.at[a, k], recv.at[a, k], (d, to))
                )

    def start(self):
        for one in self.sent:
            one.start()

    def finish(self):
        for one in self.sent:
            one.wait()


def flat(value):
    return [leaf for one in value for leaf in flat(one)] if isinstance(value, list) else [value]


def refill(value, leaves):
    return [refill(one, leaves) for one in value] if isinstance(value, list) else next(leaves)


class Names:
    def __init__(self):
        self.ins, self.outs, self.scratch = SimpleNamespace(), SimpleNamespace(), SimpleNamespace()

    def call(self, kernel, ident, vmem):
        ins, outs, scratch = (flat(list(vars(one).values())) for one in (self.ins, self.outs, self.scratch))

        def fill(bags, refs):
            leaves, found = iter(refs), SimpleNamespace()
            for bag in bags:
                for name, value in vars(bag).items():
                    vars(found)[name] = refill(value, leaves)
            return found

        results = pl.pallas_call(
            lambda *refs: kernel(fill((self.ins, self.outs, self.scratch), refs)),
            out_shape=[one for one, _ in outs],
            in_specs=[where for _, where in ins],
            out_specs=[where for _, where in outs],
            scratch_shapes=scratch,
            compiler_params=pltpu.CompilerParams(
                collective_id=ident, has_side_effects=True, vmem_limit_bytes=vmem * 2**20
            ),
            cost_estimate=pl.CostEstimate(flops=2**36, bytes_accessed=2**26, transcendentals=0),
        )(*[one for one, _ in ins])
        return fill((self.outs,), results)


def add_exchanges(names, width):
    names.scratch.spreads = [spread_scratch(width) for _ in range(2)]
    names.scratch.parts, names.scratch.out = collect_scratch(width)[:2]
    names.scratch.collects = [collect_scratch(width)[2:] for _ in range(2)]


def exchange_set(r, turn):
    return r.spreads[turn] + [r.parts, r.out] + r.collects[turn]


def whole_kernel(lead, layers, size, r):
    wide = 3 * TILE
    r.wqkv, r.wproj = r.wup.at[:, 0:wide], r.wdown.at[0:TILE]
    r.qkv_buf, r.o_buf = r.gall.at[:, 0:wide], r.gall.at[:, wide : wide + TILE]
    r.vt, r.rate_buf = r.dwdown.at[TILE : 2 * TILE], r.rates_buf
    r.hidden, r.slope_buf = r.dwup, r.du
    r.state, r.middle, r.branch_buf, r.result_buf = r.grad, r.dmid, r.load_a, r.load_b
    if lead:
        r.columns = r.hall.at[:, 0 : r.ada_in.shape[2]]
    forward_part(lead, layers, size, r)
    backward_part(layers, size, r)


def forward_part(lead, layers, size, r):
    dps, blks = sizes()
    d, b = place()
    sibling, peer = partners()
    ada = r.ada
    qkv_shard = r.qkv_shard if lead else [r.qkv_first] + r.qkv_shard
    up_shard = r.up_shard if lead else [r.up_first] + r.up_shard
    gathers = []
    for layer in range(layers):
        first = [qkv_shard[layer], r.proj_shard.at[layer]]
        second = [up_shard[layer], r.w_down.at[layer]]
        for part, (srcs, dsts) in enumerate(((first, (r.wq, r.wp)), (second, (r.wu, r.wd)))):
            job = DpGather()
            job.bind(srcs, [one[layer] for one in dsts], r.gather_sems[2 * layer + part])
            gathers.append(job)
    arrived = greet_all()
    r.state[...] = r.tokens[...].astype(f32)
    r.message[...] = jnp.zeros_like(r.message)
    arrived()
    swaps = [
        PieceSwap(
            [(r.qkv_cols[n], r.qkv_shard[n]), (r.up_cols[n], r.up_shard[n])],
            r.swap_send[n],
            r.swap_recv[n],
        )
        for n in range(len(r.qkv_cols))
    ]
    if lead:
        permutes = [
            Permute(
                r.w_proj.at[n], r.proj_shard.at[n], r.permute_send.at[n], r.permute_recv.at[n], False
            )
            for n in range(layers)
        ]
        permutes[0].start()
        swaps[0].start()
        moves = modulations_start(
            r.rows_in,
            r.ada_in,
            r.rows,
            r.columns,
            (r.dp_send, r.dp_recv, r.ada_send, r.ada_recv, r.ada_local),
        )
        swaps[0].finish()
        permutes[0].finish()
        gathers[0].start_far()
        gathers[0].start_near()
        for one in moves:
            one.wait()
        replies = modulations_answer(
            r.rows, r.columns, r.answers, r.quarters, (r.answer_send, r.answer_recv)
        )
        for one in permutes[1:]:
            one.start()
        share = Share(r.quarters, r.share_send, r.share_recv)
        for one in replies:
            one.wait()
        share.start()
        share.forward()
        gathers[0].step(0)
        share.finish()
        slots = r.answers.shape[1]
        wide = r.answers.shape[2]
        each = ada.shape[2]
        for i in range(dps * blks):
            value = r.quarters[i % blks, i // blks]
            layer, at = (i * wide) // each, (i * wide) % each
            high = value.astype(bf16)
            ada[layer, 0:slots, at : at + wide] = high
            ada[layer, slots : 2 * slots, at : at + wide] = (value - high.astype(f32)).astype(bf16)
    else:
        gathers[0].start_far()
        gathers[0].start_near()
        gathers[0].step(0)
    gathers[1].start_far()
    for one in swaps[-(layers - 1) :]:
        one.start()

    def need_first(layer):
        job, following = gathers[2 * layer], gathers[2 * layer + 1]
        if layer == 0:
            job.step(1)
            job.step(2)
        following.start_near()
        job.finish()

    def early(layer):
        if layer == 0:
            for one in swaps[-(layers - 1) :]:
                one.finish()
            if lead:
                for one in permutes[1:]:
                    one.finish()
            for one in gathers[2:]:
                one.start_far()
        else:
            gathers[2 * layer + 1].step(0)

    def middle(layer):
        gathers[2 * layer + 1].step(0 if layer == 0 else 1)

    def late(layer):
        gathers[2 * layer + 1].step(1 if layer == 0 else 2)

    def need_second(layer):
        if layer == 0:
            gathers[1].step(2)
        if layer + 1 < layers:
            gathers[2 * layer + 2].start_near()
        gathers[2 * layer + 1].finish()

    def weights(ref, rows):
        return ref.reshape(rows, ref.shape[-1])

    def begin_back():
        hbuf, _, spread, _ = exchange(exchange_set(r, 0))
        r.grad[...] = r.cotangent[...].astype(f32)
        scaled_rows(r.grad, r.gamma, hbuf, spread)

    pending = []
    saver = Moves(r.save_sems)
    width = r.state.shape[1]
    for layer in range(layers):
        last = layer + 1 == layers
        attend_segment(
            Hooks(
                need=partial(need_first, layer),
                a=partial(early, layer),
                b=partial(middle, layer),
                c=partial(late, layer),
            ),
            size,
            r.state,
            r.onehot,
            ada.at[layer],
            r.qscale.at[layer],
            r.keyc,
            r.keyr,
            (weights(r.wq[layer], width), weights(r.wp[layer], width // 4)),
            (r.wqkv, r.wproj),
            (r.h.at[layer], r.qkv.at[layer], r.rates.at[layer]),
            r.inverse.at[layer],
            r.branch_buf,
            r.middle,
            (r.qkv_buf, r.vt, r.rate_buf, r.o_buf),
            (r.gamma, r.scale, r.shift),
            r.moves.at[2 * layer],
            exchange_set(r, 0),
        )
        for one in pending:
            one.wait()
        pending = [
            saver.copy(r.o_buf, r.o.at[layer]),
            saver.copy(r.branch_buf, r.branch.at[layer]),
            saver.copy(r.middle, r.mids.at[layer]),
        ]
        hooks = Hooks(need=partial(need_second, layer))
        if last:
            hooks.c = begin_back
        else:
            hooks.a, hooks.b, hooks.c = [partial(gathers[2 * layer + 2].step, i) for i in range(3)]
        mlp_segment(
            hooks,
            r.middle,
            r.onehot,
            ada.at[layer],
            (weights(r.wu[layer], width), weights(r.wd[layer], width)),
            (r.wup, r.wdown),
            (r.h2.at[layer], r.g.at[layer], r.slope.at[layer]),
            r.result_buf,
            r.shift if last else r.state,
            (r.hidden, r.slope_buf),
            (r.gamma, r.scale, r.shift),
            r.moves.at[2 * layer + 1],
            exchange_set(r, 1),
        )
        for one in pending:
            one.wait()
        pending = [saver.copy(r.result_buf, r.result.at[layer])]
        if not last:
            pending.append(saver.copy(r.state, r.states.at[layer]))
    r.output[...] = r.shift[...].astype(bf16)
    for one in pending:
        one.wait()


def declare_forward(n, tokens, onehot, keyc, keyr, qscale, w_down, proj, qkv_cols, up_cols, rows_in, ada_in, ada, qkv_shard, up_shard):
    lead = ada_in is not None
    dps, blks = sizes()
    count = dps * blks
    rows, width = tokens.shape
    layers = proj.shape[0]
    length = rows * blks
    wide, ff = qkv_cols[0].shape[2], up_cols[0].shape[2]
    sems = pltpu.SemaphoreType.DMA
    vars(n.ins).update(
        tokens=(tokens, VMEM), onehot=(onehot, VMEM), keyc=(keyc, VMEM), keyr=(keyr, VMEM), qscale=(qscale, VMEM)
    )
    n.ins.w_down = (w_down, ANY)
    low = partial(shaped, dtype=bf16)
    if lead:
        vars(n.ins).update(rows_in=(rows_in, ANY), ada_in=(ada_in, ANY), w_proj=(proj, ANY))
        slots = rows_in.shape[0]
        columns = ada_in.shape[2]
        vars(n.outs).update(
            rows=(low(dps, slots, width), VMEM),
            proj_shard=(low(*proj.shape), ANY),
        )
        vars(n.scratch).update(
            ada=pltpu.VMEM((layers, 2 * slots, count * columns // layers), bf16),
            answers=pltpu.VMEM((dps, slots, columns), f32),
            quarters=pltpu.VMEM((blks, dps, slots, columns), f32),
            dp_send=sems((dps,)),
            dp_recv=sems((dps,)),
            answer_send=sems((dps,)),
            answer_recv=sems((dps,)),
            ada_send=sems((count,)),
            ada_recv=sems((count,)),
            ada_local=sems((2,)),
            share_send=sems((3,)),
            share_recv=sems((3,)),
            permute_send=sems((layers,)),
            permute_recv=sems((layers,)),
        )
    else:
        vars(n.ins).update(
            ada=(ada, VMEM), rows=(rows_in, VMEM), proj_shard=(proj, ANY), qkv_first=(qkv_shard, ANY), up_first=(up_shard, ANY)
        )
    moved_qkv, moved_up = (one if lead else one[1:] for one in (qkv_cols, up_cols))
    n.ins.qkv_cols = [(one, ANY) for one in moved_qkv]
    n.ins.up_cols = [(one, ANY) for one in moved_up]
    n.outs.qkv_shard = [(low(*one.shape), ANY) for one in moved_qkv]
    n.outs.up_shard = [(low(*one.shape), ANY) for one in moved_up]
    n.scratch.swap_send = [sems((2, 4)) for _ in moved_qkv]
    n.scratch.swap_recv = [sems((2, 4)) for _ in moved_qkv]
    n.outs.wq = [(low(dps, *one.shape), ANY) for one in qkv_cols]
    n.outs.wp = [(low(dps, *proj.shape[1:]), ANY)] * layers
    n.outs.wu = [(low(dps, *one.shape), ANY) for one in up_cols]
    n.outs.wd = [(low(dps, *w_down.shape[1:]), ANY)] * layers
    n.scratch.gather_sems = [[sems((2, dps)), sems((2, dps)), sems((2,))] for _ in range(2 * layers)]
    vars(n.outs).update(
        output=(low(rows, width), VMEM),
        h=(low(layers, length, width), ANY),
        qkv=(low(layers, length, wide), ANY),
        rates=(shaped(layers, length, 2 * TILE), ANY),
        o=(low(layers, length, TILE), ANY),
        branch=(shaped(layers, rows, width), ANY),
        mids=(shaped(layers, rows, width), ANY),
        h2=(low(layers, length, width), ANY),
        g=(low(layers, length, ff), ANY),
        slope=(low(layers, length, ff), ANY),
        result=(shaped(layers, rows, width), ANY),
        states=(shaped(layers, rows, width), ANY),
    )
    vars(n.scratch).update(
        shift=pltpu.VMEM((rows, width), f32),
        inverse=pltpu.VMEM((layers, 4, 8, TILE), f32),
        moves=sems((2 * layers, 5)),
        save_sems=sems((5 * layers,)),
    )
    return n


def backward_part(layers, size, r):
    dps, blks = sizes()
    d, b = place()
    width = r.grad.shape[1]
    rows = r.w_ada.shape[1]
    people = r.cond.shape[1]
    value = r.rows[...].astype(f32)
    value = (value / (1.0 + jnp.exp(-value))).astype(bf16).reshape(people, width)
    line = lax.broadcasted_iota(jnp.int32, (rows, width), 0) + flat_place() * rows
    own_columns = (line == lax.broadcasted_iota(jnp.int32, (rows, width), 1)).astype(bf16)
    r.cond[...] = mm_t(own_columns, value).astype(bf16)

    wides, narrows, swaps, permutes, items = {}, {}, {}, {}, {}
    r.dadas = r.near_dada + r.far_dadas
    for n in range(layers):
        wides[n], narrows[n] = DpScatter(), DpScatter()
        shared = r.wide
        wides[n].bind([r.dwu[n], r.dwd[n]], [r.up_sum[n], r.down_grad.at[n]], shared)
        shared = r.narrow
        narrows[n].bind([r.dwq[n], r.dwp[n]], [r.qkv_sum[n], r.proj_sum[n]], shared)
        for k, (src, dst) in enumerate(((r.up_sum, r.up_grad), (r.qkv_sum, r.qkv_grad))):
            swaps[k, n] = PieceSwap(
                [(src[n], dst.at[n])], r.back_swap_send.at[2 * n + k], r.back_swap_recv.at[2 * n + k]
            )
        permutes[n] = Permute(
            r.proj_sum[n], r.proj_grad.at[n], r.back_permute_send.at[n], r.back_permute_recv.at[n], True
        )
        for part in range(2):
            at = 2 * n + part
            items[n, part] = Items(r.items[at], r.dadas[at], r.items_scratch[at])

    def fold(layer, part):
        dada = r.dadas[2 * layer + part]
        if layer or part or not r.near_dada:
            load = pltpu.make_async_copy(dada, r.dada, r.dada_sem)
            load.start()
            load.wait()
            dada = r.dada
        quarter = dada.shape[3]
        total = r.message[0:rows, :]
        for c in range(0, 3 * width, TILE):
            at = (c // width) * 2 * width + part * width + c % width
            inner = c % quarter
            value = dada[c // quarter, :, :, inner : inner + TILE].reshape(people, TILE)
            r.ada_grad[layer, :, at : at + TILE] = mm(r.cond[...], value)
            total = total + mm_t(r.w_ada[layer, :, at : at + TILE], value)
        r.message[0:rows, :] = total

    def wide_done(n):
        wides[n].finish()
        swaps[0, n].start()
        if n:
            wides[n].release(r.credit.at[0])

    def narrow_done(n):
        narrows[n].finish()
        swaps[1, n].start()
        permutes[n].start()
        if n:
            narrows[n].release(r.credit.at[1])

    def weights(ref, count):
        return ref.reshape(count, ref.shape[-1])

    wide = 3 * TILE
    length = 4 * TILE
    for layer in reversed(range(layers)):
        top = layer + 1 == layers
        above = layer + 1

        def begin_mlp():
            if not top:
                items[above, 0].start()

        def late_mlp():
            if not top:
                narrows[above].step(2)
                items[above, 1].spread()
                items[above, 0].sum()

        def done_mlp():
            if not top:
                wide_done(above)
                wides[layer].acquire(r.credit.at[0])
            wides[layer].start()

        hooks = Hooks(start=begin_mlp, c=late_mlp, dw=done_mlp)
        if not top:
            hooks.sent = wides[above].own
            hooks.a, hooks.b = [partial(narrows[above].step, i) for i in range(2)]
        ff = r.slope.shape[2]
        mlp_back_segment(
            hooks,
            top,
            r.grad,
            r.onehot,
            r.onehot_t,
            r.ada.at[layer],
            (
                weights(r.wu[layer], width),
                weights(r.wd[layer], ff),
                r.h2.at[layer],
                r.g.at[layer],
                r.slope.at[layer],
                r.result.at[layer],
                r.mids.at[layer],
            ),
            (weights(r.dwu[layer], width), weights(r.dwd[layer], ff)),
            r.dmid,
            r.items[2 * layer + 1],
            (r.wup, r.wdown, r.hall, r.gall, r.du, r.dwup, r.dwdown, r.load_a, r.load_b),
            (r.gamma, r.scale),
            (r.dgamma, r.dscale, r.dshift),
            r.back_moves.at[2 * layer],
            exchange_set(r, 0),
        )

        def begin_attend():
            items[layer, 1].start()

        def sent_attend():
            if not top:
                narrows[above].own()

        def second_attend():
            wides[layer].step(1)
            if not top:
                narrow_done(above)

        def late_attend():
            wides[layer].step(2)
            items[layer, 1].sum()
            if not top:
                items[above, 1].forward()
                items[above, 0].spread()

        def done_attend():
            if not top:
                narrows[layer].acquire(r.credit.at[1])
            narrows[layer].start()
            if not top:
                items[above, 1].finish()
                fold(above, 1)

        attend_back_segment(
            Hooks(
                start=begin_attend,
                sent=sent_attend,
                a=partial(wides[layer].step, 0),
                b=second_attend,
                d=late_attend,
                dw=done_attend,
            ),
            size,
            r.dmid,
            r.onehot,
            r.onehot_t,
            r.ada.at[layer],
            r.qscale.at[layer],
            r.keyc,
            r.keyr,
            r.inverse.at[layer],
            (
                weights(r.wq[layer], width),
                weights(r.wp[layer], TILE),
                r.h.at[layer],
                r.qkv.at[layer],
                r.rates.at[layer],
                r.o.at[layer],
                r.branch.at[layer],
                r.states.at[layer - 1] if layer else None,
            ),
            (weights(r.dwq[layer], width), weights(r.dwp[layer], TILE)),
            r.grad,
            r.items[2 * layer],
            r.heads.at[layer],
            (
                r.wup.at[:, 0:wide],
                r.wdown.at[0:TILE],
                r.hall,
                r.gall.at[:, 0:wide],
                r.rates_buf,
                r.gall.at[:, wide : wide + TILE],
                r.dwdown.at[TILE : 2 * TILE],
                r.dkeys,
                r.dvalues,
                r.du.at[:, 0:wide],
                r.dwup.at[:, 0:wide],
                r.dwdown.at[0:TILE],
                r.load_a,
                r.load_b if layer else r.tokens,
            ),
            (r.gamma, r.scale),
            (r.dgamma, r.dscale, r.dshift),
            r.back_moves.at[2 * layer + 1],
            exchange_set(r, 1),
        )
    items[0, 0].start()
    r.tokens_grad[...] = r.grad[...].astype(bf16)
    items[1, 0].forward()
    items[0, 0].sum()
    wides[0].own()
    items[1, 0].finish()
    narrows[0].step(0)
    fold(1, 0)
    items[0, 1].spread()
    narrows[0].step(1)
    items[0, 1].forward()
    narrows[0].step(2)
    items[0, 1].finish()
    fold(0, 1)
    items[0, 0].spread()
    items[0, 0].forward()
    narrows[0].own()
    items[0, 0].finish()
    fold(0, 0)
    message = r.message
    message[rows:, :] = r.notes[...]
    lane = lax.broadcasted_iota(jnp.int32, (TILE, people), 0)
    pick = (lane == lax.broadcasted_iota(jnp.int32, (TILE, people), 1) * size).astype(bf16)
    for layer in range(layers):
        message[rows + layer : rows + layer + 1, :] = split_three(r.heads[layer], pick)
    told = [
        remote(message, r.heard.at[b, d], r.told_send.at[k], r.told_recv.at[k], ((d + k) % dps, b))
        for k in range(1, dps)
    ]
    told.append(pltpu.make_async_copy(message, r.heard.at[b, d], r.told_send.at[0]))
    for one in told:
        one.start()
    wide_done(0)
    for one in told:
        one.wait()
    share = Share(r.heard, r.back_share_send, r.back_share_recv)
    share.start()
    share.forward()
    narrow_done(0)
    share.finish()
    for one in list(swaps.values()) + list(permutes.values()):
        one.finish()


def split_three(values, ones):
    high = values.astype(bf16)
    rest = values - high.astype(f32)
    low = rest.astype(bf16)
    least = (rest - low.astype(f32)).astype(bf16)
    return mm(high, ones) + (mm(low, ones) + mm(least, ones))


def declare_backward(n, layers, cotangent, w_ada, onehot_t, notes, wide, ff):
    dps, blks = sizes()
    rows, width = cotangent.shape
    length = rows * blks
    wrows = w_ada.shape[1]
    slots, people = onehot_t.shape[0], notes.shape[1]
    sems = pltpu.SemaphoreType.DMA
    low = partial(shaped, dtype=bf16)
    vars(n.ins).update(
        cotangent=(cotangent, VMEM), w_ada=(w_ada, VMEM), onehot_t=(onehot_t, VMEM), notes=(notes, VMEM)
    )
    pairs = dps // 2

    def scatter_scratch(shapes):
        found = []
        for shape in shapes:
            found += [pltpu.VMEM((pairs, *shape), bf16)] * 3
            found += [sems((2 * pairs,)), sems((2 * pairs,)), sems((pairs,))]
        return found

    quarter = 3 * width // 4
    whole = (4, dps, slots, quarter)
    sets = 2 * layers
    n.outs.dwu = [(low(dps, blks * wrows, ff), ANY)] * layers
    n.outs.dwd = [(low(dps, ff // dps, width), ANY)] * layers
    n.outs.dwq = [(low(dps, blks * wrows, wide), ANY)] * layers
    n.outs.dwp = [(low(dps, TILE // dps, width), ANY)] * layers
    near = [pltpu.VMEM(whole, bf16)] if people <= 128 else []
    n.outs.far_dadas = [(low(*whole), ANY)] * (sets - len(near))
    n.scratch.near_dada = near
    n.scratch.dada = pltpu.VMEM(whole, bf16)
    n.scratch.dada_sem = sems
    n.scratch.up_sum = [pltpu.VMEM((blks, wrows, ff), bf16)] * layers
    n.scratch.qkv_sum = [pltpu.VMEM((blks, wrows, wide), bf16)] * layers
    n.scratch.proj_sum = [pltpu.VMEM((TILE // dps, width), f32)] * layers
    n.scratch.items = [pltpu.VMEM((slots, 3 * width), f32)] * sets
    n.scratch.items_scratch = [
        [
            pltpu.VMEM((4, slots, quarter), f32),
            pltpu.VMEM((1, slots, quarter), bf16),
            sems((8,)),
            sems((7,)),
            sems((dps,)),
            sems((dps,)),
        ]
    ] * sets
    n.scratch.wide = scatter_scratch([(blks * wrows, ff), (ff // dps, width)])
    n.scratch.narrow = scatter_scratch([(blks * wrows, wide), (TILE // dps, width)])
    vars(n.outs).update(
        tokens_grad=(low(rows, width), VMEM),
        ada_grad=(shaped(layers, wrows, 6 * width), VMEM),
        up_grad=(low(layers, blks, wrows, ff), ANY),
        qkv_grad=(low(layers, blks, wrows, wide), ANY),
        proj_grad=(shaped(layers, TILE // dps, width), ANY),
        down_grad=(shaped(layers, ff // dps, width), VMEM),
        heard=(shaped(blks, dps, wrows + 8, people), ANY),
    )
    big, small = pltpu.VMEM((rows, width), f32), pltpu.VMEM((rows, width), bf16)
    vars(n.scratch).update(
        grad=big,
        dmid=big,
        load_a=big,
        load_b=big,
        gamma=big,
        scale=big,
        dgamma=small,
        dscale=small,
        dshift=small,
        wup=pltpu.VMEM((width, ff), bf16),
        wdown=pltpu.VMEM((ff, width), bf16),
        hall=pltpu.VMEM((length, width), bf16),
        gall=pltpu.VMEM((length, ff), bf16),
        du=pltpu.VMEM((length, ff), bf16),
        dwup=pltpu.VMEM((width, ff), bf16),
        dwdown=pltpu.VMEM((ff, width), bf16),
        rates_buf=pltpu.VMEM((length, 2 * TILE), f32),
        dkeys=pltpu.VMEM((length, TILE), f32),
        dvalues=pltpu.VMEM((length, TILE), f32),
        heads=pltpu.VMEM((layers, 1, TILE), f32),
        message=pltpu.VMEM((wrows + 8, people), f32),
        cond=pltpu.VMEM((wrows, people), bf16),
        back_moves=sems((2 * layers, 10)),
        credit=pltpu.SemaphoreType.REGULAR((2,)),
        back_permute_send=sems((layers,)),
        back_permute_recv=sems((layers,)),
        told_send=sems((dps,)),
        told_recv=sems((dps,)),
        back_share_send=sems((3,)),
        back_share_recv=sems((3,)),
    )
    n.scratch.back_swap_send = sems((2 * layers, 1, 4))
    n.scratch.back_swap_recv = sems((2 * layers, 1, 4))
    add_exchanges(n, width)


ANY = pl.BlockSpec(memory_space=pl.ANY)
VMEM = pl.BlockSpec(memory_space=pltpu.VMEM)


def shaped(*shape, dtype=f32):
    return jax.ShapeDtypeStruct(shape, dtype)


def per_device(
    tokens,
    cotangent,
    stop_scale,
    labels,
    class_table,
    head_scale,
    w_qkv,
    w_proj,
    w_up,
    w_down,
    w_ada,
):
    rows, width = tokens.shape[1:]
    layers, heads = head_scale.shape
    size = width // heads
    dps, blks = sizes()
    count = dps * blks
    length = rows * blks
    d, b = place()
    own_heads = heads // blks
    piece = own_heads * size
    wrows = w_qkv.shape[1]
    ffrows = w_down.shape[1]
    ff = ffrows * dps
    slots = labels.shape[1]
    padded = 16

    item_all, level_all = token_meta(stop_scale[0], length)
    item_own = lax.dynamic_slice_in_dim(item_all, b * rows, rows)
    key = (item_all * 16 + level_all).reshape(blks, rows)
    sib = b + 1 - 2 * (b % 2)
    far, far_sib = (b + 2) % 4, (sib + 2) % 4
    key = jnp.concatenate(
        [key[b], key[sib], key[far, :HALF], key[far_sib, :HALF], key[far, HALF:], key[far_sib, HALF:]]
    )
    keyc, keyr = key[:, None], key.reshape(4, 1, TILE)
    slot_id = jnp.arange(padded, dtype=jnp.int32)
    onehot_t = (slot_id[:, None] == item_own[None, :]).astype(bf16)
    onehot = (item_own[:, None] == jnp.concatenate([slot_id, slot_id])[None, :]).astype(bf16)

    names = jnp.pad(labels[0], (0, padded - slots), constant_values=-1)

    def one_hot(names):
        return (names[:, None] == jnp.arange(class_table.shape[0], dtype=jnp.int32)[None, :]).astype(bf16)

    wide = w_ada.shape[2]
    columns = layers * wide // count
    ada_cols = w_ada.transpose(1, 0, 2).reshape(wrows, count, columns).transpose(1, 0, 2)
    qkv_cols = w_qkv.reshape(layers, wrows, 3, blks, piece).transpose(0, 3, 1, 2, 4)
    qkv_cols = qkv_cols.reshape(layers, blks, wrows, 3 * piece)
    up_cols = w_up.reshape(layers, wrows, dps, blks, ffrows).transpose(0, 3, 1, 2, 4)
    up_cols = up_cols.reshape(layers, blks, wrows, ff)
    class_rows = mm(one_hot(names), class_table).astype(bf16)
    own_scale = lax.dynamic_slice_in_dim(head_scale, b * own_heads, own_heads, axis=1)
    qscales = jnp.repeat(jnp.exp(own_scale), size, axis=1)
    common = (tokens[0], onehot, keyc, keyr, qscales[:, None, :], w_down)
    qkv_list, up_list = [qkv_cols[i] for i in range(layers)], [up_cols[i] for i in range(layers)]
    n = Names()
    lead = columns % 128 == 0 and wrows % 16 == 0
    if lead:
        declare_forward(n, *common, w_proj, qkv_list, up_list, class_rows, ada_cols, None, None, None)
    else:
        to_heads = [(i, (i % dps) * blks + i // dps) for i in range(count)]
        proj_own = lax.ppermute(w_proj, ("dp", "blk"), to_heads)
        class_rows = gather(class_rows, "dp")
        cond_all = jax.nn.silu(class_rows.astype(f32)).astype(bf16)
        ada_cols = lax.all_to_all(ada_cols, ("dp", "blk"), 0, 0, tiled=True)
        ada_part = mm(cond_all, ada_cols.reshape(count * wrows, columns))
        ada_part = lax.all_to_all(ada_part.reshape(dps, padded, columns), "dp", 0, 0, tiled=True)
        ada_all = lax.all_gather(ada_part, "blk", axis=1, tiled=False)
        ada_all = ada_all.transpose(2, 0, 1, 3).reshape(padded, layers, wide).transpose(1, 0, 2)
        ada_high = ada_all.astype(bf16)
        ada_low = (ada_all - ada_high.astype(f32)).astype(bf16)
        ada = jnp.concatenate([ada_high, ada_low], axis=1)
        qkv_shard = lax.all_to_all(qkv_cols[0], "blk", 0, 0, tiled=True)
        up_shard = lax.all_to_all(up_cols[0], "blk", 0, 0, tiled=True)
        rows_all = class_rows.reshape(dps, padded, width)
        declare_forward(n, *common, proj_own, qkv_list, up_list, rows_all, None, ada, qkv_shard, up_shard)
    lanes = dps * padded
    notes = jnp.pad(names.astype(f32)[None, :], ((layers, 7 - layers), (0, lanes - padded)))
    declare_backward(n, layers, cotangent[0], w_ada, onehot_t, notes, 3 * piece, ff)
    grads = n.call(partial(whole_kernel, lead, layers, size), 8, 60)
    output = grads.output[None]
    if lead:
        class_rows = grads.rows.reshape(dps * padded, width)
    one = grads.qkv_grad.reshape(layers, blks, wrows, 3, piece)
    qkv_grad = one.transpose(0, 2, 3, 1, 4).reshape(layers, wrows, 3 * width).astype(f32)
    one = grads.up_grad.reshape(layers, blks, wrows, dps, ffrows)
    up_grad = one.transpose(0, 2, 3, 1, 4).reshape(layers, wrows, ff * blks).astype(f32)
    told = grads.heard
    head_grad = jnp.sum(told[:, :, wrows : wrows + layers, :own_heads], axis=1)
    head_grad = head_grad.transpose(1, 0, 2).reshape(layers, heads)
    every_name = told[0, :, wrows + layers, :padded].reshape(-1).astype(jnp.int32)
    cond_grad = told[:, :, :wrows, :].transpose(1, 0, 2, 3).reshape(width, lanes).T
    _, silu_pull = jax.vjp(jax.nn.silu, class_rows.astype(f32))
    cond_pre = silu_pull(cond_grad)[0]
    pre_high = cond_pre.astype(bf16)
    pre_low = (cond_pre - pre_high.astype(f32)).astype(bf16)
    chosen = one_hot(jnp.concatenate([every_name, every_name]))
    table_grad = rows_mm(chosen, jnp.concatenate([pre_high, pre_low]))
    return (
        output,
        grads.tokens_grad[None],
        table_grad,
        head_grad,
        qkv_grad,
        grads.proj_grad,
        up_grad,
        grads.down_grad,
        grads.ada_grad,
    )


def solution(mesh):
    in_specs = (
        P("dp", "blk", None),
        P("dp", "blk", None),
        P("dp", None),
        P("dp", None),
        P(),
        P(),
        P(None, ("dp", "blk"), None),
        P(None, ("dp", "blk"), None),
        P(None, ("dp", "blk"), None),
        P(None, ("dp", "blk"), None),
        P(None, ("dp", "blk"), None),
    )
    out_specs = (
        P("dp", "blk", None),
        P("dp", "blk", None),
        P(),
        P(),
        P(None, ("dp", "blk"), None),
        P(None, ("dp", "blk"), None),
        P(None, ("dp", "blk"), None),
        P(None, ("dp", "blk"), None),
        P(None, ("dp", "blk"), None),
    )
    return jax.shard_map(
        per_device, mesh=mesh, in_specs=in_specs, out_specs=out_specs, check_vma=False
    )
```

```python
from functools import partial
from types import SimpleNamespace

import jax
import jax.numpy as jnp
from jax import lax
from jax.experimental import pallas as pl
from jax.experimental.pallas import tpu as pltpu
from jax.sharding import PartitionSpec as P

patch_areas = (1, 4, 9, 16, 25, 36, 64, 100, 169)
scale_starts = (1, 5, 14, 30, 55, 91, 155, 255)
f32 = jnp.float32
bf16 = jnp.bfloat16
MESH = pl.DeviceIdType.MESH
TILE = 256
HALF = 128
STEP = 32


def sizes():
    return lax.axis_size("dp"), lax.axis_size("blk")


def place():
    return lax.axis_index("dp"), lax.axis_index("blk")


def flat_place():
    return place()[0] * sizes()[1] + place()[1]


def token_meta(stops, length):
    areas = jnp.array(patch_areas, dtype=jnp.int32)
    levels = jnp.arange(9, dtype=jnp.int32)
    counts = jnp.sum(jnp.where(levels[None, :] < stops[:, None], areas[None, :], 0), axis=1)
    ends = jnp.cumsum(counts)
    places = jnp.arange(length, dtype=jnp.int32)
    passed = places[:, None] >= ends[None, :]
    item = jnp.sum(passed.astype(jnp.int32), axis=1)
    begin = jnp.sum(jnp.where(passed, counts[None, :], 0), axis=1)
    inner = places - begin
    bounds = jnp.array(scale_starts, dtype=jnp.int32)
    level = jnp.sum((inner[:, None] >= bounds[None, :]).astype(jnp.int32), axis=1)
    level = jnp.where(item == stops.shape[0], 0, level)
    return (item, level)


def mm(left, right):
    return jnp.dot(left, right, preferred_element_type=f32)


def mm_t(left, right):
    return lax.dot_general(left, right, (((1,), (1,)), ((), ())), preferred_element_type=f32)


def rows_mm(left, right, precision=None):
    return lax.dot_general(
        left, right, (((0,), (0,)), ((), ())), precision=precision, preferred_element_type=f32
    )


def gather(values, axes):
    return lax.all_gather(values, axes, axis=0, tiled=True)


def scatter(values, axes):
    return lax.psum_scatter(values, axes, scatter_dimension=0, tiled=True)


def partners():
    d, b = place()
    return (d, b + 1 - 2 * (b % 2)), (d, (b + 2) % 4)


def greet(others):
    barrier = pltpu.get_barrier_semaphore()
    for other in others:
        pl.semaphore_signal(barrier, inc=1, device_id=other, device_id_type=MESH)
    return lambda: pl.semaphore_wait(barrier, len(others))


def greet_all():
    dps, blks = sizes()
    me = flat_place()
    others = [(me + k) % (dps * blks) for k in range(1, dps * blks)]
    return greet([(t // blks, t % blks) for t in others])


def remote(src, dst, send, recv, target):
    return pltpu.make_async_remote_copy(
        src_ref=src, dst_ref=dst, send_sem=send, recv_sem=recv, device_id=target, device_id_type=MESH
    )


class Spread:
    def __init__(self, buf, send, recv, sibling, peer):
        def copy(src, dst, k, target):
            return remote(
                buf.at[pl.ds(src, HALF)], buf.at[pl.ds(dst, HALF)], send.at[k], recv.at[k], target
            )

        self.to_peer = [copy(HALF * c, 2 * TILE + TILE * c, c, peer) for c in range(2)]
        self.to_sibling = [copy(HALF * c, TILE + HALF * c, 2 + c, sibling) for c in range(2)]
        self.forward = [
            copy(2 * TILE + TILE * c, 2 * TILE + TILE * c + HALF, 4 + c, sibling) for c in range(2)
        ]

    def start(self, c):
        self.to_peer[c].start()
        self.to_sibling[c].start()

    def wait_block(self, i):
        @pl.when(i == 1)
        def _():
            for c in range(2):
                self.to_sibling[c].wait_recv()

        for c in range(2):

            @pl.when(i == 2 + c)
            def _():
                self.to_peer[c].wait_recv()
                self.forward[c].start()
                self.forward[c].wait_recv()

    def ready(self):
        for c in range(2):
            self.to_sibling[c].wait_recv()
        for c in range(2):
            self.to_peer[c].wait_recv()
            self.forward[c].start()
        for c in range(2):
            self.forward[c].wait_recv()

    def finish(self):
        for c in range(2):
            self.to_peer[c].wait_send()
            self.to_sibling[c].wait_send()
            self.forward[c].wait_send()


class Collect:
    def __init__(self, parts, out, mid, own, far, send, recv, sibling, peer):
        self.parts, self.out, self.mid, self.own, self.far = parts, out, mid, own, far
        self.cross = [
            remote(
                parts.at[pl.ds(2 * TILE + TILE * c + HALF, HALF)],
                mid.at[pl.ds(HALF * c, HALF)],
                send.at[c],
                recv.at[c],
                sibling,
            )
            for c in range(2)
        ]
        self.over = [
            remote(
                out.at[pl.ds(HALF * c, HALF)],
                far.at[pl.ds(HALF * c, HALF)],
                send.at[2 + c],
                recv.at[2 + c],
                peer,
            )
            for c in range(2)
        ]
        self.home = remote(parts.at[pl.ds(TILE, TILE)], own, send.at[4], recv.at[4], sibling)

    def block_done(self, j):
        for c in range(2):

            @pl.when(j == 2 + c)
            def _():
                self.cross[c].start()
                self.cross[c].wait_recv()

                @pl.loop(0, HALF // STEP)
                def _(s):
                    at = pl.multiple_of(s * STEP, STEP)
                    mine = self.parts[pl.ds(2 * TILE + TILE * c + at, STEP), :].astype(f32)
                    theirs = self.mid[pl.ds(HALF * c + at, STEP), :].astype(f32)
                    self.out[pl.ds(HALF * c + at, STEP), :] = (mine + theirs).astype(bf16)

                self.over[c].start()

        @pl.when(j == 1)
        def _():
            self.home.start()

    def wait(self):
        self.home.wait_recv()
        for c in range(2):
            self.over[c].wait_recv()

    def rows(self, at):
        span = pl.ds(at, STEP)
        total = self.parts[span, :].astype(f32) + self.own[span, :].astype(f32)
        return total + self.far[span, :].astype(f32)

    def sent(self):
        self.home.wait_send()
        for c in range(2):
            self.cross[c].wait_send()

    def over_sent(self):
        for c in range(2):
            self.over[c].wait_send()

    def finish(self):
        self.sent()
        self.over_sent()


def spread_scratch(width):
    return [
        pltpu.VMEM((4 * TILE, width), bf16),
        pltpu.SemaphoreType.DMA((6,)),
        pltpu.SemaphoreType.DMA((6,)),
    ]


def collect_scratch(width):
    return [pltpu.VMEM((4 * TILE, width), bf16)] + [pltpu.VMEM((TILE, width), bf16)] * 4 + [
        pltpu.SemaphoreType.DMA((5,)),
        pltpu.SemaphoreType.DMA((5,)),
    ]


class Moves:
    def __init__(self, sems):
        self.sems, self.used = sems, 0

    def copy(self, src, dst):
        made = pltpu.make_async_copy(src, dst, self.sems.at[self.used])
        self.used += 1
        made.start()
        return made


def expand(onehot, ada, which, outs):
    width = outs[0].shape[1]
    for k, out in zip(which, outs):
        for n in range(0, width, TILE):
            out[:, n : n + TILE] = mm(onehot[...], ada[:, k * width + n : k * width + n + TILE])


def normed(values):
    centre = jnp.mean(values, axis=-1, keepdims=True)
    centred = values - centre
    spread = jnp.mean(centred * centred, axis=-1, keepdims=True)
    rate = lax.rsqrt(spread + 1e-06)
    return centred * rate, rate


def norm_back(grad, values_hat, rate):
    first = jnp.mean(grad, axis=-1, keepdims=True)
    second = jnp.mean(grad * values_hat, axis=-1, keepdims=True)
    return rate * (grad - first - values_hat * second)


def row_steps(start, rows, body):
    @pl.loop(0, rows // STEP)
    def _(s):
        body(pl.multiple_of(start + s * STEP, STEP))


def block_ones(size):
    shape = (TILE, TILE)
    one = lax.broadcasted_iota(jnp.int32, shape, 0) // size
    two = lax.broadcasted_iota(jnp.int32, shape, 1) // size
    return (one == two).astype(bf16)


def split_mm(dot, values, ones):
    high = values.astype(bf16)
    low = (values - high.astype(f32)).astype(bf16)
    return dot(high, ones) + dot(low, ones)


def head_lanes(values, h, size):
    lane = lax.broadcasted_iota(jnp.int32, values.shape, 1) // size
    return jnp.where(lane == h, values, jnp.zeros_like(values))


def hidden_bias(keyc, keyr, rows, cols):
    keys = keyc[pl.ds(rows, TILE), :]
    top = keyr[cols]
    low = top - top % 16
    return jnp.where((keys >= low) & (keys <= top), 0.0, -1e30)


def nothing():
    pass


class Hooks:
    def __init__(self, **table):
        self.start = self.sent = self.need = self.a = self.b = self.c = self.d = self.dw = nothing
        vars(self).update(table)


def modulate_rows(x, scale, shift, hbuf, spread):
    def modulated(at):
        span = pl.ds(at, STEP)
        hat, _ = normed(x[span, :])
        hbuf[span, :] = (hat * (1.0 + scale[span, :]) + shift[span, :]).astype(bf16)

    for c in range(2):
        row_steps(HALF * c, HALF, modulated)
        spread.start(c)


def exchange(refs):
    hbuf, ag_send, ag_recv, parts, out, mid, own, far, rs_send, rs_recv = refs
    sibling, peer = partners()
    spread = Spread(hbuf, ag_send, ag_recv, sibling, peer)
    collect = Collect(parts, out, mid, own, far, rs_send, rs_recv, sibling, peer)
    return hbuf, parts, spread, collect


def attend_segment(
    hooks,
    size,
    x,
    onehot,
    ada,
    qscale,
    keyc,
    keyr,
    weights_in,
    weights,
    saves_out,
    inv_out,
    branch_out,
    mid_out,
    held,
    mods,
    moves,
    refs,
):
    qkv, vt, rates, o_out = held
    gamma, scale, shift = mods
    wqkv, wproj = weights
    hbuf, parts, spread, collect = exchange(refs)
    mover = Moves(moves)
    expand(onehot, ada, (0, 2, 4), (gamma, scale, shift))
    modulate_rows(x, scale, shift, hbuf, spread)
    hooks.need()
    load_qkv = mover.copy(weights_in[0], wqkv)
    load_proj = mover.copy(weights_in[1], wproj)
    load_qkv.wait()
    ones = block_ones(size)

    @pl.loop(0, 4)
    def _(i):
        spread.wait_block(i)
        span = pl.ds(pl.multiple_of(i * TILE, TILE), TILE)
        h = hbuf[span, :]
        for part in range(3):
            columns = slice(part * TILE, (part + 1) * TILE)
            value = mm(h, wqkv[:, columns])
            if part < 2:
                rate = lax.rsqrt(split_mm(mm, value * value, ones) + 1e-06)
                if part == 0:
                    rate = rate * qscale[...]
                rates[span, columns] = rate
                value = value * rate
            else:
                vt[:, span] = value.T.astype(bf16)
            qkv[span, columns] = value.astype(bf16)

    hooks.a()
    saves = [mover.copy(a, b) for a, b in zip((hbuf, qkv, rates), saves_out)]
    load_proj.wait()
    heads = TILE // size

    @pl.loop(0, 4)
    def _(i):
        j = (i + 2) % 4
        span = pl.ds(pl.multiple_of(j * TILE, TILE), TILE)
        queries = [head_lanes(qkv[span, 0:TILE], h, size) for h in range(heads)]
        sums = [jnp.zeros((1, TILE), f32)] * heads
        mixed = [jnp.zeros((size, TILE), f32)] * heads
        for k in range(4):
            keys = qkv[k * TILE : (k + 1) * TILE, TILE : 2 * TILE]
            bias = hidden_bias(keyc, keyr, k * TILE, j)
            for h in range(heads):
                grown = jnp.exp(mm_t(keys, queries[h]) + bias)
                sums[h] = sums[h] + jnp.sum(grown, axis=0, keepdims=True)
                mixed[h] = mixed[h] + mm(
                    vt[h * size : (h + 1) * size, k * TILE : (k + 1) * TILE], grown.astype(bf16)
                )
        inverse = [1.0 / one for one in sums]
        for h in range(heads):
            inv_out[j, h : h + 1, :] = inverse[h]
        whole = jnp.concatenate([mixed[h] * inverse[h] for h in range(heads)], axis=0)
        low = whole.T.astype(bf16)
        o_out[span, :] = low
        for n in range(0, parts.shape[1], TILE):
            parts[span, n : n + TILE] = mm(low, wproj[:, n : n + TILE]).astype(bf16)
        collect.block_done(j)

    hooks.b()
    collect.wait()
    hooks.c()

    def added(at):
        span = pl.ds(at, STEP)
        branch = collect.rows(at)
        branch_out[span, :] = branch
        mid_out[span, :] = x[span, :] + gamma[span, :] * branch

    row_steps(0, TILE, added)
    spread.finish()
    collect.finish()
    for one in saves:
        one.wait()


def mlp_block(h, span, wup, wdown, hidden, slope, parts):
    for n in range(0, wup.shape[1], TILE):
        columns = slice(n, n + TILE)
        up = mm(h, wup[:, columns])
        square = up * up
        bent = jnp.tanh(0.7978845608 * (up * (1.0 + 0.044715 * square)))
        half = 0.5 * (1.0 + bent)
        hidden[span, columns] = (up * half).astype(bf16)
        inner = 0.7978845608 + (3.0 * 0.044715 * 0.7978845608) * square
        slope[span, columns] = (half + 0.5 * up * (1.0 - bent * bent) * inner).astype(bf16)
    g = hidden[span, :]
    for n in range(0, parts.shape[1], TILE):
        parts[span, n : n + TILE] = mm(g, wdown[:, n : n + TILE]).astype(bf16)


def mlp_segment(
    hooks, x, onehot, ada, weights_in, weights, saves_out, result_out, x_out, held, mods, moves, refs
):
    hidden, slope = held
    gamma, scale, shift = mods
    wup, wdown = weights
    hbuf, parts, spread, collect = exchange(refs)
    mover = Moves(moves)
    expand(onehot, ada, (1, 3, 5), (gamma, scale, shift))
    modulate_rows(x, scale, shift, hbuf, spread)
    hooks.need()
    loads = [mover.copy(a, b) for a, b in zip(weights_in, weights)]
    for one in loads:
        one.wait()

    @pl.loop(0, 4)
    def _(i):
        spread.wait_block(i)
        for at, hook in ((2, hooks.a), (3, hooks.b)):

            @pl.when(i == at)
            def _():
                hook()

        span = pl.ds(pl.multiple_of(i * TILE, TILE), TILE)
        h = hbuf[span, :]
        mlp_block(h, span, wup, wdown, hidden, slope, parts)
        collect.block_done(i)

    hooks.c()
    saves = [mover.copy(a, b) for a, b in zip((hbuf, hidden, slope), saves_out)]
    collect.wait()

    def added(at):
        span = pl.ds(at, STEP)
        result = collect.rows(at)
        result_out[span, :] = result
        x_out[span, :] = x[span, :] + gamma[span, :] * result

    row_steps(0, TILE, added)
    spread.finish()
    collect.finish()
    for one in saves:
        one.wait()


def item_sums(onehot_t, terms, out):
    for k, term in enumerate(terms):
        width = term.shape[1]
        out[:, k * width : (k + 1) * width] = mm(onehot_t[...], term[...])


def scaled_rows(x, gamma, hbuf, spread):
    def scaled(at):
        span = pl.ds(at, STEP)
        hbuf[span, :] = (gamma[span, :] * x[span, :]).astype(bf16)

    for c in range(2):
        row_steps(HALF * c, HALF, scaled)
        spread.start(c)


def back_rows(collect, x, grad, branch, scale, terms, out):
    dgamma, dscale, dshift = terms

    def added(at):
        span = pl.ds(at, STEP)
        dh = collect.rows(at)
        hat, rate = normed(x[span, :])
        above = grad[span, :]
        dgamma[span, :] = (above * branch[span, :]).astype(bf16)
        dscale[span, :] = (dh * hat).astype(bf16)
        dshift[span, :] = dh.astype(bf16)
        out[span, :] = above + norm_back(dh * (1.0 + scale[span, :]), hat, rate)

    row_steps(0, TILE, added)


def mlp_back_block(dm, span, wup, wdown, slope, parts):
    for n in range(0, slope.shape[1], TILE):
        columns = slice(n, n + TILE)
        dg = mm_t(dm, wdown[columns, :])
        slope[span, columns] = (dg * slope[span, columns].astype(f32)).astype(bf16)
    du = slope[span, :]
    for n in range(0, parts.shape[1], TILE):
        parts[span, n : n + TILE] = mm_t(du, wup[n : n + TILE, :]).astype(bf16)


def mlp_weight_grads(mover, hall, gall, dm, du, dwup, dwdown, outs):
    @pl.loop(0, gall.shape[1] // TILE)
    def _(k):
        columns = pl.ds(pl.multiple_of(k * TILE, TILE), TILE)
        for n in range(0, dm.shape[1], 2 * TILE):
            dwdown[columns, n : n + 2 * TILE] = rows_mm(
                gall[:, columns], dm[:, n : n + 2 * TILE]
            ).astype(bf16)

    save_down = mover.copy(dwdown, outs[1])

    @pl.loop(0, hall.shape[1] // TILE)
    def _(k):
        columns = pl.ds(pl.multiple_of(k * TILE, TILE), TILE)
        for n in range(0, du.shape[1], 2 * TILE):
            dwup[columns, n : n + 2 * TILE] = rows_mm(
                hall[:, columns], du[:, n : n + 2 * TILE]
            ).astype(bf16)

    save_up = mover.copy(dwup, outs[0])
    save_down.wait()
    save_up.wait()


def mlp_top_segment(
    hooks, x, dx, onehot, onehot_t, ada, cotangent, weights_in, weights, outs, result, x_out, items, held, mods, terms, moves, refs, back_refs, free
):
    hidden, du, dwup, dwdown = held
    gamma, scale, shift = mods
    wup, wdown = weights
    dgamma, _, dshift = terms
    refs = refs[:4] + [dgamma] + refs[5:]
    hbuf, parts, spread, collect = exchange(refs)
    back_hbuf, _, back_spread, back_collect = exchange(back_refs)
    mover = Moves(moves)
    expand(onehot, ada, (1, 3, 5), (gamma, scale, shift))
    modulate_rows(x, scale, shift, hbuf, spread)
    dx[...] = cotangent[...].astype(f32)
    spread.ready()
    scaled_rows(dx, gamma, back_hbuf, back_spread)
    hooks.need()
    loads = [mover.copy(a, b) for a, b in zip(weights_in, weights)]
    for one in loads:
        one.wait()

    @pl.loop(0, 4)
    def _(i):
        span = pl.ds(pl.multiple_of(i * TILE, TILE), TILE)
        mlp_block(hbuf[span, :], span, wup, wdown, hidden, du, parts)
        collect.block_done(i)

    collect.sent()
    dshift[...] = parts[0:TILE, :]

    @pl.loop(0, 4)
    def _(i):
        back_spread.wait_block(i)
        span = pl.ds(pl.multiple_of(i * TILE, TILE), TILE)
        mlp_back_block(back_hbuf[span, :], span, wup, wdown, du, parts)
        back_collect.block_done(i)

    mlp_weight_grads(mover, hbuf, hidden, back_hbuf, du, dwup, dwdown, outs)
    spread.finish()
    for other in partners():
        pl.semaphore_signal(free, inc=1, device_id=other, device_id_type=MESH)
    hooks.dw()
    collect.wait()
    collect.over_sent()

    def added(at):
        span = pl.ds(at, STEP)
        total = dshift[span, :].astype(f32) + collect.own[span, :].astype(f32)
        total = total + collect.far[span, :].astype(f32)
        result[span, :] = total
        x_out[span, :] = x[span, :] + gamma[span, :] * total

    row_steps(0, TILE, added)
    back_collect.wait()
    back_rows(back_collect, x, dx, result, scale, terms, x)
    item_sums(onehot_t, terms, items)
    back_spread.finish()
    back_collect.finish()
    pl.semaphore_wait(free, 2)


def mlp_back_segment(
    hooks, dx, onehot, onehot_t, ada, ins, outs, dmid, items, held, mods, terms, moves, refs
):
    wup_in, wdown_in, h_in, g_in, slope_in, result_in, mid_in = ins
    wup, wdown, hall, gall, slope, dwup, dwdown, result, mid_state = held
    gamma, scale = mods
    hbuf, parts, spread, collect = exchange(refs)
    mover = Moves(moves)
    load_down = mover.copy(wdown_in, wdown)
    load_slope = mover.copy(slope_in, slope)
    load_up = mover.copy(wup_in, wup)
    later = [mover.copy(g_in, gall), mover.copy(h_in, hall)]
    later += [mover.copy(result_in, result), mover.copy(mid_in, mid_state)]
    expand(onehot, ada, (1, 3), (gamma, scale))
    hooks.start()
    scaled_rows(dx, gamma, hbuf, spread)
    hooks.sent()
    for one in (load_down, load_slope, load_up):
        one.wait()

    @pl.loop(0, 4)
    def _(i):
        spread.wait_block(i)
        for at, hook in ((2, hooks.a), (3, hooks.b)):

            @pl.when(i == at)
            def _():
                hook()

        span = pl.ds(pl.multiple_of(i * TILE, TILE), TILE)
        dm = hbuf[span, :]
        mlp_back_block(dm, span, wup, wdown, slope, parts)
        collect.block_done(i)

    hooks.c()
    for one in later:
        one.wait()

    mlp_weight_grads(mover, hall, gall, hbuf, slope, dwup, dwdown, outs)
    hooks.dw()
    collect.wait()
    back_rows(collect, mid_state, dx, result, scale, terms, dmid)
    item_sums(onehot_t, terms, items)
    spread.finish()
    collect.finish()


def attend_back_segment(
    hooks,
    size,
    dmid,
    onehot,
    onehot_t,
    ada,
    qscale,
    keyc,
    keyr,
    inverse,
    ins,
    outs,
    dx,
    items,
    head_out,
    held,
    mods,
    terms,
    moves,
    refs,
):
    wqkv_in, wproj_in, h_in, qkv_in, rate_in, o_in, branch_in, x_in = ins
    wqkv, wproj, hall, qkv, rates, oall, kt, dkeys, dvalues, dqkv, dwqkv, dwproj, branch, x = held
    gamma, scale = mods
    hbuf, parts, spread, collect = exchange(refs)
    mover = Moves(moves)
    loads = [mover.copy(wproj_in, wproj), mover.copy(qkv_in, qkv)]
    loads += [mover.copy(o_in, oall), mover.copy(rate_in, rates)]
    load_w = mover.copy(wqkv_in, wqkv)
    later = [mover.copy(h_in, hall), mover.copy(branch_in, branch)]
    if x_in is not None:
        later.append(mover.copy(x_in, x))
    expand(onehot, ada, (0, 2), (gamma, scale))
    hooks.start()
    scaled_rows(dmid, gamma, hbuf, spread)
    hooks.sent()
    for one in loads:
        one.wait()
    heads = TILE // size
    ones = block_ones(size)
    inv_square = 1.0 / (qscale[...] * qscale[...])
    select = (
        lax.broadcasted_iota(jnp.int32, (8, TILE), 1) // size
        == lax.broadcasted_iota(jnp.int32, (8, TILE), 0)
    ).astype(bf16)
    dkeys[...] = jnp.zeros_like(dkeys)
    dvalues[...] = jnp.zeros_like(dvalues)
    head_out[...] = jnp.zeros_like(head_out)
    for k in range(4):
        rows = slice(k * TILE, (k + 1) * TILE)
        kt[:, rows] = qkv[rows, TILE : 2 * TILE].astype(f32).T.astype(bf16)

    @pl.loop(0, 4)
    def _(i):
        spread.wait_block(i)
        for at, hook in ((2, hooks.a), (3, hooks.b)):

            @pl.when(i == at)
            def _():
                hook()

        span = pl.ds(pl.multiple_of(i * TILE, TILE), TILE)
        dout = mm_t(hbuf[span, :], wproj[...]).astype(bf16)
        product = dout.astype(f32) * oall[span, :].astype(f32)
        row_term = split_mm(lambda a, b: mm_t(b, a), product, select)
        q_low = qkv[span, 0:TILE]
        queries = [head_lanes(q_low, h, size) for h in range(heads)]
        douts = [head_lanes(dout, h, size) for h in range(heads)]
        dquery = [jnp.zeros((size, TILE), f32)] * heads
        for k in range(4):
            rows = slice(k * TILE, (k + 1) * TILE)
            keys = qkv[rows, TILE : 2 * TILE]
            values = qkv[rows, 2 * TILE : 3 * TILE]
            bias = hidden_bias(keyc, keyr, k * TILE, i)
            dkey = jnp.zeros((TILE, TILE), f32)
            dvalue = jnp.zeros((TILE, TILE), f32)
            for h in range(heads):
                share = jnp.exp(mm_t(keys, queries[h]) + bias) * inverse[i, h : h + 1, :]
                dshare = mm_t(values, douts[h])
                dscore = (share * (dshare - row_term[h : h + 1, :])).astype(bf16)
                dvalue = dvalue + mm(share.astype(bf16), douts[h])
                dkey = dkey + mm(dscore, queries[h])
                dquery[h] = dquery[h] + mm(kt[h * size : (h + 1) * size, rows], dscore)
            dkeys[rows, :] += dkey
            dvalues[rows, :] += dvalue
        dq = jnp.concatenate(dquery, axis=0).T
        qhat = q_low.astype(f32)
        along = split_mm(mm, dq * qhat, ones)
        head_out[...] += jnp.sum(along, axis=0, keepdims=True)
        dqkv[span, 0:TILE] = (rates[span, 0:TILE] * (dq - qhat * (along * inv_square))).astype(bf16)

    load_w.wait()
    hooks.c()

    @pl.loop(0, 4)
    def _(i):
        j = (i + 2) % 4
        span = pl.ds(pl.multiple_of(j * TILE, TILE), TILE)
        dk = dkeys[span, :]
        khat = qkv[span, TILE : 2 * TILE].astype(f32)
        along = split_mm(mm, dk * khat, ones)
        dqkv[span, TILE : 2 * TILE] = (
            rates[span, TILE : 2 * TILE] * (dk - khat * along)
        ).astype(bf16)
        dqkv[span, 2 * TILE : 3 * TILE] = dvalues[span, :].astype(bf16)
        low = dqkv[span, :]
        for n in range(0, parts.shape[1], TILE):
            parts[span, n : n + TILE] = mm_t(low, wqkv[n : n + TILE, :]).astype(bf16)
        collect.block_done(j)

    hooks.d()
    for n in range(0, hbuf.shape[1], 2 * TILE):
        dwproj[:, n : n + 2 * TILE] = rows_mm(oall[...], hbuf[:, n : n + 2 * TILE]).astype(bf16)
    save_proj = mover.copy(dwproj, outs[1])
    for one in later:
        one.wait()

    @pl.loop(0, hall.shape[1] // TILE)
    def _(k):
        columns = pl.ds(pl.multiple_of(k * TILE, TILE), TILE)
        dwqkv[columns, :] = rows_mm(hall[:, columns], dqkv[...]).astype(bf16)

    save_w = mover.copy(dwqkv, outs[0])
    save_proj.wait()
    save_w.wait()
    hooks.dw()
    collect.wait()
    back_rows(collect, x, dmid, branch, scale, terms, dx)
    item_sums(onehot_t, terms, items)
    spread.finish()
    collect.finish()


def groups(dps):
    d, b = place()
    side, pairs = d % 2, dps // 2
    pair = d // 2
    ahead = [((pair + k) % pairs) * 2 + side for k in range(pairs)]
    behind = [((pair - k + pairs) % pairs) * 2 + side for k in range(pairs)]
    return d, b, d + 1 - 2 * side, ahead, behind


class DpGather:
    def __init__(self):
        self.dps = sizes()[0]

    def bind(self, ins, outs, scratch):
        send, recv, local = scratch
        d, b, other, ahead, behind = groups(self.dps)
        pairs = self.dps // 2
        self.partners = [(other, b)] + [(t, b) for t in ahead[1:]]
        self.first, self.direct, self.forward, self.local = [], [], [], []
        for a, (src, dst) in enumerate(zip(ins, outs)):
            self.local.append(pltpu.make_async_copy(src, dst.at[d], local.at[a]))
            self.first.append(remote(src, dst.at[d], send.at[a, 0], recv.at[a, 0], (other, b)))
            self.direct.append([None])
            self.forward.append([None])
            for k in range(1, pairs):
                self.direct[a].append(
                    remote(src, dst.at[d], send.at[a, k], recv.at[a, k], (ahead[k], b))
                )
                at = pairs + k
                self.forward[a].append(
                    remote(
                        dst.at[behind[k]], dst.at[behind[k]], send.at[a, at], recv.at[a, at], (other, b)
                    )
                )
        self.order = [(k, a) for k in range(1, pairs) for a in range(len(ins))]

    def start_far(self):
        for k, a in self.order:
            self.direct[a][k].start()
        for one in self.local:
            one.start()

    def start_near(self):
        for one in self.first:
            one.start()

    def step(self, hook, hooks=3):
        low, high = (len(self.order) * hook) // hooks, (len(self.order) * (hook + 1)) // hooks
        for k, a in self.order[low:high]:
            self.direct[a][k].wait_recv()
            self.forward[a][k].start()

    def finish(self):
        for one in self.local:
            one.wait()
        for one in self.first:
            one.wait()
        for k, a in self.order:
            self.direct[a][k].wait_send()
            self.forward[a][k].wait()


class DpScatter:
    def __init__(self):
        self.dps = sizes()[0]

    def bind(self, ins, outs, scratch):
        d, b, other, ahead, behind = groups(self.dps)
        pairs = self.dps // 2
        self.partners = [(other, b)] + [(t, b) for t in ahead[1:]]
        self.results = outs
        self.bufs, self.local, self.cross, self.direct = [], [], [], []
        for a, src in enumerate(ins):
            mine, near, far, send, recv, local = scratch[6 * a : 6 * a + 6]
            self.bufs.append((mine, near, far))
            self.local.append([])
            self.cross.append([])
            self.direct.append([None])
            for k in range(pairs):
                target = ahead[k]
                theirs = target + 1 - 2 * (target % 2)
                self.local[a].append(
                    pltpu.make_async_copy(src.at[target], mine.at[k], local.at[k])
                )
                self.cross[a].append(
                    remote(src.at[theirs], near.at[k], send.at[k], recv.at[k], (other, b))
                )
                if k:
                    at = pairs + k
                    self.direct[a].append(
                        remote(mine.at[k], far.at[k], send.at[at], recv.at[at], (target, b))
                    )
        self.order = [(k, a) for k in range(1, pairs) for a in range(len(ins))]
        self.last = [(0, a) for a in range(len(ins))]

    def start(self):
        for k, a in self.order + self.last:
            self.cross[a][k].start()
            self.local[a][k].start()

    def add(self, a, k):
        self.local[a][k].wait()
        self.cross[a][k].wait_recv()
        mine, near, _ = self.bufs[a]
        rows = mine.shape[1]
        step = min(rows, STEP)

        @pl.loop(0, rows // step)
        def _(s):
            span = pl.ds(pl.multiple_of(s * step, step), step)
            total = mine[k, span, :].astype(f32) + near[k, span, :].astype(f32)
            mine[k, span, :] = total.astype(bf16)

    def step(self, hook, hooks=3):
        low, high = (len(self.order) * hook) // hooks, (len(self.order) * (hook + 1)) // hooks
        for k, a in self.order[low:high]:
            self.add(a, k)
            self.direct[a][k].start()

    def own(self):
        for k, a in self.last:
            self.add(a, k)
        for k, a in self.order + self.last:
            self.cross[a][k].wait_send()

    def finish(self):
        for k, a in self.order:
            self.direct[a][k].wait()
        for a, result in enumerate(self.results):
            mine, _, far = self.bufs[a]
            step = result.shape[1] if len(result.shape) == 3 else min(mine.shape[1], STEP)

            @pl.loop(0, mine.shape[1] // step)
            def _(s):
                span = pl.ds(pl.multiple_of(s * step, step), step)
                total = mine[0, span, :].astype(f32)
                for k in range(1, self.dps // 2):
                    total = total + far[k, span, :].astype(f32)
                if len(result.shape) == 3:
                    result[s] = total.astype(result.dtype)
                else:
                    result[span, :] = total.astype(result.dtype)

    def release(self, credit):
        for other in self.partners:
            pl.semaphore_signal(credit, inc=1, device_id=other, device_id_type=MESH)

    def acquire(self, credit):
        pl.semaphore_wait(credit, len(self.partners))


class Items:
    def __init__(self, src, out, scratch):
        self.terms, self.held, send, recv, dp_send, dp_recv = scratch
        dps = sizes()[0]
        d, b = place()
        self.here, self.out = (d, b), out
        wide = self.held.shape[2]

        def quarter(i):
            return src.at[:, pl.ds(pl.multiple_of(i * wide, 128), wide)]

        self.first = [pltpu.make_async_copy(quarter(b), self.terms.at[0], send.at[0])]
        for k in range(1, 4):
            to = (b + k) % 4
            self.first.append(
                remote(quarter(to), self.terms.at[k], send.at[k], recv.at[k], (d, to))
            )
        self.over = [
            remote(self.held.at[0], out.at[b, d], dp_send.at[k], dp_recv.at[k], ((d + k) % dps, b))
            for k in range(1, dps)
        ]
        self.keep = pltpu.make_async_copy(self.held.at[0], out.at[b, d], send.at[7])
        self.share = Share(out, send.at[pl.ds(4, 3)], recv.at[pl.ds(4, 3)])

    def start(self):
        for one in self.first:
            one.start()

    def sum(self):
        d, b = self.here
        for one in self.first:
            one.wait()
        total = (self.terms[0] + self.terms[1]) + (self.terms[2] + self.terms[3])
        low = total.astype(bf16)
        self.held[0] = low
        for one in self.over + [self.keep]:
            one.start()

    def spread(self):
        for one in self.over + [self.keep]:
            one.wait()
        self.share.start()

    def forward(self):
        self.share.forward()

    def finish(self):
        self.share.finish()


class Permute:
    def __init__(self, src, dst, send, recv, back):
        dps, blks = sizes()
        d, b = place()
        owner, user = d * blks + b, b * dps + d
        self.moves = owner != user
        to = (user // blks, user % blks) if back else (owner % dps, owner // dps)
        self.away = remote(src, dst, send, recv, to)
        self.stay = pltpu.make_async_copy(src, dst, send)

    def start(self):
        @pl.when(self.moves)
        def _():
            self.away.start()

        @pl.when(jnp.logical_not(self.moves))
        def _():
            self.stay.start()

    def finish(self):
        @pl.when(self.moves)
        def _():
            self.away.wait()

        @pl.when(jnp.logical_not(self.moves))
        def _():
            self.stay.wait()


def modulations_start(rows_in, ada_in, rows_out, columns, sems):
    dp_send, dp_recv, ada_send, ada_recv, local = sems
    dps, blks = sizes()
    count = dps * blks
    d, b = place()
    me = d * blks + b
    rows = ada_in.shape[1]
    span = pl.ds(pl.multiple_of(me * rows, rows), rows)
    sends = [
        pltpu.make_async_copy(rows_in, rows_out.at[d], local.at[0]),
        pltpu.make_async_copy(ada_in.at[me], columns.at[span], local.at[1]),
    ]
    for k in range(1, dps):
        to = ((d + k) % dps, b)
        sends.append(remote(rows_in, rows_out.at[d], dp_send.at[k], dp_recv.at[k], to))
    for k in range(1, count):
        t = (me + k) % count
        to = (t // blks, t % blks)
        sends.append(remote(ada_in.at[t], columns.at[span], ada_send.at[k], ada_recv.at[k], to))
    for one in sends:
        one.start()
    return sends


def modulations_answer(rows_out, columns, answers, quarters, sems):
    send, recv = sems
    dps = sizes()[0]
    d, b = place()
    slots, wide = answers.shape[1:]
    value = rows_out[...].astype(f32)
    value = (value / (1.0 + jnp.exp(-value))).astype(bf16)
    whole = mm(value.reshape(dps * slots, rows_out.shape[2]), columns[...])
    answers[...] = whole.reshape(dps, slots, wide)
    replies = []
    for k in range(1, dps):
        to = (d + k) % dps
        replies.append(
            remote(answers.at[to], quarters.at[b, d], send.at[k], recv.at[k], (to, b))
        )
    for one in replies:
        one.start()
    quarters[b, d] = answers[d]
    return replies


class Share:
    def __init__(self, buf, send, recv):
        d, b = place()
        sibling, peer = partners()
        far = peer[1]
        self.moves = [
            remote(buf.at[b], buf.at[b], send.at[0], recv.at[0], peer),
            remote(buf.at[b], buf.at[b], send.at[1], recv.at[1], sibling),
            remote(buf.at[far], buf.at[far], send.at[2], recv.at[2], sibling),
        ]

    def start(self):
        self.moves[0].start()
        self.moves[1].start()

    def forward(self):
        self.moves[0].wait_recv()
        self.moves[2].start()

    def finish(self):
        self.moves[1].wait_recv()
        self.moves[2].wait_recv()
        for one in self.moves:
            one.wait_send()


class PieceSwap:
    def __init__(self, pairs, send, recv):
        d, b = place()
        self.sent = []
        for a, (src, dst) in enumerate(pairs):
            self.sent.append(pltpu.make_async_copy(src.at[b], dst.at[b], send.at[a, 0]))
            for k in range(1, 4):
                to = (b + k) % 4
                self.sent.append(
                    remote(src.at[to], dst.at[b], send.at[a, k], recv.at[a, k], (d, to))
                )

    def start(self):
        for one in self.sent:
            one.start()

    def finish(self):
        for one in self.sent:
            one.wait()


def flat(value):
    return [leaf for one in value for leaf in flat(one)] if isinstance(value, list) else [value]


def refill(value, leaves):
    return [refill(one, leaves) for one in value] if isinstance(value, list) else next(leaves)


class Names:
    def __init__(self):
        self.ins, self.outs, self.scratch = SimpleNamespace(), SimpleNamespace(), SimpleNamespace()

    def call(self, kernel, ident, vmem):
        ins, outs, scratch = (flat(list(vars(one).values())) for one in (self.ins, self.outs, self.scratch))

        def fill(bags, refs):
            leaves, found = iter(refs), SimpleNamespace()
            for bag in bags:
                for name, value in vars(bag).items():
                    vars(found)[name] = refill(value, leaves)
            return found

        results = pl.pallas_call(
            lambda *refs: kernel(fill((self.ins, self.outs, self.scratch), refs)),
            out_shape=[one for one, _ in outs],
            in_specs=[where for _, where in ins],
            out_specs=[where for _, where in outs],
            scratch_shapes=scratch,
            compiler_params=pltpu.CompilerParams(
                collective_id=ident, has_side_effects=True, vmem_limit_bytes=vmem * 2**20
            ),
            cost_estimate=pl.CostEstimate(flops=2**36, bytes_accessed=2**26, transcendentals=0),
        )(*[one for one, _ in ins])
        return fill((self.outs,), results)


def add_exchanges(names, width):
    names.scratch.spreads = [spread_scratch(width) for _ in range(2)]
    names.scratch.parts, names.scratch.out = collect_scratch(width)[:2]
    names.scratch.collects = [collect_scratch(width)[2:] for _ in range(2)]


def exchange_set(r, turn):
    return r.spreads[turn] + [r.parts, r.out] + r.collects[turn]


def whole_kernel(lead, layers, size, r):
    wide = 3 * TILE
    r.wqkv, r.wproj = r.wup.at[:, 0:wide], r.wdown.at[0:TILE]
    r.qkv_buf, r.o_buf = r.gall.at[:, 0:wide], r.gall.at[:, wide : wide + TILE]
    r.vt, r.rate_buf = r.dwdown.at[TILE : 2 * TILE], r.rates_buf
    r.hidden, r.slope_buf = r.dwup, r.du
    r.state, r.middle, r.branch_buf, r.result_buf = r.grad, r.dmid, r.load_a, r.load_b
    if lead:
        r.columns = r.hall.at[:, 0 : r.ada_in.shape[2]]
    need_top, pending = forward_part(lead, layers, size, r)
    backward_part(layers, size, r, need_top, pending)


def forward_part(lead, layers, size, r):
    dps, blks = sizes()
    d, b = place()
    sibling, peer = partners()
    ada = r.ada
    qkv_shard = r.qkv_shard if lead else [r.qkv_first] + r.qkv_shard
    up_shard = r.up_shard if lead else [r.up_first] + r.up_shard
    gathers = []
    for layer in range(layers):
        first = [qkv_shard[layer], r.proj_shard.at[layer]]
        second = [up_shard[layer], r.w_down.at[layer]]
        for part, (srcs, dsts) in enumerate(((first, (r.wq, r.wp)), (second, (r.wu, r.wd)))):
            job = DpGather()
            job.bind(srcs, [one[layer] for one in dsts], r.gather_sems[2 * layer + part])
            gathers.append(job)
    arrived = greet_all()
    r.state[...] = r.tokens[...].astype(f32)
    r.message[...] = jnp.zeros_like(r.message)
    arrived()
    swaps = [
        PieceSwap(
            [(r.qkv_cols[n], r.qkv_shard[n]), (r.up_cols[n], r.up_shard[n])],
            r.swap_send[n],
            r.swap_recv[n],
        )
        for n in range(len(r.qkv_cols))
    ]
    if lead:
        permutes = [
            Permute(
                r.w_proj.at[n], r.proj_shard.at[n], r.permute_send.at[n], r.permute_recv.at[n], False
            )
            for n in range(layers)
        ]
        permutes[0].start()
        swaps[0].start()
        moves = modulations_start(
            r.rows_in,
            r.ada_in,
            r.rows,
            r.columns,
            (r.dp_send, r.dp_recv, r.ada_send, r.ada_recv, r.ada_local),
        )
        swaps[0].finish()
        permutes[0].finish()
        gathers[0].start_far()
        gathers[0].start_near()
        for one in moves:
            one.wait()
        replies = modulations_answer(
            r.rows, r.columns, r.answers, r.quarters, (r.answer_send, r.answer_recv)
        )
        for one in permutes[1:]:
            one.start()
        share = Share(r.quarters, r.share_send, r.share_recv)
        for one in replies:
            one.wait()
        share.start()
        share.forward()
        gathers[0].step(0)
        share.finish()
        slots = r.answers.shape[1]
        wide = r.answers.shape[2]
        each = ada.shape[2]
        for i in range(dps * blks):
            value = r.quarters[i % blks, i // blks]
            layer, at = (i * wide) // each, (i * wide) % each
            high = value.astype(bf16)
            ada[layer, 0:slots, at : at + wide] = high
            ada[layer, slots : 2 * slots, at : at + wide] = (value - high.astype(f32)).astype(bf16)
    else:
        gathers[0].start_far()
        gathers[0].start_near()
        gathers[0].step(0)
    gathers[1].start_far()
    for one in swaps[-(layers - 1) :]:
        one.start()

    def need_first(layer):
        job, following = gathers[2 * layer], gathers[2 * layer + 1]
        if layer == 0:
            job.step(1)
            job.step(2)
        job.finish()
        following.start_near()

    def early(layer):
        if layer == 0:
            for one in swaps[-(layers - 1) :]:
                one.finish()
            if lead:
                for one in permutes[1:]:
                    one.finish()
        else:
            gathers[2 * layer + 1].step(0)

    def middle(layer):
        gathers[2 * layer + 1].step(0 if layer == 0 else 1)

    def late(layer):
        gathers[2 * layer + 1].step(1 if layer == 0 else 2)

    def need_second(layer):
        if layer == 0:
            gathers[1].step(2)
            for one in gathers[2:]:
                one.start_far()
        if layer + 1 < layers:
            gathers[2 * layer + 2].start_near()
        gathers[2 * layer + 1].finish()

    def weights(ref, rows):
        return ref.reshape(rows, ref.shape[-1])

    pending = []
    saver = Moves(r.save_sems)
    width = r.state.shape[1]
    for layer in range(layers):
        last = layer + 1 == layers
        attend_segment(
            Hooks(
                need=partial(need_first, layer),
                a=partial(early, layer),
                b=partial(middle, layer),
                c=partial(late, layer),
            ),
            size,
            r.state,
            r.onehot,
            ada.at[layer],
            r.qscale.at[layer],
            r.keyc,
            r.keyr,
            (weights(r.wq[layer], width), weights(r.wp[layer], width // 4)),
            (r.wqkv, r.wproj),
            (r.h.at[layer], r.qkv.at[layer], r.rates.at[layer]),
            r.inverse.at[layer],
            r.branch_buf,
            r.middle,
            (r.qkv_buf, r.vt, r.rate_buf, r.o_buf),
            (r.gamma, r.scale, r.shift),
            r.moves.at[2 * layer],
            exchange_set(r, 0),
        )
        for one in pending:
            one.wait()
        pending = [
            saver.copy(r.o_buf, r.o.at[layer]),
            saver.copy(r.branch_buf, r.branch.at[layer]),
            saver.copy(r.middle, r.mids.at[layer]),
        ]
        if last:
            return partial(need_second, layer), pending
        hooks = Hooks(need=partial(need_second, layer))
        hooks.a, hooks.b, hooks.c = [partial(gathers[2 * layer + 2].step, i) for i in range(3)]
        mlp_segment(
            hooks,
            r.middle,
            r.onehot,
            ada.at[layer],
            (weights(r.wu[layer], width), weights(r.wd[layer], width)),
            (r.wup, r.wdown),
            (r.h2.at[layer], r.g.at[layer], r.slope.at[layer]),
            r.result_buf,
            r.state,
            (r.hidden, r.slope_buf),
            (r.gamma, r.scale, r.shift),
            r.moves.at[2 * layer + 1],
            exchange_set(r, 1),
        )
        for one in pending:
            one.wait()
        pending = [saver.copy(r.result_buf, r.result.at[layer]), saver.copy(r.state, r.states.at[layer])]


def declare_forward(n, tokens, onehot, keyc, keyr, qscale, w_down, proj, qkv_cols, up_cols, rows_in, ada_in, ada, qkv_shard, up_shard):
    lead = ada_in is not None
    dps, blks = sizes()
    count = dps * blks
    rows, width = tokens.shape
    layers = proj.shape[0]
    length = rows * blks
    wide, ff = qkv_cols[0].shape[2], up_cols[0].shape[2]
    sems = pltpu.SemaphoreType.DMA
    vars(n.ins).update(
        tokens=(tokens, VMEM), onehot=(onehot, VMEM), keyc=(keyc, VMEM), keyr=(keyr, VMEM), qscale=(qscale, VMEM)
    )
    n.ins.w_down = (w_down, ANY)
    low = partial(shaped, dtype=bf16)
    if lead:
        vars(n.ins).update(rows_in=(rows_in, ANY), ada_in=(ada_in, ANY), w_proj=(proj, ANY))
        slots = rows_in.shape[0]
        columns = ada_in.shape[2]
        vars(n.outs).update(
            rows=(low(dps, slots, width), VMEM),
            proj_shard=(low(*proj.shape), ANY),
        )
        vars(n.scratch).update(
            ada=pltpu.VMEM((layers, 2 * slots, count * columns // layers), bf16),
            answers=pltpu.VMEM((dps, slots, columns), f32),
            quarters=pltpu.VMEM((blks, dps, slots, columns), f32),
            dp_send=sems((dps,)),
            dp_recv=sems((dps,)),
            answer_send=sems((dps,)),
            answer_recv=sems((dps,)),
            ada_send=sems((count,)),
            ada_recv=sems((count,)),
            ada_local=sems((2,)),
            share_send=sems((3,)),
            share_recv=sems((3,)),
            permute_send=sems((layers,)),
            permute_recv=sems((layers,)),
        )
    else:
        vars(n.ins).update(
            ada=(ada, VMEM), rows=(rows_in, VMEM), proj_shard=(proj, ANY), qkv_first=(qkv_shard, ANY), up_first=(up_shard, ANY)
        )
    moved_qkv, moved_up = (one if lead else one[1:] for one in (qkv_cols, up_cols))
    n.ins.qkv_cols = [(one, ANY) for one in moved_qkv]
    n.ins.up_cols = [(one, ANY) for one in moved_up]
    n.outs.qkv_shard = [(low(*one.shape), ANY) for one in moved_qkv]
    n.outs.up_shard = [(low(*one.shape), ANY) for one in moved_up]
    n.scratch.swap_send = [sems((2, 4)) for _ in moved_qkv]
    n.scratch.swap_recv = [sems((2, 4)) for _ in moved_qkv]
    n.outs.wq = [(low(dps, *one.shape), ANY) for one in qkv_cols]
    n.outs.wp = [(low(dps, *proj.shape[1:]), ANY)] * layers
    n.outs.wu = [(low(dps, *one.shape), ANY) for one in up_cols]
    n.outs.wd = [(low(dps, *w_down.shape[1:]), ANY)] * layers
    n.scratch.gather_sems = [[sems((2, dps)), sems((2, dps)), sems((2,))] for _ in range(2 * layers)]
    vars(n.outs).update(
        output=(low(rows, width), VMEM),
        h=(low(layers, length, width), ANY),
        qkv=(low(layers, length, wide), ANY),
        rates=(shaped(layers, length, 2 * TILE), ANY),
        o=(low(layers, length, TILE), ANY),
        branch=(shaped(layers, rows, width), ANY),
        mids=(shaped(layers, rows, width), ANY),
        h2=(low(layers, length, width), ANY),
        g=(low(layers, length, ff), ANY),
        slope=(low(layers, length, ff), ANY),
        result=(shaped(layers, rows, width), ANY),
        states=(shaped(layers, rows, width), ANY),
    )
    vars(n.scratch).update(
        shift=pltpu.VMEM((rows, width), f32),
        inverse=pltpu.VMEM((layers, 4, 8, TILE), f32),
        moves=sems((2 * layers, 5)),
        save_sems=sems((5 * layers,)),
    )
    return n


def backward_part(layers, size, r, need_top, pending):
    dps, blks = sizes()
    d, b = place()
    width = r.grad.shape[1]
    rows = r.w_ada.shape[1]
    people = r.cond.shape[1]
    value = r.rows[...].astype(f32)
    value = (value / (1.0 + jnp.exp(-value))).astype(bf16).reshape(people, width)
    line = lax.broadcasted_iota(jnp.int32, (rows, width), 0) + flat_place() * rows
    own_columns = (line == lax.broadcasted_iota(jnp.int32, (rows, width), 1)).astype(bf16)
    r.cond[...] = mm_t(own_columns, value).astype(bf16)

    wides, narrows, swaps, permutes, items = {}, {}, {}, {}, {}
    r.dadas = r.near_dada + r.far_dadas
    for n in range(layers):
        wides[n], narrows[n] = DpScatter(), DpScatter()
        shared = r.wide
        wides[n].bind([r.dwu[n], r.dwd[n]], [r.up_sum[n], r.down_grad.at[n]], shared)
        shared = r.narrow
        narrows[n].bind([r.dwq[n], r.dwp[n]], [r.qkv_sum[n], r.proj_sum[n]], shared)
        for k, (src, dst) in enumerate(((r.up_sum, r.up_grad), (r.qkv_sum, r.qkv_grad))):
            swaps[k, n] = PieceSwap(
                [(src[n], dst.at[n])], r.back_swap_send.at[2 * n + k], r.back_swap_recv.at[2 * n + k]
            )
        permutes[n] = Permute(
            r.proj_sum[n], r.proj_grad.at[n], r.back_permute_send.at[n], r.back_permute_recv.at[n], True
        )
        for part in range(2):
            at = 2 * n + part
            items[n, part] = Items(r.items[at], r.dadas[at], r.items_scratch[at])

    def fold(layer, part):
        dada = r.dadas[2 * layer + part]
        if layer or part or not r.near_dada:
            load = pltpu.make_async_copy(dada, r.dada, r.dada_sem)
            load.start()
            load.wait()
            dada = r.dada
        quarter = dada.shape[3]
        total = r.message[0:rows, :]
        for c in range(0, 3 * width, TILE):
            at = (c // width) * 2 * width + part * width + c % width
            inner = c % quarter
            value = dada[c // quarter, :, :, inner : inner + TILE].reshape(people, TILE)
            r.ada_grad[layer, :, at : at + TILE] = mm(r.cond[...], value)
            total = total + mm_t(r.w_ada[layer, :, at : at + TILE], value)
        r.message[0:rows, :] = total

    def wide_done(n):
        wides[n].finish()
        swaps[0, n].start()
        if n:
            wides[n].release(r.credit.at[0])

    def narrow_done(n):
        narrows[n].finish()
        swaps[1, n].start()
        permutes[n].start()
        if n:
            narrows[n].release(r.credit.at[1])

    def weights(ref, count):
        return ref.reshape(count, ref.shape[-1])

    wide = 3 * TILE
    length = 4 * TILE
    for layer in reversed(range(layers)):
        top = layer + 1 == layers
        above = layer + 1

        def begin_mlp():
            if not top:
                items[above, 0].start()

        def late_mlp():
            if not top:
                narrows[above].step(2)
                items[above, 0].sum()

        def done_mlp():
            if not top:
                wide_done(above)
                wides[layer].acquire(r.credit.at[0])
            wides[layer].start()

        hooks = Hooks(start=begin_mlp, c=late_mlp, dw=done_mlp)
        if not top:
            hooks.sent = wides[above].own
            hooks.a, hooks.b = [partial(narrows[above].step, i) for i in range(2)]
        ff = r.slope.shape[2]
        if top:

            def need():
                need_top()
                for one in pending:
                    one.wait()

            hooks.need = need
            mlp_top_segment(
                hooks,
                r.dmid,
                r.grad,
                r.onehot,
                r.onehot_t,
                r.ada.at[layer],
                r.cotangent,
                (weights(r.wu[layer], width), weights(r.wd[layer], ff)),
                (r.wup, r.wdown),
                (weights(r.dwu[layer], width), weights(r.dwd[layer], ff)),
                r.load_b,
                r.shift,
                r.items[2 * layer + 1],
                (r.hidden, r.du, r.dwup, r.dwdown),
                (r.gamma, r.scale, r.shift),
                (r.dgamma, r.dscale, r.dshift),
                r.back_moves.at[2 * layer],
                exchange_set(r, 1),
                exchange_set(r, 0),
                r.credit.at[2],
            )
            r.output[...] = r.shift[...].astype(bf16)
        else:
            mlp_back_segment(
                hooks,
                r.grad,
                r.onehot,
                r.onehot_t,
                r.ada.at[layer],
                (
                    weights(r.wu[layer], width),
                    weights(r.wd[layer], ff),
                    r.h2.at[layer],
                    r.g.at[layer],
                    r.slope.at[layer],
                    r.result.at[layer],
                    r.mids.at[layer],
                ),
                (weights(r.dwu[layer], width), weights(r.dwd[layer], ff)),
                r.dmid,
                r.items[2 * layer + 1],
                (r.wup, r.wdown, r.hall, r.gall, r.du, r.dwup, r.dwdown, r.load_a, r.load_b),
                (r.gamma, r.scale),
                (r.dgamma, r.dscale, r.dshift),
                r.back_moves.at[2 * layer],
                exchange_set(r, 0),
            )

        def begin_attend():
            items[layer, 1].start()

        def sent_attend():
            if not top:
                narrows[above].own()
                items[above, 1].spread()

        def second_attend():
            wides[layer].step(1)
            if not top:
                narrow_done(above)

        def late_attend():
            wides[layer].step(2)
            items[layer, 1].sum()
            if not top:
                items[above, 1].forward()

        def done_attend():
            if not top:
                narrows[layer].acquire(r.credit.at[1])
            narrows[layer].start()
            if not top:
                items[above, 1].finish()
                fold(above, 1)
                items[above, 0].spread()

        attend_back_segment(
            Hooks(
                start=begin_attend,
                sent=sent_attend,
                a=partial(wides[layer].step, 0),
                b=second_attend,
                d=late_attend,
                dw=done_attend,
            ),
            size,
            r.dmid,
            r.onehot,
            r.onehot_t,
            r.ada.at[layer],
            r.qscale.at[layer],
            r.keyc,
            r.keyr,
            r.inverse.at[layer],
            (
                weights(r.wq[layer], width),
                weights(r.wp[layer], TILE),
                r.h.at[layer],
                r.qkv.at[layer],
                r.rates.at[layer],
                r.o.at[layer],
                r.branch.at[layer],
                r.states.at[layer - 1] if layer else None,
            ),
            (weights(r.dwq[layer], width), weights(r.dwp[layer], TILE)),
            r.grad,
            r.items[2 * layer],
            r.heads.at[layer],
            (
                r.wup.at[:, 0:wide],
                r.wdown.at[0:TILE],
                r.hall,
                r.gall.at[:, 0:wide],
                r.rates_buf,
                r.gall.at[:, wide : wide + TILE],
                r.dwdown.at[TILE : 2 * TILE],
                r.dkeys,
                r.dvalues,
                r.du.at[:, 0:wide],
                r.dwup.at[:, 0:wide],
                r.dwdown.at[0:TILE],
                r.load_a,
                r.load_b if layer else r.tokens,
            ),
            (r.gamma, r.scale),
            (r.dgamma, r.dscale, r.dshift),
            r.back_moves.at[2 * layer + 1],
            exchange_set(r, 1),
        )
    items[0, 0].start()
    r.tokens_grad[...] = r.grad[...].astype(bf16)
    items[1, 0].forward()
    items[0, 0].sum()
    items[0, 1].spread()
    wides[0].own()
    narrows[0].step(0)
    items[1, 0].finish()
    fold(1, 0)
    items[0, 1].forward()
    items[0, 0].spread()
    narrows[0].step(1)
    items[0, 1].finish()
    fold(0, 1)
    items[0, 0].forward()
    narrows[0].step(2)
    items[0, 0].finish()
    fold(0, 0)
    message = r.message
    message[rows:, :] = r.notes[...]
    lane = lax.broadcasted_iota(jnp.int32, (TILE, people), 0)
    pick = (lane == lax.broadcasted_iota(jnp.int32, (TILE, people), 1) * size).astype(bf16)
    for layer in range(layers):
        message[rows + layer : rows + layer + 1, :] = split_three(r.heads[layer], pick)
    told = [
        remote(message, r.heard.at[b, d], r.told_send.at[k], r.told_recv.at[k], ((d + k) % dps, b))
        for k in range(1, dps)
    ]
    told.append(pltpu.make_async_copy(message, r.heard.at[b, d], r.told_send.at[0]))
    for one in told:
        one.start()
    narrows[0].own()
    wide_done(0)
    for one in told:
        one.wait()
    share = Share(r.heard, r.back_share_send, r.back_share_recv)
    share.start()
    share.forward()
    narrow_done(0)
    share.finish()
    for one in list(swaps.values()) + list(permutes.values()):
        one.finish()


def split_three(values, ones):
    high = values.astype(bf16)
    rest = values - high.astype(f32)
    low = rest.astype(bf16)
    least = (rest - low.astype(f32)).astype(bf16)
    return mm(high, ones) + (mm(low, ones) + mm(least, ones))


def declare_backward(n, layers, cotangent, w_ada, onehot_t, notes, wide, ff):
    dps, blks = sizes()
    rows, width = cotangent.shape
    length = rows * blks
    wrows = w_ada.shape[1]
    slots, people = onehot_t.shape[0], notes.shape[1]
    sems = pltpu.SemaphoreType.DMA
    low = partial(shaped, dtype=bf16)
    vars(n.ins).update(
        cotangent=(cotangent, VMEM), w_ada=(w_ada, VMEM), onehot_t=(onehot_t, VMEM), notes=(notes, VMEM)
    )
    pairs = dps // 2

    def scatter_scratch(shapes):
        found = []
        for shape in shapes:
            found += [pltpu.VMEM((pairs, *shape), bf16)] * 3
            found += [sems((2 * pairs,)), sems((2 * pairs,)), sems((pairs,))]
        return found

    quarter = 3 * width // 4
    whole = (4, dps, slots, quarter)
    sets = 2 * layers
    n.outs.dwu = [(low(dps, blks * wrows, ff), ANY)] * layers
    n.outs.dwd = [(low(dps, ff // dps, width), ANY)] * layers
    n.outs.dwq = [(low(dps, blks * wrows, wide), ANY)] * layers
    n.outs.dwp = [(low(dps, TILE // dps, width), ANY)] * layers
    near = [pltpu.VMEM(whole, bf16)] if people <= 128 else []
    n.outs.far_dadas = [(low(*whole), ANY)] * (sets - len(near))
    n.scratch.near_dada = near
    n.scratch.dada = pltpu.VMEM(whole, bf16)
    n.scratch.dada_sem = sems
    n.scratch.up_sum = [pltpu.VMEM((blks, wrows, ff), bf16)] * layers
    n.scratch.qkv_sum = [pltpu.VMEM((blks, wrows, wide), bf16)] * layers
    n.scratch.proj_sum = [pltpu.VMEM((TILE // dps, width), f32)] * layers
    n.scratch.items = [pltpu.VMEM((slots, 3 * width), f32)] * sets
    n.scratch.items_scratch = [
        [
            pltpu.VMEM((4, slots, quarter), f32),
            pltpu.VMEM((1, slots, quarter), bf16),
            sems((8,)),
            sems((7,)),
            sems((dps,)),
            sems((dps,)),
        ]
    ] * sets
    n.scratch.wide = scatter_scratch([(blks * wrows, ff), (ff // dps, width)])
    n.scratch.narrow = scatter_scratch([(blks * wrows, wide), (TILE // dps, width)])
    vars(n.outs).update(
        tokens_grad=(low(rows, width), VMEM),
        ada_grad=(shaped(layers, wrows, 6 * width), VMEM),
        up_grad=(low(layers, blks, wrows, ff), ANY),
        qkv_grad=(low(layers, blks, wrows, wide), ANY),
        proj_grad=(shaped(layers, TILE // dps, width), ANY),
        down_grad=(shaped(layers, ff // dps, width), VMEM),
        heard=(shaped(blks, dps, wrows + 8, people), ANY),
    )
    big, small = pltpu.VMEM((rows, width), f32), pltpu.VMEM((rows, width), bf16)
    vars(n.scratch).update(
        grad=big,
        dmid=big,
        load_a=big,
        load_b=big,
        gamma=big,
        scale=big,
        dgamma=small,
        dscale=small,
        dshift=small,
        wup=pltpu.VMEM((width, ff), bf16),
        wdown=pltpu.VMEM((ff, width), bf16),
        hall=pltpu.VMEM((length, width), bf16),
        gall=pltpu.VMEM((length, ff), bf16),
        du=pltpu.VMEM((length, ff), bf16),
        dwup=pltpu.VMEM((width, ff), bf16),
        dwdown=pltpu.VMEM((ff, width), bf16),
        rates_buf=pltpu.VMEM((length, 2 * TILE), f32),
        dkeys=pltpu.VMEM((length, TILE), f32),
        dvalues=pltpu.VMEM((length, TILE), f32),
        heads=pltpu.VMEM((layers, 1, TILE), f32),
        message=pltpu.VMEM((wrows + 8, people), f32),
        cond=pltpu.VMEM((wrows, people), bf16),
        back_moves=sems((2 * layers, 10)),
        credit=pltpu.SemaphoreType.REGULAR((3,)),
        back_permute_send=sems((layers,)),
        back_permute_recv=sems((layers,)),
        told_send=sems((dps,)),
        told_recv=sems((dps,)),
        back_share_send=sems((3,)),
        back_share_recv=sems((3,)),
    )
    n.scratch.back_swap_send = sems((2 * layers, 1, 4))
    n.scratch.back_swap_recv = sems((2 * layers, 1, 4))
    add_exchanges(n, width)


ANY = pl.BlockSpec(memory_space=pl.ANY)
VMEM = pl.BlockSpec(memory_space=pltpu.VMEM)


def shaped(*shape, dtype=f32):
    return jax.ShapeDtypeStruct(shape, dtype)


def per_device(
    tokens,
    cotangent,
    stop_scale,
    labels,
    class_table,
    head_scale,
    w_qkv,
    w_proj,
    w_up,
    w_down,
    w_ada,
):
    rows, width = tokens.shape[1:]
    layers, heads = head_scale.shape
    size = width // heads
    dps, blks = sizes()
    count = dps * blks
    length = rows * blks
    d, b = place()
    own_heads = heads // blks
    piece = own_heads * size
    wrows = w_qkv.shape[1]
    ffrows = w_down.shape[1]
    ff = ffrows * dps
    slots = labels.shape[1]
    padded = 16

    item_all, level_all = token_meta(stop_scale[0], length)
    item_own = lax.dynamic_slice_in_dim(item_all, b * rows, rows)
    key = (item_all * 16 + level_all).reshape(blks, rows)
    sib = b + 1 - 2 * (b % 2)
    far, far_sib = (b + 2) % 4, (sib + 2) % 4
    key = jnp.concatenate(
        [key[b], key[sib], key[far, :HALF], key[far_sib, :HALF], key[far, HALF:], key[far_sib, HALF:]]
    )
    keyc, keyr = key[:, None], key.reshape(4, 1, TILE)
    slot_id = jnp.arange(padded, dtype=jnp.int32)
    onehot_t = (slot_id[:, None] == item_own[None, :]).astype(bf16)
    onehot = (item_own[:, None] == jnp.concatenate([slot_id, slot_id])[None, :]).astype(bf16)

    names = jnp.pad(labels[0], (0, padded - slots), constant_values=-1)

    def one_hot(names):
        return (names[:, None] == jnp.arange(class_table.shape[0], dtype=jnp.int32)[None, :]).astype(bf16)

    wide = w_ada.shape[2]
    columns = layers * wide // count
    ada_cols = w_ada.transpose(1, 0, 2).reshape(wrows, count, columns).transpose(1, 0, 2)
    qkv_cols = w_qkv.reshape(layers, wrows, 3, blks, piece).transpose(0, 3, 1, 2, 4)
    qkv_cols = qkv_cols.reshape(layers, blks, wrows, 3 * piece)
    up_cols = w_up.reshape(layers, wrows, dps, blks, ffrows).transpose(0, 3, 1, 2, 4)
    up_cols = up_cols.reshape(layers, blks, wrows, ff)
    class_rows = mm(one_hot(names), class_table).astype(bf16)
    own_scale = lax.dynamic_slice_in_dim(head_scale, b * own_heads, own_heads, axis=1)
    qscales = jnp.repeat(jnp.exp(own_scale), size, axis=1)
    common = (tokens[0], onehot, keyc, keyr, qscales[:, None, :], w_down)
    qkv_list, up_list = [qkv_cols[i] for i in range(layers)], [up_cols[i] for i in range(layers)]
    n = Names()
    lead = columns % 128 == 0 and wrows % 16 == 0
    if lead:
        declare_forward(n, *common, w_proj, qkv_list, up_list, class_rows, ada_cols, None, None, None)
    else:
        to_heads = [(i, (i % dps) * blks + i // dps) for i in range(count)]
        proj_own = lax.ppermute(w_proj, ("dp", "blk"), to_heads)
        class_rows = gather(class_rows, "dp")
        cond_all = jax.nn.silu(class_rows.astype(f32)).astype(bf16)
        ada_cols = lax.all_to_all(ada_cols, ("dp", "blk"), 0, 0, tiled=True)
        ada_part = mm(cond_all, ada_cols.reshape(count * wrows, columns))
        ada_part = lax.all_to_all(ada_part.reshape(dps, padded, columns), "dp", 0, 0, tiled=True)
        ada_all = lax.all_gather(ada_part, "blk", axis=1, tiled=False)
        ada_all = ada_all.transpose(2, 0, 1, 3).reshape(padded, layers, wide).transpose(1, 0, 2)
        ada_high = ada_all.astype(bf16)
        ada_low = (ada_all - ada_high.astype(f32)).astype(bf16)
        ada = jnp.concatenate([ada_high, ada_low], axis=1)
        qkv_shard = lax.all_to_all(qkv_cols[0], "blk", 0, 0, tiled=True)
        up_shard = lax.all_to_all(up_cols[0], "blk", 0, 0, tiled=True)
        rows_all = class_rows.reshape(dps, padded, width)
        declare_forward(n, *common, proj_own, qkv_list, up_list, rows_all, None, ada, qkv_shard, up_shard)
    lanes = dps * padded
    notes = jnp.pad(names.astype(f32)[None, :], ((layers, 7 - layers), (0, lanes - padded)))
    declare_backward(n, layers, cotangent[0], w_ada, onehot_t, notes, 3 * piece, ff)
    grads = n.call(partial(whole_kernel, lead, layers, size), 8, 60)
    output = grads.output[None]
    if lead:
        class_rows = grads.rows.reshape(dps * padded, width)
    one = grads.qkv_grad.reshape(layers, blks, wrows, 3, piece)
    qkv_grad = one.transpose(0, 2, 3, 1, 4).reshape(layers, wrows, 3 * width).astype(f32)
    one = grads.up_grad.reshape(layers, blks, wrows, dps, ffrows)
    up_grad = one.transpose(0, 2, 3, 1, 4).reshape(layers, wrows, ff * blks).astype(f32)
    told = grads.heard
    head_grad = jnp.sum(told[:, :, wrows : wrows + layers, :own_heads], axis=1)
    head_grad = head_grad.transpose(1, 0, 2).reshape(layers, heads)
    every_name = told[0, :, wrows + layers, :padded].reshape(-1).astype(jnp.int32)
    cond_grad = told[:, :, :wrows, :].transpose(1, 0, 2, 3).reshape(width, lanes).T
    _, silu_pull = jax.vjp(jax.nn.silu, class_rows.astype(f32))
    cond_pre = silu_pull(cond_grad)[0]
    pre_high = cond_pre.astype(bf16)
    pre_low = (cond_pre - pre_high.astype(f32)).astype(bf16)
    chosen = one_hot(jnp.concatenate([every_name, every_name]))
    table_grad = rows_mm(chosen, jnp.concatenate([pre_high, pre_low]))
    return (
        output,
        grads.tokens_grad[None],
        table_grad,
        head_grad,
        qkv_grad,
        grads.proj_grad,
        up_grad,
        grads.down_grad,
        grads.ada_grad,
    )


def solution(mesh):
    in_specs = (
        P("dp", "blk", None),
        P("dp", "blk", None),
        P("dp", None),
        P("dp", None),
        P(),
        P(),
        P(None, ("dp", "blk"), None),
        P(None, ("dp", "blk"), None),
        P(None, ("dp", "blk"), None),
        P(None, ("dp", "blk"), None),
        P(None, ("dp", "blk"), None),
    )
    out_specs = (
        P("dp", "blk", None),
        P("dp", "blk", None),
        P(),
        P(),
        P(None, ("dp", "blk"), None),
        P(None, ("dp", "blk"), None),
        P(None, ("dp", "blk"), None),
        P(None, ("dp", "blk"), None),
        P(None, ("dp", "blk"), None),
    )
    return jax.shard_map(
        per_device, mesh=mesh, in_specs=in_specs, out_specs=out_specs, check_vma=False
    )
```

```python
from functools import partial
from types import SimpleNamespace

import jax
import jax.numpy as jnp
from jax import lax
from jax.experimental import pallas as pl
from jax.experimental.pallas import tpu as pltpu
from jax.sharding import PartitionSpec as P

patch_areas = (1, 4, 9, 16, 25, 36, 64, 100, 169)
scale_starts = (1, 5, 14, 30, 55, 91, 155, 255)
f32 = jnp.float32
bf16 = jnp.bfloat16
MESH = pl.DeviceIdType.MESH
TILE = 256
HALF = 128
STEP = 32


def sizes():
    return lax.axis_size("dp"), lax.axis_size("blk")


def place():
    return lax.axis_index("dp"), lax.axis_index("blk")


def flat_place():
    return place()[0] * sizes()[1] + place()[1]


def token_meta(stops, length):
    areas = jnp.array(patch_areas, dtype=jnp.int32)
    levels = jnp.arange(9, dtype=jnp.int32)
    counts = jnp.sum(jnp.where(levels[None, :] < stops[:, None], areas[None, :], 0), axis=1)
    ends = jnp.cumsum(counts)
    places = jnp.arange(length, dtype=jnp.int32)
    passed = places[:, None] >= ends[None, :]
    item = jnp.sum(passed.astype(jnp.int32), axis=1)
    begin = jnp.sum(jnp.where(passed, counts[None, :], 0), axis=1)
    inner = places - begin
    bounds = jnp.array(scale_starts, dtype=jnp.int32)
    level = jnp.sum((inner[:, None] >= bounds[None, :]).astype(jnp.int32), axis=1)
    level = jnp.where(item == stops.shape[0], 0, level)
    return (item, level)


def mm(left, right):
    return jnp.dot(left, right, preferred_element_type=f32)


def mm_t(left, right):
    return lax.dot_general(left, right, (((1,), (1,)), ((), ())), preferred_element_type=f32)


def rows_mm(left, right, precision=None):
    return lax.dot_general(
        left, right, (((0,), (0,)), ((), ())), precision=precision, preferred_element_type=f32
    )


def gather(values, axes):
    return lax.all_gather(values, axes, axis=0, tiled=True)


def scatter(values, axes):
    return lax.psum_scatter(values, axes, scatter_dimension=0, tiled=True)


def partners():
    d, b = place()
    return (d, b + 1 - 2 * (b % 2)), (d, (b + 2) % 4)


def greet(others):
    barrier = pltpu.get_barrier_semaphore()
    for other in others:
        pl.semaphore_signal(barrier, inc=1, device_id=other, device_id_type=MESH)
    return lambda: pl.semaphore_wait(barrier, len(others))


def greet_all():
    dps, blks = sizes()
    me = flat_place()
    others = [(me + k) % (dps * blks) for k in range(1, dps * blks)]
    return greet([(t // blks, t % blks) for t in others])


def remote(src, dst, send, recv, target):
    return pltpu.make_async_remote_copy(
        src_ref=src, dst_ref=dst, send_sem=send, recv_sem=recv, device_id=target, device_id_type=MESH
    )


class Spread:
    def __init__(self, buf, send, recv, sibling, peer):
        def copy(src, dst, k, target):
            return remote(
                buf.at[pl.ds(src, HALF)], buf.at[pl.ds(dst, HALF)], send.at[k], recv.at[k], target
            )

        self.to_peer = [copy(HALF * c, 2 * TILE + TILE * c, c, peer) for c in range(2)]
        self.to_sibling = [copy(HALF * c, TILE + HALF * c, 2 + c, sibling) for c in range(2)]
        self.forward = [
            copy(2 * TILE + TILE * c, 2 * TILE + TILE * c + HALF, 4 + c, sibling) for c in range(2)
        ]

    def start(self, c):
        self.to_peer[c].start()
        self.to_sibling[c].start()

    def wait_block(self, i):
        @pl.when(i == 1)
        def _():
            for c in range(2):
                self.to_sibling[c].wait_recv()

        for c in range(2):

            @pl.when(i == 2 + c)
            def _():
                self.to_peer[c].wait_recv()
                self.forward[c].start()
                self.forward[c].wait_recv()

    def ready(self):
        for c in range(2):
            self.to_sibling[c].wait_recv()
        for c in range(2):
            self.to_peer[c].wait_recv()
            self.forward[c].start()
        for c in range(2):
            self.forward[c].wait_recv()

    def finish(self):
        for c in range(2):
            self.to_peer[c].wait_send()
            self.to_sibling[c].wait_send()
            self.forward[c].wait_send()


class Collect:
    def __init__(self, parts, out, mid, own, far, send, recv, sibling, peer):
        self.parts, self.out, self.mid, self.own, self.far = parts, out, mid, own, far
        self.cross = [
            remote(
                parts.at[pl.ds(2 * TILE + TILE * c + HALF, HALF)],
                mid.at[pl.ds(HALF * c, HALF)],
                send.at[c],
                recv.at[c],
                sibling,
            )
            for c in range(2)
        ]
        self.over = [
            remote(
                out.at[pl.ds(HALF * c, HALF)],
                far.at[pl.ds(HALF * c, HALF)],
                send.at[2 + c],
                recv.at[2 + c],
                peer,
            )
            for c in range(2)
        ]
        self.home = remote(parts.at[pl.ds(TILE, TILE)], own, send.at[4], recv.at[4], sibling)

    def block_done(self, j):
        for c in range(2):

            @pl.when(j == 2 + c)
            def _():
                self.cross[c].start()
                self.cross[c].wait_recv()

                @pl.loop(0, HALF // STEP)
                def _(s):
                    at = pl.multiple_of(s * STEP, STEP)
                    mine = self.parts[pl.ds(2 * TILE + TILE * c + at, STEP), :].astype(f32)
                    theirs = self.mid[pl.ds(HALF * c + at, STEP), :].astype(f32)
                    self.out[pl.ds(HALF * c + at, STEP), :] = (mine + theirs).astype(bf16)

                self.over[c].start()

        @pl.when(j == 1)
        def _():
            self.home.start()

    def wait(self):
        self.home.wait_recv()
        for c in range(2):
            self.over[c].wait_recv()

    def rows(self, at):
        span = pl.ds(at, STEP)
        total = self.parts[span, :].astype(f32) + self.own[span, :].astype(f32)
        return total + self.far[span, :].astype(f32)

    def sent(self):
        self.home.wait_send()
        for c in range(2):
            self.cross[c].wait_send()

    def over_sent(self):
        for c in range(2):
            self.over[c].wait_send()

    def finish(self):
        self.sent()
        self.over_sent()


def spread_scratch(width):
    return [
        pltpu.VMEM((4 * TILE, width), bf16),
        pltpu.SemaphoreType.DMA((6,)),
        pltpu.SemaphoreType.DMA((6,)),
    ]


def collect_scratch(width):
    return [pltpu.VMEM((4 * TILE, width), bf16)] + [pltpu.VMEM((TILE, width), bf16)] * 4 + [
        pltpu.SemaphoreType.DMA((5,)),
        pltpu.SemaphoreType.DMA((5,)),
    ]


class Moves:
    def __init__(self, sems):
        self.sems, self.used = sems, 0

    def copy(self, src, dst):
        made = pltpu.make_async_copy(src, dst, self.sems.at[self.used])
        self.used += 1
        made.start()
        return made


def expand(onehot, ada, which, outs):
    width = outs[0].shape[1]
    for k, out in zip(which, outs):
        for n in range(0, width, TILE):
            out[:, n : n + TILE] = mm(onehot[...], ada[:, k * width + n : k * width + n + TILE])


def normed(values):
    centre = jnp.mean(values, axis=-1, keepdims=True)
    centred = values - centre
    spread = jnp.mean(centred * centred, axis=-1, keepdims=True)
    rate = lax.rsqrt(spread + 1e-06)
    return centred * rate, rate


def norm_back(grad, values_hat, rate):
    first = jnp.mean(grad, axis=-1, keepdims=True)
    second = jnp.mean(grad * values_hat, axis=-1, keepdims=True)
    return rate * (grad - first - values_hat * second)


def row_steps(start, rows, body):
    @pl.loop(0, rows // STEP)
    def _(s):
        body(pl.multiple_of(start + s * STEP, STEP))


def block_ones(size):
    shape = (TILE, TILE)
    one = lax.broadcasted_iota(jnp.int32, shape, 0) // size
    two = lax.broadcasted_iota(jnp.int32, shape, 1) // size
    return (one == two).astype(bf16)


def split_mm(dot, values, ones):
    high = values.astype(bf16)
    low = (values - high.astype(f32)).astype(bf16)
    return dot(high, ones) + dot(low, ones)


def head_lanes(values, h, size):
    lane = lax.broadcasted_iota(jnp.int32, values.shape, 1) // size
    return jnp.where(lane == h, values, jnp.zeros_like(values))


def hidden_bias(keyc, keyr, rows, cols):
    keys = keyc[pl.ds(rows, TILE), :]
    top = keyr[cols]
    low = top - top % 16
    return jnp.where((keys >= low) & (keys <= top), 0.0, -1e30)


def nothing():
    pass


class Hooks:
    def __init__(self, **table):
        self.start = self.sent = self.need = self.a = self.b = self.c = self.d = self.dw = nothing
        vars(self).update(table)


def modulate_rows(x, scale, shift, hbuf, spread):
    def modulated(at):
        span = pl.ds(at, STEP)
        hat, _ = normed(x[span, :])
        hbuf[span, :] = (hat * (1.0 + scale[span, :]) + shift[span, :]).astype(bf16)

    for c in range(2):
        row_steps(HALF * c, HALF, modulated)
        spread.start(c)


def exchange(refs):
    hbuf, ag_send, ag_recv, parts, out, mid, own, far, rs_send, rs_recv = refs
    sibling, peer = partners()
    spread = Spread(hbuf, ag_send, ag_recv, sibling, peer)
    collect = Collect(parts, out, mid, own, far, rs_send, rs_recv, sibling, peer)
    return hbuf, parts, spread, collect


def attend_segment(
    hooks,
    size,
    x,
    onehot,
    ada,
    qscale,
    keyc,
    keyr,
    weights_in,
    weights,
    saves_out,
    inv_out,
    branch_out,
    mid_out,
    held,
    mods,
    moves,
    refs,
):
    qkv, vt, rates, o_out = held
    gamma, scale, shift = mods
    wqkv, wproj = weights
    hbuf, parts, spread, collect = exchange(refs)
    mover = Moves(moves)
    expand(onehot, ada, (0, 2, 4), (gamma, scale, shift))
    modulate_rows(x, scale, shift, hbuf, spread)
    hooks.need()
    load_qkv = mover.copy(weights_in[0], wqkv)
    load_proj = mover.copy(weights_in[1], wproj)
    load_qkv.wait()
    ones = block_ones(size)

    @pl.loop(0, 4)
    def _(i):
        spread.wait_block(i)
        span = pl.ds(pl.multiple_of(i * TILE, TILE), TILE)
        h = hbuf[span, :]
        for part in range(3):
            columns = slice(part * TILE, (part + 1) * TILE)
            value = mm(h, wqkv[:, columns])
            if part < 2:
                rate = lax.rsqrt(split_mm(mm, value * value, ones) + 1e-06)
                if part == 0:
                    rate = rate * qscale[...]
                rates[span, columns] = rate
                value = value * rate
            else:
                vt[:, span] = value.T.astype(bf16)
            qkv[span, columns] = value.astype(bf16)

    hooks.a()
    saves = [mover.copy(a, b) for a, b in zip((hbuf, qkv, rates), saves_out)]
    load_proj.wait()
    heads = TILE // size

    @pl.loop(0, 4)
    def _(i):
        j = (i + 2) % 4
        span = pl.ds(pl.multiple_of(j * TILE, TILE), TILE)
        queries = [head_lanes(qkv[span, 0:TILE], h, size) for h in range(heads)]
        sums = [jnp.zeros((1, TILE), f32)] * heads
        mixed = [jnp.zeros((size, TILE), f32)] * heads
        for k in range(4):
            keys = qkv[k * TILE : (k + 1) * TILE, TILE : 2 * TILE]
            bias = hidden_bias(keyc, keyr, k * TILE, j)
            for h in range(heads):
                grown = jnp.exp(mm_t(keys, queries[h]) + bias)
                sums[h] = sums[h] + jnp.sum(grown, axis=0, keepdims=True)
                mixed[h] = mixed[h] + mm(
                    vt[h * size : (h + 1) * size, k * TILE : (k + 1) * TILE], grown.astype(bf16)
                )
        inverse = [1.0 / one for one in sums]
        for h in range(heads):
            inv_out[j, h : h + 1, :] = inverse[h]
        whole = jnp.concatenate([mixed[h] * inverse[h] for h in range(heads)], axis=0)
        low = whole.T.astype(bf16)
        o_out[span, :] = low
        for n in range(0, parts.shape[1], TILE):
            parts[span, n : n + TILE] = mm(low, wproj[:, n : n + TILE]).astype(bf16)
        collect.block_done(j)

    hooks.b()
    collect.wait()
    hooks.c()

    def added(at):
        span = pl.ds(at, STEP)
        branch = collect.rows(at)
        branch_out[span, :] = branch
        mid_out[span, :] = x[span, :] + gamma[span, :] * branch

    row_steps(0, TILE, added)
    spread.finish()
    collect.finish()
    for one in saves:
        one.wait()


def mlp_block(h, span, wup, wdown, hidden, slope, parts):
    for n in range(0, wup.shape[1], TILE):
        columns = slice(n, n + TILE)
        up = mm(h, wup[:, columns])
        square = up * up
        bent = jnp.tanh(0.7978845608 * (up * (1.0 + 0.044715 * square)))
        half = 0.5 * (1.0 + bent)
        hidden[span, columns] = (up * half).astype(bf16)
        inner = 0.7978845608 + (3.0 * 0.044715 * 0.7978845608) * square
        slope[span, columns] = (half + 0.5 * up * (1.0 - bent * bent) * inner).astype(bf16)
    g = hidden[span, :]
    for n in range(0, parts.shape[1], TILE):
        parts[span, n : n + TILE] = mm(g, wdown[:, n : n + TILE]).astype(bf16)


def mlp_segment(
    hooks, x, onehot, ada, weights_in, weights, saves_out, result_out, x_out, held, mods, moves, refs
):
    hidden, slope = held
    gamma, scale, shift = mods
    wup, wdown = weights
    hbuf, parts, spread, collect = exchange(refs)
    mover = Moves(moves)
    expand(onehot, ada, (1, 3, 5), (gamma, scale, shift))
    modulate_rows(x, scale, shift, hbuf, spread)
    hooks.need()
    loads = [mover.copy(a, b) for a, b in zip(weights_in, weights)]
    for one in loads:
        one.wait()

    @pl.loop(0, 4)
    def _(i):
        spread.wait_block(i)
        for at, hook in ((2, hooks.a), (3, hooks.b)):

            @pl.when(i == at)
            def _():
                hook()

        span = pl.ds(pl.multiple_of(i * TILE, TILE), TILE)
        h = hbuf[span, :]
        mlp_block(h, span, wup, wdown, hidden, slope, parts)
        collect.block_done(i)

    hooks.c()
    saves = [mover.copy(a, b) for a, b in zip((hbuf, hidden, slope), saves_out)]
    collect.wait()

    def added(at):
        span = pl.ds(at, STEP)
        result = collect.rows(at)
        result_out[span, :] = result
        x_out[span, :] = x[span, :] + gamma[span, :] * result

    row_steps(0, TILE, added)
    spread.finish()
    collect.finish()
    for one in saves:
        one.wait()


def item_sums(onehot_t, terms, out):
    for k, term in enumerate(terms):
        width = term.shape[1]
        out[:, k * width : (k + 1) * width] = mm(onehot_t[...], term[...])


def scaled_rows(x, gamma, hbuf, spread):
    def scaled(at):
        span = pl.ds(at, STEP)
        hbuf[span, :] = (gamma[span, :] * x[span, :]).astype(bf16)

    for c in range(2):
        row_steps(HALF * c, HALF, scaled)
        spread.start(c)


def back_rows(collect, x, grad, branch, scale, terms, out):
    dgamma, dscale, dshift = terms

    def added(at):
        span = pl.ds(at, STEP)
        dh = collect.rows(at)
        hat, rate = normed(x[span, :])
        above = grad[span, :]
        dgamma[span, :] = (above * branch[span, :]).astype(bf16)
        dscale[span, :] = (dh * hat).astype(bf16)
        dshift[span, :] = dh.astype(bf16)
        out[span, :] = above + norm_back(dh * (1.0 + scale[span, :]), hat, rate)

    row_steps(0, TILE, added)


def mlp_back_block(dm, span, wup, wdown, slope, parts):
    for n in range(0, slope.shape[1], TILE):
        columns = slice(n, n + TILE)
        dg = mm_t(dm, wdown[columns, :])
        slope[span, columns] = (dg * slope[span, columns].astype(f32)).astype(bf16)
    du = slope[span, :]
    for n in range(0, parts.shape[1], TILE):
        parts[span, n : n + TILE] = mm_t(du, wup[n : n + TILE, :]).astype(bf16)


def mlp_weight_grads(mover, hall, gall, dm, du, dwup, dwdown, outs):
    @pl.loop(0, gall.shape[1] // TILE)
    def _(k):
        columns = pl.ds(pl.multiple_of(k * TILE, TILE), TILE)
        for n in range(0, dm.shape[1], 2 * TILE):
            dwdown[columns, n : n + 2 * TILE] = rows_mm(
                gall[:, columns], dm[:, n : n + 2 * TILE]
            ).astype(bf16)

    save_down = mover.copy(dwdown, outs[1])

    @pl.loop(0, hall.shape[1] // TILE)
    def _(k):
        columns = pl.ds(pl.multiple_of(k * TILE, TILE), TILE)
        for n in range(0, du.shape[1], 2 * TILE):
            dwup[columns, n : n + 2 * TILE] = rows_mm(
                hall[:, columns], du[:, n : n + 2 * TILE]
            ).astype(bf16)

    save_up = mover.copy(dwup, outs[0])
    save_down.wait()
    save_up.wait()


def mlp_top_segment(
    hooks, x, dx, onehot, onehot_t, ada, cotangent, weights_in, weights, outs, result, x_out, items, held, mods, terms, moves, refs, back_refs, free
):
    hidden, du, dwup, dwdown = held
    gamma, scale, shift = mods
    wup, wdown = weights
    dgamma, _, dshift = terms
    refs = refs[:4] + [dgamma] + refs[5:]
    hbuf, parts, spread, collect = exchange(refs)
    back_hbuf, _, back_spread, back_collect = exchange(back_refs)
    mover = Moves(moves)
    expand(onehot, ada, (1, 3, 5), (gamma, scale, shift))
    modulate_rows(x, scale, shift, hbuf, spread)
    dx[...] = cotangent[...].astype(f32)
    spread.ready()
    scaled_rows(dx, gamma, back_hbuf, back_spread)
    hooks.need()
    loads = [mover.copy(a, b) for a, b in zip(weights_in, weights)]
    for one in loads:
        one.wait()

    @pl.loop(0, 4)
    def _(i):
        span = pl.ds(pl.multiple_of(i * TILE, TILE), TILE)
        mlp_block(hbuf[span, :], span, wup, wdown, hidden, du, parts)
        collect.block_done(i)

    collect.sent()
    dshift[...] = parts[0:TILE, :]

    @pl.loop(0, 4)
    def _(i):
        back_spread.wait_block(i)
        span = pl.ds(pl.multiple_of(i * TILE, TILE), TILE)
        mlp_back_block(back_hbuf[span, :], span, wup, wdown, du, parts)
        back_collect.block_done(i)

    mlp_weight_grads(mover, hbuf, hidden, back_hbuf, du, dwup, dwdown, outs)
    spread.finish()
    for other in partners():
        pl.semaphore_signal(free, inc=1, device_id=other, device_id_type=MESH)
    hooks.dw()
    collect.wait()
    collect.over_sent()

    def added(at):
        span = pl.ds(at, STEP)
        total = dshift[span, :].astype(f32) + collect.own[span, :].astype(f32)
        total = total + collect.far[span, :].astype(f32)
        result[span, :] = total
        x_out[span, :] = x[span, :] + gamma[span, :] * total

    row_steps(0, TILE, added)
    back_collect.wait()
    back_rows(back_collect, x, dx, result, scale, terms, x)
    item_sums(onehot_t, terms, items)
    back_spread.finish()
    back_collect.finish()
    pl.semaphore_wait(free, 2)


def mlp_back_segment(
    hooks, dx, onehot, onehot_t, ada, ins, outs, dmid, items, held, mods, terms, moves, refs
):
    wup_in, wdown_in, h_in, g_in, slope_in, result_in, mid_in = ins
    wup, wdown, hall, gall, slope, dwup, dwdown, result, mid_state = held
    gamma, scale = mods
    hbuf, parts, spread, collect = exchange(refs)
    mover = Moves(moves)
    load_down = mover.copy(wdown_in, wdown)
    load_slope = mover.copy(slope_in, slope)
    load_up = mover.copy(wup_in, wup)
    later = [mover.copy(g_in, gall), mover.copy(h_in, hall)]
    later += [mover.copy(result_in, result), mover.copy(mid_in, mid_state)]
    expand(onehot, ada, (1, 3), (gamma, scale))
    hooks.start()
    scaled_rows(dx, gamma, hbuf, spread)
    hooks.sent()
    for one in (load_down, load_slope, load_up):
        one.wait()

    @pl.loop(0, 4)
    def _(i):
        spread.wait_block(i)
        for at, hook in ((2, hooks.a), (3, hooks.b)):

            @pl.when(i == at)
            def _():
                hook()

        span = pl.ds(pl.multiple_of(i * TILE, TILE), TILE)
        dm = hbuf[span, :]
        mlp_back_block(dm, span, wup, wdown, slope, parts)
        collect.block_done(i)

    hooks.c()
    for one in later:
        one.wait()

    mlp_weight_grads(mover, hall, gall, hbuf, slope, dwup, dwdown, outs)
    hooks.dw()
    collect.wait()
    back_rows(collect, mid_state, dx, result, scale, terms, dmid)
    item_sums(onehot_t, terms, items)
    spread.finish()
    collect.finish()


def attend_back_segment(
    hooks,
    size,
    dmid,
    onehot,
    onehot_t,
    ada,
    qscale,
    keyc,
    keyr,
    inverse,
    ins,
    outs,
    dx,
    items,
    head_out,
    held,
    mods,
    terms,
    moves,
    refs,
):
    wqkv_in, wproj_in, h_in, qkv_in, rate_in, o_in, branch_in, x_in = ins
    wqkv, wproj, hall, qkv, rates, oall, kt, dkeys, dvalues, dqkv, dwqkv, dwproj, branch, x = held
    gamma, scale = mods
    hbuf, parts, spread, collect = exchange(refs)
    mover = Moves(moves)
    loads = [mover.copy(wproj_in, wproj), mover.copy(qkv_in, qkv)]
    loads += [mover.copy(o_in, oall), mover.copy(rate_in, rates)]
    load_w = mover.copy(wqkv_in, wqkv)
    later = [mover.copy(h_in, hall), mover.copy(branch_in, branch)]
    if x_in is not None:
        later.append(mover.copy(x_in, x))
    expand(onehot, ada, (0, 2), (gamma, scale))
    hooks.start()
    scaled_rows(dmid, gamma, hbuf, spread)
    hooks.sent()
    for one in loads:
        one.wait()
    heads = TILE // size
    ones = block_ones(size)
    inv_square = 1.0 / (qscale[...] * qscale[...])
    select = (
        lax.broadcasted_iota(jnp.int32, (8, TILE), 1) // size
        == lax.broadcasted_iota(jnp.int32, (8, TILE), 0)
    ).astype(bf16)
    dkeys[...] = jnp.zeros_like(dkeys)
    dvalues[...] = jnp.zeros_like(dvalues)
    head_out[...] = jnp.zeros_like(head_out)
    for k in range(4):
        rows = slice(k * TILE, (k + 1) * TILE)
        kt[:, rows] = qkv[rows, TILE : 2 * TILE].astype(f32).T.astype(bf16)

    @pl.loop(0, 4)
    def _(i):
        spread.wait_block(i)
        for at, hook in ((2, hooks.a), (3, hooks.b)):

            @pl.when(i == at)
            def _():
                hook()

        span = pl.ds(pl.multiple_of(i * TILE, TILE), TILE)
        dout = mm_t(hbuf[span, :], wproj[...]).astype(bf16)
        product = dout.astype(f32) * oall[span, :].astype(f32)
        row_term = split_mm(lambda a, b: mm_t(b, a), product, select)
        q_low = qkv[span, 0:TILE]
        queries = [head_lanes(q_low, h, size) for h in range(heads)]
        douts = [head_lanes(dout, h, size) for h in range(heads)]
        dquery = [jnp.zeros((size, TILE), f32)] * heads
        for k in range(4):
            rows = slice(k * TILE, (k + 1) * TILE)
            keys = qkv[rows, TILE : 2 * TILE]
            values = qkv[rows, 2 * TILE : 3 * TILE]
            bias = hidden_bias(keyc, keyr, k * TILE, i)
            dkey = jnp.zeros((TILE, TILE), f32)
            dvalue = jnp.zeros((TILE, TILE), f32)
            for h in range(heads):
                share = jnp.exp(mm_t(keys, queries[h]) + bias) * inverse[i, h : h + 1, :]
                dshare = mm_t(values, douts[h])
                dscore = (share * (dshare - row_term[h : h + 1, :])).astype(bf16)
                dvalue = dvalue + mm(share.astype(bf16), douts[h])
                dkey = dkey + mm(dscore, queries[h])
                dquery[h] = dquery[h] + mm(kt[h * size : (h + 1) * size, rows], dscore)
            dkeys[rows, :] += dkey
            dvalues[rows, :] += dvalue
        dq = jnp.concatenate(dquery, axis=0).T
        qhat = q_low.astype(f32)
        along = split_mm(mm, dq * qhat, ones)
        head_out[...] += jnp.sum(along, axis=0, keepdims=True)
        dqkv[span, 0:TILE] = (rates[span, 0:TILE] * (dq - qhat * (along * inv_square))).astype(bf16)

    load_w.wait()
    hooks.c()

    @pl.loop(0, 4)
    def _(i):
        j = (i + 2) % 4
        span = pl.ds(pl.multiple_of(j * TILE, TILE), TILE)
        dk = dkeys[span, :]
        khat = qkv[span, TILE : 2 * TILE].astype(f32)
        along = split_mm(mm, dk * khat, ones)
        dqkv[span, TILE : 2 * TILE] = (
            rates[span, TILE : 2 * TILE] * (dk - khat * along)
        ).astype(bf16)
        dqkv[span, 2 * TILE : 3 * TILE] = dvalues[span, :].astype(bf16)
        low = dqkv[span, :]
        for n in range(0, parts.shape[1], TILE):
            parts[span, n : n + TILE] = mm_t(low, wqkv[n : n + TILE, :]).astype(bf16)
        collect.block_done(j)

    hooks.d()
    for n in range(0, hbuf.shape[1], 2 * TILE):
        dwproj[:, n : n + 2 * TILE] = rows_mm(oall[...], hbuf[:, n : n + 2 * TILE]).astype(bf16)
    save_proj = mover.copy(dwproj, outs[1])
    for one in later:
        one.wait()

    @pl.loop(0, hall.shape[1] // TILE)
    def _(k):
        columns = pl.ds(pl.multiple_of(k * TILE, TILE), TILE)
        dwqkv[columns, :] = rows_mm(hall[:, columns], dqkv[...]).astype(bf16)

    save_w = mover.copy(dwqkv, outs[0])
    save_proj.wait()
    save_w.wait()
    hooks.dw()
    collect.wait()
    back_rows(collect, x, dmid, branch, scale, terms, dx)
    item_sums(onehot_t, terms, items)
    spread.finish()
    collect.finish()


def groups(dps):
    d, b = place()
    side, pairs = d % 2, dps // 2
    pair = d // 2
    ahead = [((pair + k) % pairs) * 2 + side for k in range(pairs)]
    behind = [((pair - k + pairs) % pairs) * 2 + side for k in range(pairs)]
    return d, b, d + 1 - 2 * side, ahead, behind


class DpGather:
    def __init__(self):
        self.dps = sizes()[0]

    def bind(self, ins, outs, scratch):
        send, recv, local = scratch
        d, b, other, ahead, behind = groups(self.dps)
        pairs = self.dps // 2
        self.partners = [(other, b)] + [(t, b) for t in ahead[1:]]
        self.first, self.direct, self.forward, self.local = [], [], [], []
        for a, (src, dst) in enumerate(zip(ins, outs)):
            self.local.append(pltpu.make_async_copy(src, dst.at[d], local.at[a]))
            self.first.append(remote(src, dst.at[d], send.at[a, 0], recv.at[a, 0], (other, b)))
            self.direct.append([None])
            self.forward.append([None])
            for k in range(1, pairs):
                self.direct[a].append(
                    remote(src, dst.at[d], send.at[a, k], recv.at[a, k], (ahead[k], b))
                )
                at = pairs + k
                self.forward[a].append(
                    remote(
                        dst.at[behind[k]], dst.at[behind[k]], send.at[a, at], recv.at[a, at], (other, b)
                    )
                )
        self.order = [(k, a) for k in range(1, pairs) for a in range(len(ins))]

    def start_far(self):
        for k, a in self.order:
            self.direct[a][k].start()
        for one in self.local:
            one.start()

    def start_near(self):
        for one in self.first:
            one.start()

    def step(self, hook, hooks=3):
        low, high = (len(self.order) * hook) // hooks, (len(self.order) * (hook + 1)) // hooks
        for k, a in self.order[low:high]:
            self.direct[a][k].wait_recv()
            self.forward[a][k].start()

    def finish(self):
        for one in self.local:
            one.wait()
        for one in self.first:
            one.wait()
        for k, a in self.order:
            self.direct[a][k].wait_send()
            self.forward[a][k].wait()


class DpScatter:
    def __init__(self):
        self.dps = sizes()[0]

    def bind(self, ins, outs, scratch):
        d, b, other, ahead, behind = groups(self.dps)
        pairs = self.dps // 2
        self.partners = [(other, b)] + [(t, b) for t in ahead[1:]]
        self.results = outs
        self.bufs, self.local, self.cross, self.direct = [], [], [], []
        for a, src in enumerate(ins):
            mine, near, far, send, recv, local = scratch[6 * a : 6 * a + 6]
            self.bufs.append((mine, near, far))
            self.local.append([])
            self.cross.append([])
            self.direct.append([None])
            for k in range(pairs):
                target = ahead[k]
                theirs = target + 1 - 2 * (target % 2)
                self.local[a].append(
                    pltpu.make_async_copy(src.at[target], mine.at[k], local.at[k])
                )
                self.cross[a].append(
                    remote(src.at[theirs], near.at[k], send.at[k], recv.at[k], (other, b))
                )
                if k:
                    at = pairs + k
                    self.direct[a].append(
                        remote(mine.at[k], far.at[k], send.at[at], recv.at[at], (target, b))
                    )
        self.order = [(k, a) for k in range(1, pairs) for a in range(len(ins))]
        self.last = [(0, a) for a in range(len(ins))]

    def start(self):
        for k, a in self.order + self.last:
            self.cross[a][k].start()
            self.local[a][k].start()

    def add(self, a, k):
        self.local[a][k].wait()
        self.cross[a][k].wait_recv()
        mine, near, _ = self.bufs[a]
        rows = mine.shape[1]
        step = min(rows, STEP)

        @pl.loop(0, rows // step)
        def _(s):
            span = pl.ds(pl.multiple_of(s * step, step), step)
            total = mine[k, span, :].astype(f32) + near[k, span, :].astype(f32)
            mine[k, span, :] = total.astype(bf16)

    def step(self, hook, hooks=3):
        low, high = (len(self.order) * hook) // hooks, (len(self.order) * (hook + 1)) // hooks
        for k, a in self.order[low:high]:
            self.add(a, k)
            self.direct[a][k].start()

    def own(self):
        for k, a in self.last:
            self.add(a, k)
        for k, a in self.order + self.last:
            self.cross[a][k].wait_send()

    def finish(self):
        for k, a in self.order:
            self.direct[a][k].wait()
        for a, result in enumerate(self.results):
            mine, _, far = self.bufs[a]
            step = result.shape[1] if len(result.shape) == 3 else min(mine.shape[1], STEP)

            @pl.loop(0, mine.shape[1] // step)
            def _(s):
                span = pl.ds(pl.multiple_of(s * step, step), step)
                total = mine[0, span, :].astype(f32)
                for k in range(1, self.dps // 2):
                    total = total + far[k, span, :].astype(f32)
                if len(result.shape) == 3:
                    result[s] = total.astype(result.dtype)
                else:
                    result[span, :] = total.astype(result.dtype)

    def release(self, credit):
        for other in self.partners:
            pl.semaphore_signal(credit, inc=1, device_id=other, device_id_type=MESH)

    def acquire(self, credit):
        pl.semaphore_wait(credit, len(self.partners))


class Items:
    def __init__(self, src, out, scratch):
        self.terms, self.held, send, recv, dp_send, dp_recv = scratch
        dps = sizes()[0]
        d, b = place()
        self.here, self.out = (d, b), out
        wide = self.held.shape[2]

        def quarter(i):
            return src.at[:, pl.ds(pl.multiple_of(i * wide, 128), wide)]

        self.first = [pltpu.make_async_copy(quarter(b), self.terms.at[0], send.at[0])]
        for k in range(1, 4):
            to = (b + k) % 4
            self.first.append(
                remote(quarter(to), self.terms.at[k], send.at[k], recv.at[k], (d, to))
            )
        self.over = [
            remote(self.held.at[0], out.at[b, d], dp_send.at[k], dp_recv.at[k], ((d + k) % dps, b))
            for k in range(1, dps)
        ]
        self.keep = pltpu.make_async_copy(self.held.at[0], out.at[b, d], send.at[7])
        self.share = Share(out, send.at[pl.ds(4, 3)], recv.at[pl.ds(4, 3)])

    def start(self):
        for one in self.first:
            one.start()

    def sum(self):
        d, b = self.here
        for one in self.first:
            one.wait()
        total = (self.terms[0] + self.terms[1]) + (self.terms[2] + self.terms[3])
        low = total.astype(bf16)
        self.held[0] = low
        for one in self.over + [self.keep]:
            one.start()

    def spread(self):
        for one in self.over + [self.keep]:
            one.wait()
        self.share.start()

    def forward(self):
        self.share.forward()

    def finish(self):
        self.share.finish()


class Permute:
    def __init__(self, src, dst, send, recv, back):
        dps, blks = sizes()
        d, b = place()
        owner, user = d * blks + b, b * dps + d
        self.moves = owner != user
        to = (user // blks, user % blks) if back else (owner % dps, owner // dps)
        self.away = remote(src, dst, send, recv, to)
        self.stay = pltpu.make_async_copy(src, dst, send)

    def start(self):
        @pl.when(self.moves)
        def _():
            self.away.start()

        @pl.when(jnp.logical_not(self.moves))
        def _():
            self.stay.start()

    def finish(self):
        @pl.when(self.moves)
        def _():
            self.away.wait()

        @pl.when(jnp.logical_not(self.moves))
        def _():
            self.stay.wait()


def modulations_start(rows_in, ada_in, rows_out, columns, sems):
    dp_send, dp_recv, ada_send, ada_recv, local = sems
    dps, blks = sizes()
    count = dps * blks
    d, b = place()
    me = d * blks + b
    rows = ada_in.shape[1]
    span = pl.ds(pl.multiple_of(me * rows, rows), rows)
    sends = [
        pltpu.make_async_copy(rows_in, rows_out.at[d], local.at[0]),
        pltpu.make_async_copy(ada_in.at[me], columns.at[span], local.at[1]),
    ]
    for k in range(1, dps):
        to = ((d + k) % dps, b)
        sends.append(remote(rows_in, rows_out.at[d], dp_send.at[k], dp_recv.at[k], to))
    for k in range(1, count):
        t = (me + k) % count
        to = (t // blks, t % blks)
        sends.append(remote(ada_in.at[t], columns.at[span], ada_send.at[k], ada_recv.at[k], to))
    for one in sends:
        one.start()
    return sends


def modulations_answer(rows_out, columns, answers, quarters, sems):
    send, recv = sems
    dps = sizes()[0]
    d, b = place()
    slots, wide = answers.shape[1:]
    value = rows_out[...].astype(f32)
    value = (value / (1.0 + jnp.exp(-value))).astype(bf16)
    whole = mm(value.reshape(dps * slots, rows_out.shape[2]), columns[...])
    answers[...] = whole.reshape(dps, slots, wide)
    replies = []
    for k in range(1, dps):
        to = (d + k) % dps
        replies.append(
            remote(answers.at[to], quarters.at[b, d], send.at[k], recv.at[k], (to, b))
        )
    for one in replies:
        one.start()
    quarters[b, d] = answers[d]
    return replies


class Share:
    def __init__(self, buf, send, recv):
        d, b = place()
        sibling, peer = partners()
        far = peer[1]
        self.moves = [
            remote(buf.at[b], buf.at[b], send.at[0], recv.at[0], peer),
            remote(buf.at[b], buf.at[b], send.at[1], recv.at[1], sibling),
            remote(buf.at[far], buf.at[far], send.at[2], recv.at[2], sibling),
        ]

    def start(self):
        self.moves[0].start()
        self.moves[1].start()

    def forward(self):
        self.moves[0].wait_recv()
        self.moves[2].start()

    def finish(self):
        self.moves[1].wait_recv()
        self.moves[2].wait_recv()
        for one in self.moves:
            one.wait_send()


class PieceSwap:
    def __init__(self, pairs, send, recv):
        d, b = place()
        self.sent = []
        for a, (src, dst) in enumerate(pairs):
            self.sent.append(pltpu.make_async_copy(src.at[b], dst.at[b], send.at[a, 0]))
            for k in range(1, 4):
                to = (b + k) % 4
                self.sent.append(
                    remote(src.at[to], dst.at[b], send.at[a, k], recv.at[a, k], (d, to))
                )

    def start(self):
        for one in self.sent:
            one.start()

    def finish(self):
        for one in self.sent:
            one.wait()


def flat(value):
    return [leaf for one in value for leaf in flat(one)] if isinstance(value, list) else [value]


def refill(value, leaves):
    return [refill(one, leaves) for one in value] if isinstance(value, list) else next(leaves)


class Names:
    def __init__(self):
        self.ins, self.outs, self.scratch = SimpleNamespace(), SimpleNamespace(), SimpleNamespace()

    def call(self, kernel, ident, vmem):
        ins, outs, scratch = (flat(list(vars(one).values())) for one in (self.ins, self.outs, self.scratch))

        def fill(bags, refs):
            leaves, found = iter(refs), SimpleNamespace()
            for bag in bags:
                for name, value in vars(bag).items():
                    vars(found)[name] = refill(value, leaves)
            return found

        results = pl.pallas_call(
            lambda *refs: kernel(fill((self.ins, self.outs, self.scratch), refs)),
            out_shape=[one for one, _ in outs],
            in_specs=[where for _, where in ins],
            out_specs=[where for _, where in outs],
            scratch_shapes=scratch,
            compiler_params=pltpu.CompilerParams(
                collective_id=ident, has_side_effects=True, vmem_limit_bytes=vmem * 2**20
            ),
            cost_estimate=pl.CostEstimate(flops=2**36, bytes_accessed=2**26, transcendentals=0),
        )(*[one for one, _ in ins])
        return fill((self.outs,), results)


def add_exchanges(names, width):
    names.scratch.spreads = [spread_scratch(width) for _ in range(2)]
    names.scratch.parts, names.scratch.out = collect_scratch(width)[:2]
    names.scratch.collects = [collect_scratch(width)[2:] for _ in range(2)]


def exchange_set(r, turn):
    return r.spreads[turn] + [r.parts, r.out] + r.collects[turn]


def whole_kernel(lead, layers, size, r):
    wide = 3 * TILE
    r.wqkv, r.wproj = r.wup.at[:, 0:wide], r.wdown.at[0:TILE]
    r.qkv_buf, r.o_buf = r.gall.at[:, 0:wide], r.gall.at[:, wide : wide + TILE]
    r.vt, r.rate_buf = r.dwdown.at[TILE : 2 * TILE], r.rates_buf
    r.hidden, r.slope_buf = r.dwup, r.du
    r.state, r.middle, r.branch_buf, r.result_buf = r.grad, r.dmid, r.load_a, r.load_b
    if lead:
        r.columns = r.hall.at[:, 0 : r.ada_in.shape[2]]
    need_top, pending = forward_part(lead, layers, size, r)
    backward_part(layers, size, r, need_top, pending)


def forward_part(lead, layers, size, r):
    dps, blks = sizes()
    d, b = place()
    sibling, peer = partners()
    ada = r.ada
    qkv_shard = r.qkv_shard if lead else [r.qkv_first] + r.qkv_shard
    up_shard = r.up_shard if lead else [r.up_first] + r.up_shard
    gathers = []
    for layer in range(layers):
        first = [qkv_shard[layer], r.proj_shard.at[layer]]
        second = [up_shard[layer], r.w_down.at[layer]]
        for part, (srcs, dsts) in enumerate(((first, (r.wq, r.wp)), (second, (r.wu, r.wd)))):
            job = DpGather()
            job.bind(srcs, [one[layer] for one in dsts], r.gather_sems[2 * layer + part])
            gathers.append(job)
    arrived = greet_all()
    r.state[...] = r.tokens[...].astype(f32)
    r.message[...] = jnp.zeros_like(r.message)
    arrived()
    swaps = [
        PieceSwap(
            [(r.qkv_cols[n], r.qkv_shard[n]), (r.up_cols[n], r.up_shard[n])],
            r.swap_send[n],
            r.swap_recv[n],
        )
        for n in range(len(r.qkv_cols))
    ]
    if lead:
        permutes = [
            Permute(
                r.w_proj.at[n], r.proj_shard.at[n], r.permute_send.at[n], r.permute_recv.at[n], False
            )
            for n in range(layers)
        ]
        permutes[0].start()
        swaps[0].start()
        moves = modulations_start(
            r.rows_in,
            r.ada_in,
            r.rows,
            r.columns,
            (r.dp_send, r.dp_recv, r.ada_send, r.ada_recv, r.ada_local),
        )
        swaps[0].finish()
        permutes[0].finish()
        gathers[0].start_far()
        gathers[0].start_near()
        for one in moves:
            one.wait()
        replies = modulations_answer(
            r.rows, r.columns, r.answers, r.quarters, (r.answer_send, r.answer_recv)
        )
        for one in permutes[1:]:
            one.start()
        share = Share(r.quarters, r.share_send, r.share_recv)
        for one in replies:
            one.wait()
        share.start()
        share.forward()
        gathers[0].step(0)
        share.finish()
        slots = r.answers.shape[1]
        wide = r.answers.shape[2]
        each = ada.shape[2]
        for i in range(dps * blks):
            value = r.quarters[i % blks, i // blks]
            layer, at = (i * wide) // each, (i * wide) % each
            high = value.astype(bf16)
            ada[layer, 0:slots, at : at + wide] = high
            ada[layer, slots : 2 * slots, at : at + wide] = (value - high.astype(f32)).astype(bf16)
    else:
        gathers[0].start_far()
        gathers[0].start_near()
        gathers[0].step(0)
    gathers[1].start_far()
    for one in swaps[-(layers - 1) :]:
        one.start()

    def need_first(layer):
        job, following = gathers[2 * layer], gathers[2 * layer + 1]
        if layer == 0:
            job.step(1)
            job.step(2)
        job.finish()
        following.start_near()

    def early(layer):
        if layer == 0:
            for one in swaps[-(layers - 1) :]:
                one.finish()
            if lead:
                for one in permutes[1:]:
                    one.finish()
        else:
            gathers[2 * layer + 1].step(0)

    def middle(layer):
        gathers[2 * layer + 1].step(0 if layer == 0 else 1)

    def late(layer):
        gathers[2 * layer + 1].step(1 if layer == 0 else 2)

    def need_second(layer):
        if layer == 0:
            gathers[1].step(2)
            for one in gathers[2:]:
                one.start_far()
        if layer + 1 < layers:
            gathers[2 * layer + 2].start_near()
        gathers[2 * layer + 1].finish()

    def weights(ref, rows):
        return ref.reshape(rows, ref.shape[-1])

    pending = []
    saver = Moves(r.save_sems)
    width = r.state.shape[1]
    for layer in range(layers):
        last = layer + 1 == layers
        attend_segment(
            Hooks(
                need=partial(need_first, layer),
                a=partial(early, layer),
                b=partial(middle, layer),
                c=partial(late, layer),
            ),
            size,
            r.state,
            r.onehot,
            ada.at[layer],
            r.qscale.at[layer],
            r.keyc,
            r.keyr,
            (weights(r.wq[layer], width), weights(r.wp[layer], width // 4)),
            (r.wqkv, r.wproj),
            (r.h.at[layer], r.qkv.at[layer], r.rates.at[layer]),
            r.inverse.at[layer],
            r.branch_buf,
            r.middle,
            (r.qkv_buf, r.vt, r.rate_buf, r.o_buf),
            (r.gamma, r.scale, r.shift),
            r.moves.at[2 * layer],
            exchange_set(r, 0),
        )
        for one in pending:
            one.wait()
        pending = [
            saver.copy(r.o_buf, r.o.at[layer]),
            saver.copy(r.branch_buf, r.branch.at[layer]),
            saver.copy(r.middle, r.mids.at[layer]),
        ]
        if last:
            return partial(need_second, layer), pending
        hooks = Hooks(need=partial(need_second, layer))
        hooks.a, hooks.b, hooks.c = [partial(gathers[2 * layer + 2].step, i) for i in range(3)]
        mlp_segment(
            hooks,
            r.middle,
            r.onehot,
            ada.at[layer],
            (weights(r.wu[layer], width), weights(r.wd[layer], width)),
            (r.wup, r.wdown),
            (r.h2.at[layer], r.g.at[layer], r.slope.at[layer]),
            r.result_buf,
            r.state,
            (r.hidden, r.slope_buf),
            (r.gamma, r.scale, r.shift),
            r.moves.at[2 * layer + 1],
            exchange_set(r, 1),
        )
        for one in pending:
            one.wait()
        pending = [saver.copy(r.result_buf, r.result.at[layer]), saver.copy(r.state, r.states.at[layer])]


def declare_forward(n, tokens, onehot, keyc, keyr, qscale, w_down, proj, qkv_cols, up_cols, rows_in, ada_in, ada, qkv_shard, up_shard):
    lead = ada_in is not None
    dps, blks = sizes()
    count = dps * blks
    rows, width = tokens.shape
    layers = proj.shape[0]
    length = rows * blks
    wide, ff = qkv_cols[0].shape[2], up_cols[0].shape[2]
    sems = pltpu.SemaphoreType.DMA
    vars(n.ins).update(
        tokens=(tokens, VMEM), onehot=(onehot, VMEM), keyc=(keyc, VMEM), keyr=(keyr, VMEM), qscale=(qscale, VMEM)
    )
    n.ins.w_down = (w_down, ANY)
    low = partial(shaped, dtype=bf16)
    if lead:
        vars(n.ins).update(rows_in=(rows_in, ANY), ada_in=(ada_in, ANY), w_proj=(proj, ANY))
        slots = rows_in.shape[0]
        columns = ada_in.shape[2]
        vars(n.outs).update(
            rows=(low(dps, slots, width), VMEM),
            proj_shard=(low(*proj.shape), ANY),
        )
        vars(n.scratch).update(
            ada=pltpu.VMEM((layers, 2 * slots, count * columns // layers), bf16),
            answers=pltpu.VMEM((dps, slots, columns), f32),
            quarters=pltpu.VMEM((blks, dps, slots, columns), f32),
            dp_send=sems((dps,)),
            dp_recv=sems((dps,)),
            answer_send=sems((dps,)),
            answer_recv=sems((dps,)),
            ada_send=sems((count,)),
            ada_recv=sems((count,)),
            ada_local=sems((2,)),
            share_send=sems((3,)),
            share_recv=sems((3,)),
            permute_send=sems((layers,)),
            permute_recv=sems((layers,)),
        )
    else:
        vars(n.ins).update(
            ada=(ada, VMEM), rows=(rows_in, VMEM), proj_shard=(proj, ANY), qkv_first=(qkv_shard, ANY), up_first=(up_shard, ANY)
        )
    moved_qkv, moved_up = (one if lead else one[1:] for one in (qkv_cols, up_cols))
    n.ins.qkv_cols = [(one, ANY) for one in moved_qkv]
    n.ins.up_cols = [(one, ANY) for one in moved_up]
    n.outs.qkv_shard = [(low(*one.shape), ANY) for one in moved_qkv]
    n.outs.up_shard = [(low(*one.shape), ANY) for one in moved_up]
    n.scratch.swap_send = [sems((2, 4)) for _ in moved_qkv]
    n.scratch.swap_recv = [sems((2, 4)) for _ in moved_qkv]
    n.outs.wq = [(low(dps, *one.shape), ANY) for one in qkv_cols]
    n.outs.wp = [(low(dps, *proj.shape[1:]), ANY)] * layers
    n.outs.wu = [(low(dps, *one.shape), ANY) for one in up_cols]
    n.outs.wd = [(low(dps, *w_down.shape[1:]), ANY)] * layers
    n.scratch.gather_sems = [[sems((2, dps)), sems((2, dps)), sems((2,))] for _ in range(2 * layers)]
    vars(n.outs).update(
        output=(low(rows, width), VMEM),
        h=(low(layers, length, width), ANY),
        qkv=(low(layers, length, wide), ANY),
        rates=(shaped(layers, length, 2 * TILE), ANY),
        o=(low(layers, length, TILE), ANY),
        branch=(shaped(layers, rows, width), ANY),
        mids=(shaped(layers, rows, width), ANY),
        h2=(low(layers, length, width), ANY),
        g=(low(layers, length, ff), ANY),
        slope=(low(layers, length, ff), ANY),
        result=(shaped(layers, rows, width), ANY),
        states=(shaped(layers, rows, width), ANY),
    )
    vars(n.scratch).update(
        shift=pltpu.VMEM((rows, width), f32),
        inverse=pltpu.VMEM((layers, 4, 8, TILE), f32),
        moves=sems((2 * layers, 5)),
        save_sems=sems((5 * layers,)),
    )
    return n


def backward_part(layers, size, r, need_top, pending):
    dps, blks = sizes()
    d, b = place()
    width = r.grad.shape[1]
    rows = r.w_ada.shape[1]
    people = r.cond.shape[1]
    value = r.rows[...].astype(f32)
    value = (value / (1.0 + jnp.exp(-value))).astype(bf16).reshape(people, width)
    line = lax.broadcasted_iota(jnp.int32, (rows, width), 0) + flat_place() * rows
    own_columns = (line == lax.broadcasted_iota(jnp.int32, (rows, width), 1)).astype(bf16)
    r.cond[...] = mm_t(own_columns, value).astype(bf16)

    wides, narrows, swaps, permutes, items = {}, {}, {}, {}, {}
    r.dadas = r.near_dada + r.far_dadas
    for n in range(layers):
        wides[n], narrows[n] = DpScatter(), DpScatter()
        shared = r.wide
        wides[n].bind([r.dwu[n], r.dwd[n]], [r.up_sum[n], r.down_grad.at[n]], shared)
        shared = r.narrow
        narrows[n].bind([r.dwq[n], r.dwp[n]], [r.qkv_sum[n], r.proj_sum[n]], shared)
        for k, (src, dst) in enumerate(((r.up_sum, r.up_grad), (r.qkv_sum, r.qkv_grad))):
            swaps[k, n] = PieceSwap(
                [(src[n], dst.at[n])], r.back_swap_send.at[2 * n + k], r.back_swap_recv.at[2 * n + k]
            )
        permutes[n] = Permute(
            r.proj_sum[n], r.proj_grad.at[n], r.back_permute_send.at[n], r.back_permute_recv.at[n], True
        )
        for part in range(2):
            at = 2 * n + part
            items[n, part] = Items(r.items[at], r.dadas[at], r.items_scratch[at])

    def fold(layer, part):
        dada = r.dadas[2 * layer + part]
        if layer or part or not r.near_dada:
            load = pltpu.make_async_copy(dada, r.dada, r.dada_sem)
            load.start()
            load.wait()
            dada = r.dada
        quarter = dada.shape[3]
        total = r.message[0:rows, :]
        for c in range(0, 3 * width, TILE):
            at = (c // width) * 2 * width + part * width + c % width
            inner = c % quarter
            value = dada[c // quarter, :, :, inner : inner + TILE].reshape(people, TILE)
            r.ada_grad[layer, :, at : at + TILE] = mm(r.cond[...], value)
            total = total + mm_t(r.w_ada[layer, :, at : at + TILE], value)
        r.message[0:rows, :] = total

    def wide_done(n):
        wides[n].finish()
        swaps[0, n].start()
        if n:
            wides[n].release(r.credit.at[0])

    def narrow_done(n):
        narrows[n].finish()
        swaps[1, n].start()
        permutes[n].start()
        if n:
            narrows[n].release(r.credit.at[1])

    def weights(ref, count):
        return ref.reshape(count, ref.shape[-1])

    wide = 3 * TILE
    length = 4 * TILE
    for layer in reversed(range(layers)):
        top = layer + 1 == layers
        above = layer + 1

        def begin_mlp():
            if not top:
                items[above, 0].start()

        def late_mlp():
            if not top:
                narrows[above].step(2)
                items[above, 0].sum()

        def done_mlp():
            if not top:
                wide_done(above)
                wides[layer].acquire(r.credit.at[0])
            wides[layer].start()

        hooks = Hooks(start=begin_mlp, c=late_mlp, dw=done_mlp)
        if not top:
            hooks.sent = wides[above].own
            hooks.a, hooks.b = [partial(narrows[above].step, i) for i in range(2)]
        ff = r.slope.shape[2]
        if top:

            def need():
                need_top()
                for one in pending:
                    one.wait()

            hooks.need = need
            mlp_top_segment(
                hooks,
                r.dmid,
                r.grad,
                r.onehot,
                r.onehot_t,
                r.ada.at[layer],
                r.cotangent,
                (weights(r.wu[layer], width), weights(r.wd[layer], ff)),
                (r.wup, r.wdown),
                (weights(r.dwu[layer], width), weights(r.dwd[layer], ff)),
                r.load_b,
                r.shift,
                r.items[2 * layer + 1],
                (r.hidden, r.du, r.dwup, r.dwdown),
                (r.gamma, r.scale, r.shift),
                (r.dgamma, r.dscale, r.dshift),
                r.back_moves.at[2 * layer],
                exchange_set(r, 1),
                exchange_set(r, 0),
                r.credit.at[2],
            )
            r.output[...] = r.shift[...].astype(bf16)
        else:
            mlp_back_segment(
                hooks,
                r.grad,
                r.onehot,
                r.onehot_t,
                r.ada.at[layer],
                (
                    weights(r.wu[layer], width),
                    weights(r.wd[layer], ff),
                    r.h2.at[layer],
                    r.g.at[layer],
                    r.slope.at[layer],
                    r.result.at[layer],
                    r.mids.at[layer],
                ),
                (weights(r.dwu[layer], width), weights(r.dwd[layer], ff)),
                r.dmid,
                r.items[2 * layer + 1],
                (r.wup, r.wdown, r.hall, r.gall, r.du, r.dwup, r.dwdown, r.load_a, r.load_b),
                (r.gamma, r.scale),
                (r.dgamma, r.dscale, r.dshift),
                r.back_moves.at[2 * layer],
                exchange_set(r, 0),
            )

        def begin_attend():
            items[layer, 1].start()

        def sent_attend():
            if not top:
                narrows[above].own()
                items[above, 1].spread()

        def second_attend():
            wides[layer].step(1)

        def late_attend():
            items[layer, 1].sum()
            if not top:
                items[above, 1].forward()
                narrow_done(above)

        def done_attend():
            if not top:
                narrows[layer].acquire(r.credit.at[1])
            narrows[layer].start()
            if not top:
                items[above, 1].finish()
                fold(above, 1)
                items[above, 0].spread()

        attend_back_segment(
            Hooks(
                start=begin_attend,
                sent=sent_attend,
                a=partial(wides[layer].step, 0),
                b=second_attend,
                c=partial(wides[layer].step, 2),
                d=late_attend,
                dw=done_attend,
            ),
            size,
            r.dmid,
            r.onehot,
            r.onehot_t,
            r.ada.at[layer],
            r.qscale.at[layer],
            r.keyc,
            r.keyr,
            r.inverse.at[layer],
            (
                weights(r.wq[layer], width),
                weights(r.wp[layer], TILE),
                r.h.at[layer],
                r.qkv.at[layer],
                r.rates.at[layer],
                r.o.at[layer],
                r.branch.at[layer],
                r.states.at[layer - 1] if layer else None,
            ),
            (weights(r.dwq[layer], width), weights(r.dwp[layer], TILE)),
            r.grad,
            r.items[2 * layer],
            r.heads.at[layer],
            (
                r.wup.at[:, 0:wide],
                r.wdown.at[0:TILE],
                r.hall,
                r.gall.at[:, 0:wide],
                r.rates_buf,
                r.gall.at[:, wide : wide + TILE],
                r.dwdown.at[TILE : 2 * TILE],
                r.dkeys,
                r.dvalues,
                r.du.at[:, 0:wide],
                r.dwup.at[:, 0:wide],
                r.dwdown.at[0:TILE],
                r.load_a,
                r.load_b if layer else r.tokens,
            ),
            (r.gamma, r.scale),
            (r.dgamma, r.dscale, r.dshift),
            r.back_moves.at[2 * layer + 1],
            exchange_set(r, 1),
        )
    items[0, 0].start()
    r.tokens_grad[...] = r.grad[...].astype(bf16)
    items[1, 0].forward()
    items[0, 0].sum()
    items[0, 1].spread()
    wides[0].own()
    narrows[0].step(0)
    items[1, 0].finish()
    fold(1, 0)
    items[0, 1].forward()
    items[0, 0].spread()
    narrows[0].step(1)
    items[0, 1].finish()
    fold(0, 1)
    items[0, 0].forward()
    narrows[0].step(2)
    items[0, 0].finish()
    fold(0, 0)
    message = r.message
    message[rows:, :] = r.notes[...]
    lane = lax.broadcasted_iota(jnp.int32, (TILE, people), 0)
    pick = (lane == lax.broadcasted_iota(jnp.int32, (TILE, people), 1) * size).astype(bf16)
    for layer in range(layers):
        message[rows + layer : rows + layer + 1, :] = split_three(r.heads[layer], pick)
    told = [
        remote(message, r.heard.at[b, d], r.told_send.at[k], r.told_recv.at[k], ((d + k) % dps, b))
        for k in range(1, dps)
    ]
    told.append(pltpu.make_async_copy(message, r.heard.at[b, d], r.told_send.at[0]))
    for one in told:
        one.start()
    narrows[0].own()
    wide_done(0)
    for one in told:
        one.wait()
    share = Share(r.heard, r.back_share_send, r.back_share_recv)
    share.start()
    share.forward()
    narrow_done(0)
    share.finish()
    for one in list(swaps.values()) + list(permutes.values()):
        one.finish()


def split_three(values, ones):
    high = values.astype(bf16)
    rest = values - high.astype(f32)
    low = rest.astype(bf16)
    least = (rest - low.astype(f32)).astype(bf16)
    return mm(high, ones) + (mm(low, ones) + mm(least, ones))


def declare_backward(n, layers, cotangent, w_ada, onehot_t, notes, wide, ff):
    dps, blks = sizes()
    rows, width = cotangent.shape
    length = rows * blks
    wrows = w_ada.shape[1]
    slots, people = onehot_t.shape[0], notes.shape[1]
    sems = pltpu.SemaphoreType.DMA
    low = partial(shaped, dtype=bf16)
    vars(n.ins).update(
        cotangent=(cotangent, VMEM), w_ada=(w_ada, VMEM), onehot_t=(onehot_t, VMEM), notes=(notes, VMEM)
    )
    pairs = dps // 2

    def scatter_scratch(shapes):
        found = []
        for shape in shapes:
            found += [pltpu.VMEM((pairs, *shape), bf16)] * 3
            found += [sems((2 * pairs,)), sems((2 * pairs,)), sems((pairs,))]
        return found

    quarter = 3 * width // 4
    whole = (4, dps, slots, quarter)
    sets = 2 * layers
    n.outs.dwu = [(low(dps, blks * wrows, ff), ANY)] * layers
    n.outs.dwd = [(low(dps, ff // dps, width), ANY)] * layers
    n.outs.dwq = [(low(dps, blks * wrows, wide), ANY)] * layers
    n.outs.dwp = [(low(dps, TILE // dps, width), ANY)] * layers
    near = [pltpu.VMEM(whole, bf16)] if people <= 128 else []
    n.outs.far_dadas = [(low(*whole), ANY)] * (sets - len(near))
    n.scratch.near_dada = near
    n.scratch.dada = pltpu.VMEM(whole, bf16)
    n.scratch.dada_sem = sems
    n.scratch.up_sum = [pltpu.VMEM((blks, wrows, ff), bf16)] * layers
    n.scratch.qkv_sum = [pltpu.VMEM((blks, wrows, wide), bf16)] * layers
    n.scratch.proj_sum = [pltpu.VMEM((TILE // dps, width), f32)] * layers
    n.scratch.items = [pltpu.VMEM((slots, 3 * width), f32)] * sets
    n.scratch.items_scratch = [
        [
            pltpu.VMEM((4, slots, quarter), f32),
            pltpu.VMEM((1, slots, quarter), bf16),
            sems((8,)),
            sems((7,)),
            sems((dps,)),
            sems((dps,)),
        ]
    ] * sets
    n.scratch.wide = scatter_scratch([(blks * wrows, ff), (ff // dps, width)])
    n.scratch.narrow = scatter_scratch([(blks * wrows, wide), (TILE // dps, width)])
    vars(n.outs).update(
        tokens_grad=(low(rows, width), VMEM),
        ada_grad=(shaped(layers, wrows, 6 * width), VMEM),
        up_grad=(low(layers, blks, wrows, ff), ANY),
        qkv_grad=(low(layers, blks, wrows, wide), ANY),
        proj_grad=(shaped(layers, TILE // dps, width), ANY),
        down_grad=(shaped(layers, ff // dps, width), VMEM),
        heard=(shaped(blks, dps, wrows + 8, people), ANY),
    )
    big, small = pltpu.VMEM((rows, width), f32), pltpu.VMEM((rows, width), bf16)
    vars(n.scratch).update(
        grad=big,
        dmid=big,
        load_a=big,
        load_b=big,
        gamma=big,
        scale=big,
        dgamma=small,
        dscale=small,
        dshift=small,
        wup=pltpu.VMEM((width, ff), bf16),
        wdown=pltpu.VMEM((ff, width), bf16),
        hall=pltpu.VMEM((length, width), bf16),
        gall=pltpu.VMEM((length, ff), bf16),
        du=pltpu.VMEM((length, ff), bf16),
        dwup=pltpu.VMEM((width, ff), bf16),
        dwdown=pltpu.VMEM((ff, width), bf16),
        rates_buf=pltpu.VMEM((length, 2 * TILE), f32),
        dkeys=pltpu.VMEM((length, TILE), f32),
        dvalues=pltpu.VMEM((length, TILE), f32),
        heads=pltpu.VMEM((layers, 1, TILE), f32),
        message=pltpu.VMEM((wrows + 8, people), f32),
        cond=pltpu.VMEM((wrows, people), bf16),
        back_moves=sems((2 * layers, 10)),
        credit=pltpu.SemaphoreType.REGULAR((3,)),
        back_permute_send=sems((layers,)),
        back_permute_recv=sems((layers,)),
        told_send=sems((dps,)),
        told_recv=sems((dps,)),
        back_share_send=sems((3,)),
        back_share_recv=sems((3,)),
    )
    n.scratch.back_swap_send = sems((2 * layers, 1, 4))
    n.scratch.back_swap_recv = sems((2 * layers, 1, 4))
    add_exchanges(n, width)


ANY = pl.BlockSpec(memory_space=pl.ANY)
VMEM = pl.BlockSpec(memory_space=pltpu.VMEM)


def shaped(*shape, dtype=f32):
    return jax.ShapeDtypeStruct(shape, dtype)


def per_device(
    tokens,
    cotangent,
    stop_scale,
    labels,
    class_table,
    head_scale,
    w_qkv,
    w_proj,
    w_up,
    w_down,
    w_ada,
):
    rows, width = tokens.shape[1:]
    layers, heads = head_scale.shape
    size = width // heads
    dps, blks = sizes()
    count = dps * blks
    length = rows * blks
    d, b = place()
    own_heads = heads // blks
    piece = own_heads * size
    wrows = w_qkv.shape[1]
    ffrows = w_down.shape[1]
    ff = ffrows * dps
    slots = labels.shape[1]
    padded = 16

    item_all, level_all = token_meta(stop_scale[0], length)
    item_own = lax.dynamic_slice_in_dim(item_all, b * rows, rows)
    key = (item_all * 16 + level_all).reshape(blks, rows)
    sib = b + 1 - 2 * (b % 2)
    far, far_sib = (b + 2) % 4, (sib + 2) % 4
    key = jnp.concatenate(
        [key[b], key[sib], key[far, :HALF], key[far_sib, :HALF], key[far, HALF:], key[far_sib, HALF:]]
    )
    keyc, keyr = key[:, None], key.reshape(4, 1, TILE)
    slot_id = jnp.arange(padded, dtype=jnp.int32)
    onehot_t = (slot_id[:, None] == item_own[None, :]).astype(bf16)
    onehot = (item_own[:, None] == jnp.concatenate([slot_id, slot_id])[None, :]).astype(bf16)

    names = jnp.pad(labels[0], (0, padded - slots), constant_values=-1)

    def one_hot(names):
        return (names[:, None] == jnp.arange(class_table.shape[0], dtype=jnp.int32)[None, :]).astype(bf16)

    wide = w_ada.shape[2]
    columns = layers * wide // count
    ada_cols = w_ada.transpose(1, 0, 2).reshape(wrows, count, columns).transpose(1, 0, 2)
    qkv_cols = w_qkv.reshape(layers, wrows, 3, blks, piece).transpose(0, 3, 1, 2, 4)
    qkv_cols = qkv_cols.reshape(layers, blks, wrows, 3 * piece)
    up_cols = w_up.reshape(layers, wrows, dps, blks, ffrows).transpose(0, 3, 1, 2, 4)
    up_cols = up_cols.reshape(layers, blks, wrows, ff)
    class_rows = mm(one_hot(names), class_table).astype(bf16)
    own_scale = lax.dynamic_slice_in_dim(head_scale, b * own_heads, own_heads, axis=1)
    qscales = jnp.repeat(jnp.exp(own_scale), size, axis=1)
    common = (tokens[0], onehot, keyc, keyr, qscales[:, None, :], w_down)
    qkv_list, up_list = [qkv_cols[i] for i in range(layers)], [up_cols[i] for i in range(layers)]
    n = Names()
    lead = columns % 128 == 0 and wrows % 16 == 0
    if lead:
        declare_forward(n, *common, w_proj, qkv_list, up_list, class_rows, ada_cols, None, None, None)
    else:
        to_heads = [(i, (i % dps) * blks + i // dps) for i in range(count)]
        proj_own = lax.ppermute(w_proj, ("dp", "blk"), to_heads)
        class_rows = gather(class_rows, "dp")
        cond_all = jax.nn.silu(class_rows.astype(f32)).astype(bf16)
        ada_cols = lax.all_to_all(ada_cols, ("dp", "blk"), 0, 0, tiled=True)
        ada_part = mm(cond_all, ada_cols.reshape(count * wrows, columns))
        ada_part = lax.all_to_all(ada_part.reshape(dps, padded, columns), "dp", 0, 0, tiled=True)
        ada_all = lax.all_gather(ada_part, "blk", axis=1, tiled=False)
        ada_all = ada_all.transpose(2, 0, 1, 3).reshape(padded, layers, wide).transpose(1, 0, 2)
        ada_high = ada_all.astype(bf16)
        ada_low = (ada_all - ada_high.astype(f32)).astype(bf16)
        ada = jnp.concatenate([ada_high, ada_low], axis=1)
        qkv_shard = lax.all_to_all(qkv_cols[0], "blk", 0, 0, tiled=True)
        up_shard = lax.all_to_all(up_cols[0], "blk", 0, 0, tiled=True)
        rows_all = class_rows.reshape(dps, padded, width)
        declare_forward(n, *common, proj_own, qkv_list, up_list, rows_all, None, ada, qkv_shard, up_shard)
    lanes = dps * padded
    notes = jnp.pad(names.astype(f32)[None, :], ((layers, 7 - layers), (0, lanes - padded)))
    declare_backward(n, layers, cotangent[0], w_ada, onehot_t, notes, 3 * piece, ff)
    grads = n.call(partial(whole_kernel, lead, layers, size), 8, 60)
    output = grads.output[None]
    if lead:
        class_rows = grads.rows.reshape(dps * padded, width)
    one = grads.qkv_grad.reshape(layers, blks, wrows, 3, piece)
    qkv_grad = one.transpose(0, 2, 3, 1, 4).reshape(layers, wrows, 3 * width).astype(f32)
    one = grads.up_grad.reshape(layers, blks, wrows, dps, ffrows)
    up_grad = one.transpose(0, 2, 3, 1, 4).reshape(layers, wrows, ff * blks).astype(f32)
    told = grads.heard
    head_grad = jnp.sum(told[:, :, wrows : wrows + layers, :own_heads], axis=1)
    head_grad = head_grad.transpose(1, 0, 2).reshape(layers, heads)
    every_name = told[0, :, wrows + layers, :padded].reshape(-1).astype(jnp.int32)
    cond_grad = told[:, :, :wrows, :].transpose(1, 0, 2, 3).reshape(width, lanes).T
    _, silu_pull = jax.vjp(jax.nn.silu, class_rows.astype(f32))
    cond_pre = silu_pull(cond_grad)[0]
    pre_high = cond_pre.astype(bf16)
    pre_low = (cond_pre - pre_high.astype(f32)).astype(bf16)
    chosen = one_hot(jnp.concatenate([every_name, every_name]))
    table_grad = rows_mm(chosen, jnp.concatenate([pre_high, pre_low]))
    return (
        output,
        grads.tokens_grad[None],
        table_grad,
        head_grad,
        qkv_grad,
        grads.proj_grad,
        up_grad,
        grads.down_grad,
        grads.ada_grad,
    )


def solution(mesh):
    in_specs = (
        P("dp", "blk", None),
        P("dp", "blk", None),
        P("dp", None),
        P("dp", None),
        P(),
        P(),
        P(None, ("dp", "blk"), None),
        P(None, ("dp", "blk"), None),
        P(None, ("dp", "blk"), None),
        P(None, ("dp", "blk"), None),
        P(None, ("dp", "blk"), None),
    )
    out_specs = (
        P("dp", "blk", None),
        P("dp", "blk", None),
        P(),
        P(),
        P(None, ("dp", "blk"), None),
        P(None, ("dp", "blk"), None),
        P(None, ("dp", "blk"), None),
        P(None, ("dp", "blk"), None),
        P(None, ("dp", "blk"), None),
    )
    return jax.shard_map(
        per_device, mesh=mesh, in_specs=in_specs, out_specs=out_specs, check_vma=False
    )
```
